32 devices in a mesh: grp: 8 (over y, x, core), die: 4 (over z).
Axes of the slice: x: 2, y: 2, z: 4, core: 2. Of those that a mesh axis runs over, the one named last changes fastest.
Arguments:
- die_volt: float32 [1024, 1024], P('grp', 'die'), may hold values from -6 to 6
- die_load: float32 [1024, 1024], P('grp', 'die'), may hold values from 0.05 to 1
- die_shunt: float32 [1024, 1024], P('grp', 'die'), may hold values from 0.1 to 1
- bump_node: int32 [2048, 128], P(('grp', 'die')), may hold values from -1 to 32767, as said below
- bump_block: int32 [2048], P(('grp', 'die')), may hold values from 0 to 16383, as said below
- bump_cond: float32 [2048, 128], P(('grp', 'die')), may hold values from 0.3 to 3
- pkg_volt: float32 [16384, 128], P('die'), may hold values from -6 to 6
- pkg_diag: float32 [16384, 128], P('die'), may hold values from 4 to 6
- pkg_pattern: int32 [4, 16384], P(None, 'die'), may hold values from 0 to 16383, as said below
- pkg_weight: float32 [4, 16384], P(None, 'die'), may hold values from -0.5 to 0.5
- block_coupling: float32 [128, 128], replicated, may hold values from -0.5 to 0.5
Outputs:
- die_out: float32 [1024, 1024], P('grp', 'die')
- pkg_out: float32 [16384, 128], P('die')
- bump_out: float32 [2048, 128], P(('grp', 'die'))
The draws below stay inside these ranges and needn't reach their ends.
Inputs may be any that keep to these rules, and one draw needn't show every extreme that they name: `bump_node`: live slots of a block come first; each block has 52 or more live slots. `bump_block`: bump block j of a device (j counted within the device) targets a package block of die shard j // 16, that is a block b with b // 4096 = j // 16. pkg_pattern[k, b] lies within 32 blocks of b.
All inputs are finite; a program needn't handle non-finite values.
Results may differ from the reference program's by a relative error of at most 0.0001.
Values sent between devices are 32-bit elements; how exact they have to be, the bound alone decides.
No kernel may reach another device: no remote copies, remote signals or barrier semaphores. Data moves between devices by JAX's collectives and lax.ppermute only.
A program may use at most 64 MiB of HBM per device.

```python
import math
import jax
import jax.numpy as jnp
from jax import lax

CX = 128
CY = 256
BUMPBLK = 64
KNB = 4
RADIUS = 32
SWEEPS = 4
ITERS = 4
NX = 1024
NY = 1024
CELLS = 32768
SLOTBLK = 2048
CAP = 16
PB = 16384
PBD = 4096
N_DIE = 4


def draw_bump_node(key, part):
    key_node, key_count = jax.random.split(jax.random.fold_in(key, 11))
    chosen = jax.random.randint(key_node, (SLOTBLK, 128), 0, CELLS, dtype=jnp.int32)
    counted = jax.random.randint(key_count, (SLOTBLK, 1), 52, 129, dtype=jnp.int32)
    lanes = jnp.arange(128, dtype=jnp.int32)[None, :]
    chosen = jnp.where(lanes < counted, chosen, -1)
    chosen = chosen.at[0, 0].set(CELLS - 1)
    chosen = chosen.at[0, 127].set(-1)
    return chosen


def draw_bump_block(key, part):
    offsets = jax.random.randint(jax.random.fold_in(key, 23), (SLOTBLK,), 0, PBD, dtype=jnp.int32)
    within = jnp.arange(SLOTBLK, dtype=jnp.int32) % BUMPBLK
    owner = within // CAP
    blocks = owner * PBD + offsets
    blocks = blocks.at[0].set(0)
    blocks = blocks.at[BUMPBLK - 1].set(PB - 1)
    return blocks


def draw_pkg_pattern(key, part):
    offsets = jax.random.randint(jax.random.fold_in(key, 37), (KNB, PB), -RADIUS, RADIUS + 1, dtype=jnp.int32)
    blocks = jnp.arange(PB, dtype=jnp.int32)
    reach = jnp.where(blocks % 2 == 0, -RADIUS, RADIUS).astype(jnp.int32)
    offsets = offsets.at[0].set(reach)
    return jnp.clip(blocks[None, :] + offsets, 0, PB - 1).astype(jnp.int32)


def levels(key, extent, shards, smallest, top_value):
    factor_of, own = 1.0, jax.random.fold_in(key, 6)
    for axis_at, shards_of in shards:
        draws = jnp.exp(jax.random.uniform(jax.random.fold_in(own, axis_at), (shards_of,), jnp.float32, smallest / len(shards), top_value / len(shards)))
        factor_of = factor_of * jnp.repeat(draws, extent[axis_at] // shards_of).reshape([-1 if axis == axis_at else 1 for axis in range(len(extent))])
    return factor_of


def normal_values(rng, shape, deviation, bound, cuts=(), held_as=jnp.bfloat16):
    entries = deviation * jax.random.normal(rng, shape, jnp.float32)
    if cuts:
        entries = entries * levels(rng, shape, cuts, -0.22, 0.18)
    return jnp.clip(entries, -bound, bound).astype(held_as)


def setup_inputs(seed: int = 0) -> dict:
    arg_keys = jax.random.split(jax.random.key(seed), 12)
    die_volt = normal_values(arg_keys[0], (NX, NY), 1.0, 6.0, ((0, 8), (1, 4)), jnp.float32)
    die_load = jnp.clip(jnp.exp(math.log(1.0) - 2.9957323 * jax.random.uniform(arg_keys[1], (NX, NY), jnp.float32) ** levels(arg_keys[1], (NX, NY), ((0, 8), (1, 4)), -0.2, 0.2)), 0.05, 1.0)
    die_shunt = jnp.clip(jnp.exp(math.log(1.0) - 2.3025851 * jax.random.uniform(arg_keys[2], (NX, NY), jnp.float32) ** levels(arg_keys[2], (NX, NY), ((0, 8), (1, 4)), -0.2, 0.2)), 0.1, 1.0)
    bump_node = draw_bump_node(jax.random.fold_in(arg_keys[11], 71), 0)
    bump_block = draw_bump_block(jax.random.fold_in(arg_keys[11], 71), 0)
    bump_cond = jnp.clip(jnp.exp(math.log(3.0) - 2.3025851 * jax.random.uniform(arg_keys[5], (SLOTBLK, 128), jnp.float32) ** levels(arg_keys[5], (SLOTBLK, 128), ((0, 32),), -0.2, 0.2)), 0.3, 3.0)
    pkg_volt = normal_values(arg_keys[6], (PB, 128), 1.0, 6.0, ((0, 4),), jnp.float32)
    pkg_diag = jnp.clip(4.0 + 2.0 * jax.random.uniform(arg_keys[7], (PB, 128), jnp.float32) ** levels(arg_keys[7], (PB, 128), ((0, 4),), -0.2, 0.2), 4.0, 6.0)
    pkg_pattern = draw_pkg_pattern(jax.random.fold_in(arg_keys[11], 71), 0)
    pkg_weight = jnp.clip(jax.random.uniform(arg_keys[9], (KNB, PB), jnp.float32, -0.5, 0.5) * levels(arg_keys[9], (KNB, PB), ((1, 4),), -0.4, 0.0), -0.5, 0.5)
    block_coupling = normal_values(arg_keys[10], (128, 128), 128 ** -0.5, 0.5, (), jnp.float32)
    return {"die_volt": die_volt, "die_load": die_load, "die_shunt": die_shunt, "bump_node": bump_node, "bump_block": bump_block, "bump_cond": bump_cond, "pkg_volt": pkg_volt, "pkg_diag": pkg_diag, "pkg_pattern": pkg_pattern, "pkg_weight": pkg_weight, "block_coupling": block_coupling}


def sweep_weights(sweeps):
    return [1.0 / (1.0 + 0.8 * math.cos(math.pi * (2 * index + 1) / (2 * sweeps))) for index in range(sweeps)]


def reference(die_volt, die_load, die_shunt, bump_node, bump_block, bump_cond, pkg_volt, pkg_diag, pkg_pattern, pkg_weight, block_coupling):
    live_slot = bump_node >= 0
    safe_node = jnp.where(live_slot, bump_node, 0).astype(jnp.int32)
    device = (jnp.arange(SLOTBLK, dtype=jnp.int32) // BUMPBLK)[:, None]
    row_index = (device // N_DIE) * CX + safe_node // CY
    col_index = (device % N_DIE) * CY + safe_node % CY
    conductance = jnp.where(live_slot, bump_cond, jnp.float32(0.0))
    bump_start = pkg_volt[bump_block]
    grid_zero = jnp.zeros((NX, NY), jnp.float32)
    gsum = grid_zero.at[row_index, col_index].add(conductance)
    inject = grid_zero.at[row_index, col_index].add(conductance * bump_start)
    diagonal = 4.0 + die_shunt + gsum
    right_side = inject - die_load
    voltage = die_volt
    for weight in sweep_weights(SWEEPS):
        padded = jnp.pad(voltage, 1)
        beside = padded[2:, 1:-1] + padded[:-2, 1:-1] + padded[1:-1, 2:] + padded[1:-1, :-2]
        voltage = voltage + weight * (right_side - diagonal * voltage + beside) / diagonal
    at_bump = voltage[row_index, col_index]
    current = conductance * (bump_start - at_bump)
    inflow = jnp.zeros((PB, 128), jnp.float32).at[bump_block].add(current)
    plane = pkg_volt
    for iteration in range(ITERS):
        coupled = jnp.dot(plane, block_coupling, precision=lax.Precision.HIGHEST, preferred_element_type=jnp.float32)
        for neighbour in range(KNB):
            coupled = coupled + pkg_weight[neighbour][:, None] * plane[pkg_pattern[neighbour]]
        plane = (-inflow - coupled) / pkg_diag
    bump_out = plane[bump_block]
    return voltage, plane, bump_out
```

```python
import functools
import math

import jax
import jax.numpy as jnp
from jax import lax
from jax.experimental import pallas as pl
from jax.experimental.pallas import tpu as pltpu
from jax.sharding import PartitionSpec as P

RADIUS = 32
SWEEPS = 4
ITERS = 4
LANES = 128
HALO_ROWS = 8
REACH = RADIUS * ITERS
WINDOW = LANES + 2 * RADIUS
F32 = jnp.float32
BF16 = jnp.bfloat16
VMEM = pl.BlockSpec(memory_space=pltpu.VMEM)
SMEM = pl.BlockSpec(memory_space=pltpu.SMEM)


def sweep_weights(sweeps):
    return [
        1.0 / (1.0 + 0.8 * math.cos(math.pi * (2 * index + 1) / (2 * sweeps)))
        for index in range(sweeps)
    ]


def call(body, name, outs, args, specs, scratch=(), flops=0, vmem=48):
    bytes_accessed = sum(4 * math.prod(arg.shape) for arg in args)
    return pl.pallas_call(
        body,
        name=name,
        out_shape=outs,
        in_specs=specs,
        out_specs=[VMEM] * len(outs),
        scratch_shapes=list(scratch),
        compiler_params=pltpu.CompilerParams(vmem_limit_bytes=vmem * 1024 * 1024),
        cost_estimate=pl.CostEstimate(
            flops=flops, bytes_accessed=bytes_accessed, transcendentals=0
        ),
    )(*args)


def shape(*dims, dtype=F32):
    return jax.ShapeDtypeStruct(dims, dtype)


def halves(values):
    high = values.astype(BF16)
    low = (values - high.astype(F32)).astype(BF16)
    return high, low


def shift_pair(values, axis):
    count = lax.axis_size(axis)
    first, last = values
    up = [(i, i + 1) for i in range(count - 1)]
    down = [(i + 1, i) for i in range(count - 1)]
    return lax.ppermute(last, axis, up), lax.ppermute(first, axis, down)


def pick_body(cap, die_count, where_ref, ids_ref, plane_ref, out_ref):
    start, mine = where_ref[0], where_ref[1]
    per_row = LANES // cap
    for die in range(die_count):
        sender = mine * die_count + die
        lane = lax.rem(sender, per_row) * cap
        for slot in range(cap):
            row = ids_ref[sender, lane + slot] - start
            at = die * cap + slot
            out_ref[pl.ds(at, 1), :] = plane_ref[pl.ds(row, 1), :]


def package_body(
    where_ref, volt_ref, diag_ref, pat_ref, wgt_ref, coup_ref, lo_ref, hi_ref,
    band_ref, base_ref, inv_ref, mix_ref, plane_ref,
):
    tiles = volt_ref.shape[0] // LANES
    neighbours = pat_ref.shape[0]
    start = where_ref[0]
    pad = jnp.zeros((RADIUS, 2 * LANES), BF16)
    plane_ref[0:RADIUS, :] = pad
    plane_ref[plane_ref.shape[0] - RADIUS :, :] = pad

    c_hi, c_lo = halves(coup_ref[...])
    mix = jnp.concatenate([c_hi, c_lo], axis=1)
    mix_ref[...] = jnp.concatenate([mix, mix], axis=0)

    def put(tile, volts, diag):
        rows = pl.ds(pl.multiple_of(tile * LANES + RADIUS, RADIUS), LANES)
        plane_ref[rows, :] = jnp.concatenate(halves(volts), axis=1)
        out = pl.ds(pl.multiple_of(tile * LANES, LANES), LANES)
        inv_ref[out, :] = jnp.where(diag > 0.0, 1.0 / jnp.where(diag > 0.0, diag, 1.0), 0.0)

    put(0, lo_ref[0:LANES, :], lo_ref[LANES : 2 * LANES, :])
    put(tiles + 1, hi_ref[0:LANES, :], hi_ref[LANES : 2 * LANES, :])

    @pl.loop(0, tiles)
    def _(tile):
        rows = pl.ds(pl.multiple_of(tile * LANES, LANES), LANES)
        put(tile + 1, volt_ref[rows, :], diag_ref[rows, :])

    def build(tile, pattern, weights):
        first = start - REACH + tile * LANES - RADIUS
        place = lax.broadcasted_iota(jnp.int32, (2 * LANES, LANES), 0)
        band = jnp.zeros((2 * LANES, LANES), F32)
        for k in range(neighbours):
            hit = place == (pattern[k : k + 1, :] - first)
            band = band + jnp.where(hit, weights[k : k + 1, :], 0.0)
        band = jnp.concatenate(halves(band.T), axis=0)
        band_ref[tile] = band
        rows = pl.multiple_of(tile * LANES, LANES)
        window = plane_ref[pl.ds(rows, WINDOW), :]
        own = plane_ref[pl.ds(pl.multiple_of(tile * LANES + RADIUS, RADIUS), LANES), :]
        base_ref[pl.ds(rows, LANES), :] = couple(band, window, own, mix_ref[...])

    halo_pat = 2 * LANES
    halo_wgt = 2 * LANES + neighbours
    for tile, ref in ((0, lo_ref), (tiles + 1, hi_ref)):
        build(
            tile,
            ref[halo_pat : halo_pat + neighbours, :].astype(jnp.int32),
            ref[halo_wgt : halo_wgt + neighbours, :],
        )

    @pl.loop(0, tiles)
    def _(tile):
        lanes = pl.ds(pl.multiple_of(tile * LANES, LANES), LANES)
        build(tile + 1, pat_ref[:, lanes], wgt_ref[:, lanes])


def couple(band, window, own, mix):
    beside = jnp.dot(band[:, :WINDOW], window, preferred_element_type=F32)
    within = jnp.dot(own, mix, preferred_element_type=F32)
    beside = beside[:LANES] + beside[LANES:]
    both = beside + within
    return both[:, :LANES] + both[:, LANES:]


def scatter_body(cols, node_ref, cond_ref, start_ref, volt_ref, load_ref, shunt_ref,
                 right_ref, inv_ref, top_ref, bottom_ref):
    blocks = node_ref.shape[0]
    rows = volt_ref.shape[0]
    group = 8
    row_at = lax.broadcasted_iota(jnp.int32, (rows, LANES), 0)
    col_at = lax.broadcasted_iota(jnp.int32, (cols, LANES), 0)
    total = jnp.zeros((4 * rows, cols), F32)
    for first in range(0, blocks, group):
        node = node_ref[first : first + group, :]
        live = node >= 0
        cond = jnp.where(live, cond_ref[first : first + group, :], 0.0)
        flow = cond * start_ref[first : first + group, :]
        safe = jnp.where(live, node, 0)
        row, col = safe // cols, safe % cols
        parts = halves(cond) + halves(flow)
        left, right = [], []
        for i in range(group):
            spot = jnp.where(row_at == row[i : i + 1, :], 1.0, 0.0).astype(BF16)
            left.append(
                jnp.concatenate([spot * part[i : i + 1, :] for part in parts], axis=0)
            )
            right.append(jnp.where(col_at == col[i : i + 1, :], 1.0, 0.0).astype(BF16))
        total = total + lax.dot_general(
            jnp.concatenate(left, axis=1),
            jnp.concatenate(right, axis=1),
            (((1,), (1,)), ((), ())),
            preferred_element_type=F32,
        )
    gsum = total[:rows] + total[rows : 2 * rows]
    inject = total[2 * rows : 3 * rows] + total[3 * rows :]
    inv = 1.0 / (4.0 + shunt_ref[...] + gsum)
    right_side = (inject - load_ref[...]) * inv
    right_ref[...] = right_side
    inv_ref[...] = inv
    volt = volt_ref[...]
    for ref, cut in ((top_ref, slice(0, HALO_ROWS)), (bottom_ref, slice(rows - HALO_ROWS, rows))):
        ref[...] = jnp.concatenate([volt[cut], right_side[cut], inv[cut]], axis=0)


def extended(own, top, bottom, index):
    cut = slice(index * HALO_ROWS, (index + 1) * HALO_ROWS)
    return jnp.concatenate([top[cut], own, bottom[cut]], axis=0)


def edge_body(volt_ref, right_ref, inv_ref, top_ref, bottom_ref, west_ref, east_ref):
    cols = volt_ref.shape[1]
    width = SWEEPS
    lane = lax.broadcasted_iota(jnp.int32, west_ref.shape, 1)
    west, east = None, None
    for index, ref in enumerate((volt_ref, right_ref, inv_ref)):
        whole = extended(ref[...], top_ref[...], bottom_ref[...], index)
        head, tail = whole[:, :LANES], whole[:, cols - LANES :]
        if index == 0:
            west, east = head, tail
        else:
            shift = index * width
            west = jnp.where(lane >= shift, pltpu.roll(head, shift, 1), west)
            east = jnp.where(lane < LANES - shift, pltpu.roll(tail, LANES - shift, 1), east)
    west_ref[...] = west
    east_ref[...] = east


def sweep_body(copies, node_ref, cond_ref, start_ref, volt_ref, right_ref, inv_ref,
               top_ref, bottom_ref, west_ref, east_ref, out_ref, current_ref):
    rows, cols = volt_ref.shape
    blocks = node_ref.shape[0]
    cap = current_ref.shape[1]
    whole = []
    for index, ref in enumerate((volt_ref, right_ref, inv_ref)):
        own = extended(ref[...], top_ref[...], bottom_ref[...], index)
        west, east = west_ref[...], east_ref[...]
        if index:
            shift = index * SWEEPS
            west = pltpu.roll(west, shift, 1)
            east = pltpu.roll(east, LANES - shift, 1)
        whole.append(jnp.concatenate([west, own, east], axis=1))
    volt, right_side, inv = whole
    high, wide = volt.shape
    for weight in sweep_weights(SWEEPS):
        beside = (
            pltpu.roll(volt, 1, 0)
            + pltpu.roll(volt, high - 1, 0)
            + pltpu.roll(volt, 1, 1)
            + pltpu.roll(volt, wide - 1, 1)
        )
        volt = (1.0 - weight) * volt + weight * (right_side + beside * inv)
    volt = volt[HALO_ROWS : HALO_ROWS + rows, LANES : LANES + cols]
    out_ref[...] = volt
    both = jnp.concatenate(halves(volt), axis=0)
    group = 8
    row_at = lax.broadcasted_iota(jnp.int32, (rows, LANES), 0)
    col_at = lax.broadcasted_iota(jnp.int32, (cols, LANES), 0)
    dies = blocks // cap
    for first in range(0, blocks, group):
        node = node_ref[first : first + group, :]
        live = node >= 0
        cond = jnp.where(live, cond_ref[first : first + group, :], 0.0)
        safe = jnp.where(live, node, 0)
        row, col = safe // cols, safe % cols
        spots = jnp.concatenate(
            [
                jnp.where(col_at == col[i : i + 1, :], 1.0, 0.0).astype(BF16)
                for i in range(group)
            ],
            axis=1,
        )
        found = jnp.dot(both, spots, preferred_element_type=F32)
        found = found[:rows] + found[rows:]
        for i in range(group):
            mine = found[:, i * LANES : (i + 1) * LANES]
            at_bump = jnp.sum(
                jnp.where(row_at == row[i : i + 1, :], mine, 0.0), axis=0, keepdims=True
            )
            block = first + i
            current = cond[i : i + 1, :] * (start_ref[block : block + 1, :] - at_bump)
            current_ref[block // cap, block % cap : block % cap + 1, :] = current
    for copy in range(1, copies):
        current_ref[copy * dies : (copy + 1) * dies] = current_ref[0:dies]


def slot_places(ids_ref, per_row):
    return [
        jnp.sum(ids_ref[at : at + per_row, :], axis=0, keepdims=True)
        for at in range(0, ids_ref.shape[0], per_row)
    ]


def gather_inflow(places, first, rows, current):
    at = lax.broadcasted_iota(jnp.int32, (rows, LANES), 0) + first
    hits = [jnp.where(at == place, 1.0, 0.0).astype(BF16) for place in places]
    both = jnp.dot(jnp.concatenate(hits, axis=1), current, preferred_element_type=F32)
    return both[:, :LANES] + both[:, LANES:]


def inflow_edge_body(blocks, per_row, where_ref, ids_ref, current_ref, first_ref, last_ref):
    places = slot_places(ids_ref, per_row)
    current = jnp.concatenate(halves(current_ref[...]), axis=1)
    start = where_ref[0]
    first_ref[...] = gather_inflow(places, start, REACH, current)
    last_ref[...] = gather_inflow(places, start + blocks - REACH, REACH, current)


def iterate_body(
    cap, die_count, per_row, where_ref, asked_ref, ids_ref, current_ref, lo_ref, hi_ref,
    band_ref, base_ref, inv_ref, mix_ref, out_ref, picked_ref, inflow_ref, here_ref, there_ref,
):
    tiles = out_ref.shape[0] // LANES
    start = where_ref[0]
    places = slot_places(ids_ref, per_row)
    current = jnp.concatenate(halves(current_ref[...]), axis=1)
    pad = jnp.zeros((RADIUS, 2 * LANES), BF16)
    for ref in (here_ref, there_ref):
        ref[0:RADIUS, :] = pad
        ref[ref.shape[0] - RADIUS :, :] = pad

    def span(tile, offset=0, size=LANES):
        return pl.ds(pl.multiple_of(tile * LANES + offset, RADIUS), size)

    def store(ref, tile, values):
        ref[span(tile, RADIUS), :] = jnp.concatenate(halves(values), axis=1)

    def first_step(tile, inflow):
        inflow_ref[span(tile), :] = inflow
        store(here_ref, tile, -(inflow + base_ref[span(tile), :]) * inv_ref[span(tile), :])

    first_step(0, lo_ref[...])
    first_step(tiles + 1, hi_ref[...])

    @pl.loop(0, tiles, unroll=2)
    def _(tile):
        first_step(tile + 1, gather_inflow(places, start + tile * LANES, LANES, current))

    def step(source, tile):
        window = source[span(tile, 0, WINDOW), :]
        own = source[span(tile, RADIUS), :]
        coupled = couple(band_ref[tile], window, own, mix_ref[...])
        return -(inflow_ref[span(tile), :] + coupled) * inv_ref[span(tile), :]

    refs = (here_ref, there_ref)
    for iteration in range(1, ITERS - 1):
        source, target = refs[(iteration - 1) % 2], refs[iteration % 2]

        @pl.loop(0, tiles + 2, unroll=2)
        def _(tile):
            store(target, tile, step(source, tile))

    source = refs[(ITERS - 2) % 2]

    @pl.loop(0, tiles, unroll=2)
    def _(tile):
        out_ref[pl.ds(pl.multiple_of(tile * LANES, LANES), LANES), :] = step(source, tile + 1)

    pick_body(cap, die_count, where_ref, asked_ref, out_ref, picked_ref)


def local(
    die_volt,
    die_load,
    die_shunt,
    bump_node,
    bump_block,
    bump_cond,
    pkg_volt,
    pkg_diag,
    pkg_pattern,
    pkg_weight,
    block_coupling,
):
    die_count = lax.axis_size("die")
    group_count = lax.axis_size("grp")
    devices = die_count * group_count
    blocks = pkg_volt.shape[0]
    tiles = blocks // LANES
    neighbours = pkg_pattern.shape[0]
    slots = bump_block.shape[0]
    cap = slots // die_count
    per_row = LANES // cap
    rows, cols = die_volt.shape
    group, die = lax.axis_index("grp"), lax.axis_index("die")
    where = jnp.stack([die * blocks, group]).astype(jnp.int32)

    def packed(cut):
        return jnp.concatenate(
            [
                pkg_volt[cut],
                pkg_diag[cut],
                pkg_pattern[:, cut].astype(F32),
                pkg_weight[:, cut],
            ],
            axis=0,
        )

    pkg_lo, pkg_hi = shift_pair(
        (packed(slice(0, REACH)), packed(slice(blocks - REACH, blocks))), "die"
    )

    mine = lax.rem(group * die_count + die, per_row)
    lane = jnp.arange(LANES, dtype=jnp.int32)
    spread = jnp.where(
        lane // cap == mine, jnp.tile(bump_block.reshape(die_count, cap), (1, per_row)), 0
    )
    spread = jnp.broadcast_to(spread[None, :, None, :], (group_count, die_count, 1, LANES))
    ids = lax.all_to_all(
        spread.reshape(devices, 1, LANES), ("grp", "die"), split_axis=0, concat_axis=0, tiled=True
    ).reshape(devices, LANES)

    (picked,) = call(
        functools.partial(pick_body, cap, die_count),
        "pick_rows",
        [shape(slots, LANES)],
        (where, ids, pkg_volt),
        [SMEM, SMEM, VMEM],
    )
    bump_start = lax.all_to_all(
        picked.reshape(die_count, cap, LANES), "die", split_axis=0, concat_axis=0, tiled=True
    ).reshape(slots, LANES)

    right_side, inv, top, bottom = call(
        functools.partial(scatter_body, cols),
        "scatter_bumps",
        [shape(rows, cols), shape(rows, cols)] + [shape(3 * HALO_ROWS, cols)] * 2,
        (bump_node, bump_cond, bump_start, die_volt, die_load, die_shunt),
        [VMEM] * 6,
        flops=8 * rows * slots * LANES * cols,
    )
    above, below = shift_pair((top, bottom), "grp")

    ext = (tiles + 2) * LANES
    band, base, pkg_inv, mix = call(
        package_body,
        "package_setup",
        [
            shape(tiles + 2, 2 * LANES, 2 * LANES, dtype=BF16),
            shape(ext, LANES),
            shape(ext, LANES),
            shape(2 * LANES, 2 * LANES, dtype=BF16),
        ],
        (where, pkg_volt, pkg_diag, pkg_pattern, pkg_weight, block_coupling, pkg_lo, pkg_hi),
        [SMEM] + [VMEM] * 7,
        [pltpu.VMEM((ext + 2 * RADIUS, 2 * LANES), BF16)],
        flops=6 * ext * 2 * LANES * 2 * LANES,
    )

    high = rows + 2 * HALO_ROWS
    west, east = call(
        edge_body,
        "edge_columns",
        [shape(high, LANES)] * 2,
        (die_volt, right_side, inv, above, below),
        [VMEM] * 5,
    )
    west, east = shift_pair((west, east), "die")

    die_out, current = call(
        functools.partial(sweep_body, group_count),
        "sweeps",
        [shape(rows, cols), shape(devices, cap, LANES)],
        (bump_node, bump_cond, bump_start, die_volt, right_side, inv, above, below, west, east),
        [VMEM] * 10,
        flops=4 * rows * slots * LANES * cols,
    )
    current = lax.all_to_all(
        current, ("grp", "die"), split_axis=0, concat_axis=0, tiled=True
    ).reshape(devices * cap, LANES)

    edges = call(
        functools.partial(inflow_edge_body, blocks, per_row),
        "inflow_edges",
        [shape(REACH, LANES)] * 2,
        (where, ids, current),
        [SMEM, VMEM, VMEM],
    )
    inflow_lo, inflow_hi = shift_pair(edges, "die")

    pkg_out, picked = call(
        functools.partial(iterate_body, cap, die_count, per_row),
        "package_iterations",
        [shape(blocks, LANES), shape(slots, LANES)],
        (where, ids, ids, current, inflow_lo, inflow_hi, band, base, pkg_inv, mix),
        [SMEM, SMEM] + [VMEM] * 8,
        [pltpu.VMEM((ext, LANES), F32)] + [pltpu.VMEM((ext + 2 * RADIUS, 2 * LANES), BF16)] * 2,
        flops=24 * ext * 2 * LANES * 2 * LANES,
    )
    bump_out = lax.all_to_all(
        picked.reshape(die_count, cap, LANES), "die", split_axis=0, concat_axis=0, tiled=True
    ).reshape(slots, LANES)
    return (die_out, pkg_out, bump_out)


def solution(mesh):
    return jax.shard_map(
        local,
        mesh=mesh,
        in_specs=(
            P("grp", "die"),
            P("grp", "die"),
            P("grp", "die"),
            P(("grp", "die"), None),
            P(("grp", "die")),
            P(("grp", "die"), None),
            P("die", None),
            P("die", None),
            P(None, "die"),
            P(None, "die"),
            P(),
        ),
        out_specs=(P("grp", "die"), P("die", None), P(("grp", "die"), None)),
        check_vma=False,
    )
```

```python
import functools
import math

import jax
import jax.numpy as jnp
from jax import lax
from jax.experimental import pallas as pl
from jax.experimental.pallas import tpu as pltpu
from jax.sharding import PartitionSpec as P

RADIUS = 32
SWEEPS = 4
ITERS = 4
LANES = 128
HALO_ROWS = 8
REACH = RADIUS * ITERS
WINDOW = LANES + 2 * RADIUS
F32 = jnp.float32
BF16 = jnp.bfloat16
VMEM = pl.BlockSpec(memory_space=pltpu.VMEM)
SMEM = pl.BlockSpec(memory_space=pltpu.SMEM)
ANY = pl.BlockSpec(memory_space=pl.ANY)
HBM = pl.BlockSpec(memory_space=pltpu.HBM)


def sweep_weights(sweeps):
    return [
        1.0 / (1.0 + 0.8 * math.cos(math.pi * (2 * index + 1) / (2 * sweeps)))
        for index in range(sweeps)
    ]


def call(body, name, outs, args, specs, scratch=(), flops=0, vmem=16):
    bytes_accessed = sum(4 * math.prod(arg.shape) for arg in args)
    return pl.pallas_call(
        body,
        name=name,
        out_shape=outs,
        in_specs=specs,
        out_specs=[VMEM] * len(outs),
        scratch_shapes=list(scratch),
        compiler_params=pltpu.CompilerParams(vmem_limit_bytes=vmem * 1024 * 1024),
        cost_estimate=pl.CostEstimate(
            flops=flops, bytes_accessed=bytes_accessed, transcendentals=0
        ),
    )(*args)


def shape(*dims, dtype=F32):
    return jax.ShapeDtypeStruct(dims, dtype)


def halves(values):
    high = values.astype(BF16)
    low = (values - high.astype(F32)).astype(BF16)
    return high, low


def shift_pair(values, axis):
    count = lax.axis_size(axis)
    first, last = values
    up = [(i, i + 1) for i in range(count - 1)]
    down = [(i + 1, i) for i in range(count - 1)]
    return lax.ppermute(last, axis, up), lax.ppermute(first, axis, down)


def spread_body(cap, die_count, where_ref, block_ref, out_ref):
    mine = lax.rem(where_ref[1] * die_count + where_ref[2], LANES // cap) * cap
    slots = block_ref.shape[1]
    lane = lax.broadcasted_iota(jnp.int32, (1, LANES), 1)
    block = jnp.concatenate(
        [block_ref[...], jnp.zeros((1, LANES - slots), jnp.int32)], axis=1
    )
    own = (lane >= mine) & (lane < mine + cap)
    for die in range(die_count):
        shift = lax.rem(mine + LANES - die * cap, LANES)
        row = jnp.where(own, pltpu.roll(block, shift, 1), 0)
        for at in range(die, out_ref.shape[0], die_count):
            out_ref[at] = row


def asked_rows(cap, die_count, where_ref, ids_ref):
    start, mine = where_ref[0], where_ref[1]
    per_row = LANES // cap
    for die in range(die_count):
        sender = mine * die_count + die
        lane = lax.rem(sender, per_row) * cap
        for slot in range(cap):
            yield die * cap + slot, ids_ref[sender, lane + slot] - start


def pick_body(cap, die_count, where_ref, ids_ref, plane_ref, after_ref, out_ref, sem):
    for at, row in asked_rows(cap, die_count, where_ref, ids_ref):
        pltpu.make_async_copy(
            plane_ref.at[pl.ds(row, 1), :], out_ref.at[pl.ds(at, 1), :], sem
        ).start()
    pltpu.make_async_copy(plane_ref.at[0 : out_ref.shape[0], :], out_ref, sem).wait()


def build_band(first, pattern, weights):
    place = lax.broadcasted_iota(jnp.int32, (WINDOW, LANES), 0)
    band = None
    for k in range(pattern.shape[0]):
        hit = place == (pattern[k : k + 1, :] - first)
        term = jnp.where(hit, weights[k : k + 1, :], 0.0)
        band = term if band is None else band + term
    fill = jnp.zeros((2 * LANES - WINDOW, LANES), F32)
    return jnp.concatenate(halves(jnp.concatenate([band, fill], axis=0).T), axis=0)


def band_body(first_tile, where_ref, pat_ref, wgt_ref, after_ref, band_ref):
    start = where_ref[0]

    @pl.loop(0, band_ref.shape[0], unroll=4)
    def _(at):
        tile = at + first_tile
        lanes = pl.ds(pl.multiple_of(tile * LANES, LANES), LANES)
        band_ref[at] = build_band(
            start + tile * LANES - RADIUS, pat_ref[:, lanes], wgt_ref[:, lanes]
        )


def pack_body(volt_ref, diag_ref, pat_ref, wgt_ref, after_ref, lo_ref, hi_ref, sems):
    blocks = volt_ref.shape[0]
    copies = []
    for end, ref in enumerate((lo_ref, hi_ref)):
        cut = pl.ds(end * (blocks - REACH), REACH)
        for at, source in enumerate((volt_ref, diag_ref)):
            copies.append(
                pltpu.make_async_copy(
                    source.at[cut, :],
                    ref.at[pl.ds(at * REACH, REACH), :],
                    sems.at[2 * end + at],
                )
            )
            copies[-1].start()
    count = pat_ref.shape[0]
    for end, ref in enumerate((lo_ref, hi_ref)):
        cut = slice(end * (blocks - REACH), end * (blocks - REACH) + REACH)
        ref[2 * REACH : 2 * REACH + count, :] = pat_ref[:, cut].astype(F32)
        ref[2 * REACH + count : 2 * REACH + 2 * count, :] = wgt_ref[:, cut]
    for copy in copies:
        copy.wait()


def reciprocal(diag):
    safe = jnp.where(diag > 0.0, diag, 1.0)
    return jnp.where(diag > 0.0, 1.0 / safe, 0.0)


def span(tile, offset=0, size=LANES):
    return pl.ds(pl.multiple_of(tile * LANES + offset, RADIUS), size)


def chunk_of(tiles):
    return math.gcd(tiles, 4)


def base_body(
    where_ref, volt_ref, diag_ref, coup_ref, lo_ref, hi_ref, low_ref, high_ref, after_ref,
    base_ref, inv_ref, mix_ref, ends_ref, plane_ref,
):
    tiles = volt_ref.shape[0] // LANES
    count = (lo_ref.shape[0] - 2 * REACH) // 2
    start = where_ref[0]
    pad = jnp.zeros((RADIUS, 2 * LANES), BF16)
    plane_ref[0:RADIUS, :] = pad
    plane_ref[plane_ref.shape[0] - RADIUS :, :] = pad
    c_hi, c_lo = halves(coup_ref[...])
    mix = jnp.concatenate([c_hi, c_lo], axis=1)
    mix_ref[...] = jnp.concatenate([mix, mix], axis=0)

    def put(tile, volts, diag):
        plane_ref[span(tile, RADIUS), :] = jnp.concatenate(halves(volts), axis=1)
        inv_ref[span(tile), :] = reciprocal(diag)

    for end, ref in enumerate((lo_ref, hi_ref)):
        tile = end * (tiles + 1)
        put(tile, ref[0:LANES, :], ref[LANES : 2 * LANES, :])
        ends_ref[end] = build_band(
            start + (tile - 1) * LANES - RADIUS,
            ref[2 * REACH : 2 * REACH + count, :].astype(jnp.int32),
            ref[2 * REACH + count : 2 * REACH + 2 * count, :],
        )

    @pl.loop(0, tiles, unroll=4)
    def _(tile):
        put(tile + 1, volt_ref[span(tile), :], diag_ref[span(tile), :])

    mix = mix_ref[...]

    def write(tile, values):
        base_ref[span(tile), :] = values

    couple_all(plane_ref, (low_ref, high_ref), ends_ref, mix, write)


def couple_all(source, bands, ends_ref, mix, write, with_ends=True):
    if with_ends:
        tiles = sum(ref.shape[0] for ref in bands)
        for end in range(2):
            couple(source, end * (tiles + 1), [ends_ref[end]], mix, write)
    done = 1
    for ref in bands:
        size = chunk_of(ref.shape[0])

        @pl.loop(0, ref.shape[0] // size)
        def _(chunk, ref=ref, done=done, size=size):
            couple(
                source, done + chunk * size, [ref[chunk * size + i] for i in range(size)], mix, write
            )

        done += ref.shape[0]


def couple(source, tile, bands, mix, write):
    own = source[span(tile, RADIUS, len(bands) * LANES), :]
    within = jnp.dot(own, mix, preferred_element_type=F32)
    for i, band in enumerate(bands):
        window = source[span(tile + i, 0, WINDOW), :]
        beside = jnp.dot(band[:, :WINDOW], window, preferred_element_type=F32)
        both = beside[:LANES] + beside[LANES:] + within[i * LANES : (i + 1) * LANES]
        write(tile + i, both[:, :LANES] + both[:, LANES:])


def scatter_body(cols, where_ref, node_ref, cond_ref, start_ref, volt_ref, load_ref, shunt_ref,
                 after_ref, right_ref, inv_ref, edge_ref):
    blocks = node_ref.shape[0]
    rows = volt_ref.shape[0]
    group = 8
    row_at = lax.broadcasted_iota(jnp.int32, (rows, LANES), 0)
    col_at = lax.broadcasted_iota(jnp.int32, (cols, LANES), 0)
    total = jnp.zeros((4 * rows, cols), F32)
    for first in range(0, blocks, group):
        node = node_ref[first : first + group, :]
        live = node >= 0
        cond = jnp.where(live, cond_ref[first : first + group, :], 0.0)
        flow = cond * start_ref[first : first + group, :]
        safe = jnp.where(live, node, 0)
        row, col = safe // cols, safe % cols
        parts = halves(cond) + halves(flow)
        left, right = [], []
        for i in range(group):
            spot = jnp.where(row_at == row[i : i + 1, :], 1.0, 0.0).astype(BF16)
            left.append(
                jnp.concatenate([spot * part[i : i + 1, :] for part in parts], axis=0)
            )
            right.append(jnp.where(col_at == col[i : i + 1, :], 1.0, 0.0).astype(BF16))
        total = total + lax.dot_general(
            jnp.concatenate(left, axis=1),
            jnp.concatenate(right, axis=1),
            (((1,), (1,)), ((), ())),
            preferred_element_type=F32,
        )
    gsum = total[:rows] + total[rows : 2 * rows]
    inject = total[2 * rows : 3 * rows] + total[3 * rows :]
    inv = 1.0 / (4.0 + shunt_ref[...] + gsum)
    right_side = (inject - load_ref[...]) * inv
    right_ref[...] = right_side
    inv_ref[...] = inv
    volt = volt_ref[...]
    top, bottom = (
        jnp.concatenate([volt[cut], right_side[cut], inv[cut]], axis=0)
        for cut in (slice(0, HALO_ROWS), slice(rows - HALO_ROWS, rows))
    )
    send_beside(edge_ref, where_ref[1], top, bottom)


def send_beside(ref, mine, first, last):
    count = ref.shape[0]
    ref[...] = jnp.zeros(ref.shape, F32)

    @pl.when(mine > 0)
    def _():
        ref[jnp.maximum(mine - 1, 0)] = first

    @pl.when(mine < count - 1)
    def _():
        ref[jnp.minimum(mine + 1, count - 1)] = last


def from_beside(ref, mine):
    count = ref.shape[0]
    before = jnp.where(mine > 0, ref[jnp.maximum(mine - 1, 0)], 0.0)
    after = jnp.where(mine < count - 1, ref[jnp.minimum(mine + 1, count - 1)], 0.0)
    return before, after


def extended(own, top, bottom, index):
    cut = slice(index * HALO_ROWS, (index + 1) * HALO_ROWS)
    return jnp.concatenate([top[cut], own, bottom[cut]], axis=0)


def edge_body(where_ref, volt_ref, right_ref, inv_ref, beside_ref, out_ref):
    cols = volt_ref.shape[1]
    top, bottom = from_beside(beside_ref, where_ref[1])
    out_rows, high = out_ref.shape[1:]
    west, east = None, None
    for index, ref in enumerate((volt_ref, right_ref, inv_ref)):
        whole = extended(ref[...], top, bottom, index)
        lane = lax.broadcasted_iota(jnp.int32, (whole.shape[0], LANES), 1)
        head, tail = whole[:, :LANES], whole[:, cols - LANES :]
        at = index * SWEEPS
        head = pltpu.roll(head, at, 1) if at else head
        tail = pltpu.roll(tail, at + SWEEPS, 1)
        west = head if west is None else jnp.where(lane >= at, head, west)
        east = tail if east is None else jnp.where(lane >= at, tail, east)
    fill = jnp.zeros((high - west.shape[0], LANES), F32)
    west, east = (
        jnp.concatenate([part, fill], axis=0).T[:out_rows] for part in (west, east)
    )
    send_beside(out_ref, where_ref[2], west, east)


def sweep_body(copies, where_ref, node_ref, cond_ref, start_ref, volt_ref, right_ref, inv_ref,
               beside_ref, column_ref, out_ref, current_ref):
    rows, cols = volt_ref.shape
    blocks = node_ref.shape[0]
    cap = current_ref.shape[1]
    whole = []
    top, bottom = from_beside(beside_ref, where_ref[1])
    out_rows, high = column_ref.shape[1:]
    fill = jnp.zeros((LANES - out_rows, high), F32)
    wests, easts = (
        jnp.concatenate([part, fill], axis=0).T[: rows + 2 * HALO_ROWS]
        for part in from_beside(column_ref, where_ref[2])
    )
    for index, ref in enumerate((volt_ref, right_ref, inv_ref)):
        own = extended(ref[...], top, bottom, index)
        at = index * SWEEPS
        west = pltpu.roll(wests, LANES - SWEEPS - at, 1)
        east = pltpu.roll(easts, LANES - at, 1) if at else easts
        whole.append(jnp.concatenate([west, own, east], axis=1))
    volt, right_side, inv = whole
    high, wide = volt.shape
    for weight in sweep_weights(SWEEPS):
        beside = (
            pltpu.roll(volt, 1, 0)
            + pltpu.roll(volt, high - 1, 0)
            + pltpu.roll(volt, 1, 1)
            + pltpu.roll(volt, wide - 1, 1)
        )
        volt = (1.0 - weight) * volt + weight * (right_side + beside * inv)
    volt = volt[HALO_ROWS : HALO_ROWS + rows, LANES : LANES + cols]
    out_ref[...] = volt
    both = jnp.concatenate(halves(volt), axis=0)
    group = 8
    row_at = lax.broadcasted_iota(jnp.int32, (rows, LANES), 0)
    col_at = lax.broadcasted_iota(jnp.int32, (cols, LANES), 0)
    dies = blocks // cap
    for first in range(0, blocks, group):
        node = node_ref[first : first + group, :]
        live = node >= 0
        cond = jnp.where(live, cond_ref[first : first + group, :], 0.0)
        safe = jnp.where(live, node, 0)
        row, col = safe // cols, safe % cols
        spots = jnp.concatenate(
            [
                jnp.where(col_at == col[i : i + 1, :], 1.0, 0.0).astype(BF16)
                for i in range(group)
            ],
            axis=1,
        )
        found = jnp.dot(both, spots, preferred_element_type=F32)
        found = found[:rows] + found[rows:]
        for i in range(group):
            mine = found[:, i * LANES : (i + 1) * LANES]
            at_bump = jnp.sum(
                jnp.where(row_at == row[i : i + 1, :], mine, 0.0), axis=0, keepdims=True
            )
            block = first + i
            current = cond[i : i + 1, :] * (start_ref[block : block + 1, :] - at_bump)
            current_ref[block // cap, block % cap : block % cap + 1, :] = current
    for copy in range(1, copies):
        current_ref[copy * dies : (copy + 1) * dies] = current_ref[0:dies]


def slot_places(ids_ref, per_row):
    return [
        jnp.sum(ids_ref[at : at + per_row, :], axis=0, keepdims=True)
        for at in range(0, ids_ref.shape[0], per_row)
    ]


def gather_inflow(places, first, rows, current):
    at = lax.broadcasted_iota(jnp.int32, (rows, LANES), 0) + first
    hits = [jnp.where(at == place, 1.0, 0.0).astype(BF16) for place in places]
    both = jnp.dot(jnp.concatenate(hits, axis=1), current, preferred_element_type=F32)
    return both[:, :LANES] + both[:, LANES:]


def inflow_edge_body(
    blocks, per_row, where_ref, ids_ref, current_ref, after_ref, first_ref, last_ref
):
    places = slot_places(ids_ref, per_row)
    current = jnp.concatenate(halves(current_ref[...]), axis=1)
    start = where_ref[0]
    first_ref[...] = gather_inflow(places, start, REACH, current)
    last_ref[...] = gather_inflow(places, start + blocks - REACH, REACH, current)


def iterate_body(
    cap, die_count, per_row, where_ref, asked_ref, ids_ref, current_ref, lo_ref, hi_ref,
    low_ref, high_ref, ends_ref, base_ref, inv_ref, mix_ref,
    out_ref, picked_ref, inflow_ref, here_ref, there_ref,
):
    tiles = out_ref.shape[0] // LANES
    start = where_ref[0]
    places = slot_places(ids_ref, per_row)
    current = jnp.concatenate(halves(current_ref[...]), axis=1)
    pad = jnp.zeros((RADIUS, 2 * LANES), BF16)
    for ref in (here_ref, there_ref):
        ref[0:RADIUS, :] = pad
        ref[ref.shape[0] - RADIUS :, :] = pad

    def store(ref, tile, values, size=1):
        ref[span(tile, RADIUS, size * LANES), :] = jnp.concatenate(halves(values), axis=1)

    def first_step(tile, inflow, size=1):
        at = span(tile, 0, size * LANES)
        inflow_ref[at, :] = inflow
        store(here_ref, tile, -(inflow + base_ref[at, :]) * inv_ref[at, :], size)

    first_step(0, lo_ref[...])
    first_step(tiles + 1, hi_ref[...])
    size = chunk_of(tiles)

    @pl.loop(0, tiles // size)
    def _(chunk):
        tile = chunk * size
        inflow = gather_inflow(places, start + tile * LANES, size * LANES, current)
        first_step(tile + 1, inflow, size)

    mix = mix_ref[...]

    def next_values(tile, coupled):
        return -(inflow_ref[span(tile), :] + coupled) * inv_ref[span(tile), :]

    refs = (here_ref, there_ref)
    for iteration in range(1, ITERS):
        source, target = refs[(iteration - 1) % 2], refs[iteration % 2]
        last = iteration == ITERS - 1

        def write(tile, coupled, target=target, last=last):
            values = next_values(tile, coupled)
            if last:
                out_ref[span(tile - 1), :] = values
            else:
                store(target, tile, values)

        couple_all(source, (low_ref, high_ref), ends_ref, mix, write, not last)

    for at, row in asked_rows(cap, die_count, where_ref, asked_ref):
        picked_ref[pl.ds(at, 1), :] = out_ref[pl.ds(row, 1), :]


def local(
    die_volt,
    die_load,
    die_shunt,
    bump_node,
    bump_block,
    bump_cond,
    pkg_volt,
    pkg_diag,
    pkg_pattern,
    pkg_weight,
    block_coupling,
):
    die_count = lax.axis_size("die")
    group_count = lax.axis_size("grp")
    devices = die_count * group_count
    blocks = pkg_volt.shape[0]
    tiles = blocks // LANES
    neighbours = pkg_pattern.shape[0]
    slots = bump_block.shape[0]
    cap = slots // die_count
    per_row = LANES // cap
    rows, cols = die_volt.shape
    group, die = lax.axis_index("grp"), lax.axis_index("die")
    where = jnp.stack([die * blocks, group, die]).astype(jnp.int32)

    (spread,) = call(
        functools.partial(spread_body, cap, die_count),
        "spread_blocks",
        [shape(devices, 1, LANES, dtype=jnp.int32)],
        (where, bump_block.reshape(1, slots)),
        [SMEM, VMEM],
    )
    ids = lax.all_to_all(
        spread, ("grp", "die"), split_axis=0, concat_axis=0, tiled=True
    ).reshape(devices, LANES)

    part = tiles // 2

    def build_bands(first, count, after):
        return call(
            functools.partial(band_body, first),
            "bands",
            [shape(count, 2 * LANES, 2 * LANES, dtype=BF16)],
            (where, pkg_pattern, pkg_weight, after),
            [SMEM, VMEM, VMEM, ANY],
            flops=2 * count * LANES**3,
        )[0]

    bands = [build_bands(0, part, spread)]

    (picked,) = call(
        functools.partial(pick_body, cap, die_count),
        "pick_rows",
        [shape(slots, LANES)],
        (where, ids, pkg_volt, bands[0]),
        [SMEM, SMEM, HBM, ANY],
        [pltpu.SemaphoreType.DMA(())],
    )
    bump_start = lax.all_to_all(
        picked.reshape(die_count, cap, LANES), "die", split_axis=0, concat_axis=0, tiled=True
    ).reshape(slots, LANES)

    bands.append(build_bands(part, tiles - part, picked))
    right_side, inv, edge = call(
        functools.partial(scatter_body, cols),
        "scatter_bumps",
        [shape(rows, cols), shape(rows, cols), shape(group_count, 3 * HALO_ROWS, cols)],
        (where, bump_node, bump_cond, bump_start, die_volt, die_load, die_shunt, bands[1]),
        [SMEM] + [VMEM] * 6 + [ANY],
        flops=8 * rows * slots * LANES * cols,
    )
    beside = lax.all_to_all(edge, "grp", split_axis=0, concat_axis=0, tiled=True)

    edge_rows = -(-3 * SWEEPS // 8) * 8
    edge_cols = -(-(rows + 2 * HALO_ROWS) // LANES) * LANES
    (column,) = call(
        edge_body,
        "edge_columns",
        [shape(die_count, edge_rows, edge_cols)],
        (where, die_volt, right_side, inv, beside),
        [SMEM] + [VMEM] * 4,
    )
    column = lax.all_to_all(column, "die", split_axis=0, concat_axis=0, tiled=True)

    die_out, current = call(
        functools.partial(sweep_body, group_count),
        "sweeps",
        [shape(rows, cols), shape(devices, cap, LANES)],
        (where, bump_node, bump_cond, bump_start, die_volt, right_side, inv, beside, column),
        [SMEM] + [VMEM] * 8,
        flops=4 * rows * slots * LANES * cols,
    )
    packs = call(
        pack_body,
        "pack_halo",
        [shape(2 * REACH + 2 * neighbours, LANES)] * 2,
        (pkg_volt, pkg_diag, pkg_pattern, pkg_weight, current),
        [HBM, HBM, VMEM, VMEM, ANY],
        [pltpu.SemaphoreType.DMA((4,))],
    )
    pkg_lo, pkg_hi = shift_pair(packs, "die")

    ext = (tiles + 2) * LANES
    base, pkg_inv, mix, ends = call(
        base_body,
        "package_base",
        [
            shape(ext, LANES),
            shape(ext, LANES),
            shape(2 * LANES, 2 * LANES, dtype=BF16),
            shape(2, 2 * LANES, 2 * LANES, dtype=BF16),
        ],
        (where, pkg_volt, pkg_diag, block_coupling, pkg_lo, pkg_hi, *bands, current),
        [SMEM] + [VMEM] * 7 + [ANY],
        [pltpu.VMEM((ext + 2 * RADIUS, 2 * LANES), BF16)],
        flops=6 * ext * 2 * LANES * 2 * LANES,
        vmem=28,
    )

    current = lax.all_to_all(
        current, ("grp", "die"), split_axis=0, concat_axis=0, tiled=True
    ).reshape(devices * cap, LANES)

    edges = call(
        functools.partial(inflow_edge_body, blocks, per_row),
        "inflow_edges",
        [shape(REACH, LANES)] * 2,
        (where, ids, current, mix),
        [SMEM, VMEM, VMEM, ANY],
    )
    inflow_lo, inflow_hi = shift_pair(edges, "die")

    pkg_out, picked = call(
        functools.partial(iterate_body, cap, die_count, per_row),
        "package_iterations",
        [shape(blocks, LANES), shape(slots, LANES)],
        (where, ids, ids, current, inflow_lo, inflow_hi, *bands, ends, base, pkg_inv, mix),
        [SMEM, SMEM] + [VMEM] * 10,
        [pltpu.VMEM((ext, LANES), F32)] + [pltpu.VMEM((ext + 2 * RADIUS, 2 * LANES), BF16)] * 2,
        flops=24 * ext * 2 * LANES * 2 * LANES,
        vmem=28,
    )
    bump_out = lax.all_to_all(
        picked.reshape(die_count, cap, LANES), "die", split_axis=0, concat_axis=0, tiled=True
    ).reshape(slots, LANES)
    return (die_out, pkg_out, bump_out)


def solution(mesh):
    return jax.shard_map(
        local,
        mesh=mesh,
        in_specs=(
            P("grp", "die"),
            P("grp", "die"),
            P("grp", "die"),
            P(("grp", "die"), None),
            P(("grp", "die")),
            P(("grp", "die"), None),
            P("die", None),
            P("die", None),
            P(None, "die"),
            P(None, "die"),
            P(),
        ),
        out_specs=(P("grp", "die"), P("die", None), P(("grp", "die"), None)),
        check_vma=False,
    )
```

```python
import functools
import math

import jax
import jax.numpy as jnp
from jax import lax
from jax.experimental import pallas as pl
from jax.experimental.pallas import tpu as pltpu
from jax.sharding import PartitionSpec as P

RADIUS = 32
SWEEPS = 4
ITERS = 4
LANES = 128
HALO_ROWS = 8
REACH = RADIUS * ITERS
WINDOW = LANES + 2 * RADIUS
F32 = jnp.float32
BF16 = jnp.bfloat16
MOST_VMEM = 62
VMEM = pl.BlockSpec(memory_space=pltpu.VMEM)
SMEM = pl.BlockSpec(memory_space=pltpu.SMEM)
ANY = pl.BlockSpec(memory_space=pl.ANY)
HBM = pl.BlockSpec(memory_space=pltpu.HBM)


def sweep_weights(sweeps):
    return [
        1.0 / (1.0 + 0.8 * math.cos(math.pi * (2 * index + 1) / (2 * sweeps)))
        for index in range(sweeps)
    ]


def call(
    body, name, outs, args, specs, scratch=(), flops=0, vmem=16, out_specs=None, aliases=None
):
    bytes_accessed = sum(4 * math.prod(arg.shape) for arg in args)
    return pl.pallas_call(
        body,
        name=name,
        out_shape=outs,
        in_specs=specs,
        out_specs=out_specs or [VMEM] * len(outs),
        input_output_aliases=aliases or {},
        scratch_shapes=list(scratch),
        compiler_params=pltpu.CompilerParams(vmem_limit_bytes=vmem * 1024 * 1024),
        cost_estimate=pl.CostEstimate(
            flops=flops, bytes_accessed=bytes_accessed, transcendentals=0
        ),
    )(*args)


def shape(*dims, dtype=F32):
    return jax.ShapeDtypeStruct(dims, dtype)


def halves(values):
    high = values.astype(BF16)
    low = (values - high.astype(F32)).astype(BF16)
    return high, low


def spread_body(cap, die_count, block_ref, out_ref):
    slots = block_ref.shape[1]
    block = jnp.concatenate(
        [block_ref[...], jnp.zeros((1, LANES - slots), jnp.int32)], axis=1
    )
    for die in range(die_count):
        row = pltpu.roll(block, LANES - die * cap, 1) if die else block
        for at in range(die, out_ref.shape[0], die_count):
            out_ref[at] = row


def asked_rows(cap, die_count, group, start, ids_ref):
    for die in range(die_count):
        for slot in range(cap):
            yield die * cap + slot, ids_ref[group * die_count + die, slot] - start


def pick_body(cap, die_count, where_ref, ids_ref, plane_ref, out_ref, sem):
    for at, row in asked_rows(cap, die_count, where_ref[1], where_ref[0], ids_ref):
        pltpu.make_async_copy(
            plane_ref.at[pl.ds(row, 1), :], out_ref.at[pl.ds(at, 1), :], sem
        ).start()
    pltpu.make_async_copy(plane_ref.at[0 : out_ref.shape[0], :], out_ref, sem).wait()


def build_band(first, pattern, weights):
    place = lax.broadcasted_iota(jnp.int32, (WINDOW, LANES), 0)
    band = None
    for k in range(pattern.shape[0]):
        hit = place == (pattern[k : k + 1, :] - first)
        term = jnp.where(hit, weights[k : k + 1, :], 0.0)
        band = term if band is None else band + term
    fill = jnp.zeros((2 * LANES - WINDOW, LANES), F32)
    return jnp.concatenate(halves(jnp.concatenate([band, fill], axis=0).T), axis=0)


def reciprocal(diag):
    safe = jnp.where(diag > 0.0, diag, 1.0)
    return jnp.where(diag > 0.0, 1.0 / safe, 0.0)


def span(tile, offset=0, size=LANES):
    return pl.ds(pl.multiple_of(tile * LANES + offset, RADIUS), size)


def mixer(coup_ref):
    mix = jnp.concatenate(halves(coup_ref[...]), axis=1)
    return jnp.concatenate([mix, mix], axis=0)


def clear_pads(ref):
    pad = jnp.zeros((RADIUS, 2 * LANES), BF16)
    ref[0:RADIUS, :] = pad
    ref[ref.shape[0] - RADIUS :, :] = pad


def store(ref, tile, values):
    ref[span(tile, RADIUS, values.shape[0]), :] = jnp.concatenate(halves(values), axis=1)


def couple(source, tile, bands, mix, write):
    own = source[span(tile, RADIUS, len(bands) * LANES), :]
    within = jnp.dot(own, mix, preferred_element_type=F32)
    for i, band in enumerate(bands):
        window = source[span(tile + i, 0, WINDOW), :]
        beside = jnp.dot(band[:, :WINDOW], window, preferred_element_type=F32)
        both = beside[:LANES] + beside[LANES:] + within[i * LANES : (i + 1) * LANES]
        write(tile + i, both[:, :LANES] + both[:, LANES:])


def in_chunks(first, count, body, size=4):
    whole = count // size

    @pl.loop(0, whole)
    def _(chunk):
        body(first + chunk * size, size)

    if count % size:
        body(first + whole * size, count % size)


def half_of(where_ref, tiles):
    half = lax.rem(where_ref[1], 2)
    own = tiles // 2
    return half, own, half * own - 1


def prepare_body(
    where_ref, pat_ref, wgt_ref, coup_ref, volt_hbm, diag_hbm, after_ref,
    band_hbm, base_hbm, inv_hbm,
    volt_ref, diag_ref, band_ref, base_ref, inv_ref, plane_ref, sems,
):
    tiles = volt_hbm.shape[0] // LANES
    half, own, shift = half_of(where_ref, tiles)
    first, count = 1 - half, own + 1
    rows = count * LANES
    source = pl.ds(pl.multiple_of((first + shift) * LANES, LANES), rows)
    loads = [
        pltpu.make_async_copy(hbm.at[source, :], ref, sems.at[i])
        for i, (hbm, ref) in enumerate(((volt_hbm, volt_ref), (diag_hbm, diag_ref)))
    ]
    for load in loads:
        load.start()
    clear_pads(plane_ref)
    plane_ref[span(half * (own + 1), RADIUS), :] = jnp.zeros((LANES, 2 * LANES), BF16)
    begin = where_ref[0] + shift * LANES

    def bands(at, size):
        for i in range(size):
            tile = first + at + i
            lanes = pl.ds(pl.multiple_of((tile + shift) * LANES, LANES), LANES)
            band_ref[at + i] = build_band(
                begin + tile * LANES - RADIUS, pat_ref[:, lanes], wgt_ref[:, lanes]
            )
        pltpu.make_async_copy(
            band_ref.at[pl.ds(at, size)], band_hbm.at[pl.ds(at, size)], sems.at[2]
        ).start()

    in_chunks(0, count, bands)
    for load in loads:
        load.wait()

    def place(at, size):
        cut = span(at, 0, size * LANES)
        store(plane_ref, first + at, volt_ref[cut, :])
        inv_ref[cut, :] = reciprocal(diag_ref[cut, :])

    in_chunks(0, count, place)
    inv_out = pltpu.make_async_copy(inv_ref, inv_hbm, sems.at[3])
    inv_out.start()
    mix = mixer(coup_ref)

    def base(at, size):
        def write(tile, values):
            base_ref[span(tile - first), :] = values

        couple(plane_ref, first + at, [band_ref[at + i] for i in range(size)], mix, write)
        cut = span(at, 0, size * LANES)
        pltpu.make_async_copy(base_ref.at[cut, :], base_hbm.at[cut, :], sems.at[4]).start()

    in_chunks(0, count, base)
    pltpu.make_async_copy(band_ref, band_hbm, sems.at[2]).wait()
    inv_out.wait()
    pltpu.make_async_copy(base_ref, base_hbm, sems.at[4]).wait()


def slot_places(cap, ids_ref):
    per_row = LANES // cap
    lane = lax.broadcasted_iota(jnp.int32, (1, LANES), 1)
    places = []
    for at in range(0, ids_ref.shape[0], per_row):
        total = None
        for i in range(per_row):
            row = jnp.where(lane < cap, ids_ref[at + i : at + i + 1, :], 0)
            row = pltpu.roll(row, i * cap, 1) if i else row
            total = row if total is None else total + row
        places.append(total)
    return places


def gather_inflow(places, first, rows, current):
    at = lax.broadcasted_iota(jnp.int32, (rows, LANES), 0) + first
    hits = [jnp.where(at == place, 1.0, 0.0).astype(BF16) for place in places]
    both = jnp.dot(jnp.concatenate(hits, axis=1), current, preferred_element_type=F32)
    return both[:, :LANES] + both[:, LANES:]


PACK_PARTS = 3


def ends_body(
    cap, where_ref, ids_ref, current_ref, pat_ref, wgt_ref, volt_hbm, diag_hbm, after_ref,
    send_ref, own_ref, near_ref, sems,
):
    blocks = volt_hbm.shape[0]
    half, _, _ = half_of(where_ref, blocks // LANES)
    low, high = 0, blocks - LANES
    mine = pl.multiple_of(half * high, LANES)
    theirs = pl.multiple_of((1 - half) * high, LANES)
    copies = []

    def fetch(source, start, rows, target):
        copies.append(
            pltpu.make_async_copy(source.at[pl.ds(start, rows), :], target, sems.at[len(copies)])
        )
        copies[-1].start()

    for ref, start in ((own_ref, mine), (send_ref, theirs)):
        fetch(volt_hbm, start, LANES, ref.at[0:LANES, :])
        fetch(diag_hbm, start, LANES, ref.at[LANES : 2 * LANES, :])
    fetch(volt_hbm, LANES, RADIUS, near_ref.at[0:RADIUS, :])
    fetch(volt_hbm, blocks - LANES - RADIUS, RADIUS, near_ref.at[RADIUS : 2 * RADIUS, :])
    places = slot_places(cap, ids_ref)
    current = jnp.concatenate(halves(current_ref[...]), axis=1)
    count = pat_ref.shape[0]
    at = PACK_PARTS * LANES
    for ref, start in ((own_ref, mine), (send_ref, theirs)):
        ref[2 * LANES : at, :] = gather_inflow(places, where_ref[0] + start, LANES, current)
        lanes = pl.ds(start, LANES)
        ref[at : at + count, :] = pat_ref[:, lanes].astype(F32)
        ref[at + count : at + 2 * count, :] = wgt_ref[:, lanes]
    for copy in copies:
        copy.wait()


def interior_body(
    cap, die_count, where_ref, asked_ref, ids_ref, current_ref, coup_ref,
    band_hbm, base_hbm, inv_hbm,
    out_hbm, picked_ref, near_ref,
    band_ref, base_ref, inv_ref, out_ref, inflow_ref, here_ref, there_ref, sems,
):
    own = out_hbm.shape[0] // LANES
    half, _, shift = half_of(where_ref, 2 * own)
    first, count = 1 - half, own + 1
    loads = [
        pltpu.make_async_copy(hbm, ref, sems.at[i])
        for i, (hbm, ref) in enumerate(
            ((base_hbm, base_ref), (inv_hbm, inv_ref), (band_hbm, band_ref))
        )
    ]
    for load in loads:
        load.start()
    begin = where_ref[0] + (first + shift) * LANES
    places = slot_places(cap, ids_ref)
    current = jnp.concatenate(halves(current_ref[...]), axis=1)
    outer = half * (own + 1)
    for ref in (here_ref, there_ref):
        clear_pads(ref)
        ref[span(outer, RADIUS), :] = jnp.zeros((LANES, 2 * LANES), BF16)

    def inflow(at, size):
        rows = size * LANES
        inflow_ref[span(at, 0, rows), :] = gather_inflow(
            places, begin + at * LANES, rows, current
        )

    in_chunks(0, count, inflow)
    loads[0].wait()
    loads[1].wait()

    def start(at, size):
        cut = span(at, 0, size * LANES)
        store(here_ref, first + at, -(inflow_ref[cut, :] + base_ref[cut, :]) * inv_ref[cut, :])

    in_chunks(0, count, start)
    loads[2].wait()
    mix = mixer(coup_ref)
    beyond = jnp.where(half == 0, 2 * LANES, own * LANES - RADIUS)
    near = pl.ds(pl.multiple_of(beyond + RADIUS, RADIUS), RADIUS)
    refs = (here_ref, there_ref)
    for iteration in range(1, ITERS):
        source, target = refs[(iteration - 1) % 2], refs[iteration % 2]
        last = iteration == ITERS - 1
        near_ref[iteration - 1] = source[near, :]

        def write(tile, coupled, target=target, last=last):
            cut = span(tile - first)
            values = -(inflow_ref[cut, :] + coupled) * inv_ref[cut, :]
            if last:
                out_ref[span(tile - 1), :] = values
            else:
                store(target, tile, values)

        def step(at, size, source=source, write=write):
            bands = [band_ref[at - first + i] for i in range(size)]
            couple(source, at, bands, mix, write)

        def final(at, size, step=step):
            step(at, size)
            cut = span(at - 1, 0, size * LANES)
            pltpu.make_async_copy(out_ref.at[cut, :], out_hbm.at[cut, :], sems.at[3]).start()

        if last:
            in_chunks(1, own, final)
        else:
            in_chunks(first, count, step)

    base_row = where_ref[0] + half * own * LANES
    pair = where_ref[1] - half
    for member in range(2):
        offset = member * (picked_ref.shape[0] // 2)
        for at, row in asked_rows(cap, die_count, pair + member, base_row, asked_ref):
            inside = (row >= 0) & (row < own * LANES)
            safe = jnp.clip(row, 0, own * LANES - 1)
            values = out_ref[pl.ds(safe, 1), :]
            picked_ref[pl.ds(offset + at, 1), :] = jnp.where(inside, values, 0.0)
    pltpu.make_async_copy(out_ref, out_hbm, sems.at[3]).wait()


def outermost_body(
    cap, die_count, where_ref, asked_ref, coup_ref, halo_ref, own_ref, volt_near_ref, near_ref,
    picked_in_ref, out_in_hbm, picked_ref, out_hbm,
    band_ref, here_ref, there_ref, out_ref, sem,
):
    own = out_hbm.shape[0] // LANES
    half, _, _ = half_of(where_ref, 2 * own)
    count = (own_ref.shape[0] - PACK_PARTS * LANES) // 2
    mix = mixer(coup_ref)
    packs = [
        jnp.where(half == at, halo_ref[...], own_ref[...]) for at in range(2)
    ]
    begin = where_ref[0] + (2 * half * own - 1) * LANES
    at = PACK_PARTS * LANES
    inv, inflow = [], []

    def put_near(ref, values):
        size = ref.shape[0]
        ref[0:RADIUS, :] = jnp.where(half == 0, jnp.zeros_like(values), values)
        ref[size - RADIUS : size, :] = jnp.where(half == 0, values, jnp.zeros_like(values))

    for tile, pack in enumerate(packs):
        band_ref[tile] = build_band(
            begin + tile * LANES - RADIUS,
            pack[at : at + count].astype(jnp.int32),
            pack[at + count : at + 2 * count],
        )
        store(here_ref, tile, pack[:LANES])
        inv.append(reciprocal(pack[LANES : 2 * LANES]))
        inflow.append(pack[2 * LANES : at])
    volt_near = jnp.where(half == 0, volt_near_ref[0:RADIUS, :], volt_near_ref[RADIUS:, :])
    put_near(here_ref, jnp.concatenate(halves(volt_near), axis=1))
    refs = (here_ref, there_ref)
    for iteration in range(ITERS):
        source, target = refs[iteration % 2], refs[(iteration + 1) % 2]
        results = []
        couple(
            source, 0, [band_ref[0], band_ref[1]], mix, lambda tile, values: results.append(values)
        )
        results = [
            -(inflow[tile] + values) * inv[tile] for tile, values in enumerate(results)
        ]
        if iteration < ITERS - 1:
            for tile, values in enumerate(results):
                store(target, tile, values)
            put_near(target, near_ref[iteration])
    out_ref[...] = jnp.where(half == 0, results[1], results[0])
    row = pl.multiple_of(half * (own - 1) * LANES, LANES)
    copy = pltpu.make_async_copy(out_ref, out_hbm.at[pl.ds(row, LANES), :], sem)
    copy.start()
    base_row = where_ref[0] + half * (2 * own - 1) * LANES
    pair = where_ref[1] - half
    for member in range(2):
        offset = member * (picked_ref.shape[0] // 2)
        for at, row in asked_rows(cap, die_count, pair + member, base_row, asked_ref):
            inside = (row >= 0) & (row < LANES)
            values = out_ref[pl.ds(jnp.clip(row, 0, LANES - 1), 1), :]
            cut = pl.ds(offset + at, 1)
            picked_ref[cut, :] = jnp.where(inside, values, picked_in_ref[cut, :])
    copy.wait()


def join_body(where_ref, mine_hbm, other_hbm, out_hbm, sems):
    rows = mine_hbm.shape[0]
    half = lax.rem(where_ref[1], 2)
    copies = [
        pltpu.make_async_copy(
            source, out_hbm.at[pl.ds(pl.multiple_of(at * rows, LANES), rows), :], sems.at[i]
        )
        for i, (source, at) in enumerate(((mine_hbm, half), (other_hbm, 1 - half)))
    ]
    for copy in copies:
        copy.start()
    for copy in copies:
        copy.wait()


def scatter_body(cols, where_ref, node_ref, cond_ref, start_ref, volt_ref, load_ref, shunt_ref,
                 right_ref, inv_ref, edge_ref):
    blocks = node_ref.shape[0]
    rows = volt_ref.shape[0]
    group = 8
    row_at = lax.broadcasted_iota(jnp.int32, (rows, LANES), 0)
    col_at = lax.broadcasted_iota(jnp.int32, (cols, LANES), 0)
    total = jnp.zeros((4 * rows, cols), F32)
    for first in range(0, blocks, group):
        node = node_ref[first : first + group, :]
        live = node >= 0
        cond = jnp.where(live, cond_ref[first : first + group, :], 0.0)
        flow = cond * start_ref[first : first + group, :]
        safe = jnp.where(live, node, 0)
        row, col = safe // cols, safe % cols
        parts = halves(cond) + halves(flow)
        left, right = [], []
        for i in range(group):
            spot = jnp.where(row_at == row[i : i + 1, :], 1.0, 0.0).astype(BF16)
            left.append(
                jnp.concatenate([spot * part[i : i + 1, :] for part in parts], axis=0)
            )
            right.append(jnp.where(col_at == col[i : i + 1, :], 1.0, 0.0).astype(BF16))
        total = total + lax.dot_general(
            jnp.concatenate(left, axis=1),
            jnp.concatenate(right, axis=1),
            (((1,), (1,)), ((), ())),
            preferred_element_type=F32,
        )
    gsum = total[:rows] + total[rows : 2 * rows]
    inject = total[2 * rows : 3 * rows] + total[3 * rows :]
    inv = 1.0 / (4.0 + shunt_ref[...] + gsum)
    right_side = (inject - load_ref[...]) * inv
    right_ref[...] = right_side
    inv_ref[...] = inv
    volt = volt_ref[...]
    top, bottom = (
        jnp.concatenate([volt[cut], right_side[cut], inv[cut]], axis=0)
        for cut in (slice(0, HALO_ROWS), slice(rows - HALO_ROWS, rows))
    )
    send_beside(edge_ref, where_ref[1], top, bottom)


def send_beside(ref, mine, first, last):
    count = ref.shape[0]
    ref[...] = jnp.zeros(ref.shape, F32)

    @pl.when(mine > 0)
    def _():
        ref[jnp.maximum(mine - 1, 0)] = first

    @pl.when(mine < count - 1)
    def _():
        ref[jnp.minimum(mine + 1, count - 1)] = last


def from_beside(ref, mine):
    count = ref.shape[0]
    before = jnp.where(mine > 0, ref[jnp.maximum(mine - 1, 0)], 0.0)
    after = jnp.where(mine < count - 1, ref[jnp.minimum(mine + 1, count - 1)], 0.0)
    return before, after


def extended(own, top, bottom, index):
    cut = slice(index * HALO_ROWS, (index + 1) * HALO_ROWS)
    return jnp.concatenate([top[cut], own, bottom[cut]], axis=0)


def edge_body(where_ref, volt_ref, right_ref, inv_ref, beside_ref, out_ref):
    cols = volt_ref.shape[1]
    top, bottom = from_beside(beside_ref, where_ref[1])
    out_rows, high = out_ref.shape[1:]
    west, east = None, None
    for index, ref in enumerate((volt_ref, right_ref, inv_ref)):
        whole = extended(ref[...], top, bottom, index)
        lane = lax.broadcasted_iota(jnp.int32, (whole.shape[0], LANES), 1)
        head, tail = whole[:, :LANES], whole[:, cols - LANES :]
        at = index * SWEEPS
        head = pltpu.roll(head, at, 1) if at else head
        tail = pltpu.roll(tail, at + SWEEPS, 1)
        west = head if west is None else jnp.where(lane >= at, head, west)
        east = tail if east is None else jnp.where(lane >= at, tail, east)
    fill = jnp.zeros((high - west.shape[0], LANES), F32)
    west, east = (
        jnp.concatenate([part, fill], axis=0).T[:out_rows] for part in (west, east)
    )
    send_beside(out_ref, where_ref[2], west, east)


def sweep_body(copies, where_ref, node_ref, cond_ref, start_ref, volt_ref, right_ref, inv_ref,
               beside_ref, column_ref, out_ref, current_ref):
    rows, cols = volt_ref.shape
    blocks = node_ref.shape[0]
    cap = current_ref.shape[1]
    whole = []
    top, bottom = from_beside(beside_ref, where_ref[1])
    out_rows, high = column_ref.shape[1:]
    fill = jnp.zeros((LANES - out_rows, high), F32)
    wests, easts = (
        jnp.concatenate([part, fill], axis=0).T[: rows + 2 * HALO_ROWS]
        for part in from_beside(column_ref, where_ref[2])
    )
    for index, ref in enumerate((volt_ref, right_ref, inv_ref)):
        own = extended(ref[...], top, bottom, index)
        at = index * SWEEPS
        west = pltpu.roll(wests, LANES - SWEEPS - at, 1)
        east = pltpu.roll(easts, LANES - at, 1) if at else easts
        whole.append(jnp.concatenate([west, own, east], axis=1))
    volt, right_side, inv = whole
    high, wide = volt.shape
    for weight in sweep_weights(SWEEPS):
        beside = (
            pltpu.roll(volt, 1, 0)
            + pltpu.roll(volt, high - 1, 0)
            + pltpu.roll(volt, 1, 1)
            + pltpu.roll(volt, wide - 1, 1)
        )
        volt = (1.0 - weight) * volt + weight * (right_side + beside * inv)
    volt = volt[HALO_ROWS : HALO_ROWS + rows, LANES : LANES + cols]
    out_ref[...] = volt
    both = jnp.concatenate(halves(volt), axis=0)
    group = 8
    row_at = lax.broadcasted_iota(jnp.int32, (rows, LANES), 0)
    col_at = lax.broadcasted_iota(jnp.int32, (cols, LANES), 0)
    dies = blocks // cap
    for first in range(0, blocks, group):
        node = node_ref[first : first + group, :]
        live = node >= 0
        cond = jnp.where(live, cond_ref[first : first + group, :], 0.0)
        safe = jnp.where(live, node, 0)
        row, col = safe // cols, safe % cols
        spots = jnp.concatenate(
            [
                jnp.where(col_at == col[i : i + 1, :], 1.0, 0.0).astype(BF16)
                for i in range(group)
            ],
            axis=1,
        )
        found = jnp.dot(both, spots, preferred_element_type=F32)
        found = found[:rows] + found[rows:]
        for i in range(group):
            mine = found[:, i * LANES : (i + 1) * LANES]
            at_bump = jnp.sum(
                jnp.where(row_at == row[i : i + 1, :], mine, 0.0), axis=0, keepdims=True
            )
            block = first + i
            current = cond[i : i + 1, :] * (start_ref[block : block + 1, :] - at_bump)
            current_ref[block // cap, block % cap : block % cap + 1, :] = current
    for copy in range(1, copies):
        current_ref[copy * dies : (copy + 1) * dies] = current_ref[0:dies]


def local(
    die_volt,
    die_load,
    die_shunt,
    bump_node,
    bump_block,
    bump_cond,
    pkg_volt,
    pkg_diag,
    pkg_pattern,
    pkg_weight,
    block_coupling,
):
    die_count = lax.axis_size("die")
    group_count = lax.axis_size("grp")
    devices = die_count * group_count
    blocks = pkg_volt.shape[0]
    tiles = blocks // LANES
    neighbours = pkg_pattern.shape[0]
    slots = bump_block.shape[0]
    cap = slots // die_count
    rows, cols = die_volt.shape
    group, die = lax.axis_index("grp"), lax.axis_index("die")
    where = jnp.stack([die * blocks, group, die]).astype(jnp.int32)

    (spread,) = call(
        functools.partial(spread_body, cap, die_count),
        "spread_blocks",
        [shape(devices, 1, LANES, dtype=jnp.int32)],
        (bump_block.reshape(1, slots),),
        [VMEM],
    )
    ids = lax.all_to_all(
        spread, ("grp", "die"), split_axis=0, concat_axis=0, tiled=True
    ).reshape(devices, LANES)

    (picked,) = call(
        functools.partial(pick_body, cap, die_count),
        "pick_rows",
        [shape(slots, LANES)],
        (where, ids, pkg_volt),
        [SMEM, SMEM, HBM],
        [pltpu.SemaphoreType.DMA(())],
        vmem=MOST_VMEM,
    )
    bump_start = lax.all_to_all(
        picked.reshape(die_count, cap, LANES), "die", split_axis=0, concat_axis=0, tiled=True
    ).reshape(slots, LANES)

    right_side, inv, edge = call(
        functools.partial(scatter_body, cols),
        "scatter_bumps",
        [shape(rows, cols), shape(rows, cols), shape(group_count, 3 * HALO_ROWS, cols)],
        (where, bump_node, bump_cond, bump_start, die_volt, die_load, die_shunt),
        [SMEM] + [VMEM] * 6,
        flops=8 * rows * slots * LANES * cols,
    )
    beside = lax.all_to_all(edge, "grp", split_axis=0, concat_axis=0, tiled=True)

    edge_rows = -(-3 * SWEEPS // 8) * 8
    edge_cols = -(-(rows + 2 * HALO_ROWS) // LANES) * LANES
    (column,) = call(
        edge_body,
        "edge_columns",
        [shape(die_count, edge_rows, edge_cols)],
        (where, die_volt, right_side, inv, beside),
        [SMEM] + [VMEM] * 4,
    )
    column = lax.all_to_all(column, "die", split_axis=0, concat_axis=0, tiled=True)

    die_out, current = call(
        functools.partial(sweep_body, group_count),
        "sweeps",
        [shape(rows, cols), shape(devices, cap, LANES)],
        (where, bump_node, bump_cond, bump_start, die_volt, right_side, inv, beside, column),
        [SMEM] + [VMEM] * 8,
        flops=4 * rows * slots * LANES * cols,
    )
    own = tiles // 2
    count = own + 1
    dma = pltpu.SemaphoreType.DMA
    plane = pltpu.VMEM(((own + 2) * LANES + 2 * RADIUS, 2 * LANES), BF16)
    half_rows = pltpu.VMEM((count * LANES, LANES), F32)
    half_bands = pltpu.VMEM((count, 2 * LANES, 2 * LANES), BF16)
    band, base, pkg_inv = call(
        prepare_body,
        "package_prepare",
        [
            shape(count, 2 * LANES, 2 * LANES, dtype=BF16),
            shape(count * LANES, LANES),
            shape(count * LANES, LANES),
        ],
        (where, pkg_pattern, pkg_weight, block_coupling, pkg_volt, pkg_diag, die_out),
        [SMEM, VMEM, VMEM, VMEM, HBM, HBM, HBM],
        [half_rows, half_rows, half_bands, half_rows, half_rows, plane, dma((5,))],
        flops=8 * count * LANES**3,
        vmem=MOST_VMEM,
        out_specs=[HBM] * 3,
    )

    current = lax.all_to_all(
        current, ("grp", "die"), split_axis=0, concat_axis=0, tiled=True
    ).reshape(devices * cap, LANES)

    pack_rows = PACK_PARTS * LANES + 2 * neighbours
    send, outermost, volt_near = call(
        functools.partial(ends_body, cap),
        "package_ends",
        [shape(pack_rows, LANES), shape(pack_rows, LANES), shape(2 * RADIUS, LANES)],
        (where, ids, current, pkg_pattern, pkg_weight, pkg_volt, pkg_diag, base),
        [SMEM] + [VMEM] * 4 + [HBM, HBM, HBM],
        [dma((6,))],
        vmem=MOST_VMEM,
    )
    halo = lax.ppermute(
        send,
        ("grp", "die"),
        [
            (g * die_count + d, g * die_count + d + 1 - 2 * (g % 2))
            for g in range(group_count)
            for d in range(die_count)
            if 0 <= d + 1 - 2 * (g % 2) < die_count
        ],
    )
    half_out, picked, near = call(
        functools.partial(interior_body, cap, die_count),
        "package_interior",
        [
            shape(own * LANES, LANES),
            shape(2 * slots, LANES),
            shape(ITERS - 1, RADIUS, 2 * LANES, dtype=BF16),
        ],
        (where, ids, ids, current, block_coupling, band, base, pkg_inv),
        [SMEM, SMEM, VMEM, VMEM, VMEM, HBM, HBM, HBM],
        [
            half_bands, half_rows, half_rows, pltpu.VMEM((own * LANES, LANES), F32),
            half_rows, plane, plane, dma((4,)),
        ],
        flops=24 * count * LANES**3,
        vmem=MOST_VMEM,
        out_specs=[HBM, VMEM, VMEM],
    )
    edge_plane = pltpu.VMEM((2 * LANES + 2 * RADIUS, 2 * LANES), BF16)
    picked, half_out = call(
        functools.partial(outermost_body, cap, die_count),
        "package_outermost",
        [shape(2 * slots, LANES), shape(own * LANES, LANES)],
        (where, ids, block_coupling, halo, outermost, volt_near, near, picked, half_out),
        [SMEM, SMEM] + [VMEM] * 6 + [HBM],
        [
            pltpu.VMEM((2, 2 * LANES, 2 * LANES), BF16), edge_plane, edge_plane,
            pltpu.VMEM((LANES, LANES), F32), dma(()),
        ],
        flops=8 * LANES**3,
        vmem=MOST_VMEM,
        out_specs=[VMEM, HBM],
        aliases={8: 1},
    )
    pair = 2 * die_count
    bump_out = lax.all_to_all(
        picked.reshape(pair, cap, LANES),
        ("grp", "die"),
        split_axis=0,
        concat_axis=0,
        axis_index_groups=[
            [first + i for i in range(pair)] for first in range(0, devices, pair)
        ],
        tiled=True,
    ).reshape(2, slots, LANES)
    bump_out = bump_out[0] + bump_out[1]
    other = lax.ppermute(half_out, "grp", [(g, g ^ 1) for g in range(group_count)])
    (pkg_out,) = call(
        join_body,
        "join_halves",
        [shape(blocks, LANES)],
        (where, half_out, other),
        [SMEM, HBM, HBM],
        [dma((2,))],
        vmem=MOST_VMEM,
        out_specs=[HBM],
    )
    return (die_out, pkg_out, bump_out)


def solution(mesh):
    return jax.shard_map(
        local,
        mesh=mesh,
        in_specs=(
            P("grp", "die"),
            P("grp", "die"),
            P("grp", "die"),
            P(("grp", "die"), None),
            P(("grp", "die")),
            P(("grp", "die"), None),
            P("die", None),
            P("die", None),
            P(None, "die"),
            P(None, "die"),
            P(),
        ),
        out_specs=(P("grp", "die"), P("die", None), P(("grp", "die"), None)),
        check_vma=False,
    )
```

```python
import functools
import math

import jax
import jax.numpy as jnp
from jax import lax
from jax.experimental import pallas as pl
from jax.experimental.pallas import tpu as pltpu
from jax.sharding import PartitionSpec as P

RADIUS = 32
SWEEPS = 4
ITERS = 4
LANES = 128
HALO_ROWS = 8
REACH = RADIUS * ITERS
WINDOW = LANES + 2 * RADIUS
F32 = jnp.float32
BF16 = jnp.bfloat16
MOST_VMEM = 60
VMEM = pl.BlockSpec(memory_space=pltpu.VMEM)
SMEM = pl.BlockSpec(memory_space=pltpu.SMEM)
ANY = pl.BlockSpec(memory_space=pl.ANY)
HBM = pl.BlockSpec(memory_space=pltpu.HBM)


def sweep_weights(sweeps):
    return [
        1.0 / (1.0 + 0.8 * math.cos(math.pi * (2 * index + 1) / (2 * sweeps)))
        for index in range(sweeps)
    ]


def call(
    body, name, outs, args, specs, scratch=(), flops=0, vmem=16, out_specs=None, aliases=None
):
    bytes_accessed = sum(4 * math.prod(arg.shape) for arg in args)
    return pl.pallas_call(
        body,
        name=name,
        out_shape=outs,
        in_specs=specs,
        out_specs=out_specs or [VMEM] * len(outs),
        input_output_aliases=aliases or {},
        scratch_shapes=list(scratch),
        compiler_params=pltpu.CompilerParams(vmem_limit_bytes=vmem * 1024 * 1024),
        cost_estimate=pl.CostEstimate(
            flops=flops, bytes_accessed=bytes_accessed, transcendentals=0
        ),
    )(*args)


def shape(*dims, dtype=F32):
    return jax.ShapeDtypeStruct(dims, dtype)


def halves(values):
    high = values.astype(BF16)
    low = (values - high.astype(F32)).astype(BF16)
    return high, low


def spread_body(cap, die_count, block_ref, out_ref):
    slots = block_ref.shape[1]
    block = jnp.concatenate(
        [block_ref[...], jnp.zeros((1, LANES - slots), jnp.int32)], axis=1
    )
    for die in range(die_count):
        row = pltpu.roll(block, LANES - die * cap, 1) if die else block
        for at in range(die, out_ref.shape[0], die_count):
            out_ref[at] = row


def asked_rows(cap, die_count, group, start, ids_ref):
    for die in range(die_count):
        for slot in range(cap):
            yield die * cap + slot, ids_ref[group * die_count + die, slot] - start


def pick_body(cap, die_count, where_ref, ids_ref, plane_ref, out_ref, sem):
    for at, row in asked_rows(cap, die_count, where_ref[1], where_ref[0], ids_ref):
        pltpu.make_async_copy(
            plane_ref.at[pl.ds(row, 1), :], out_ref.at[pl.ds(at, 1), :], sem
        ).start()
    pltpu.make_async_copy(plane_ref.at[0 : out_ref.shape[0], :], out_ref, sem).wait()


def build_band(first, pattern, weights):
    place = lax.broadcasted_iota(jnp.int32, (WINDOW, LANES), 0)
    band = None
    for k in range(pattern.shape[0]):
        hit = place == (pattern[k : k + 1, :] - first)
        term = jnp.where(hit, weights[k : k + 1, :], 0.0)
        band = term if band is None else band + term
    fill = jnp.zeros((2 * LANES - WINDOW, LANES), F32)
    return jnp.concatenate(halves(jnp.concatenate([band, fill], axis=0).T), axis=0)


def reciprocal(diag):
    safe = jnp.where(diag > 0.0, diag, 1.0)
    return jnp.where(diag > 0.0, 1.0 / safe, 0.0)


def span(tile, offset=0, size=LANES):
    return pl.ds(pl.multiple_of(tile * LANES + offset, RADIUS), size)


def mixer(coup_ref):
    mix = jnp.concatenate(halves(coup_ref[...]), axis=1)
    return jnp.concatenate([mix, mix], axis=0)


def clear_pads(ref):
    pad = jnp.zeros((RADIUS, 2 * LANES), BF16)
    ref[0:RADIUS, :] = pad
    ref[ref.shape[0] - RADIUS :, :] = pad


def store(ref, tile, values):
    ref[span(tile, RADIUS, values.shape[0]), :] = jnp.concatenate(halves(values), axis=1)


def couple(source, tile, bands, mix, write):
    own = source[span(tile, RADIUS, len(bands) * LANES), :]
    within = jnp.dot(own, mix, preferred_element_type=F32)
    for i, band in enumerate(bands):
        window = source[span(tile + i, 0, WINDOW), :]
        beside = jnp.dot(band[:, :WINDOW], window, preferred_element_type=F32)
        both = beside[:LANES] + beside[LANES:] + within[i * LANES : (i + 1) * LANES]
        write(tile + i, both[:, :LANES] + both[:, LANES:])


def in_chunks(first, count, body, size=4):
    whole = count // size

    @pl.loop(0, whole)
    def _(chunk):
        body(first + chunk * size, size)

    if count % size:
        body(first + whole * size, count % size)


def half_of(where_ref, tiles):
    half = lax.rem(where_ref[1], 2)
    own = tiles // 2
    return half, own, half * own - 1


def prepare_body(
    where_ref, pat_ref, wgt_ref, coup_ref, volt_hbm, diag_hbm, after_ref,
    band_hbm, base_hbm, inv_hbm, send_ref, own_ref, near_ref,
    volt_ref, diag_ref, band_ref, base_ref, inv_ref, plane_ref, sems,
):
    tiles = volt_hbm.shape[0] // LANES
    half, own, shift = half_of(where_ref, tiles)
    first, count = 1 - half, own + 1
    rows = count * LANES
    source = pl.ds(pl.multiple_of((first + shift) * LANES, LANES), rows)
    loads = [
        pltpu.make_async_copy(hbm.at[source, :], ref, sems.at[i])
        for i, (hbm, ref) in enumerate(((volt_hbm, volt_ref), (diag_hbm, diag_ref)))
    ]
    for load in loads:
        load.start()
    high = (tiles - 1) * LANES
    mine, theirs = (
        pl.multiple_of(at * high, LANES) for at in (half, 1 - half)
    )
    neighbours = pat_ref.shape[0]

    def fetch(hbm, start, target):
        rows = target.shape[0]
        loads.append(pltpu.make_async_copy(hbm.at[pl.ds(start, rows), :], target, sems.at[len(loads) + 3]))
        loads[-1].start()

    for ref, start in ((own_ref, mine), (send_ref, theirs)):
        fetch(volt_hbm, start, ref.at[0:LANES, :])
        fetch(diag_hbm, start, ref.at[LANES : 2 * LANES, :])
        lanes = pl.ds(start, LANES)
        at = 2 * LANES
        ref[at : at + neighbours, :] = pat_ref[:, lanes].astype(F32)
        ref[at + neighbours : at + 2 * neighbours, :] = wgt_ref[:, lanes]
    fetch(volt_hbm, LANES, near_ref.at[0:RADIUS, :])
    fetch(volt_hbm, high - RADIUS, near_ref.at[RADIUS : 2 * RADIUS, :])
    clear_pads(plane_ref)
    plane_ref[span(half * (own + 1), RADIUS), :] = jnp.zeros((LANES, 2 * LANES), BF16)
    begin = where_ref[0] + shift * LANES

    def bands(at, size):
        for i in range(size):
            tile = first + at + i
            lanes = pl.ds(pl.multiple_of((tile + shift) * LANES, LANES), LANES)
            band_ref[at + i] = build_band(
                begin + tile * LANES - RADIUS, pat_ref[:, lanes], wgt_ref[:, lanes]
            )
        pltpu.make_async_copy(
            band_ref.at[pl.ds(at, size)], band_hbm.at[pl.ds(at, size)], sems.at[2]
        ).start()

    in_chunks(0, count, bands)
    for load in loads:
        load.wait()

    def place(at, size):
        cut = span(at, 0, size * LANES)
        store(plane_ref, first + at, volt_ref[cut, :])
        inv_ref[cut, :] = reciprocal(diag_ref[cut, :])

    in_chunks(0, count, place)
    inv_out = pltpu.make_async_copy(inv_ref, inv_hbm, sems.at[3])
    inv_out.start()
    mix = mixer(coup_ref)

    def base(at, size):
        def write(tile, values):
            base_ref[span(tile - first), :] = values

        couple(plane_ref, first + at, [band_ref[at + i] for i in range(size)], mix, write)
        cut = span(at, 0, size * LANES)
        pltpu.make_async_copy(base_ref.at[cut, :], base_hbm.at[cut, :], sems.at[4]).start()

    in_chunks(0, count, base)
    pltpu.make_async_copy(band_ref, band_hbm, sems.at[2]).wait()
    inv_out.wait()
    pltpu.make_async_copy(base_ref, base_hbm, sems.at[4]).wait()


def slot_places(cap, ids_ref):
    per_row = LANES // cap
    lane = lax.broadcasted_iota(jnp.int32, (1, LANES), 1)
    places = []
    for at in range(0, ids_ref.shape[0], per_row):
        total = None
        for i in range(per_row):
            row = jnp.where(lane < cap, ids_ref[at + i : at + i + 1, :], 0)
            row = pltpu.roll(row, i * cap, 1) if i else row
            total = row if total is None else total + row
        places.append(total)
    return places


def gather_inflow(places, first, rows, current):
    at = lax.broadcasted_iota(jnp.int32, (rows, LANES), 0) + first
    hits = [jnp.where(at == place, 1.0, 0.0).astype(BF16) for place in places]
    both = jnp.dot(jnp.concatenate(hits, axis=1), current, preferred_element_type=F32)
    return both[:, :LANES] + both[:, LANES:]


def ends_body(cap, where_ref, ids_ref, current_ref, pack_ref, after_ref, send_ref, own_ref):
    tiles = where_ref[3]
    half = lax.rem(where_ref[1], 2)
    high = (tiles - 1) * LANES
    places = slot_places(cap, ids_ref)
    current = jnp.concatenate(halves(current_ref[...]), axis=1)
    own_ref[...] = gather_inflow(places, where_ref[0] + half * high, LANES, current)
    send_ref[0:LANES, :] = gather_inflow(
        places, where_ref[0] + (1 - half) * high, LANES, current
    )
    send_ref[LANES:, :] = pack_ref[...]


def interior_body(
    cap, die_count, where_ref, asked_ref, ids_ref, current_ref, coup_ref, after_ref,
    band_hbm, base_hbm, inv_hbm,
    out_hbm, full_hbm, picked_ref, near_ref,
    band_ref, base_ref, inv_ref, out_ref, inflow_ref, here_ref, there_ref, sems,
):
    own = out_hbm.shape[0] // LANES
    half, _, shift = half_of(where_ref, 2 * own)
    first, count = 1 - half, own + 1
    loads = [
        pltpu.make_async_copy(hbm, ref, sems.at[i])
        for i, (hbm, ref) in enumerate(
            ((base_hbm, base_ref), (inv_hbm, inv_ref), (band_hbm, band_ref))
        )
    ]
    for load in loads:
        load.start()
    begin = where_ref[0] + (first + shift) * LANES
    places = slot_places(cap, ids_ref)
    current = jnp.concatenate(halves(current_ref[...]), axis=1)
    outer = half * (own + 1)
    for ref in (here_ref, there_ref):
        clear_pads(ref)
        ref[span(outer, RADIUS), :] = jnp.zeros((LANES, 2 * LANES), BF16)

    def inflow(at, size):
        rows = size * LANES
        inflow_ref[span(at, 0, rows), :] = gather_inflow(
            places, begin + at * LANES, rows, current
        )

    in_chunks(0, count, inflow)
    loads[0].wait()
    loads[1].wait()

    def start(at, size):
        cut = span(at, 0, size * LANES)
        store(here_ref, first + at, -(inflow_ref[cut, :] + base_ref[cut, :]) * inv_ref[cut, :])

    in_chunks(0, count, start)
    loads[2].wait()
    mix = mixer(coup_ref)
    beyond = jnp.where(half == 0, 2 * LANES, own * LANES - RADIUS)
    near = pl.ds(pl.multiple_of(beyond + RADIUS, RADIUS), RADIUS)
    refs = (here_ref, there_ref)
    for iteration in range(1, ITERS):
        source, target = refs[(iteration - 1) % 2], refs[iteration % 2]
        last = iteration == ITERS - 1
        near_ref[iteration - 1] = source[near, :]

        def write(tile, coupled, target=target, last=last):
            cut = span(tile - first)
            values = -(inflow_ref[cut, :] + coupled) * inv_ref[cut, :]
            if last:
                out_ref[span(tile - 1), :] = values
            else:
                store(target, tile, values)

        def step(at, size, source=source, write=write):
            bands = [band_ref[at - first + i] for i in range(size)]
            couple(source, at, bands, mix, write)

        def final(at, size, step=step):
            step(at, size)
            cut = span(at - 1, 0, size * LANES)
            whole = span(half * own + at - 1, 0, size * LANES)
            pltpu.make_async_copy(out_ref.at[cut, :], out_hbm.at[cut, :], sems.at[3]).start()
            pltpu.make_async_copy(out_ref.at[cut, :], full_hbm.at[whole, :], sems.at[4]).start()

        if last:
            in_chunks(1, own, final)
        else:
            in_chunks(first, count, step)

    base_row = where_ref[0] + half * own * LANES
    pair = where_ref[1] - half
    for member in range(2):
        offset = member * (picked_ref.shape[0] // 2)
        for at, row in asked_rows(cap, die_count, pair + member, base_row, asked_ref):
            inside = (row >= 0) & (row < own * LANES)
            safe = jnp.clip(row, 0, own * LANES - 1)
            values = out_ref[pl.ds(safe, 1), :]
            picked_ref[pl.ds(offset + at, 1), :] = jnp.where(inside, values, 0.0)
    pltpu.make_async_copy(out_ref, out_hbm, sems.at[3]).wait()
    pltpu.make_async_copy(out_ref, full_hbm.at[0 : own * LANES, :], sems.at[4]).wait()


def outermost_body(
    cap, die_count, where_ref, asked_ref, coup_ref, halo_ref, own_ref, inflow_ref, volt_near_ref,
    near_ref, picked_in_ref, picked_ref, out_ref, band_ref, here_ref, there_ref,
):
    half = lax.rem(where_ref[1], 2)
    own = where_ref[3] // 2
    count = (own_ref.shape[0] - 2 * LANES) // 2
    mix = mixer(coup_ref)
    packs = [
        jnp.where(half == at, halo_ref[LANES:, :], own_ref[...]) for at in range(2)
    ]
    inflow = [
        jnp.where(half == at, halo_ref[0:LANES, :], inflow_ref[...]) for at in range(2)
    ]
    begin = where_ref[0] + (2 * half * own - 1) * LANES
    at = 2 * LANES
    inv = []

    def put_near(ref, values):
        size = ref.shape[0]
        ref[0:RADIUS, :] = jnp.where(half == 0, jnp.zeros_like(values), values)
        ref[size - RADIUS : size, :] = jnp.where(half == 0, values, jnp.zeros_like(values))

    for tile, pack in enumerate(packs):
        band_ref[tile] = build_band(
            begin + tile * LANES - RADIUS,
            pack[at : at + count].astype(jnp.int32),
            pack[at + count : at + 2 * count],
        )
        store(here_ref, tile, pack[:LANES])
        inv.append(reciprocal(pack[LANES : 2 * LANES]))
    volt_near = jnp.where(half == 0, volt_near_ref[0:RADIUS, :], volt_near_ref[RADIUS:, :])
    put_near(here_ref, jnp.concatenate(halves(volt_near), axis=1))
    refs = (here_ref, there_ref)
    for iteration in range(ITERS):
        source, target = refs[iteration % 2], refs[(iteration + 1) % 2]
        results = []
        couple(
            source, 0, [band_ref[0], band_ref[1]], mix, lambda tile, values: results.append(values)
        )
        results = [
            -(inflow[tile] + values) * inv[tile] for tile, values in enumerate(results)
        ]
        if iteration < ITERS - 1:
            for tile, values in enumerate(results):
                store(target, tile, values)
            put_near(target, near_ref[iteration])
    out_ref[...] = jnp.where(half == 0, results[1], results[0])
    base_row = where_ref[0] + half * (2 * own - 1) * LANES
    pair = where_ref[1] - half
    for member in range(2):
        offset = member * (picked_ref.shape[0] // 2)
        for at, row in asked_rows(cap, die_count, pair + member, base_row, asked_ref):
            inside = (row >= 0) & (row < LANES)
            values = out_ref[pl.ds(jnp.clip(row, 0, LANES - 1), 1), :]
            cut = pl.ds(offset + at, 1)
            picked_ref[cut, :] = jnp.where(inside, values, picked_in_ref[cut, :])


def join_body(
    where_ref, other_ref, other_tile_ref, tile_ref, full_in_hbm, full_hbm, done_ref, sems
):
    own = other_ref.shape[0] // LANES
    half = lax.rem(where_ref[1], 2)
    inner = pl.multiple_of(half * LANES, LANES)
    rows = (own - 1) * LANES
    last = 2 * own - 1
    copies = [
        pltpu.make_async_copy(
            source, full_hbm.at[pl.ds(pl.multiple_of(tile * LANES, LANES), size), :], sems.at[i]
        )
        for i, (source, tile, size) in enumerate(
            (
                (other_ref.at[pl.ds(inner, rows), :], (1 - half) * own + half, rows),
                (other_tile_ref, (1 - half) * last, LANES),
                (tile_ref, half * last, LANES),
            )
        )
    ]
    for copy in copies:
        copy.start()
    done_ref[...] = jnp.zeros(done_ref.shape, F32)
    for copy in copies:
        copy.wait()


def add_body(parts_ref, after_ref, out_ref):
    rows = out_ref.shape[0]
    out_ref[...] = parts_ref[0:rows, :] + parts_ref[rows:, :]


def scatter_body(cols, where_ref, node_ref, cond_ref, start_ref, volt_ref, load_ref, shunt_ref,
                 right_ref, inv_ref, inner_ref, outer_ref):
    blocks = node_ref.shape[0]
    rows = volt_ref.shape[0]
    group = 8
    row_at = lax.broadcasted_iota(jnp.int32, (rows, LANES), 0)
    col_at = lax.broadcasted_iota(jnp.int32, (cols, LANES), 0)
    total = jnp.zeros((4 * rows, cols), F32)
    for first in range(0, blocks, group):
        node = node_ref[first : first + group, :]
        live = node >= 0
        cond = jnp.where(live, cond_ref[first : first + group, :], 0.0)
        flow = cond * start_ref[first : first + group, :]
        safe = jnp.where(live, node, 0)
        row, col = safe // cols, safe % cols
        parts = halves(cond) + halves(flow)
        left, right = [], []
        for i in range(group):
            spot = jnp.where(row_at == row[i : i + 1, :], 1.0, 0.0).astype(BF16)
            left.append(
                jnp.concatenate([spot * part[i : i + 1, :] for part in parts], axis=0)
            )
            right.append(jnp.where(col_at == col[i : i + 1, :], 1.0, 0.0).astype(BF16))
        total = total + lax.dot_general(
            jnp.concatenate(left, axis=1),
            jnp.concatenate(right, axis=1),
            (((1,), (1,)), ((), ())),
            preferred_element_type=F32,
        )
    gsum = total[:rows] + total[rows : 2 * rows]
    inject = total[2 * rows : 3 * rows] + total[3 * rows :]
    inv = 1.0 / (4.0 + shunt_ref[...] + gsum)
    right_side = (inject - load_ref[...]) * inv
    right_ref[...] = right_side
    inv_ref[...] = inv
    volt = volt_ref[...]
    top, bottom = (
        jnp.concatenate([volt[cut], right_side[cut], inv[cut]], axis=0)
        for cut in (slice(0, HALO_ROWS), slice(rows - HALO_ROWS, rows))
    )
    swap_parts(inner_ref, outer_ref, where_ref[1], top, bottom)


def swap_parts(inner_ref, outer_ref, mine, first, last):
    even = lax.rem(mine, 2) == 0
    inner_ref[...] = jnp.where(even, last, first)
    outer_ref[...] = jnp.where(even, first, last)


def swapped(inner, outer, mine):
    even = lax.rem(mine, 2) == 0
    return jnp.where(even, outer, inner), jnp.where(even, inner, outer)


def swap(inner, outer, axis):
    count = lax.axis_size(axis)

    def pairs(start):
        return [
            pair
            for i in range(start, count - 1, 2)
            for pair in ((i, i + 1), (i + 1, i))
        ]

    outer = lax.ppermute(outer, axis, pairs(1))
    return lax.ppermute(inner, axis, pairs(0)), outer


def extended(own, top, bottom, index):
    cut = slice(index * HALO_ROWS, (index + 1) * HALO_ROWS)
    return jnp.concatenate([top[cut], own, bottom[cut]], axis=0)


def edge_body(where_ref, volt_ref, right_ref, inv_ref, inner_ref, outer_ref, west_ref, east_ref):
    cols = volt_ref.shape[1]
    top, bottom = swapped(inner_ref[...], outer_ref[...], where_ref[1])
    out_rows, high = west_ref.shape
    west, east = None, None
    for index, ref in enumerate((volt_ref, right_ref, inv_ref)):
        whole = extended(ref[...], top, bottom, index)
        lane = lax.broadcasted_iota(jnp.int32, (whole.shape[0], LANES), 1)
        head, tail = whole[:, :LANES], whole[:, cols - LANES :]
        at = index * SWEEPS
        head = pltpu.roll(head, at, 1) if at else head
        tail = pltpu.roll(tail, at + SWEEPS, 1)
        west = head if west is None else jnp.where(lane >= at, head, west)
        east = tail if east is None else jnp.where(lane >= at, tail, east)
    fill = jnp.zeros((high - west.shape[0], LANES), F32)
    west, east = (
        jnp.concatenate([part, fill], axis=0).T[:out_rows] for part in (west, east)
    )
    swap_parts(west_ref, east_ref, where_ref[2], west, east)


def sweep_body(copies, where_ref, node_ref, cond_ref, start_ref, volt_ref, right_ref, inv_ref,
               row_in_ref, row_out_ref, col_in_ref, col_out_ref, out_ref, current_ref):
    rows, cols = volt_ref.shape
    blocks = node_ref.shape[0]
    cap = current_ref.shape[1]
    whole = []
    top, bottom = swapped(row_in_ref[...], row_out_ref[...], where_ref[1])
    out_rows, high = col_in_ref.shape
    fill = jnp.zeros((LANES - out_rows, high), F32)
    wests, easts = (
        jnp.concatenate([part, fill], axis=0).T[: rows + 2 * HALO_ROWS]
        for part in swapped(col_in_ref[...], col_out_ref[...], where_ref[2])
    )
    for index, ref in enumerate((volt_ref, right_ref, inv_ref)):
        own = extended(ref[...], top, bottom, index)
        at = index * SWEEPS
        west = pltpu.roll(wests, LANES - SWEEPS - at, 1)
        east = pltpu.roll(easts, LANES - at, 1) if at else easts
        whole.append(jnp.concatenate([west, own, east], axis=1))
    volt, right_side, inv = whole
    high, wide = volt.shape
    for weight in sweep_weights(SWEEPS):
        beside = (
            pltpu.roll(volt, 1, 0)
            + pltpu.roll(volt, high - 1, 0)
            + pltpu.roll(volt, 1, 1)
            + pltpu.roll(volt, wide - 1, 1)
        )
        volt = (1.0 - weight) * volt + weight * (right_side + beside * inv)
    volt = volt[HALO_ROWS : HALO_ROWS + rows, LANES : LANES + cols]
    out_ref[...] = volt
    both = jnp.concatenate(halves(volt), axis=0)
    group = 8
    row_at = lax.broadcasted_iota(jnp.int32, (rows, LANES), 0)
    col_at = lax.broadcasted_iota(jnp.int32, (cols, LANES), 0)
    dies = blocks // cap
    for first in range(0, blocks, group):
        node = node_ref[first : first + group, :]
        live = node >= 0
        cond = jnp.where(live, cond_ref[first : first + group, :], 0.0)
        safe = jnp.where(live, node, 0)
        row, col = safe // cols, safe % cols
        spots = jnp.concatenate(
            [
                jnp.where(col_at == col[i : i + 1, :], 1.0, 0.0).astype(BF16)
                for i in range(group)
            ],
            axis=1,
        )
        found = jnp.dot(both, spots, preferred_element_type=F32)
        found = found[:rows] + found[rows:]
        for i in range(group):
            mine = found[:, i * LANES : (i + 1) * LANES]
            at_bump = jnp.sum(
                jnp.where(row_at == row[i : i + 1, :], mine, 0.0), axis=0, keepdims=True
            )
            block = first + i
            current = cond[i : i + 1, :] * (start_ref[block : block + 1, :] - at_bump)
            current_ref[block // cap, block % cap : block % cap + 1, :] = current
    for copy in range(1, copies):
        current_ref[copy * dies : (copy + 1) * dies] = current_ref[0:dies]


def local(
    die_volt,
    die_load,
    die_shunt,
    bump_node,
    bump_block,
    bump_cond,
    pkg_volt,
    pkg_diag,
    pkg_pattern,
    pkg_weight,
    block_coupling,
):
    die_count = lax.axis_size("die")
    group_count = lax.axis_size("grp")
    devices = die_count * group_count
    blocks = pkg_volt.shape[0]
    tiles = blocks // LANES
    neighbours = pkg_pattern.shape[0]
    slots = bump_block.shape[0]
    cap = slots // die_count
    rows, cols = die_volt.shape
    group, die = lax.axis_index("grp"), lax.axis_index("die")
    where = jnp.stack([die * blocks, group, die, tiles]).astype(jnp.int32)

    (spread,) = call(
        functools.partial(spread_body, cap, die_count),
        "spread_blocks",
        [shape(devices, 1, LANES, dtype=jnp.int32)],
        (bump_block.reshape(1, slots),),
        [VMEM],
    )
    ids = lax.all_to_all(
        spread, ("grp", "die"), split_axis=0, concat_axis=0, tiled=True
    ).reshape(devices, LANES)

    (picked,) = call(
        functools.partial(pick_body, cap, die_count),
        "pick_rows",
        [shape(slots, LANES)],
        (where, ids, pkg_volt),
        [SMEM, SMEM, HBM],
        [pltpu.SemaphoreType.DMA(())],
        vmem=MOST_VMEM,
    )
    bump_start = lax.all_to_all(
        picked.reshape(die_count, cap, LANES), "die", split_axis=0, concat_axis=0, tiled=True
    ).reshape(slots, LANES)

    right_side, inv, *edges = call(
        functools.partial(scatter_body, cols),
        "scatter_bumps",
        [shape(rows, cols)] * 2 + [shape(3 * HALO_ROWS, cols)] * 2,
        (where, bump_node, bump_cond, bump_start, die_volt, die_load, die_shunt),
        [SMEM] + [VMEM] * 6,
        flops=8 * rows * slots * LANES * cols,
    )
    beside = swap(*edges, "grp")

    edge_rows = -(-3 * SWEEPS // 8) * 8
    edge_cols = -(-(rows + 2 * HALO_ROWS) // LANES) * LANES
    edges = call(
        edge_body,
        "edge_columns",
        [shape(edge_rows, edge_cols)] * 2,
        (where, die_volt, right_side, inv, *beside),
        [SMEM] + [VMEM] * 5,
    )
    columns = swap(*edges, "die")

    die_out, current = call(
        functools.partial(sweep_body, group_count),
        "sweeps",
        [shape(rows, cols), shape(devices, cap, LANES)],
        (where, bump_node, bump_cond, bump_start, die_volt, right_side, inv, *beside, *columns),
        [SMEM] + [VMEM] * 10,
        flops=4 * rows * slots * LANES * cols,
    )
    own = tiles // 2
    count = own + 1
    dma = pltpu.SemaphoreType.DMA
    plane = pltpu.VMEM(((own + 2) * LANES + 2 * RADIUS, 2 * LANES), BF16)
    half_rows = pltpu.VMEM((count * LANES, LANES), F32)
    half_bands = pltpu.VMEM((count, 2 * LANES, 2 * LANES), BF16)
    pack_rows = 2 * LANES + 2 * neighbours
    band, base, pkg_inv, pack, outermost, volt_near = call(
        prepare_body,
        "package_prepare",
        [
            shape(count, 2 * LANES, 2 * LANES, dtype=BF16),
            shape(count * LANES, LANES),
            shape(count * LANES, LANES),
            shape(pack_rows, LANES),
            shape(pack_rows, LANES),
            shape(2 * RADIUS, LANES),
        ],
        (where, pkg_pattern, pkg_weight, block_coupling, pkg_volt, pkg_diag, die_out),
        [SMEM, VMEM, VMEM, VMEM, HBM, HBM, HBM],
        [half_rows, half_rows, half_bands, half_rows, half_rows, plane, dma((11,))],
        flops=8 * count * LANES**3,
        vmem=MOST_VMEM,
        out_specs=[HBM] * 3 + [VMEM] * 3,
    )

    current = lax.all_to_all(
        current, ("grp", "die"), split_axis=0, concat_axis=0, tiled=True
    ).reshape(devices * cap, LANES)

    send, inflow = call(
        functools.partial(ends_body, cap),
        "package_ends",
        [shape(LANES + pack_rows, LANES), shape(LANES, LANES)],
        (where, ids, current, pack, volt_near),
        [SMEM] + [VMEM] * 3 + [ANY],
    )
    halo = lax.ppermute(
        send,
        ("grp", "die"),
        [
            (g * die_count + d, g * die_count + d + 1 - 2 * (g % 2))
            for g in range(group_count)
            for d in range(die_count)
            if 0 <= d + 1 - 2 * (g % 2) < die_count
        ],
    )
    half_out, pkg_out, picked, near = call(
        functools.partial(interior_body, cap, die_count),
        "package_interior",
        [
            shape(own * LANES, LANES),
            shape(blocks, LANES),
            shape(2 * slots, LANES),
            shape(ITERS - 1, RADIUS, 2 * LANES, dtype=BF16),
        ],
        (where, ids, ids, current, block_coupling, inflow, band, base, pkg_inv),
        [SMEM, SMEM, VMEM, VMEM, VMEM, ANY, HBM, HBM, HBM],
        [
            half_bands, half_rows, half_rows, pltpu.VMEM((own * LANES, LANES), F32),
            half_rows, plane, plane, dma((5,)),
        ],
        flops=24 * count * LANES**3,
        vmem=MOST_VMEM,
        out_specs=[HBM, HBM, VMEM, VMEM],
    )
    partners = [(g, g ^ 1) for g in range(group_count)]
    other = lax.ppermute(half_out, "grp", partners)
    edge_plane = pltpu.VMEM((2 * LANES + 2 * RADIUS, 2 * LANES), BF16)
    picked, tile = call(
        functools.partial(outermost_body, cap, die_count),
        "package_outermost",
        [shape(2 * slots, LANES), shape(LANES, LANES)],
        (where, ids, block_coupling, halo, outermost, inflow, volt_near, near, picked),
        [SMEM, SMEM] + [VMEM] * 7,
        [pltpu.VMEM((2, 2 * LANES, 2 * LANES), BF16), edge_plane, edge_plane],
        flops=8 * LANES**3,
    )
    pair = 2 * die_count
    parts = lax.all_to_all(
        picked.reshape(pair, cap, LANES),
        ("grp", "die"),
        split_axis=0,
        concat_axis=0,
        axis_index_groups=[
            [first + i for i in range(pair)] for first in range(0, devices, pair)
        ],
        tiled=True,
    ).reshape(2 * slots, LANES)
    other_tile = lax.ppermute(tile, "grp", partners)
    pkg_out, done = call(
        join_body,
        "join_halves",
        [shape(blocks, LANES), shape(8, LANES)],
        (where, other, other_tile, tile, pkg_out),
        [SMEM] + [VMEM] * 3 + [HBM],
        [dma((3,))],
        out_specs=[HBM, VMEM],
        aliases={4: 0},
    )
    (bump_out,) = call(
        add_body, "add_parts", [shape(slots, LANES)], (parts, done), [VMEM, ANY]
    )
    return (die_out, pkg_out, bump_out)


def solution(mesh):
    return jax.shard_map(
        local,
        mesh=mesh,
        in_specs=(
            P("grp", "die"),
            P("grp", "die"),
            P("grp", "die"),
            P(("grp", "die"), None),
            P(("grp", "die")),
            P(("grp", "die"), None),
            P("die", None),
            P("die", None),
            P(None, "die"),
            P(None, "die"),
            P(),
        ),
        out_specs=(P("grp", "die"), P("die", None), P(("grp", "die"), None)),
        check_vma=False,
    )
```

```python
import functools
import math

import jax
import jax.numpy as jnp
from jax import lax
from jax.experimental import pallas as pl
from jax.experimental.pallas import tpu as pltpu
from jax.sharding import PartitionSpec as P

RADIUS = 32
SWEEPS = 4
ITERS = 4
LANES = 128
HALO_ROWS = 8
REACH = RADIUS * ITERS
WINDOW = LANES + 2 * RADIUS
F32 = jnp.float32
BF16 = jnp.bfloat16
MOST_VMEM = 57
VMEM = pl.BlockSpec(memory_space=pltpu.VMEM)
SMEM = pl.BlockSpec(memory_space=pltpu.SMEM)
ANY = pl.BlockSpec(memory_space=pl.ANY)
HBM = pl.BlockSpec(memory_space=pltpu.HBM)


def sweep_weights(sweeps):
    return [
        1.0 / (1.0 + 0.8 * math.cos(math.pi * (2 * index + 1) / (2 * sweeps)))
        for index in range(sweeps)
    ]


def call(
    body, name, outs, args, specs, scratch=(), work=1, vmem=16, out_specs=None, aliases=None
):
    bytes_accessed = sum(4 * math.prod(arg.shape) for arg in args)
    return pl.pallas_call(
        body,
        name=name,
        out_shape=outs,
        in_specs=specs,
        out_specs=out_specs or [VMEM] * len(outs),
        input_output_aliases=aliases or {},
        scratch_shapes=list(scratch),
        compiler_params=pltpu.CompilerParams(vmem_limit_bytes=vmem * 1024 * 1024),
        cost_estimate=pl.CostEstimate(
            flops=work * 10**9, bytes_accessed=bytes_accessed, transcendentals=0
        ),
    )(*args)


def shape(*dims, dtype=F32):
    return jax.ShapeDtypeStruct(dims, dtype)


def halves(values):
    high = values.astype(BF16)
    low = (values - high.astype(F32)).astype(BF16)
    return high, low


def spread_body(cap, die_count, block_ref, out_ref):
    slots = block_ref.shape[1]
    block = jnp.concatenate(
        [block_ref[...], jnp.zeros((1, LANES - slots), jnp.int32)], axis=1
    )
    for die in range(die_count):
        row = pltpu.roll(block, LANES - die * cap, 1) if die else block
        for at in range(die, out_ref.shape[0], die_count):
            out_ref[at] = row


def asked_rows(cap, die_count, group, start, ids_ref):
    for die in range(die_count):
        for slot in range(cap):
            yield die * cap + slot, ids_ref[group * die_count + die, slot] - start


def pick_body(cap, die_count, where_ref, ids_ref, plane_ref, out_ref, sem):
    for at, row in asked_rows(cap, die_count, where_ref[1], where_ref[0], ids_ref):
        pltpu.make_async_copy(
            plane_ref.at[pl.ds(row, 1), :], out_ref.at[pl.ds(at, 1), :], sem
        ).start()
    pltpu.make_async_copy(plane_ref.at[0 : out_ref.shape[0], :], out_ref, sem).wait()


def build_band(first, pattern, weights):
    place = lax.broadcasted_iota(jnp.int32, (WINDOW, LANES), 0)
    band = None
    for k in range(pattern.shape[0]):
        hit = place == (pattern[k : k + 1, :] - first)
        term = jnp.where(hit, weights[k : k + 1, :], 0.0)
        band = term if band is None else band + term
    fill = jnp.zeros((2 * LANES - WINDOW, LANES), F32)
    return jnp.concatenate(halves(jnp.concatenate([band, fill], axis=0).T), axis=0)


def reciprocal(diag):
    safe = jnp.where(diag > 0.0, diag, 1.0)
    return jnp.where(diag > 0.0, 1.0 / safe, 0.0)


def span(tile, offset=0, size=LANES):
    return pl.ds(pl.multiple_of(tile * LANES + offset, RADIUS), size)


def mixer(coup_ref):
    mix = jnp.concatenate(halves(coup_ref[...]), axis=1)
    return jnp.concatenate([mix, mix], axis=0)


def clear_pads(ref):
    pad = jnp.zeros((RADIUS, 2 * LANES), BF16)
    ref[0:RADIUS, :] = pad
    ref[ref.shape[0] - RADIUS :, :] = pad


def store(ref, tile, values):
    ref[span(tile, RADIUS, values.shape[0]), :] = jnp.concatenate(halves(values), axis=1)


def couple(source, tile, bands, mix, write):
    own = source[span(tile, RADIUS, len(bands) * LANES), :]
    within = jnp.dot(own, mix, preferred_element_type=F32)
    for i, band in enumerate(bands):
        window = source[span(tile + i, 0, WINDOW), :]
        beside = jnp.dot(band[:, :WINDOW], window, preferred_element_type=F32)
        both = beside[:LANES] + beside[LANES:] + within[i * LANES : (i + 1) * LANES]
        write(tile + i, both[:, :LANES] + both[:, LANES:])


def in_chunks(first, count, body, size=4):
    whole = count // size

    @pl.loop(0, whole)
    def _(chunk):
        body(first + chunk * size, size)

    if count % size:
        body(first + whole * size, count % size)


def half_of(where_ref, tiles):
    half = lax.rem(where_ref[1] + where_ref[2], 2)
    own = tiles // 2
    return half, own, half * own - 1


def prepare_body(
    where_ref, pat_ref, wgt_ref, coup_ref, volt_hbm, diag_hbm, after_ref,
    band_hbm, base_hbm, inv_hbm, pack_ref, near_ref,
    volt_ref, diag_ref, band_ref, base_ref, inv_ref, plane_ref, sems,
):
    tiles = volt_hbm.shape[0] // LANES
    half, own, shift = half_of(where_ref, tiles)
    first, count = 1 - half, own + 1
    rows = count * LANES
    source = pl.ds(pl.multiple_of((first + shift) * LANES, LANES), rows)
    loads = [
        pltpu.make_async_copy(hbm.at[source, :], ref, sems.at[i])
        for i, (hbm, ref) in enumerate(((volt_hbm, volt_ref), (diag_hbm, diag_ref)))
    ]
    for load in loads:
        load.start()
    high = (tiles - 1) * LANES
    mine = pl.multiple_of(half * high, LANES)
    neighbours = pat_ref.shape[0]

    def fetch(hbm, start, target):
        rows = target.shape[0]
        loads.append(pltpu.make_async_copy(hbm.at[pl.ds(start, rows), :], target, sems.at[len(loads) + 3]))
        loads[-1].start()

    fetch(volt_hbm, mine, pack_ref.at[0:LANES, :])
    fetch(diag_hbm, mine, pack_ref.at[LANES : 2 * LANES, :])
    lanes = pl.ds(mine, LANES)
    at = 2 * LANES
    pack_ref[at : at + neighbours, :] = pat_ref[:, lanes].astype(F32)
    pack_ref[at + neighbours : at + 2 * neighbours, :] = wgt_ref[:, lanes]
    fetch(volt_hbm, LANES, near_ref.at[0:RADIUS, :])
    fetch(volt_hbm, high - RADIUS, near_ref.at[RADIUS : 2 * RADIUS, :])
    clear_pads(plane_ref)
    plane_ref[span(half * (own + 1), RADIUS), :] = jnp.zeros((LANES, 2 * LANES), BF16)
    begin = where_ref[0] + shift * LANES

    def bands(at, size):
        for i in range(size):
            tile = first + at + i
            lanes = pl.ds(pl.multiple_of((tile + shift) * LANES, LANES), LANES)
            band_ref[at + i] = build_band(
                begin + tile * LANES - RADIUS, pat_ref[:, lanes], wgt_ref[:, lanes]
            )
        pltpu.make_async_copy(
            band_ref.at[pl.ds(at, size)], band_hbm.at[pl.ds(at, size)], sems.at[2]
        ).start()

    in_chunks(0, count, bands)
    for load in loads:
        load.wait()

    def place(at, size):
        cut = span(at, 0, size * LANES)
        store(plane_ref, first + at, volt_ref[cut, :])
        inv_ref[cut, :] = reciprocal(diag_ref[cut, :])

    in_chunks(0, count, place)
    inv_out = pltpu.make_async_copy(inv_ref, inv_hbm, sems.at[3])
    inv_out.start()
    mix = mixer(coup_ref)

    def base(at, size):
        def write(tile, values):
            base_ref[span(tile - first), :] = values

        couple(plane_ref, first + at, [band_ref[at + i] for i in range(size)], mix, write)
        cut = span(at, 0, size * LANES)
        pltpu.make_async_copy(base_ref.at[cut, :], base_hbm.at[cut, :], sems.at[4]).start()

    in_chunks(0, count, base)
    pltpu.make_async_copy(band_ref, band_hbm, sems.at[2]).wait()
    inv_out.wait()
    pltpu.make_async_copy(base_ref, base_hbm, sems.at[4]).wait()


def slot_places(cap, ids_ref):
    per_row = LANES // cap
    lane = lax.broadcasted_iota(jnp.int32, (1, LANES), 1)
    places = []
    for at in range(0, ids_ref.shape[0], per_row):
        total = None
        for i in range(per_row):
            row = jnp.where(lane < cap, ids_ref[at + i : at + i + 1, :], 0)
            row = pltpu.roll(row, i * cap, 1) if i else row
            total = row if total is None else total + row
        places.append(total)
    return places


def gather_inflow(places, first, rows, current):
    at = lax.broadcasted_iota(jnp.int32, (rows, LANES), 0) + first
    hits = [jnp.where(at == place, 1.0, 0.0).astype(BF16) for place in places]
    both = jnp.dot(jnp.concatenate(hits, axis=1), current, preferred_element_type=F32)
    return both[:, :LANES] + both[:, LANES:]


def ends_body(cap, tiles, where_ref, ids_ref, current_ref, out_ref):
    half, _, _ = half_of(where_ref, tiles)
    places = slot_places(cap, ids_ref)
    current = jnp.concatenate(halves(current_ref[...]), axis=1)
    first = where_ref[0] + half * (tiles - 1) * LANES
    out_ref[...] = gather_inflow(places, first, LANES, current)


def interior_body(
    cap, die_count, where_ref, asked_ref, ids_ref, current_ref, coup_ref, after_ref,
    band_hbm, base_hbm, inv_hbm,
    out_hbm, full_hbm, picked_ref, near_ref,
    band_ref, base_ref, inv_ref, out_ref, inflow_ref, here_ref, there_ref, sems,
):
    own = out_hbm.shape[0] // LANES
    half, _, shift = half_of(where_ref, 2 * own)
    first, count = 1 - half, own + 1
    loads = [
        pltpu.make_async_copy(hbm, ref, sems.at[i])
        for i, (hbm, ref) in enumerate(
            ((base_hbm, base_ref), (inv_hbm, inv_ref), (band_hbm, band_ref))
        )
    ]
    for load in loads:
        load.start()
    begin = where_ref[0] + (first + shift) * LANES
    places = slot_places(cap, ids_ref)
    current = jnp.concatenate(halves(current_ref[...]), axis=1)
    outer = half * (own + 1)
    for ref in (here_ref, there_ref):
        clear_pads(ref)
        ref[span(outer, RADIUS), :] = jnp.zeros((LANES, 2 * LANES), BF16)

    def inflow(at, size):
        rows = size * LANES
        inflow_ref[span(at, 0, rows), :] = gather_inflow(
            places, begin + at * LANES, rows, current
        )

    in_chunks(0, count, inflow)
    loads[0].wait()
    loads[1].wait()

    def start(at, size):
        cut = span(at, 0, size * LANES)
        store(here_ref, first + at, -(inflow_ref[cut, :] + base_ref[cut, :]) * inv_ref[cut, :])

    in_chunks(0, count, start)
    loads[2].wait()
    mix = mixer(coup_ref)
    beyond = jnp.where(half == 0, 2 * LANES, own * LANES - RADIUS)
    near = pl.ds(pl.multiple_of(beyond + RADIUS, RADIUS), RADIUS)
    refs = (here_ref, there_ref)
    for iteration in range(1, ITERS):
        source, target = refs[(iteration - 1) % 2], refs[iteration % 2]
        last = iteration == ITERS - 1
        near_ref[iteration - 1] = source[near, :]

        def write(tile, coupled, target=target, last=last):
            cut = span(tile - first)
            values = -(inflow_ref[cut, :] + coupled) * inv_ref[cut, :]
            if last:
                out_ref[span(tile - 1), :] = values
            else:
                store(target, tile, values)

        def step(at, size, source=source, write=write):
            bands = [band_ref[at - first + i] for i in range(size)]
            couple(source, at, bands, mix, write)

        def final(at, size, step=step):
            step(at, size)
            cut = span(at - 1, 0, size * LANES)
            whole = span(half * own + at - 1, 0, size * LANES)
            pltpu.make_async_copy(out_ref.at[cut, :], out_hbm.at[cut, :], sems.at[3]).start()
            pltpu.make_async_copy(out_ref.at[cut, :], full_hbm.at[whole, :], sems.at[4]).start()

        if last:
            in_chunks(1, own, final)
        else:
            in_chunks(first, count, step)

    base_row = where_ref[0] + half * own * LANES
    pair = where_ref[1] - lax.rem(where_ref[1], 2)
    for member in range(2):
        offset = member * (picked_ref.shape[0] // 2)
        for at, row in asked_rows(cap, die_count, pair + member, base_row, asked_ref):
            inside = (row >= 0) & (row < own * LANES)
            safe = jnp.clip(row, 0, own * LANES - 1)
            values = out_ref[pl.ds(safe, 1), :]
            picked_ref[pl.ds(offset + at, 1), :] = jnp.where(inside, values, 0.0)
    pltpu.make_async_copy(out_ref, out_hbm, sems.at[3]).wait()
    pltpu.make_async_copy(out_ref, full_hbm.at[0 : own * LANES, :], sems.at[4]).wait()


def outermost_body(
    cap, die_count, tiles, where_ref, asked_ref, coup_ref, halo_ref, own_ref, halo_inflow_ref,
    inflow_ref, volt_near_ref, near_ref, picked_in_ref, picked_ref, out_ref,
    band_ref, here_ref, there_ref,
):
    half, own, _ = half_of(where_ref, tiles)
    count = (own_ref.shape[0] - 2 * LANES) // 2
    mix = mixer(coup_ref)
    packs = [
        jnp.where(half == at, halo_ref[...], own_ref[...]) for at in range(2)
    ]
    inflow = [
        jnp.where(half == at, halo_inflow_ref[...], inflow_ref[...]) for at in range(2)
    ]
    begin = where_ref[0] + (2 * half * own - 1) * LANES
    at = 2 * LANES
    inv = []

    def put_near(ref, values):
        size = ref.shape[0]
        ref[0:RADIUS, :] = jnp.where(half == 0, jnp.zeros_like(values), values)
        ref[size - RADIUS : size, :] = jnp.where(half == 0, values, jnp.zeros_like(values))

    for tile, pack in enumerate(packs):
        band_ref[tile] = build_band(
            begin + tile * LANES - RADIUS,
            pack[at : at + count].astype(jnp.int32),
            pack[at + count : at + 2 * count],
        )
        store(here_ref, tile, pack[:LANES])
        inv.append(reciprocal(pack[LANES : 2 * LANES]))
    volt_near = jnp.where(half == 0, volt_near_ref[0:RADIUS, :], volt_near_ref[RADIUS:, :])
    put_near(here_ref, jnp.concatenate(halves(volt_near), axis=1))
    refs = (here_ref, there_ref)
    for iteration in range(ITERS):
        source, target = refs[iteration % 2], refs[(iteration + 1) % 2]
        results = []
        couple(
            source, 0, [band_ref[0], band_ref[1]], mix, lambda tile, values: results.append(values)
        )
        results = [
            -(inflow[tile] + values) * inv[tile] for tile, values in enumerate(results)
        ]
        if iteration < ITERS - 1:
            for tile, values in enumerate(results):
                store(target, tile, values)
            put_near(target, near_ref[iteration])
    out_ref[...] = jnp.where(half == 0, results[1], results[0])
    base_row = where_ref[0] + half * (2 * own - 1) * LANES
    pair = where_ref[1] - lax.rem(where_ref[1], 2)
    for member in range(2):
        offset = member * (picked_ref.shape[0] // 2)
        for at, row in asked_rows(cap, die_count, pair + member, base_row, asked_ref):
            inside = (row >= 0) & (row < LANES)
            values = out_ref[pl.ds(jnp.clip(row, 0, LANES - 1), 1), :]
            cut = pl.ds(offset + at, 1)
            picked_ref[cut, :] = jnp.where(inside, values, picked_in_ref[cut, :])


def join_body(
    where_ref, other_ref, other_tile_ref, tile_ref, full_in_hbm, full_hbm, done_ref, sems
):
    own = other_ref.shape[0] // LANES
    half, _, _ = half_of(where_ref, 2 * own)
    inner = pl.multiple_of(half * LANES, LANES)
    rows = (own - 1) * LANES
    last = 2 * own - 1
    copies = [
        pltpu.make_async_copy(
            source, full_hbm.at[pl.ds(pl.multiple_of(tile * LANES, LANES), size), :], sems.at[i]
        )
        for i, (source, tile, size) in enumerate(
            (
                (other_ref.at[pl.ds(inner, rows), :], (1 - half) * own + half, rows),
                (other_tile_ref, (1 - half) * last, LANES),
                (tile_ref, half * last, LANES),
            )
        )
    ]
    for copy in copies:
        copy.start()
    done_ref[...] = jnp.zeros(done_ref.shape, F32)
    for copy in copies:
        copy.wait()


def add_body(parts_ref, after_ref, out_ref):
    rows = out_ref.shape[0]
    out_ref[...] = parts_ref[0:rows, :] + parts_ref[rows:, :]


def scatter_body(cols, where_ref, node_ref, cond_ref, start_ref, volt_ref, load_ref, shunt_ref,
                 right_ref, inv_ref, inner_ref, outer_ref):
    blocks = node_ref.shape[0]
    rows = volt_ref.shape[0]
    group = 8
    row_at = lax.broadcasted_iota(jnp.int32, (rows, LANES), 0)
    col_at = lax.broadcasted_iota(jnp.int32, (cols, LANES), 0)
    total = jnp.zeros((4 * rows, cols), F32)
    for first in range(0, blocks, group):
        node = node_ref[first : first + group, :]
        live = node >= 0
        cond = jnp.where(live, cond_ref[first : first + group, :], 0.0)
        flow = cond * start_ref[first : first + group, :]
        safe = jnp.where(live, node, 0)
        row, col = safe // cols, safe % cols
        parts = halves(cond) + halves(flow)
        left, right = [], []
        for i in range(group):
            spot = jnp.where(row_at == row[i : i + 1, :], 1.0, 0.0).astype(BF16)
            left.append(
                jnp.concatenate([spot * part[i : i + 1, :] for part in parts], axis=0)
            )
            right.append(jnp.where(col_at == col[i : i + 1, :], 1.0, 0.0).astype(BF16))
        total = total + lax.dot_general(
            jnp.concatenate(left, axis=1),
            jnp.concatenate(right, axis=1),
            (((1,), (1,)), ((), ())),
            preferred_element_type=F32,
        )
    gsum = total[:rows] + total[rows : 2 * rows]
    inject = total[2 * rows : 3 * rows] + total[3 * rows :]
    inv = 1.0 / (4.0 + shunt_ref[...] + gsum)
    right_side = (inject - load_ref[...]) * inv
    right_ref[...] = right_side
    inv_ref[...] = inv
    volt = volt_ref[...]
    top, bottom = (
        jnp.concatenate([volt[cut], right_side[cut], inv[cut]], axis=0)
        for cut in (slice(0, HALO_ROWS), slice(rows - HALO_ROWS, rows))
    )
    swap_parts(inner_ref, outer_ref, where_ref[1], top, bottom)


def swap_parts(inner_ref, outer_ref, mine, first, last):
    even = lax.rem(mine, 2) == 0
    inner_ref[...] = jnp.where(even, last, first)
    outer_ref[...] = jnp.where(even, first, last)


def swapped(inner, outer, mine):
    even = lax.rem(mine, 2) == 0
    return jnp.where(even, outer, inner), jnp.where(even, inner, outer)


def swap(inner, outer, axis):
    count = lax.axis_size(axis)

    def pairs(start):
        return [
            pair
            for i in range(start, count - 1, 2)
            for pair in ((i, i + 1), (i + 1, i))
        ]

    outer = lax.ppermute(outer, axis, pairs(1))
    return lax.ppermute(inner, axis, pairs(0)), outer


def extended(own, top, bottom, index):
    cut = slice(index * HALO_ROWS, (index + 1) * HALO_ROWS)
    return jnp.concatenate([top[cut], own, bottom[cut]], axis=0)


def edge_body(where_ref, volt_ref, right_ref, inv_ref, inner_ref, outer_ref, west_ref, east_ref):
    cols = volt_ref.shape[1]
    top, bottom = swapped(inner_ref[...], outer_ref[...], where_ref[1])
    out_rows, high = west_ref.shape
    west, east = None, None
    for index, ref in enumerate((volt_ref, right_ref, inv_ref)):
        whole = extended(ref[...], top, bottom, index)
        lane = lax.broadcasted_iota(jnp.int32, (whole.shape[0], LANES), 1)
        head, tail = whole[:, :LANES], whole[:, cols - LANES :]
        at = index * SWEEPS
        head = pltpu.roll(head, at, 1) if at else head
        tail = pltpu.roll(tail, at + SWEEPS, 1)
        west = head if west is None else jnp.where(lane >= at, head, west)
        east = tail if east is None else jnp.where(lane >= at, tail, east)
    fill = jnp.zeros((high - west.shape[0], LANES), F32)
    west, east = (
        jnp.concatenate([part, fill], axis=0).T[:out_rows] for part in (west, east)
    )
    swap_parts(west_ref, east_ref, where_ref[2], west, east)


def sweep_body(copies, where_ref, node_ref, cond_ref, start_ref, volt_ref, right_ref, inv_ref,
               row_in_ref, row_out_ref, col_in_ref, col_out_ref, out_ref, current_ref):
    rows, cols = volt_ref.shape
    blocks = node_ref.shape[0]
    cap = current_ref.shape[1]
    whole = []
    top, bottom = swapped(row_in_ref[...], row_out_ref[...], where_ref[1])
    out_rows, high = col_in_ref.shape
    fill = jnp.zeros((LANES - out_rows, high), F32)
    wests, easts = (
        jnp.concatenate([part, fill], axis=0).T[: rows + 2 * HALO_ROWS]
        for part in swapped(col_in_ref[...], col_out_ref[...], where_ref[2])
    )
    for index, ref in enumerate((volt_ref, right_ref, inv_ref)):
        own = extended(ref[...], top, bottom, index)
        at = index * SWEEPS
        west = pltpu.roll(wests, LANES - SWEEPS - at, 1)
        east = pltpu.roll(easts, LANES - at, 1) if at else easts
        whole.append(jnp.concatenate([west, own, east], axis=1))
    volt, right_side, inv = whole
    high, wide = volt.shape
    for weight in sweep_weights(SWEEPS):
        beside = (
            pltpu.roll(volt, 1, 0)
            + pltpu.roll(volt, high - 1, 0)
            + pltpu.roll(volt, 1, 1)
            + pltpu.roll(volt, wide - 1, 1)
        )
        volt = (1.0 - weight) * volt + weight * (right_side + beside * inv)
    volt = volt[HALO_ROWS : HALO_ROWS + rows, LANES : LANES + cols]
    out_ref[...] = volt
    both = jnp.concatenate(halves(volt), axis=0)
    group = 8
    row_at = lax.broadcasted_iota(jnp.int32, (rows, LANES), 0)
    col_at = lax.broadcasted_iota(jnp.int32, (cols, LANES), 0)
    dies = blocks // cap
    for first in range(0, blocks, group):
        node = node_ref[first : first + group, :]
        live = node >= 0
        cond = jnp.where(live, cond_ref[first : first + group, :], 0.0)
        safe = jnp.where(live, node, 0)
        row, col = safe // cols, safe % cols
        spots = jnp.concatenate(
            [
                jnp.where(col_at == col[i : i + 1, :], 1.0, 0.0).astype(BF16)
                for i in range(group)
            ],
            axis=1,
        )
        found = jnp.dot(both, spots, preferred_element_type=F32)
        found = found[:rows] + found[rows:]
        for i in range(group):
            mine = found[:, i * LANES : (i + 1) * LANES]
            at_bump = jnp.sum(
                jnp.where(row_at == row[i : i + 1, :], mine, 0.0), axis=0, keepdims=True
            )
            block = first + i
            current = cond[i : i + 1, :] * (start_ref[block : block + 1, :] - at_bump)
            current_ref[block // cap, block % cap : block % cap + 1, :] = current
    for copy in range(1, copies):
        current_ref[copy * dies : (copy + 1) * dies] = current_ref[0:dies]


def local(
    die_volt,
    die_load,
    die_shunt,
    bump_node,
    bump_block,
    bump_cond,
    pkg_volt,
    pkg_diag,
    pkg_pattern,
    pkg_weight,
    block_coupling,
):
    die_count = lax.axis_size("die")
    group_count = lax.axis_size("grp")
    devices = die_count * group_count
    blocks = pkg_volt.shape[0]
    tiles = blocks // LANES
    neighbours = pkg_pattern.shape[0]
    slots = bump_block.shape[0]
    cap = slots // die_count
    rows, cols = die_volt.shape
    group, die = lax.axis_index("grp"), lax.axis_index("die")
    where = jnp.stack([die * blocks, group, die]).astype(jnp.int32)

    (spread,) = call(
        functools.partial(spread_body, cap, die_count),
        "spread_blocks",
        [shape(devices, 1, LANES, dtype=jnp.int32)],
        (bump_block.reshape(1, slots),),
        [VMEM],
    )
    ids = lax.all_to_all(
        spread, ("grp", "die"), split_axis=0, concat_axis=0, tiled=True
    ).reshape(devices, LANES)

    (picked,) = call(
        functools.partial(pick_body, cap, die_count),
        "pick_rows",
        [shape(slots, LANES)],
        (where, ids, pkg_volt),
        [SMEM, SMEM, HBM],
        [pltpu.SemaphoreType.DMA(())],
        vmem=MOST_VMEM,
    )
    bump_start = lax.all_to_all(
        picked.reshape(die_count, cap, LANES), "die", split_axis=0, concat_axis=0, tiled=True
    ).reshape(slots, LANES)

    right_side, inv, *edges = call(
        functools.partial(scatter_body, cols),
        "scatter_bumps",
        [shape(rows, cols)] * 2 + [shape(3 * HALO_ROWS, cols)] * 2,
        (where, bump_node, bump_cond, bump_start, die_volt, die_load, die_shunt),
        [SMEM] + [VMEM] * 6,
        work=3,
    )
    beside = swap(*edges, "grp")

    edge_rows = -(-3 * SWEEPS // 8) * 8
    edge_cols = -(-(rows + 2 * HALO_ROWS) // LANES) * LANES
    edges = call(
        edge_body,
        "edge_columns",
        [shape(edge_rows, edge_cols)] * 2,
        (where, die_volt, right_side, inv, *beside),
        [SMEM] + [VMEM] * 5,
    )
    columns = swap(*edges, "die")

    die_out, current = call(
        functools.partial(sweep_body, group_count),
        "sweeps",
        [shape(rows, cols), shape(devices, cap, LANES)],
        (where, bump_node, bump_cond, bump_start, die_volt, right_side, inv, *beside, *columns),
        [SMEM] + [VMEM] * 10,
        work=4,
    )
    own = tiles // 2
    count = own + 1
    dma = pltpu.SemaphoreType.DMA
    plane = pltpu.VMEM(((own + 2) * LANES + 2 * RADIUS, 2 * LANES), BF16)
    half_rows = pltpu.VMEM((count * LANES, LANES), F32)
    half_bands = pltpu.VMEM((count, 2 * LANES, 2 * LANES), BF16)
    pack_rows = 2 * LANES + 2 * neighbours
    band, base, pkg_inv, pack, volt_near = call(
        prepare_body,
        "package_prepare",
        [
            shape(count, 2 * LANES, 2 * LANES, dtype=BF16),
            shape(count * LANES, LANES),
            shape(count * LANES, LANES),
            shape(pack_rows, LANES),
            shape(2 * RADIUS, LANES),
        ],
        (where, pkg_pattern, pkg_weight, block_coupling, pkg_volt, pkg_diag, die_out),
        [SMEM, VMEM, VMEM, VMEM, HBM, HBM, HBM],
        [half_rows, half_rows, half_bands, half_rows, half_rows, plane, dma((9,))],
        work=7,
        vmem=MOST_VMEM,
        out_specs=[HBM] * 3 + [VMEM] * 2,
    )

    current = lax.all_to_all(
        current, ("grp", "die"), split_axis=0, concat_axis=0, tiled=True
    ).reshape(devices * cap, LANES)

    beside_end = [
        (g * die_count + a, g * die_count + b)
        for g in range(group_count)
        for d in range((g + 1) % 2, die_count - 1, 2)
        for a, b in ((d, d + 1), (d + 1, d))
    ]
    halo = lax.ppermute(pack, ("grp", "die"), beside_end)
    (inflow,) = call(
        functools.partial(ends_body, cap, tiles),
        "package_end",
        [shape(LANES, LANES)],
        (where, ids, current),
        [SMEM, VMEM, VMEM],
    )
    halo_inflow = lax.ppermute(inflow, ("grp", "die"), beside_end)
    half_out, pkg_out, picked, near = call(
        functools.partial(interior_body, cap, die_count),
        "package_interior",
        [
            shape(own * LANES, LANES),
            shape(blocks, LANES),
            shape(2 * slots, LANES),
            shape(ITERS - 1, RADIUS, 2 * LANES, dtype=BF16),
        ],
        (where, ids, ids, current, block_coupling, inflow, band, base, pkg_inv),
        [SMEM, SMEM, VMEM, VMEM, VMEM, ANY, HBM, HBM, HBM],
        [
            half_bands, half_rows, half_rows, pltpu.VMEM((own * LANES, LANES), F32),
            half_rows, plane, plane, dma((5,)),
        ],
        work=10,
        vmem=MOST_VMEM,
        out_specs=[HBM, HBM, VMEM, VMEM],
    )
    partners = [(g, g ^ 1) for g in range(group_count)]
    other = lax.ppermute(half_out, "grp", partners)
    edge_plane = pltpu.VMEM((2 * LANES + 2 * RADIUS, 2 * LANES), BF16)
    picked, tile = call(
        functools.partial(outermost_body, cap, die_count, tiles),
        "package_outermost",
        [shape(2 * slots, LANES), shape(LANES, LANES)],
        (where, ids, block_coupling, halo, pack, halo_inflow, inflow, volt_near, near, picked),
        [SMEM, SMEM] + [VMEM] * 8,
        [pltpu.VMEM((2, 2 * LANES, 2 * LANES), BF16), edge_plane, edge_plane],
        work=20,
    )
    pair = 2 * die_count
    parts = lax.all_to_all(
        picked.reshape(pair, cap, LANES),
        ("grp", "die"),
        split_axis=0,
        concat_axis=0,
        axis_index_groups=[
            [first + i for i in range(pair)] for first in range(0, devices, pair)
        ],
        tiled=True,
    ).reshape(2 * slots, LANES)
    other_tile = lax.ppermute(tile, "grp", partners)
    pkg_out, done = call(
        join_body,
        "join_halves",
        [shape(blocks, LANES), shape(8, LANES)],
        (where, other, other_tile, tile, pkg_out),
        [SMEM] + [VMEM] * 3 + [HBM],
        [dma((3,))],
        out_specs=[HBM, VMEM],
        aliases={4: 0},
    )
    (bump_out,) = call(
        add_body, "add_parts", [shape(slots, LANES)], (parts, done), [VMEM, ANY]
    )
    return (die_out, pkg_out, bump_out)


def solution(mesh):
    return jax.shard_map(
        local,
        mesh=mesh,
        in_specs=(
            P("grp", "die"),
            P("grp", "die"),
            P("grp", "die"),
            P(("grp", "die"), None),
            P(("grp", "die")),
            P(("grp", "die"), None),
            P("die", None),
            P("die", None),
            P(None, "die"),
            P(None, "die"),
            P(),
        ),
        out_specs=(P("grp", "die"), P("die", None), P(("grp", "die"), None)),
        check_vma=False,
    )
```

```python
import functools
import math

import jax
import jax.numpy as jnp
from jax import lax
from jax.experimental import pallas as pl
from jax.experimental.pallas import tpu as pltpu
from jax.sharding import PartitionSpec as P

RADIUS = 32
SWEEPS = 4
ITERS = 4
LANES = 128
HALO_ROWS = 8
REACH = RADIUS * ITERS
WINDOW = LANES + 2 * RADIUS
F32 = jnp.float32
BF16 = jnp.bfloat16
MOST_VMEM = 57
VMEM = pl.BlockSpec(memory_space=pltpu.VMEM)
SMEM = pl.BlockSpec(memory_space=pltpu.SMEM)
ANY = pl.BlockSpec(memory_space=pl.ANY)
HBM = pl.BlockSpec(memory_space=pltpu.HBM)


def sweep_weights(sweeps):
    return [
        1.0 / (1.0 + 0.8 * math.cos(math.pi * (2 * index + 1) / (2 * sweeps)))
        for index in range(sweeps)
    ]


def call(
    body, name, outs, args, specs, scratch=(), work=1, vmem=16, out_specs=None, aliases=None
):
    bytes_accessed = sum(4 * math.prod(arg.shape) for arg in args)
    return pl.pallas_call(
        body,
        name=name,
        out_shape=outs,
        in_specs=specs,
        out_specs=out_specs or [VMEM] * len(outs),
        input_output_aliases=aliases or {},
        scratch_shapes=list(scratch),
        compiler_params=pltpu.CompilerParams(vmem_limit_bytes=vmem * 1024 * 1024),
        cost_estimate=pl.CostEstimate(
            flops=work * 10**9, bytes_accessed=bytes_accessed, transcendentals=0
        ),
    )(*args)


def place():
    return lax.axis_index("grp"), lax.axis_index("die")


def shape(*dims, dtype=F32):
    return jax.ShapeDtypeStruct(dims, dtype)


def halves(values):
    high = values.astype(BF16)
    low = (values - high.astype(F32)).astype(BF16)
    return high, low


def spread_body(cap, die_count, blocks, block_ref, out_ref):
    slots = block_ref.shape[1]
    block = jnp.concatenate(
        [block_ref[...], jnp.zeros((1, LANES - slots), jnp.int32)], axis=1
    )
    for die in range(die_count):
        row = (pltpu.roll(block, LANES - die * cap, 1) if die else block) - die * blocks
        for at in range(die, out_ref.shape[0], die_count):
            out_ref[at] = row


def asked_rows(cap, die_count, group, ids_ref):
    for die in range(die_count):
        for slot in range(cap):
            yield die * cap + slot, ids_ref[group * die_count + die, slot]


def pick_body(cap, die_count, ids_ref, plane_ref, out_ref, sem):
    group, _ = place()
    for at, row in asked_rows(cap, die_count, group, ids_ref):
        pltpu.make_async_copy(
            plane_ref.at[pl.ds(row, 1), :], out_ref.at[pl.ds(at, 1), :], sem
        ).start()
    pltpu.make_async_copy(plane_ref.at[0 : out_ref.shape[0], :], out_ref, sem).wait()


def build_band(first, pattern, weights):
    place = lax.broadcasted_iota(jnp.int32, (WINDOW, LANES), 0)
    band = None
    for k in range(pattern.shape[0]):
        hit = place == (pattern[k : k + 1, :] - first)
        term = jnp.where(hit, weights[k : k + 1, :], 0.0)
        band = term if band is None else band + term
    fill = jnp.zeros((2 * LANES - WINDOW, LANES), F32)
    return jnp.concatenate(halves(jnp.concatenate([band, fill], axis=0).T), axis=0)


def reciprocal(diag):
    safe = jnp.where(diag > 0.0, diag, 1.0)
    return jnp.where(diag > 0.0, 1.0 / safe, 0.0)


def span(tile, offset=0, size=LANES):
    return pl.ds(pl.multiple_of(tile * LANES + offset, RADIUS), size)


def mixer(coup_ref):
    mix = jnp.concatenate(halves(coup_ref[...]), axis=1)
    return jnp.concatenate([mix, mix], axis=0)


def clear_pads(ref):
    pad = jnp.zeros((RADIUS, 2 * LANES), BF16)
    ref[0:RADIUS, :] = pad
    ref[ref.shape[0] - RADIUS :, :] = pad


def store(ref, tile, values):
    ref[span(tile, RADIUS, values.shape[0]), :] = jnp.concatenate(halves(values), axis=1)


def couple(source, tile, bands, mix, write):
    own = source[span(tile, RADIUS, len(bands) * LANES), :]
    within = jnp.dot(own, mix, preferred_element_type=F32)
    for i, band in enumerate(bands):
        window = source[span(tile + i, 0, WINDOW), :]
        beside = jnp.dot(band[:, :WINDOW], window, preferred_element_type=F32)
        both = beside[:LANES] + beside[LANES:] + within[i * LANES : (i + 1) * LANES]
        write(tile + i, both[:, :LANES] + both[:, LANES:])


def in_chunks(first, count, body, size=4):
    whole = count // size

    @pl.loop(0, whole)
    def _(chunk):
        body(first + chunk * size, size)

    if count % size:
        body(first + whole * size, count % size)


def half_of(tiles):
    half = lax.rem(sum(place()), 2)
    own = tiles // 2
    return half, own, half * own - 1


def pack_body(pat_ref, wgt_ref, volt_hbm, diag_hbm, after_ref, pack_ref, sems):
    tiles = volt_hbm.shape[0] // LANES
    half, _, _ = half_of(tiles)
    mine = pl.ds(pl.multiple_of(half * (tiles - 1) * LANES, LANES), LANES)
    loads = [
        pltpu.make_async_copy(hbm.at[mine, :], pack_ref.at[i * LANES : (i + 1) * LANES, :], sems.at[i])
        for i, hbm in enumerate((volt_hbm, diag_hbm))
    ]
    for load in loads:
        load.start()
    count = pat_ref.shape[0]
    at = 2 * LANES
    pack_ref[at : at + count, :] = pat_ref[:, mine].astype(F32)
    pack_ref[at + count : at + 2 * count, :] = wgt_ref[:, mine]
    for load in loads:
        load.wait()


def prepare_body(
    pat_ref, wgt_ref, coup_ref, halo_ref, volt_hbm, diag_hbm, after_ref,
    band_hbm, base_hbm, inv_hbm,
    volt_ref, diag_ref, band_ref, base_ref, inv_ref, plane_ref, sems,
):
    blocks = volt_hbm.shape[0]
    neighbours = pat_ref.shape[0]
    half, own, shift = half_of(blocks // LANES)
    first, count, outer = 1 - half, own + 1, half * (own + 1)
    source = pl.ds(pl.multiple_of((first + shift) * LANES, LANES), count * LANES)
    target = pl.ds(pl.multiple_of(first * LANES, LANES), count * LANES)
    loads = [
        pltpu.make_async_copy(hbm.at[source, :], ref.at[target, :], sems.at[i])
        for i, (hbm, ref) in enumerate(((volt_hbm, volt_ref), (diag_hbm, diag_ref)))
    ]
    for load in loads:
        load.start()
    volt_ref[span(outer), :] = halo_ref[0:LANES, :]
    diag_ref[span(outer), :] = halo_ref[LANES : 2 * LANES, :]
    clear_pads(plane_ref)
    begin = place()[1] * blocks + shift * LANES
    at = 2 * LANES
    band_ref[outer] = build_band(
        begin + outer * LANES - RADIUS,
        halo_ref[at : at + neighbours, :].astype(jnp.int32),
        halo_ref[at + neighbours : at + 2 * neighbours, :],
    )

    def bands(tile, size):
        for i in range(size):
            lanes = pl.ds(pl.multiple_of((tile + i + shift) * LANES, LANES), LANES)
            band_ref[tile + i] = build_band(
                begin + (tile + i) * LANES - RADIUS, pat_ref[:, lanes], wgt_ref[:, lanes]
            )

    in_chunks(first, count, bands)
    band_out = pltpu.make_async_copy(band_ref, band_hbm, sems.at[2])
    band_out.start()
    for load in loads:
        load.wait()

    def spread(tile, size):
        cut = span(tile, 0, size * LANES)
        store(plane_ref, tile, volt_ref[cut, :])
        inv_ref[cut, :] = reciprocal(diag_ref[cut, :])

    in_chunks(0, own + 2, spread)
    inv_out = pltpu.make_async_copy(inv_ref, inv_hbm, sems.at[3])
    inv_out.start()
    mix = mixer(coup_ref)

    def base(tile, size):
        def write(tile, values):
            base_ref[span(tile), :] = values

        couple(plane_ref, tile, [band_ref[tile + i] for i in range(size)], mix, write)
        cut = span(tile, 0, size * LANES)
        pltpu.make_async_copy(base_ref.at[cut, :], base_hbm.at[cut, :], sems.at[4]).start()

    in_chunks(0, own + 2, base)
    band_out.wait()
    inv_out.wait()
    pltpu.make_async_copy(base_ref, base_hbm, sems.at[4]).wait()


def slot_places(cap, ids_ref):
    per_row = LANES // cap
    lane = lax.broadcasted_iota(jnp.int32, (1, LANES), 1)
    places = []
    for at in range(0, ids_ref.shape[0], per_row):
        total = None
        for i in range(per_row):
            row = jnp.where(lane < cap, ids_ref[at + i : at + i + 1, :], 0)
            row = pltpu.roll(row, i * cap, 1) if i else row
            total = row if total is None else total + row
        places.append(total)
    return places


def gather_inflow(places, first, rows, current):
    at = lax.broadcasted_iota(jnp.int32, (rows, LANES), 0) + first
    hits = [jnp.where(at == place, 1.0, 0.0).astype(BF16) for place in places]
    both = jnp.dot(jnp.concatenate(hits, axis=1), current, preferred_element_type=F32)
    return both[:, :LANES] + both[:, LANES:]


def ends_body(cap, tiles, ids_ref, current_ref, out_ref):
    half, _, _ = half_of(tiles)
    places = slot_places(cap, ids_ref)
    current = jnp.concatenate(halves(current_ref[...]), axis=1)
    out_ref[...] = gather_inflow(places, half * (tiles - 1) * LANES, LANES, current)


def iterate_body(
    cap, die_count, asked_ref, ids_ref, current_ref, coup_ref, halo_ref,
    band_hbm, base_hbm, inv_hbm,
    out_hbm, full_hbm, picked_ref,
    band_ref, base_ref, inv_ref, out_ref, inflow_ref, here_ref, there_ref, sems,
):
    own = out_hbm.shape[0] // LANES
    half, _, shift = half_of(2 * own)
    first, count, outer = 1 - half, own + 1, half * (own + 1)
    loads = [
        pltpu.make_async_copy(hbm, ref, sems.at[i])
        for i, (hbm, ref) in enumerate(
            ((base_hbm, base_ref), (inv_hbm, inv_ref), (band_hbm, band_ref))
        )
    ]
    for load in loads:
        load.start()
    places = slot_places(cap, ids_ref)
    current = jnp.concatenate(halves(current_ref[...]), axis=1)
    for ref in (here_ref, there_ref):
        clear_pads(ref)

    def inflow(tile, size):
        rows = size * LANES
        inflow_ref[span(tile, 0, rows), :] = gather_inflow(
            places, (tile + shift) * LANES, rows, current
        )

    in_chunks(first, count, inflow)
    inflow_ref[span(outer), :] = halo_ref[...]
    loads[0].wait()
    loads[1].wait()

    def start(tile, size):
        cut = span(tile, 0, size * LANES)
        store(here_ref, tile, -(inflow_ref[cut, :] + base_ref[cut, :]) * inv_ref[cut, :])

    in_chunks(0, own + 2, start)
    loads[2].wait()
    mix = mixer(coup_ref)
    refs = (here_ref, there_ref)
    for iteration in range(1, ITERS):
        source, target = refs[(iteration - 1) % 2], refs[iteration % 2]
        last = iteration == ITERS - 1

        def write(tile, coupled, target=target, last=last):
            values = -(inflow_ref[span(tile), :] + coupled) * inv_ref[span(tile), :]
            if last:
                out_ref[span(tile - 1), :] = values
            else:
                store(target, tile, values)

        def step(tile, size, source=source, write=write):
            bands = [band_ref[tile + i] for i in range(size)]
            couple(source, tile, bands, mix, write)

        def final(tile, size, step=step):
            step(tile, size)
            cut = span(tile - 1, 0, size * LANES)
            whole = span(half * own + tile - 1, 0, size * LANES)
            pltpu.make_async_copy(out_ref.at[cut, :], out_hbm.at[cut, :], sems.at[3]).start()
            pltpu.make_async_copy(out_ref.at[cut, :], full_hbm.at[whole, :], sems.at[4]).start()

        if last:
            in_chunks(1, own, final)
        else:
            in_chunks(0, own + 2, step)

    base_row = half * own * LANES
    group, _ = place()
    pair = group - lax.rem(group, 2)
    for member in range(2):
        offset = member * (picked_ref.shape[0] // 2)
        for at, row in asked_rows(cap, die_count, pair + member, asked_ref):
            row = row - base_row
            inside = (row >= 0) & (row < own * LANES)
            safe = jnp.clip(row, 0, own * LANES - 1)
            values = out_ref[pl.ds(safe, 1), :]
            picked_ref[pl.ds(offset + at, 1), :] = jnp.where(inside, values, 0.0)
    pltpu.make_async_copy(out_ref, out_hbm, sems.at[3]).wait()
    pltpu.make_async_copy(out_ref, full_hbm.at[0 : own * LANES, :], sems.at[4]).wait()


def join_body(other_ref, full_in_hbm, full_hbm, done_ref, sem):
    rows = other_ref.shape[0]
    half, _, _ = half_of(2 * rows // LANES)
    start = pl.multiple_of((1 - half) * rows, LANES)
    copy = pltpu.make_async_copy(other_ref, full_hbm.at[pl.ds(start, rows), :], sem)
    copy.start()
    done_ref[...] = jnp.zeros(done_ref.shape, F32)
    copy.wait()


def add_body(parts_ref, after_ref, out_ref):
    rows = out_ref.shape[0]
    out_ref[...] = parts_ref[0:rows, :] + parts_ref[rows:, :]


def scatter_body(cols, node_ref, cond_ref, start_ref, volt_ref, load_ref, shunt_ref,
                 right_ref, inv_ref, inner_ref, outer_ref):
    blocks = node_ref.shape[0]
    rows = volt_ref.shape[0]
    group = 8
    row_at = lax.broadcasted_iota(jnp.int32, (rows, LANES), 0)
    col_at = lax.broadcasted_iota(jnp.int32, (cols, LANES), 0)
    total = jnp.zeros((4 * rows, cols), F32)
    for first in range(0, blocks, group):
        node = node_ref[first : first + group, :]
        live = node >= 0
        cond = jnp.where(live, cond_ref[first : first + group, :], 0.0)
        flow = cond * start_ref[first : first + group, :]
        safe = jnp.where(live, node, 0)
        row, col = safe // cols, safe % cols
        parts = halves(cond) + halves(flow)
        left, right = [], []
        for i in range(group):
            spot = jnp.where(row_at == row[i : i + 1, :], 1.0, 0.0).astype(BF16)
            left.append(
                jnp.concatenate([spot * part[i : i + 1, :] for part in parts], axis=0)
            )
            right.append(jnp.where(col_at == col[i : i + 1, :], 1.0, 0.0).astype(BF16))
        total = total + lax.dot_general(
            jnp.concatenate(left, axis=1),
            jnp.concatenate(right, axis=1),
            (((1,), (1,)), ((), ())),
            preferred_element_type=F32,
        )
    gsum = total[:rows] + total[rows : 2 * rows]
    inject = total[2 * rows : 3 * rows] + total[3 * rows :]
    inv = 1.0 / (4.0 + shunt_ref[...] + gsum)
    right_side = (inject - load_ref[...]) * inv
    right_ref[...] = right_side
    inv_ref[...] = inv
    volt = volt_ref[...]
    top, bottom = (
        jnp.concatenate([volt[cut], right_side[cut], inv[cut]], axis=0)
        for cut in (slice(0, HALO_ROWS), slice(rows - HALO_ROWS, rows))
    )
    swap_parts(inner_ref, outer_ref, place()[0], top, bottom)


def swap_parts(inner_ref, outer_ref, mine, first, last):
    even = lax.rem(mine, 2) == 0
    inner_ref[...] = jnp.where(even, last, first)
    outer_ref[...] = jnp.where(even, first, last)


def swapped(inner, outer, mine):
    even = lax.rem(mine, 2) == 0
    return jnp.where(even, outer, inner), jnp.where(even, inner, outer)


def swap(inner, outer, axis):
    count = lax.axis_size(axis)

    def pairs(start):
        return [
            pair
            for i in range(start, count - 1, 2)
            for pair in ((i, i + 1), (i + 1, i))
        ]

    return lax.ppermute(inner, axis, pairs(0)), lax.ppermute(outer, axis, pairs(1))


def extended(own, top, bottom, index):
    cut = slice(index * HALO_ROWS, (index + 1) * HALO_ROWS)
    return jnp.concatenate([top[cut], own, bottom[cut]], axis=0)


def edge_body(volt_ref, right_ref, inv_ref, inner_ref, outer_ref, west_ref, east_ref):
    cols = volt_ref.shape[1]
    top, bottom = swapped(inner_ref[...], outer_ref[...], place()[0])
    out_rows, high = west_ref.shape
    west, east = None, None
    for index, ref in enumerate((volt_ref, right_ref, inv_ref)):
        whole = extended(ref[...], top, bottom, index)
        lane = lax.broadcasted_iota(jnp.int32, (whole.shape[0], LANES), 1)
        head, tail = whole[:, :LANES], whole[:, cols - LANES :]
        at = index * SWEEPS
        head = pltpu.roll(head, at, 1) if at else head
        tail = pltpu.roll(tail, at + SWEEPS, 1)
        west = head if west is None else jnp.where(lane >= at, head, west)
        east = tail if east is None else jnp.where(lane >= at, tail, east)
    fill = jnp.zeros((high - west.shape[0], LANES), F32)
    west, east = (
        jnp.concatenate([part, fill], axis=0).T[:out_rows] for part in (west, east)
    )
    swap_parts(west_ref, east_ref, place()[1], west, east)


def sweep_body(copies, node_ref, cond_ref, start_ref, volt_ref, right_ref, inv_ref,
               row_in_ref, row_out_ref, col_in_ref, col_out_ref, out_ref, current_ref):
    rows, cols = volt_ref.shape
    blocks = node_ref.shape[0]
    cap = current_ref.shape[1]
    whole = []
    top, bottom = swapped(row_in_ref[...], row_out_ref[...], place()[0])
    out_rows, high = col_in_ref.shape
    fill = jnp.zeros((LANES - out_rows, high), F32)
    wests, easts = (
        jnp.concatenate([part, fill], axis=0).T[: rows + 2 * HALO_ROWS]
        for part in swapped(col_in_ref[...], col_out_ref[...], place()[1])
    )
    for index, ref in enumerate((volt_ref, right_ref, inv_ref)):
        own = extended(ref[...], top, bottom, index)
        at = index * SWEEPS
        west = pltpu.roll(wests, LANES - SWEEPS - at, 1)
        east = pltpu.roll(easts, LANES - at, 1) if at else easts
        whole.append(jnp.concatenate([west, own, east], axis=1))
    volt, right_side, inv = whole
    high, wide = volt.shape
    for weight in sweep_weights(SWEEPS):
        beside = (
            pltpu.roll(volt, 1, 0)
            + pltpu.roll(volt, high - 1, 0)
            + pltpu.roll(volt, 1, 1)
            + pltpu.roll(volt, wide - 1, 1)
        )
        volt = (1.0 - weight) * volt + weight * (right_side + beside * inv)
    volt = volt[HALO_ROWS : HALO_ROWS + rows, LANES : LANES + cols]
    out_ref[...] = volt
    both = jnp.concatenate(halves(volt), axis=0)
    group = 8
    row_at = lax.broadcasted_iota(jnp.int32, (rows, LANES), 0)
    col_at = lax.broadcasted_iota(jnp.int32, (cols, LANES), 0)
    dies = blocks // cap
    for first in range(0, blocks, group):
        node = node_ref[first : first + group, :]
        live = node >= 0
        cond = jnp.where(live, cond_ref[first : first + group, :], 0.0)
        safe = jnp.where(live, node, 0)
        row, col = safe // cols, safe % cols
        spots = jnp.concatenate(
            [
                jnp.where(col_at == col[i : i + 1, :], 1.0, 0.0).astype(BF16)
                for i in range(group)
            ],
            axis=1,
        )
        found = jnp.dot(both, spots, preferred_element_type=F32)
        found = found[:rows] + found[rows:]
        for i in range(group):
            mine = found[:, i * LANES : (i + 1) * LANES]
            at_bump = jnp.sum(
                jnp.where(row_at == row[i : i + 1, :], mine, 0.0), axis=0, keepdims=True
            )
            block = first + i
            current = cond[i : i + 1, :] * (start_ref[block : block + 1, :] - at_bump)
            current_ref[block // cap, block % cap : block % cap + 1, :] = current
    for copy in range(1, copies):
        current_ref[copy * dies : (copy + 1) * dies] = current_ref[0:dies]


def local(
    die_volt,
    die_load,
    die_shunt,
    bump_node,
    bump_block,
    bump_cond,
    pkg_volt,
    pkg_diag,
    pkg_pattern,
    pkg_weight,
    block_coupling,
):
    die_count = lax.axis_size("die")
    group_count = lax.axis_size("grp")
    devices = die_count * group_count
    blocks = pkg_volt.shape[0]
    tiles = blocks // LANES
    neighbours = pkg_pattern.shape[0]
    slots = bump_block.shape[0]
    cap = slots // die_count
    rows, cols = die_volt.shape
    (spread,) = call(
        functools.partial(spread_body, cap, die_count, blocks),
        "spread_blocks",
        [shape(devices, 1, LANES, dtype=jnp.int32)],
        (bump_block.reshape(1, slots),),
        [VMEM],
    )
    ids = lax.all_to_all(
        spread, ("grp", "die"), split_axis=0, concat_axis=0, tiled=True
    ).reshape(devices, LANES)

    (picked,) = call(
        functools.partial(pick_body, cap, die_count),
        "pick_rows",
        [shape(slots, LANES)],
        (ids, pkg_volt),
        [SMEM, HBM],
        [pltpu.SemaphoreType.DMA(())],
        vmem=MOST_VMEM,
    )
    bump_start = lax.all_to_all(
        picked.reshape(die_count, cap, LANES), "die", split_axis=0, concat_axis=0, tiled=True
    ).reshape(slots, LANES)

    beside_end = [
        (g * die_count + a, g * die_count + b)
        for g in range(group_count)
        for d in range((g + 1) % 2, die_count - 1, 2)
        for a, b in ((d, d + 1), (d + 1, d))
    ]
    (pack,) = call(
        pack_body,
        "package_pack",
        [shape(2 * LANES + 2 * neighbours, LANES)],
        (pkg_pattern, pkg_weight, pkg_volt, pkg_diag, picked),
        [VMEM, VMEM, HBM, HBM, HBM],
        [pltpu.SemaphoreType.DMA((2,))],
        vmem=MOST_VMEM,
    )
    halo = lax.ppermute(pack, ("grp", "die"), beside_end)

    right_side, inv, *edges = call(
        functools.partial(scatter_body, cols),
        "scatter_bumps",
        [shape(rows, cols)] * 2 + [shape(3 * HALO_ROWS, cols)] * 2,
        (bump_node, bump_cond, bump_start, die_volt, die_load, die_shunt),
        [VMEM] * 6,
        work=3,
    )
    beside = swap(*edges, "grp")

    edge_rows = -(-3 * SWEEPS // 8) * 8
    edge_cols = -(-(rows + 2 * HALO_ROWS) // LANES) * LANES
    edges = call(
        edge_body,
        "edge_columns",
        [shape(edge_rows, edge_cols)] * 2,
        (die_volt, right_side, inv, *beside),
        [VMEM] * 5,
    )
    columns = swap(*edges, "die")

    die_out, current = call(
        functools.partial(sweep_body, group_count),
        "sweeps",
        [shape(rows, cols), shape(devices, cap, LANES)],
        (bump_node, bump_cond, bump_start, die_volt, right_side, inv, *beside, *columns),
        [VMEM] * 10,
        work=4,
    )
    own = tiles // 2
    dma = pltpu.SemaphoreType.DMA
    plane = pltpu.VMEM(((own + 2) * LANES + 2 * RADIUS, 2 * LANES), BF16)
    range_rows = pltpu.VMEM(((own + 2) * LANES, LANES), F32)
    range_bands = pltpu.VMEM((own + 2, 2 * LANES, 2 * LANES), BF16)
    band, base, pkg_inv = call(
        prepare_body,
        "package_prepare",
        [
            shape(own + 2, 2 * LANES, 2 * LANES, dtype=BF16),
            shape((own + 2) * LANES, LANES),
            shape((own + 2) * LANES, LANES),
        ],
        (pkg_pattern, pkg_weight, block_coupling, halo, pkg_volt, pkg_diag, die_out),
        [VMEM] * 4 + [HBM] * 3,
        [range_rows, range_rows, range_bands, range_rows, range_rows, plane, dma((5,))],
        work=7,
        vmem=MOST_VMEM,
        out_specs=[HBM] * 3,
    )

    current = lax.all_to_all(
        current, ("grp", "die"), split_axis=0, concat_axis=0, tiled=True
    ).reshape(devices * cap, LANES)

    (inflow,) = call(
        functools.partial(ends_body, cap, tiles),
        "package_end",
        [shape(LANES, LANES)],
        (ids, current),
        [VMEM, VMEM],
    )
    halo_inflow = lax.ppermute(inflow, ("grp", "die"), beside_end)
    half_out, pkg_out, picked = call(
        functools.partial(iterate_body, cap, die_count),
        "package_iterations",
        [shape(own * LANES, LANES), shape(blocks, LANES), shape(2 * slots, LANES)],
        (ids, ids, current, block_coupling, halo_inflow, band, base, pkg_inv),
        [SMEM] + [VMEM] * 4 + [HBM] * 3,
        [
            range_bands, range_rows, range_rows, pltpu.VMEM((own * LANES, LANES), F32),
            range_rows, plane, plane, dma((5,)),
        ],
        work=10,
        vmem=MOST_VMEM,
        out_specs=[HBM, HBM, VMEM],
    )
    pair = 2 * die_count
    parts = lax.all_to_all(
        picked.reshape(pair, cap, LANES),
        ("grp", "die"),
        split_axis=0,
        concat_axis=0,
        axis_index_groups=[
            [first + i for i in range(pair)] for first in range(0, devices, pair)
        ],
        tiled=True,
    ).reshape(2 * slots, LANES)
    other = lax.ppermute(half_out, "grp", [(g, g ^ 1) for g in range(group_count)])
    pkg_out, done = call(
        join_body,
        "join_halves",
        [shape(blocks, LANES), shape(8, LANES)],
        (other, pkg_out),
        [VMEM, HBM],
        [dma(())],
        out_specs=[HBM, VMEM],
        aliases={1: 0},
    )
    (bump_out,) = call(
        add_body, "add_parts", [shape(slots, LANES)], (parts, done), [VMEM, ANY]
    )
    return (die_out, pkg_out, bump_out)


def solution(mesh):
    return jax.shard_map(
        local,
        mesh=mesh,
        in_specs=(
            P("grp", "die"),
            P("grp", "die"),
            P("grp", "die"),
            P(("grp", "die"), None),
            P(("grp", "die")),
            P(("grp", "die"), None),
            P("die", None),
            P("die", None),
            P(None, "die"),
            P(None, "die"),
            P(),
        ),
        out_specs=(P("grp", "die"), P("die", None), P(("grp", "die"), None)),
        check_vma=False,
    )
```

```python
import functools
import math

import jax
import jax.numpy as jnp
from jax import lax
from jax.experimental import pallas as pl
from jax.experimental.pallas import tpu as pltpu
from jax.sharding import PartitionSpec as P

RADIUS = 32
SWEEPS = 4
ITERS = 4
LANES = 128
HALO_ROWS = 8
REACH = RADIUS * ITERS
WINDOW = LANES + 2 * RADIUS
F32 = jnp.float32
BF16 = jnp.bfloat16
MOST_VMEM = 57
VMEM = pl.BlockSpec(memory_space=pltpu.VMEM)
SMEM = pl.BlockSpec(memory_space=pltpu.SMEM)
ANY = pl.BlockSpec(memory_space=pl.ANY)
HBM = pl.BlockSpec(memory_space=pltpu.HBM)


def sweep_weights(sweeps):
    return [
        1.0 / (1.0 + 0.8 * math.cos(math.pi * (2 * index + 1) / (2 * sweeps)))
        for index in range(sweeps)
    ]


def call(
    body, name, outs, args, specs, scratch=(), work=1, vmem=16, out_specs=None, aliases=None
):
    bytes_accessed = sum(4 * math.prod(arg.shape) for arg in args)
    return pl.pallas_call(
        body,
        name=name,
        out_shape=outs,
        in_specs=specs,
        out_specs=out_specs or [VMEM] * len(outs),
        input_output_aliases=aliases or {},
        scratch_shapes=list(scratch),
        compiler_params=pltpu.CompilerParams(vmem_limit_bytes=vmem * 1024 * 1024),
        cost_estimate=pl.CostEstimate(
            flops=work * 10**9, bytes_accessed=bytes_accessed, transcendentals=0
        ),
    )(*args)


def place():
    return lax.axis_index("grp"), lax.axis_index("die")


def shape(*dims, dtype=F32):
    return jax.ShapeDtypeStruct(dims, dtype)


def halves(values):
    high = values.astype(BF16)
    low = (values - high.astype(F32)).astype(BF16)
    return high, low


def spread_body(cap, die_count, blocks, block_ref, out_ref):
    slots = block_ref.shape[1]
    block = jnp.concatenate(
        [block_ref[...], jnp.zeros((1, LANES - slots), jnp.int32)], axis=1
    )
    for die in range(die_count):
        row = (pltpu.roll(block, LANES - die * cap, 1) if die else block) - die * blocks
        for at in range(die, out_ref.shape[0], die_count):
            out_ref[at] = row


def asked_rows(cap, die_count, group, ids_ref):
    for die in range(die_count):
        for slot in range(cap):
            yield die * cap + slot, ids_ref[group * die_count + die, slot]


def pick_body(cap, die_count, ids_ref, plane_ref, after_ref, out_ref, sem):
    group, _ = place()
    for at, row in asked_rows(cap, die_count, group, ids_ref):
        pltpu.make_async_copy(
            plane_ref.at[pl.ds(row, 1), :], out_ref.at[pl.ds(at, 1), :], sem
        ).start()
    pltpu.make_async_copy(plane_ref.at[0 : out_ref.shape[0], :], out_ref, sem).wait()


def build_band(first, pattern, weights):
    place = lax.broadcasted_iota(jnp.int32, (WINDOW, LANES), 0)
    band = None
    for k in range(pattern.shape[0]):
        hit = place == (pattern[k : k + 1, :] - first)
        term = jnp.where(hit, weights[k : k + 1, :], 0.0)
        band = term if band is None else band + term
    fill = jnp.zeros((2 * LANES - WINDOW, LANES), F32)
    return jnp.concatenate(halves(jnp.concatenate([band, fill], axis=0).T), axis=0)


def reciprocal(diag):
    safe = jnp.where(diag > 0.0, diag, 1.0)
    return jnp.where(diag > 0.0, 1.0 / safe, 0.0)


def span(tile, offset=0, size=LANES):
    return pl.ds(pl.multiple_of(tile * LANES + offset, RADIUS), size)


def mixer(coup_ref):
    mix = jnp.concatenate(halves(coup_ref[...]), axis=1)
    return jnp.concatenate([mix, mix], axis=0)


def clear_pads(ref):
    pad = jnp.zeros((RADIUS, 2 * LANES), BF16)
    ref[0:RADIUS, :] = pad
    ref[ref.shape[0] - RADIUS :, :] = pad


def store(ref, tile, values):
    ref[span(tile, RADIUS, values.shape[0]), :] = jnp.concatenate(halves(values), axis=1)


def couple(source, tile, bands, mix, write):
    own = source[span(tile, RADIUS, len(bands) * LANES), :]
    within = jnp.dot(own, mix, preferred_element_type=F32)
    for i, band in enumerate(bands):
        window = source[span(tile + i, 0, WINDOW), :]
        beside = jnp.dot(band[:, :WINDOW], window, preferred_element_type=F32)
        both = beside[:LANES] + beside[LANES:] + within[i * LANES : (i + 1) * LANES]
        write(tile + i, both[:, :LANES] + both[:, LANES:])


def in_chunks(first, count, body, size=4):
    whole = count // size

    @pl.loop(0, whole)
    def _(chunk):
        body(first + chunk * size, size)

    if count % size:
        body(first + whole * size, count % size)


def half_of(tiles):
    half = lax.rem(sum(place()), 2)
    own = tiles // 2
    return half, own, half * own - 1


def pack_body(pat_ref, wgt_ref, volt_hbm, diag_hbm, pack_ref, sems):
    tiles = volt_hbm.shape[0] // LANES
    half, _, _ = half_of(tiles)
    mine = pl.ds(pl.multiple_of(half * (tiles - 1) * LANES, LANES), LANES)
    loads = [
        pltpu.make_async_copy(hbm.at[mine, :], pack_ref.at[i * LANES : (i + 1) * LANES, :], sems.at[i])
        for i, hbm in enumerate((volt_hbm, diag_hbm))
    ]
    for load in loads:
        load.start()
    count = pat_ref.shape[0]
    at = 2 * LANES
    pack_ref[at : at + count, :] = pat_ref[:, mine].astype(F32)
    pack_ref[at + count : at + 2 * count, :] = wgt_ref[:, mine]
    for load in loads:
        load.wait()


def prepare_body(
    pat_ref, wgt_ref, coup_ref, halo_ref, volt_hbm, diag_hbm, after_ref,
    band_hbm, base_hbm, inv_hbm,
    volt_ref, diag_ref, band_ref, base_ref, inv_ref, plane_ref, sems,
):
    blocks = volt_hbm.shape[0]
    neighbours = pat_ref.shape[0]
    half, own, shift = half_of(blocks // LANES)
    first, count, outer = 1 - half, own + 1, half * (own + 1)
    source = pl.ds(pl.multiple_of((first + shift) * LANES, LANES), count * LANES)
    target = pl.ds(pl.multiple_of(first * LANES, LANES), count * LANES)
    loads = [
        pltpu.make_async_copy(hbm.at[source, :], ref.at[target, :], sems.at[i])
        for i, (hbm, ref) in enumerate(((volt_hbm, volt_ref), (diag_hbm, diag_ref)))
    ]
    for load in loads:
        load.start()
    volt_ref[span(outer), :] = halo_ref[0:LANES, :]
    diag_ref[span(outer), :] = halo_ref[LANES : 2 * LANES, :]
    clear_pads(plane_ref)
    begin = place()[1] * blocks + shift * LANES
    at = 2 * LANES
    band_ref[outer] = build_band(
        begin + outer * LANES - RADIUS,
        halo_ref[at : at + neighbours, :].astype(jnp.int32),
        halo_ref[at + neighbours : at + 2 * neighbours, :],
    )

    def bands(tile, size):
        for i in range(size):
            lanes = pl.ds(pl.multiple_of((tile + i + shift) * LANES, LANES), LANES)
            band_ref[tile + i] = build_band(
                begin + (tile + i) * LANES - RADIUS, pat_ref[:, lanes], wgt_ref[:, lanes]
            )

    in_chunks(first, count, bands)
    band_out = pltpu.make_async_copy(band_ref, band_hbm, sems.at[2])
    band_out.start()
    for load in loads:
        load.wait()

    def spread(tile, size):
        cut = span(tile, 0, size * LANES)
        store(plane_ref, tile, volt_ref[cut, :])
        inv_ref[cut, :] = reciprocal(diag_ref[cut, :])

    in_chunks(0, own + 2, spread)
    inv_out = pltpu.make_async_copy(inv_ref, inv_hbm, sems.at[3])
    inv_out.start()
    mix = mixer(coup_ref)

    def base(tile, size):
        def write(tile, values):
            base_ref[span(tile), :] = values

        couple(plane_ref, tile, [band_ref[tile + i] for i in range(size)], mix, write)
        cut = span(tile, 0, size * LANES)
        pltpu.make_async_copy(base_ref.at[cut, :], base_hbm.at[cut, :], sems.at[4]).start()

    in_chunks(0, own + 2, base)
    band_out.wait()
    inv_out.wait()
    pltpu.make_async_copy(base_ref, base_hbm, sems.at[4]).wait()


def slot_places(cap, ids_ref):
    per_row = LANES // cap
    lane = lax.broadcasted_iota(jnp.int32, (1, LANES), 1)
    places = []
    for at in range(0, ids_ref.shape[0], per_row):
        total = None
        for i in range(per_row):
            row = jnp.where(lane < cap, ids_ref[at + i : at + i + 1, :], 0)
            row = pltpu.roll(row, i * cap, 1) if i else row
            total = row if total is None else total + row
        places.append(total)
    return places


def gather_inflow(places, first, rows, current):
    at = lax.broadcasted_iota(jnp.int32, (rows, LANES), 0) + first
    hits = [jnp.where(at == place, 1.0, 0.0).astype(BF16) for place in places]
    both = jnp.dot(jnp.concatenate(hits, axis=1), current, preferred_element_type=F32)
    return both[:, :LANES] + both[:, LANES:]


def ends_body(cap, tiles, ids_ref, current_ref, out_ref):
    half, _, _ = half_of(tiles)
    places = slot_places(cap, ids_ref)
    current = jnp.concatenate(halves(current_ref[...]), axis=1)
    out_ref[...] = gather_inflow(places, half * (tiles - 1) * LANES, LANES, current)


def inflow_body(cap, tiles, ids_ref, current_ref, after_ref, out_hbm, out_ref, sem):
    half, own, shift = half_of(tiles)
    first, count = 1 - half, own + 1
    places = slot_places(cap, ids_ref)
    current = jnp.concatenate(halves(current_ref[...]), axis=1)

    def inflow(tile, size):
        cut = span(tile, 0, size * LANES)
        out_ref[cut, :] = gather_inflow(
            places, (tile + shift) * LANES, size * LANES, current
        )
        pltpu.make_async_copy(out_ref.at[cut, :], out_hbm.at[cut, :], sem).start()

    in_chunks(first, count, inflow)
    whole = pl.ds(0, count * LANES)
    pltpu.make_async_copy(out_ref.at[whole, :], out_hbm.at[whole, :], sem).wait()


def iterate_body(
    cap, die_count, asked_ref, coup_ref, halo_ref,
    inflow_hbm, band_hbm, base_hbm, inv_hbm,
    out_hbm, full_hbm, picked_ref,
    band_ref, base_ref, inv_ref, out_ref, inflow_ref, here_ref, there_ref, sems,
):
    own = out_hbm.shape[0] // LANES
    half, _, _ = half_of(2 * own)
    outer = half * (own + 1)
    known = pl.ds(pl.multiple_of((1 - half) * LANES, LANES), (own + 1) * LANES)
    loads = [
        pltpu.make_async_copy(hbm, ref, sems.at[i])
        for i, (hbm, ref) in enumerate(
            (
                (inflow_hbm.at[known, :], inflow_ref.at[known, :]),
                (base_hbm, base_ref),
                (inv_hbm, inv_ref),
                (band_hbm, band_ref),
            )
        )
    ]
    for load in loads:
        load.start()
    for ref in (here_ref, there_ref):
        clear_pads(ref)
    inflow_ref[span(outer), :] = halo_ref[...]
    for load in loads[:3]:
        load.wait()

    def start(tile, size):
        cut = span(tile, 0, size * LANES)
        store(here_ref, tile, -(inflow_ref[cut, :] + base_ref[cut, :]) * inv_ref[cut, :])

    in_chunks(0, own + 2, start)
    loads[3].wait()
    mix = mixer(coup_ref)
    refs = (here_ref, there_ref)
    for iteration in range(1, ITERS):
        source, target = refs[(iteration - 1) % 2], refs[iteration % 2]
        last = iteration == ITERS - 1

        def write(tile, coupled, target=target, last=last):
            values = -(inflow_ref[span(tile), :] + coupled) * inv_ref[span(tile), :]
            if last:
                out_ref[span(tile - 1), :] = values
            else:
                store(target, tile, values)

        def step(tile, size, source=source, write=write):
            bands = [band_ref[tile + i] for i in range(size)]
            couple(source, tile, bands, mix, write)

        def final(tile, size, step=step):
            step(tile, size)
            cut = span(tile - 1, 0, size * LANES)
            whole = span(half * own + tile - 1, 0, size * LANES)
            pltpu.make_async_copy(out_ref.at[cut, :], out_hbm.at[cut, :], sems.at[4]).start()
            pltpu.make_async_copy(out_ref.at[cut, :], full_hbm.at[whole, :], sems.at[5]).start()

        if last:
            in_chunks(1, own, final)
        else:
            in_chunks(0, own + 2, step)

    base_row = half * own * LANES
    group, _ = place()
    pair = group - lax.rem(group, 2)
    for member in range(2):
        offset = member * (picked_ref.shape[0] // 2)
        for at, row in asked_rows(cap, die_count, pair + member, asked_ref):
            row = row - base_row
            inside = (row >= 0) & (row < own * LANES)
            safe = jnp.clip(row, 0, own * LANES - 1)
            values = out_ref[pl.ds(safe, 1), :]
            picked_ref[pl.ds(offset + at, 1), :] = jnp.where(inside, values, 0.0)
    pltpu.make_async_copy(out_ref, out_hbm, sems.at[4]).wait()
    pltpu.make_async_copy(out_ref, full_hbm.at[0 : own * LANES, :], sems.at[5]).wait()


def join_body(other_ref, full_in_hbm, full_hbm, done_ref, sem):
    rows = other_ref.shape[0]
    half, _, _ = half_of(2 * rows // LANES)
    start = pl.multiple_of((1 - half) * rows, LANES)
    copy = pltpu.make_async_copy(other_ref, full_hbm.at[pl.ds(start, rows), :], sem)
    copy.start()
    done_ref[...] = jnp.zeros(done_ref.shape, F32)
    copy.wait()


def add_body(parts_ref, after_ref, out_ref):
    rows = out_ref.shape[0]
    out_ref[...] = parts_ref[0:rows, :] + parts_ref[rows:, :]


def scatter_body(cols, node_ref, cond_ref, start_ref, volt_ref, load_ref, shunt_ref,
                 after_ref, right_ref, inv_ref, inner_ref, outer_ref):
    blocks = node_ref.shape[0]
    rows = volt_ref.shape[0]
    group = 8
    row_at = lax.broadcasted_iota(jnp.int32, (rows, LANES), 0)
    col_at = lax.broadcasted_iota(jnp.int32, (cols, LANES), 0)
    total = jnp.zeros((4 * rows, cols), F32)
    for first in range(0, blocks, group):
        node = node_ref[first : first + group, :]
        live = node >= 0
        cond = jnp.where(live, cond_ref[first : first + group, :], 0.0)
        flow = cond * start_ref[first : first + group, :]
        safe = jnp.where(live, node, 0)
        row, col = safe // cols, safe % cols
        parts = halves(cond) + halves(flow)
        left, right = [], []
        for i in range(group):
            spot = jnp.where(row_at == row[i : i + 1, :], 1.0, 0.0).astype(BF16)
            left.append(
                jnp.concatenate([spot * part[i : i + 1, :] for part in parts], axis=0)
            )
            right.append(jnp.where(col_at == col[i : i + 1, :], 1.0, 0.0).astype(BF16))
        total = total + lax.dot_general(
            jnp.concatenate(left, axis=1),
            jnp.concatenate(right, axis=1),
            (((1,), (1,)), ((), ())),
            preferred_element_type=F32,
        )
    gsum = total[:rows] + total[rows : 2 * rows]
    inject = total[2 * rows : 3 * rows] + total[3 * rows :]
    inv = 1.0 / (4.0 + shunt_ref[...] + gsum)
    right_side = (inject - load_ref[...]) * inv
    right_ref[...] = right_side
    inv_ref[...] = inv
    volt = volt_ref[...]
    top, bottom = (
        jnp.concatenate([volt[cut], right_side[cut], inv[cut]], axis=0)
        for cut in (slice(0, HALO_ROWS), slice(rows - HALO_ROWS, rows))
    )
    swap_parts(inner_ref, outer_ref, place()[0], top, bottom)


def swap_parts(inner_ref, outer_ref, mine, first, last):
    even = lax.rem(mine, 2) == 0
    inner_ref[...] = jnp.where(even, last, first)
    outer_ref[...] = jnp.where(even, first, last)


def swapped(inner, outer, mine):
    even = lax.rem(mine, 2) == 0
    return jnp.where(even, outer, inner), jnp.where(even, inner, outer)


def swap(inner, outer, axis):
    count = lax.axis_size(axis)

    def pairs(start):
        return [
            pair
            for i in range(start, count - 1, 2)
            for pair in ((i, i + 1), (i + 1, i))
        ]

    return lax.ppermute(inner, axis, pairs(0)), lax.ppermute(outer, axis, pairs(1))


def extended(own, top, bottom, index):
    cut = slice(index * HALO_ROWS, (index + 1) * HALO_ROWS)
    return jnp.concatenate([top[cut], own, bottom[cut]], axis=0)


def edge_body(volt_ref, right_ref, inv_ref, inner_ref, outer_ref, west_ref, east_ref):
    cols = volt_ref.shape[1]
    top, bottom = swapped(inner_ref[...], outer_ref[...], place()[0])
    out_rows, high = west_ref.shape
    west, east = None, None
    for index, ref in enumerate((volt_ref, right_ref, inv_ref)):
        whole = extended(ref[...], top, bottom, index)
        lane = lax.broadcasted_iota(jnp.int32, (whole.shape[0], LANES), 1)
        head, tail = whole[:, :LANES], whole[:, cols - LANES :]
        at = index * SWEEPS
        head = pltpu.roll(head, at, 1) if at else head
        tail = pltpu.roll(tail, at + SWEEPS, 1)
        west = head if west is None else jnp.where(lane >= at, head, west)
        east = tail if east is None else jnp.where(lane >= at, tail, east)
    fill = jnp.zeros((high - west.shape[0], LANES), F32)
    west, east = (
        jnp.concatenate([part, fill], axis=0).T[:out_rows] for part in (west, east)
    )
    swap_parts(west_ref, east_ref, place()[1], west, east)


def sweep_body(copies, node_ref, cond_ref, start_ref, volt_ref, right_ref, inv_ref,
               row_in_ref, row_out_ref, col_in_ref, col_out_ref, out_ref, current_ref):
    rows, cols = volt_ref.shape
    blocks = node_ref.shape[0]
    cap = current_ref.shape[1]
    whole = []
    top, bottom = swapped(row_in_ref[...], row_out_ref[...], place()[0])
    out_rows, high = col_in_ref.shape
    fill = jnp.zeros((LANES - out_rows, high), F32)
    wests, easts = (
        jnp.concatenate([part, fill], axis=0).T[: rows + 2 * HALO_ROWS]
        for part in swapped(col_in_ref[...], col_out_ref[...], place()[1])
    )
    for index, ref in enumerate((volt_ref, right_ref, inv_ref)):
        own = extended(ref[...], top, bottom, index)
        at = index * SWEEPS
        west = pltpu.roll(wests, LANES - SWEEPS - at, 1)
        east = pltpu.roll(easts, LANES - at, 1) if at else easts
        whole.append(jnp.concatenate([west, own, east], axis=1))
    volt, right_side, inv = whole
    high, wide = volt.shape
    for weight in sweep_weights(SWEEPS):
        beside = (
            pltpu.roll(volt, 1, 0)
            + pltpu.roll(volt, high - 1, 0)
            + pltpu.roll(volt, 1, 1)
            + pltpu.roll(volt, wide - 1, 1)
        )
        volt = (1.0 - weight) * volt + weight * (right_side + beside * inv)
    volt = volt[HALO_ROWS : HALO_ROWS + rows, LANES : LANES + cols]
    out_ref[...] = volt
    both = jnp.concatenate(halves(volt), axis=0)
    group = 8
    row_at = lax.broadcasted_iota(jnp.int32, (rows, LANES), 0)
    col_at = lax.broadcasted_iota(jnp.int32, (cols, LANES), 0)
    dies = blocks // cap
    for first in range(0, blocks, group):
        node = node_ref[first : first + group, :]
        live = node >= 0
        cond = jnp.where(live, cond_ref[first : first + group, :], 0.0)
        safe = jnp.where(live, node, 0)
        row, col = safe // cols, safe % cols
        spots = jnp.concatenate(
            [
                jnp.where(col_at == col[i : i + 1, :], 1.0, 0.0).astype(BF16)
                for i in range(group)
            ],
            axis=1,
        )
        found = jnp.dot(both, spots, preferred_element_type=F32)
        found = found[:rows] + found[rows:]
        for i in range(group):
            mine = found[:, i * LANES : (i + 1) * LANES]
            at_bump = jnp.sum(
                jnp.where(row_at == row[i : i + 1, :], mine, 0.0), axis=0, keepdims=True
            )
            block = first + i
            current = cond[i : i + 1, :] * (start_ref[block : block + 1, :] - at_bump)
            current_ref[block // cap, block % cap : block % cap + 1, :] = current
    for copy in range(1, copies):
        current_ref[copy * dies : (copy + 1) * dies] = current_ref[0:dies]


def local(
    die_volt,
    die_load,
    die_shunt,
    bump_node,
    bump_block,
    bump_cond,
    pkg_volt,
    pkg_diag,
    pkg_pattern,
    pkg_weight,
    block_coupling,
):
    die_count = lax.axis_size("die")
    group_count = lax.axis_size("grp")
    devices = die_count * group_count
    blocks = pkg_volt.shape[0]
    tiles = blocks // LANES
    neighbours = pkg_pattern.shape[0]
    slots = bump_block.shape[0]
    cap = slots // die_count
    rows, cols = die_volt.shape
    (spread,) = call(
        functools.partial(spread_body, cap, die_count, blocks),
        "spread_blocks",
        [shape(devices, 1, LANES, dtype=jnp.int32)],
        (bump_block.reshape(1, slots),),
        [VMEM],
    )
    ids = lax.all_to_all(
        spread, ("grp", "die"), split_axis=0, concat_axis=0, tiled=True
    ).reshape(devices, LANES)

    beside_end = [
        (g * die_count + a, g * die_count + b)
        for g in range(group_count)
        for d in range((g + 1) % 2, die_count - 1, 2)
        for a, b in ((d, d + 1), (d + 1, d))
    ]
    (pack,) = call(
        pack_body,
        "package_pack",
        [shape(2 * LANES + 2 * neighbours, LANES)],
        (pkg_pattern, pkg_weight, pkg_volt, pkg_diag),
        [VMEM, VMEM, HBM, HBM],
        [pltpu.SemaphoreType.DMA((2,))],
        vmem=MOST_VMEM,
    )
    halo = lax.ppermute(pack, ("grp", "die"), beside_end)

    (picked,) = call(
        functools.partial(pick_body, cap, die_count),
        "pick_rows",
        [shape(slots, LANES)],
        (ids, pkg_volt, pack),
        [SMEM, HBM, HBM],
        [pltpu.SemaphoreType.DMA(())],
        vmem=MOST_VMEM,
    )
    bump_start = lax.all_to_all(
        picked.reshape(die_count, cap, LANES), "die", split_axis=0, concat_axis=0, tiled=True
    ).reshape(slots, LANES)

    right_side, inv, *edges = call(
        functools.partial(scatter_body, cols),
        "scatter_bumps",
        [shape(rows, cols)] * 2 + [shape(3 * HALO_ROWS, cols)] * 2,
        (bump_node, bump_cond, bump_start, die_volt, die_load, die_shunt, halo),
        [VMEM] * 6 + [ANY],
        work=3,
    )
    beside = swap(*edges, "grp")

    edge_rows = -(-3 * SWEEPS // 8) * 8
    edge_cols = -(-(rows + 2 * HALO_ROWS) // LANES) * LANES
    edges = call(
        edge_body,
        "edge_columns",
        [shape(edge_rows, edge_cols)] * 2,
        (die_volt, right_side, inv, *beside),
        [VMEM] * 5,
    )
    columns = swap(*edges, "die")

    die_out, current = call(
        functools.partial(sweep_body, group_count),
        "sweeps",
        [shape(rows, cols), shape(devices, cap, LANES)],
        (bump_node, bump_cond, bump_start, die_volt, right_side, inv, *beside, *columns),
        [VMEM] * 10,
        work=4,
    )
    own = tiles // 2
    dma = pltpu.SemaphoreType.DMA
    plane = pltpu.VMEM(((own + 2) * LANES + 2 * RADIUS, 2 * LANES), BF16)
    range_rows = pltpu.VMEM(((own + 2) * LANES, LANES), F32)
    range_bands = pltpu.VMEM((own + 2, 2 * LANES, 2 * LANES), BF16)
    band, base, pkg_inv = call(
        prepare_body,
        "package_prepare",
        [
            shape(own + 2, 2 * LANES, 2 * LANES, dtype=BF16),
            shape((own + 2) * LANES, LANES),
            shape((own + 2) * LANES, LANES),
        ],
        (pkg_pattern, pkg_weight, block_coupling, halo, pkg_volt, pkg_diag, die_out),
        [VMEM] * 4 + [HBM] * 3,
        [range_rows, range_rows, range_bands, range_rows, range_rows, plane, dma((5,))],
        work=7,
        vmem=MOST_VMEM,
        out_specs=[HBM] * 3,
    )

    current = lax.all_to_all(
        current, ("grp", "die"), split_axis=0, concat_axis=0, tiled=True
    ).reshape(devices * cap, LANES)

    (inflow,) = call(
        functools.partial(ends_body, cap, tiles),
        "package_end",
        [shape(LANES, LANES)],
        (ids, current),
        [VMEM, VMEM],
    )
    halo_inflow = lax.ppermute(inflow, ("grp", "die"), beside_end)
    (all_inflow,) = call(
        functools.partial(inflow_body, cap, tiles),
        "package_inflow",
        [shape((own + 2) * LANES, LANES)],
        (ids, current, inflow),
        [VMEM, VMEM, ANY],
        [range_rows, dma(())],
        work=2,
        out_specs=[HBM],
    )
    half_out, pkg_out, picked = call(
        functools.partial(iterate_body, cap, die_count),
        "package_iterations",
        [shape(own * LANES, LANES), shape(blocks, LANES), shape(2 * slots, LANES)],
        (ids, block_coupling, halo_inflow, all_inflow, band, base, pkg_inv),
        [SMEM] + [VMEM] * 2 + [HBM] * 4,
        [
            range_bands, range_rows, range_rows, pltpu.VMEM((own * LANES, LANES), F32),
            range_rows, plane, plane, dma((6,)),
        ],
        work=10,
        vmem=MOST_VMEM,
        out_specs=[HBM, HBM, VMEM],
    )
    pair = 2 * die_count
    parts = lax.all_to_all(
        picked.reshape(pair, cap, LANES),
        ("grp", "die"),
        split_axis=0,
        concat_axis=0,
        axis_index_groups=[
            [first + i for i in range(pair)] for first in range(0, devices, pair)
        ],
        tiled=True,
    ).reshape(2 * slots, LANES)
    other = lax.ppermute(half_out, "grp", [(g, g ^ 1) for g in range(group_count)])
    pkg_out, done = call(
        join_body,
        "join_halves",
        [shape(blocks, LANES), shape(8, LANES)],
        (other, pkg_out),
        [VMEM, HBM],
        [dma(())],
        out_specs=[HBM, VMEM],
        aliases={1: 0},
    )
    (bump_out,) = call(
        add_body, "add_parts", [shape(slots, LANES)], (parts, done), [VMEM, ANY]
    )
    return (die_out, pkg_out, bump_out)


def solution(mesh):
    return jax.shard_map(
        local,
        mesh=mesh,
        in_specs=(
            P("grp", "die"),
            P("grp", "die"),
            P("grp", "die"),
            P(("grp", "die"), None),
            P(("grp", "die")),
            P(("grp", "die"), None),
            P("die", None),
            P("die", None),
            P(None, "die"),
            P(None, "die"),
            P(),
        ),
        out_specs=(P("grp", "die"), P("die", None), P(("grp", "die"), None)),
        check_vma=False,
    )
```

```python
import functools
import math

import jax
import jax.numpy as jnp
from jax import lax
from jax.experimental import pallas as pl
from jax.experimental.pallas import tpu as pltpu
from jax.sharding import PartitionSpec as P

RADIUS = 32
SWEEPS = 4
ITERS = 4
LANES = 128
HALO_ROWS = 8
REACH = RADIUS * ITERS
WINDOW = LANES + 2 * RADIUS
F32 = jnp.float32
BF16 = jnp.bfloat16
MOST_VMEM = 57
VMEM = pl.BlockSpec(memory_space=pltpu.VMEM)
SMEM = pl.BlockSpec(memory_space=pltpu.SMEM)
ANY = pl.BlockSpec(memory_space=pl.ANY)
HBM = pl.BlockSpec(memory_space=pltpu.HBM)


def sweep_weights(sweeps):
    return [
        1.0 / (1.0 + 0.8 * math.cos(math.pi * (2 * index + 1) / (2 * sweeps)))
        for index in range(sweeps)
    ]


def call(
    body, name, outs, args, specs, scratch=(), work=1, vmem=16, out_specs=None, aliases=None
):
    bytes_accessed = sum(4 * math.prod(arg.shape) for arg in args)
    return pl.pallas_call(
        body,
        name=name,
        out_shape=outs,
        in_specs=specs,
        out_specs=out_specs or [VMEM] * len(outs),
        input_output_aliases=aliases or {},
        scratch_shapes=list(scratch),
        compiler_params=pltpu.CompilerParams(vmem_limit_bytes=vmem * 1024 * 1024),
        cost_estimate=pl.CostEstimate(
            flops=work * 10**9, bytes_accessed=bytes_accessed, transcendentals=0
        ),
    )(*args)


def place():
    return lax.axis_index("grp"), lax.axis_index("die")


def shape(*dims, dtype=F32):
    return jax.ShapeDtypeStruct(dims, dtype)


def halves(values):
    high = values.astype(BF16)
    low = (values - high.astype(F32)).astype(BF16)
    return high, low


def spread_body(cap, die_count, blocks, block_ref, out_ref):
    slots = block_ref.shape[1]
    block = jnp.concatenate(
        [block_ref[...], jnp.zeros((1, LANES - slots), jnp.int32)], axis=1
    )
    for die in range(die_count):
        row = (pltpu.roll(block, LANES - die * cap, 1) if die else block) - die * blocks
        for at in range(die, out_ref.shape[0], die_count):
            out_ref[at] = row


def asked_rows(cap, die_count, group, ids_ref):
    for die in range(die_count):
        for slot in range(cap):
            yield die * cap + slot, ids_ref[group * die_count + die, slot]


def pick_body(cap, die_count, ids_ref, plane_ref, out_ref):
    group, _ = place()
    for at, row in asked_rows(cap, die_count, group, ids_ref):
        out_ref[pl.ds(at, 1), :] = plane_ref[pl.ds(row, 1), :]


def build_band(first, pattern, weights):
    place = lax.broadcasted_iota(jnp.int32, (WINDOW, LANES), 0)
    band = None
    for k in range(pattern.shape[0]):
        hit = place == (pattern[k : k + 1, :] - first)
        term = jnp.where(hit, weights[k : k + 1, :], 0.0)
        band = term if band is None else band + term
    fill = jnp.zeros((2 * LANES - WINDOW, LANES), F32)
    return jnp.concatenate(halves(jnp.concatenate([band, fill], axis=0).T), axis=0)


def reciprocal(diag):
    safe = jnp.where(diag > 0.0, diag, 1.0)
    return jnp.where(diag > 0.0, 1.0 / safe, 0.0)


def span(tile, offset=0, size=LANES):
    return pl.ds(pl.multiple_of(tile * LANES + offset, RADIUS), size)


def mixer(coup_ref):
    mix = jnp.concatenate(halves(coup_ref[...]), axis=1)
    return jnp.concatenate([mix, mix], axis=0)


def clear_pads(ref):
    pad = jnp.zeros((RADIUS, 2 * LANES), BF16)
    ref[0:RADIUS, :] = pad
    ref[ref.shape[0] - RADIUS :, :] = pad


def store(ref, tile, values):
    ref[span(tile, RADIUS, values.shape[0]), :] = jnp.concatenate(halves(values), axis=1)


def couple(source, tile, bands, mix, write):
    own = source[span(tile, RADIUS, len(bands) * LANES), :]
    within = jnp.dot(own, mix, preferred_element_type=F32)
    for i, band in enumerate(bands):
        window = source[span(tile + i, 0, WINDOW), :]
        beside = jnp.dot(band[:, :WINDOW], window, preferred_element_type=F32)
        both = beside[:LANES] + beside[LANES:] + within[i * LANES : (i + 1) * LANES]
        write(tile + i, both[:, :LANES] + both[:, LANES:])


def in_chunks(first, count, body, size=4):
    whole = count // size

    @pl.loop(0, whole)
    def _(chunk):
        body(first + chunk * size, size)

    if count % size:
        body(first + whole * size, count % size)


def half_of(tiles):
    half = lax.rem(sum(place()), 2)
    own = tiles // 2
    return half, own, half * own - 1


def pack_body(pat_ref, wgt_ref, volt_hbm, diag_hbm, after_ref, pack_ref, sems):
    tiles = volt_hbm.shape[0] // LANES
    half, _, _ = half_of(tiles)
    mine = pl.ds(pl.multiple_of(half * (tiles - 1) * LANES, LANES), LANES)
    loads = [
        pltpu.make_async_copy(hbm.at[mine, :], pack_ref.at[i * LANES : (i + 1) * LANES, :], sems.at[i])
        for i, hbm in enumerate((volt_hbm, diag_hbm))
    ]
    for load in loads:
        load.start()
    count = pat_ref.shape[0]
    at = 2 * LANES
    pack_ref[at : at + count, :] = pat_ref[:, mine].astype(F32)
    pack_ref[at + count : at + 2 * count, :] = wgt_ref[:, mine]
    for load in loads:
        load.wait()


def prepare_body(
    pat_ref, wgt_ref, coup_ref, halo_ref, volt_hbm, diag_hbm, after_ref,
    band_hbm, base_hbm, inv_hbm,
    volt_ref, diag_ref, band_ref, base_ref, inv_ref, plane_ref, sems,
):
    blocks = volt_hbm.shape[0]
    neighbours = pat_ref.shape[0]
    half, own, shift = half_of(blocks // LANES)
    first, count, outer = 1 - half, own + 1, half * (own + 1)
    source = pl.ds(pl.multiple_of((first + shift) * LANES, LANES), count * LANES)
    target = pl.ds(pl.multiple_of(first * LANES, LANES), count * LANES)
    loads = [
        pltpu.make_async_copy(hbm.at[source, :], ref.at[target, :], sems.at[i])
        for i, (hbm, ref) in enumerate(((volt_hbm, volt_ref), (diag_hbm, diag_ref)))
    ]
    for load in loads:
        load.start()
    volt_ref[span(outer), :] = halo_ref[0:LANES, :]
    diag_ref[span(outer), :] = halo_ref[LANES : 2 * LANES, :]
    clear_pads(plane_ref)
    begin = place()[1] * blocks + shift * LANES
    at = 2 * LANES
    band_ref[outer] = build_band(
        begin + outer * LANES - RADIUS,
        halo_ref[at : at + neighbours, :].astype(jnp.int32),
        halo_ref[at + neighbours : at + 2 * neighbours, :],
    )

    def bands(tile, size):
        for i in range(size):
            lanes = pl.ds(pl.multiple_of((tile + i + shift) * LANES, LANES), LANES)
            band_ref[tile + i] = build_band(
                begin + (tile + i) * LANES - RADIUS, pat_ref[:, lanes], wgt_ref[:, lanes]
            )

    in_chunks(first, count, bands)
    band_out = pltpu.make_async_copy(band_ref, band_hbm, sems.at[2])
    band_out.start()
    for load in loads:
        load.wait()

    def spread(tile, size):
        cut = span(tile, 0, size * LANES)
        store(plane_ref, tile, volt_ref[cut, :])
        inv_ref[cut, :] = reciprocal(diag_ref[cut, :])

    in_chunks(0, own + 2, spread)
    inv_out = pltpu.make_async_copy(inv_ref, inv_hbm, sems.at[3])
    inv_out.start()
    mix = mixer(coup_ref)

    def base(tile, size):
        def write(tile, values):
            base_ref[span(tile), :] = values

        couple(plane_ref, tile, [band_ref[tile + i] for i in range(size)], mix, write)
        cut = span(tile, 0, size * LANES)
        pltpu.make_async_copy(base_ref.at[cut, :], base_hbm.at[cut, :], sems.at[4]).start()

    in_chunks(0, own + 2, base)
    band_out.wait()
    inv_out.wait()
    pltpu.make_async_copy(base_ref, base_hbm, sems.at[4]).wait()


def slot_places(cap, ids_ref):
    per_row = LANES // cap
    lane = lax.broadcasted_iota(jnp.int32, (1, LANES), 1)
    places = []
    for at in range(0, ids_ref.shape[0], per_row):
        total = None
        for i in range(per_row):
            row = jnp.where(lane < cap, ids_ref[at + i : at + i + 1, :], 0)
            row = pltpu.roll(row, i * cap, 1) if i else row
            total = row if total is None else total + row
        places.append(total)
    return places


def gather_inflow(places, first, rows, current):
    at = lax.broadcasted_iota(jnp.int32, (rows, LANES), 0) + first
    hits = [jnp.where(at == place, 1.0, 0.0).astype(BF16) for place in places]
    both = jnp.dot(jnp.concatenate(hits, axis=1), current, preferred_element_type=F32)
    return both[:, :LANES] + both[:, LANES:]


def ends_body(cap, tiles, ids_ref, current_ref, out_ref):
    half, _, _ = half_of(tiles)
    places = slot_places(cap, ids_ref)
    current = jnp.concatenate(halves(current_ref[...]), axis=1)
    out_ref[...] = gather_inflow(places, half * (tiles - 1) * LANES, LANES, current)


def inflow_body(cap, tiles, ids_ref, current_ref, after_ref, out_ref):
    half, own, shift = half_of(tiles)
    first, count = 1 - half, own + 1
    places = slot_places(cap, ids_ref)
    current = jnp.concatenate(halves(current_ref[...]), axis=1)

    def inflow(tile, size):
        cut = span(tile, 0, size * LANES)
        out_ref[cut, :] = gather_inflow(
            places, (tile + shift) * LANES, size * LANES, current
        )

    in_chunks(first, count, inflow)
    out_ref[span(half * (own + 1)), :] = jnp.zeros((LANES, LANES), F32)


def iterate_body(
    cap, die_count, asked_ref, coup_ref, halo_ref, inflow_ref, band_ref, base_ref, inv_ref,
    out_hbm, full_hbm, picked_ref, out_ref, here_ref, there_ref, sems,
):
    own = out_hbm.shape[0] // LANES
    half, _, _ = half_of(2 * own)
    outer = half * (own + 1)
    for ref in (here_ref, there_ref):
        clear_pads(ref)

    def inflow(tile):
        return jnp.where(tile == outer, halo_ref[...], inflow_ref[span(tile), :])

    def start(tile, size):
        for i in range(size):
            cut = span(tile + i)
            store(
                here_ref, tile + i, -(inflow(tile + i) + base_ref[cut, :]) * inv_ref[cut, :]
            )

    in_chunks(0, own + 2, start)
    mix = mixer(coup_ref)
    refs = (here_ref, there_ref)
    for iteration in range(1, ITERS):
        source, target = refs[(iteration - 1) % 2], refs[iteration % 2]
        last = iteration == ITERS - 1

        def write(tile, coupled, target=target, last=last):
            values = -(inflow(tile) + coupled) * inv_ref[span(tile), :]
            if last:
                out_ref[span(tile - 1), :] = values
            else:
                store(target, tile, values)

        def step(tile, size, source=source, write=write):
            bands = [band_ref[tile + i] for i in range(size)]
            couple(source, tile, bands, mix, write)

        def final(tile, size, step=step):
            step(tile, size)
            cut = span(tile - 1, 0, size * LANES)
            whole = span(half * own + tile - 1, 0, size * LANES)
            pltpu.make_async_copy(out_ref.at[cut, :], out_hbm.at[cut, :], sems.at[0]).start()
            pltpu.make_async_copy(out_ref.at[cut, :], full_hbm.at[whole, :], sems.at[1]).start()

        if last:
            in_chunks(1, own, final)
        else:
            in_chunks(0, own + 2, step)

    base_row = half * own * LANES
    group, _ = place()
    pair = group - lax.rem(group, 2)
    for member in range(2):
        offset = member * (picked_ref.shape[0] // 2)
        for at, row in asked_rows(cap, die_count, pair + member, asked_ref):
            row = row - base_row
            inside = (row >= 0) & (row < own * LANES)
            safe = jnp.clip(row, 0, own * LANES - 1)
            values = out_ref[pl.ds(safe, 1), :]
            picked_ref[pl.ds(offset + at, 1), :] = jnp.where(inside, values, 0.0)
    pltpu.make_async_copy(out_ref, out_hbm, sems.at[0]).wait()
    pltpu.make_async_copy(out_ref, full_hbm.at[0 : own * LANES, :], sems.at[1]).wait()


def join_body(other_ref, full_in_hbm, full_hbm, done_ref, sem):
    rows = other_ref.shape[0]
    half, _, _ = half_of(2 * rows // LANES)
    start = pl.multiple_of((1 - half) * rows, LANES)
    copy = pltpu.make_async_copy(other_ref, full_hbm.at[pl.ds(start, rows), :], sem)
    copy.start()
    done_ref[...] = jnp.zeros(done_ref.shape, F32)
    copy.wait()


def add_body(parts_ref, after_ref, out_ref):
    rows = out_ref.shape[0]
    out_ref[...] = parts_ref[0:rows, :] + parts_ref[rows:, :]


def scatter_body(cols, node_ref, cond_ref, start_ref, volt_ref, load_ref, shunt_ref,
                 after_ref, right_ref, inv_ref, inner_ref, outer_ref):
    blocks = node_ref.shape[0]
    rows = volt_ref.shape[0]
    group = 8
    row_at = lax.broadcasted_iota(jnp.int32, (rows, LANES), 0)
    col_at = lax.broadcasted_iota(jnp.int32, (cols, LANES), 0)
    total = jnp.zeros((4 * rows, cols), F32)
    for first in range(0, blocks, group):
        node = node_ref[first : first + group, :]
        live = node >= 0
        cond = jnp.where(live, cond_ref[first : first + group, :], 0.0)
        flow = cond * start_ref[first : first + group, :]
        safe = jnp.where(live, node, 0)
        row, col = safe // cols, safe % cols
        parts = halves(cond) + halves(flow)
        left, right = [], []
        for i in range(group):
            spot = jnp.where(row_at == row[i : i + 1, :], 1.0, 0.0).astype(BF16)
            left.append(
                jnp.concatenate([spot * part[i : i + 1, :] for part in parts], axis=0)
            )
            right.append(jnp.where(col_at == col[i : i + 1, :], 1.0, 0.0).astype(BF16))
        total = total + lax.dot_general(
            jnp.concatenate(left, axis=1),
            jnp.concatenate(right, axis=1),
            (((1,), (1,)), ((), ())),
            preferred_element_type=F32,
        )
    gsum = total[:rows] + total[rows : 2 * rows]
    inject = total[2 * rows : 3 * rows] + total[3 * rows :]
    inv = 1.0 / (4.0 + shunt_ref[...] + gsum)
    right_side = (inject - load_ref[...]) * inv
    right_ref[...] = right_side
    inv_ref[...] = inv
    volt = volt_ref[...]
    top, bottom = (
        jnp.concatenate([volt[cut], right_side[cut], inv[cut]], axis=0)
        for cut in (slice(0, HALO_ROWS), slice(rows - HALO_ROWS, rows))
    )
    swap_parts(inner_ref, outer_ref, place()[0], top, bottom)


def swap_parts(inner_ref, outer_ref, mine, first, last):
    even = lax.rem(mine, 2) == 0
    inner_ref[...] = jnp.where(even, last, first)
    outer_ref[...] = jnp.where(even, first, last)


def swapped(inner, outer, mine):
    even = lax.rem(mine, 2) == 0
    return jnp.where(even, outer, inner), jnp.where(even, inner, outer)


def swap(inner, outer, axis):
    count = lax.axis_size(axis)

    def pairs(start):
        return [
            pair
            for i in range(start, count - 1, 2)
            for pair in ((i, i + 1), (i + 1, i))
        ]

    return lax.ppermute(inner, axis, pairs(0)), lax.ppermute(outer, axis, pairs(1))


def extended(own, top, bottom, index):
    cut = slice(index * HALO_ROWS, (index + 1) * HALO_ROWS)
    return jnp.concatenate([top[cut], own, bottom[cut]], axis=0)


def edge_body(volt_ref, right_ref, inv_ref, inner_ref, outer_ref, west_ref, east_ref):
    cols = volt_ref.shape[1]
    top, bottom = swapped(inner_ref[...], outer_ref[...], place()[0])
    out_rows, high = west_ref.shape
    west, east = None, None
    for index, ref in enumerate((volt_ref, right_ref, inv_ref)):
        whole = extended(ref[...], top, bottom, index)
        lane = lax.broadcasted_iota(jnp.int32, (whole.shape[0], LANES), 1)
        head, tail = whole[:, :LANES], whole[:, cols - LANES :]
        at = index * SWEEPS
        head = pltpu.roll(head, at, 1) if at else head
        tail = pltpu.roll(tail, at + SWEEPS, 1)
        west = head if west is None else jnp.where(lane >= at, head, west)
        east = tail if east is None else jnp.where(lane >= at, tail, east)
    fill = jnp.zeros((high - west.shape[0], LANES), F32)
    west, east = (
        jnp.concatenate([part, fill], axis=0).T[:out_rows] for part in (west, east)
    )
    swap_parts(west_ref, east_ref, place()[1], west, east)


def sweep_body(copies, node_ref, cond_ref, start_ref, volt_ref, right_ref, inv_ref,
               row_in_ref, row_out_ref, col_in_ref, col_out_ref, out_ref, current_ref):
    rows, cols = volt_ref.shape
    blocks = node_ref.shape[0]
    cap = current_ref.shape[1]
    whole = []
    top, bottom = swapped(row_in_ref[...], row_out_ref[...], place()[0])
    out_rows, high = col_in_ref.shape
    fill = jnp.zeros((LANES - out_rows, high), F32)
    wests, easts = (
        jnp.concatenate([part, fill], axis=0).T[: rows + 2 * HALO_ROWS]
        for part in swapped(col_in_ref[...], col_out_ref[...], place()[1])
    )
    for index, ref in enumerate((volt_ref, right_ref, inv_ref)):
        own = extended(ref[...], top, bottom, index)
        at = index * SWEEPS
        west = pltpu.roll(wests, LANES - SWEEPS - at, 1)
        east = pltpu.roll(easts, LANES - at, 1) if at else easts
        whole.append(jnp.concatenate([west, own, east], axis=1))
    volt, right_side, inv = whole
    high, wide = volt.shape
    for weight in sweep_weights(SWEEPS):
        beside = (
            pltpu.roll(volt, 1, 0)
            + pltpu.roll(volt, high - 1, 0)
            + pltpu.roll(volt, 1, 1)
            + pltpu.roll(volt, wide - 1, 1)
        )
        volt = (1.0 - weight) * volt + weight * (right_side + beside * inv)
    volt = volt[HALO_ROWS : HALO_ROWS + rows, LANES : LANES + cols]
    out_ref[...] = volt
    both = jnp.concatenate(halves(volt), axis=0)
    group = 8
    row_at = lax.broadcasted_iota(jnp.int32, (rows, LANES), 0)
    col_at = lax.broadcasted_iota(jnp.int32, (cols, LANES), 0)
    dies = blocks // cap
    for first in range(0, blocks, group):
        node = node_ref[first : first + group, :]
        live = node >= 0
        cond = jnp.where(live, cond_ref[first : first + group, :], 0.0)
        safe = jnp.where(live, node, 0)
        row, col = safe // cols, safe % cols
        spots = jnp.concatenate(
            [
                jnp.where(col_at == col[i : i + 1, :], 1.0, 0.0).astype(BF16)
                for i in range(group)
            ],
            axis=1,
        )
        found = jnp.dot(both, spots, preferred_element_type=F32)
        found = found[:rows] + found[rows:]
        for i in range(group):
            mine = found[:, i * LANES : (i + 1) * LANES]
            at_bump = jnp.sum(
                jnp.where(row_at == row[i : i + 1, :], mine, 0.0), axis=0, keepdims=True
            )
            block = first + i
            current = cond[i : i + 1, :] * (start_ref[block : block + 1, :] - at_bump)
            current_ref[block // cap, block % cap : block % cap + 1, :] = current
    for copy in range(1, copies):
        current_ref[copy * dies : (copy + 1) * dies] = current_ref[0:dies]


def local(
    die_volt,
    die_load,
    die_shunt,
    bump_node,
    bump_block,
    bump_cond,
    pkg_volt,
    pkg_diag,
    pkg_pattern,
    pkg_weight,
    block_coupling,
):
    die_count = lax.axis_size("die")
    group_count = lax.axis_size("grp")
    devices = die_count * group_count
    blocks = pkg_volt.shape[0]
    tiles = blocks // LANES
    neighbours = pkg_pattern.shape[0]
    slots = bump_block.shape[0]
    cap = slots // die_count
    rows, cols = die_volt.shape
    (spread,) = call(
        functools.partial(spread_body, cap, die_count, blocks),
        "spread_blocks",
        [shape(devices, 1, LANES, dtype=jnp.int32)],
        (bump_block.reshape(1, slots),),
        [VMEM],
    )
    ids = lax.all_to_all(
        spread, ("grp", "die"), split_axis=0, concat_axis=0, tiled=True
    ).reshape(devices, LANES)

    (picked,) = call(
        functools.partial(pick_body, cap, die_count),
        "pick_rows",
        [shape(slots, LANES)],
        (ids, pkg_volt),
        [SMEM, VMEM],
    )
    beside_end = [
        (g * die_count + a, g * die_count + b)
        for g in range(group_count)
        for d in range((g + 1) % 2, die_count - 1, 2)
        for a, b in ((d, d + 1), (d + 1, d))
    ]
    (pack,) = call(
        pack_body,
        "package_pack",
        [shape(2 * LANES + 2 * neighbours, LANES)],
        (pkg_pattern, pkg_weight, pkg_volt, pkg_diag, picked),
        [VMEM, VMEM, HBM, HBM, HBM],
        [pltpu.SemaphoreType.DMA((2,))],
        vmem=MOST_VMEM,
    )
    halo = lax.ppermute(pack, ("grp", "die"), beside_end)

    bump_start = lax.all_to_all(
        picked.reshape(die_count, cap, LANES), "die", split_axis=0, concat_axis=0, tiled=True
    ).reshape(slots, LANES)

    right_side, inv, *edges = call(
        functools.partial(scatter_body, cols),
        "scatter_bumps",
        [shape(rows, cols)] * 2 + [shape(3 * HALO_ROWS, cols)] * 2,
        (bump_node, bump_cond, bump_start, die_volt, die_load, die_shunt, halo),
        [VMEM] * 6 + [ANY],
        work=3,
    )
    beside = swap(*edges, "grp")

    edge_rows = -(-3 * SWEEPS // 8) * 8
    edge_cols = -(-(rows + 2 * HALO_ROWS) // LANES) * LANES
    edges = call(
        edge_body,
        "edge_columns",
        [shape(edge_rows, edge_cols)] * 2,
        (die_volt, right_side, inv, *beside),
        [VMEM] * 5,
    )
    columns = swap(*edges, "die")

    die_out, current = call(
        functools.partial(sweep_body, group_count),
        "sweeps",
        [shape(rows, cols), shape(devices, cap, LANES)],
        (bump_node, bump_cond, bump_start, die_volt, right_side, inv, *beside, *columns),
        [VMEM] * 10,
        work=4,
    )
    own = tiles // 2
    dma = pltpu.SemaphoreType.DMA
    plane = pltpu.VMEM(((own + 2) * LANES + 2 * RADIUS, 2 * LANES), BF16)
    range_rows = pltpu.VMEM(((own + 2) * LANES, LANES), F32)
    range_bands = pltpu.VMEM((own + 2, 2 * LANES, 2 * LANES), BF16)
    band, base, pkg_inv = call(
        prepare_body,
        "package_prepare",
        [
            shape(own + 2, 2 * LANES, 2 * LANES, dtype=BF16),
            shape((own + 2) * LANES, LANES),
            shape((own + 2) * LANES, LANES),
        ],
        (pkg_pattern, pkg_weight, block_coupling, halo, pkg_volt, pkg_diag, die_out),
        [VMEM] * 4 + [HBM] * 3,
        [range_rows, range_rows, range_bands, range_rows, range_rows, plane, dma((5,))],
        work=7,
        vmem=MOST_VMEM,
        out_specs=[HBM] * 3,
    )

    current = lax.all_to_all(
        current, ("grp", "die"), split_axis=0, concat_axis=0, tiled=True
    ).reshape(devices * cap, LANES)

    (inflow,) = call(
        functools.partial(ends_body, cap, tiles),
        "package_end",
        [shape(LANES, LANES)],
        (ids, current),
        [VMEM, VMEM],
    )
    halo_inflow = lax.ppermute(inflow, ("grp", "die"), beside_end)
    (all_inflow,) = call(
        functools.partial(inflow_body, cap, tiles),
        "package_inflow",
        [shape((own + 2) * LANES, LANES)],
        (ids, current, inflow),
        [VMEM, VMEM, ANY],
        work=2,
    )
    half_out, pkg_out, picked = call(
        functools.partial(iterate_body, cap, die_count),
        "package_iterations",
        [shape(own * LANES, LANES), shape(blocks, LANES), shape(2 * slots, LANES)],
        (ids, block_coupling, halo_inflow, all_inflow, band, base, pkg_inv),
        [SMEM] + [VMEM] * 6,
        [pltpu.VMEM((own * LANES, LANES), F32), plane, plane, dma((2,))],
        work=10,
        vmem=24,
        out_specs=[HBM, HBM, VMEM],
    )
    pair = 2 * die_count
    parts = lax.all_to_all(
        picked.reshape(pair, cap, LANES),
        ("grp", "die"),
        split_axis=0,
        concat_axis=0,
        axis_index_groups=[
            [first + i for i in range(pair)] for first in range(0, devices, pair)
        ],
        tiled=True,
    ).reshape(2 * slots, LANES)
    other = lax.ppermute(half_out, "grp", [(g, g ^ 1) for g in range(group_count)])
    pkg_out, done = call(
        join_body,
        "join_halves",
        [shape(blocks, LANES), shape(8, LANES)],
        (other, pkg_out),
        [VMEM, HBM],
        [dma(())],
        out_specs=[HBM, VMEM],
        aliases={1: 0},
    )
    (bump_out,) = call(
        add_body, "add_parts", [shape(slots, LANES)], (parts, done), [VMEM, ANY]
    )
    return (die_out, pkg_out, bump_out)


def solution(mesh):
    return jax.shard_map(
        local,
        mesh=mesh,
        in_specs=(
            P("grp", "die"),
            P("grp", "die"),
            P("grp", "die"),
            P(("grp", "die"), None),
            P(("grp", "die")),
            P(("grp", "die"), None),
            P("die", None),
            P("die", None),
            P(None, "die"),
            P(None, "die"),
            P(),
        ),
        out_specs=(P("grp", "die"), P("die", None), P(("grp", "die"), None)),
        check_vma=False,
    )
```

```python
import functools
import math

import jax
import jax.numpy as jnp
from jax import lax
from jax.experimental import pallas as pl
from jax.experimental.pallas import tpu as pltpu
from jax.sharding import PartitionSpec as P

RADIUS = 32
SWEEPS = 4
ITERS = 4
LANES = 128
HALO_ROWS = 8
REACH = RADIUS * ITERS
WINDOW = LANES + 2 * RADIUS
F32 = jnp.float32
BF16 = jnp.bfloat16
MOST_VMEM = 57
VMEM = pl.BlockSpec(memory_space=pltpu.VMEM)
SMEM = pl.BlockSpec(memory_space=pltpu.SMEM)
ANY = pl.BlockSpec(memory_space=pl.ANY)
HBM = pl.BlockSpec(memory_space=pltpu.HBM)


def sweep_weights(sweeps):
    return [
        1.0 / (1.0 + 0.8 * math.cos(math.pi * (2 * index + 1) / (2 * sweeps)))
        for index in range(sweeps)
    ]


def call(
    body, name, outs, args, specs, scratch=(), work=1, vmem=16, out_specs=None, aliases=None
):
    bytes_accessed = sum(4 * math.prod(arg.shape) for arg in args)
    return pl.pallas_call(
        body,
        name=name,
        out_shape=outs,
        in_specs=specs,
        out_specs=out_specs or [VMEM] * len(outs),
        input_output_aliases=aliases or {},
        scratch_shapes=list(scratch),
        compiler_params=pltpu.CompilerParams(vmem_limit_bytes=vmem * 1024 * 1024),
        cost_estimate=pl.CostEstimate(
            flops=work * 10**9, bytes_accessed=bytes_accessed, transcendentals=0
        ),
    )(*args)


def place():
    return lax.axis_index("grp"), lax.axis_index("die")


def shape(*dims, dtype=F32):
    return jax.ShapeDtypeStruct(dims, dtype)


def halves(values):
    high = values.astype(BF16)
    low = (values - high.astype(F32)).astype(BF16)
    return high, low


def spread_body(cap, die_count, blocks, block_ref, out_ref):
    slots = block_ref.shape[1]
    block = jnp.concatenate(
        [block_ref[...], jnp.zeros((1, LANES - slots), jnp.int32)], axis=1
    )
    for die in range(die_count):
        row = (pltpu.roll(block, LANES - die * cap, 1) if die else block) - die * blocks
        for at in range(die, out_ref.shape[0], die_count):
            out_ref[at] = row


def asked_rows(cap, die_count, group, ids_ref):
    for die in range(die_count):
        for slot in range(cap):
            yield die * cap + slot, ids_ref[group * die_count + die, slot]


def pick_body(cap, die_count, ids_ref, plane_ref, out_ref):
    group, _ = place()
    for at, row in asked_rows(cap, die_count, group, ids_ref):
        out_ref[pl.ds(at, 1), :] = plane_ref[pl.ds(row, 1), :]


def build_band(first, pattern, weights):
    place = lax.broadcasted_iota(jnp.int32, (WINDOW, LANES), 0)
    band = None
    for k in range(pattern.shape[0]):
        hit = place == (pattern[k : k + 1, :] - first)
        term = jnp.where(hit, weights[k : k + 1, :], 0.0)
        band = term if band is None else band + term
    fill = jnp.zeros((2 * LANES - WINDOW, LANES), F32)
    return jnp.concatenate(halves(jnp.concatenate([band, fill], axis=0).T), axis=0)


def reciprocal(diag):
    safe = jnp.where(diag > 0.0, diag, 1.0)
    return jnp.where(diag > 0.0, 1.0 / safe, 0.0)


def span(tile, offset=0, size=LANES):
    return pl.ds(pl.multiple_of(tile * LANES + offset, RADIUS), size)


def mixer(coup_ref):
    mix = jnp.concatenate(halves(coup_ref[...]), axis=1)
    return jnp.concatenate([mix, mix], axis=0)


def clear_pads(ref):
    pad = jnp.zeros((RADIUS, 2 * LANES), BF16)
    ref[0:RADIUS, :] = pad
    ref[ref.shape[0] - RADIUS :, :] = pad


def store(ref, tile, values):
    ref[span(tile, RADIUS, values.shape[0]), :] = jnp.concatenate(halves(values), axis=1)


def couple(source, tile, bands, mix, write):
    own = source[span(tile, RADIUS, len(bands) * LANES), :]
    within = jnp.dot(own, mix, preferred_element_type=F32)
    for i, band in enumerate(bands):
        window = source[span(tile + i, 0, WINDOW), :]
        beside = jnp.dot(band[:, :WINDOW], window, preferred_element_type=F32)
        both = beside[:LANES] + beside[LANES:] + within[i * LANES : (i + 1) * LANES]
        write(tile + i, both[:, :LANES] + both[:, LANES:])


def in_chunks(first, count, body, size=4):
    whole = count // size

    @pl.loop(0, whole)
    def _(chunk):
        body(first + chunk * size, size)

    if count % size:
        body(first + whole * size, count % size)


def half_of(tiles):
    half = lax.rem(sum(place()), 2)
    own = tiles // 2
    return half, own, half * own - 1


def prepare_body(
    pat_ref, wgt_ref, coup_ref, volt_hbm, diag_hbm, after_ref,
    band_hbm, base_hbm, inv_hbm, pack_ref, near_ref,
    volt_ref, diag_ref, band_ref, base_ref, inv_ref, plane_ref, sems,
):
    blocks = volt_hbm.shape[0]
    half, own, shift = half_of(blocks // LANES)
    first, count, outer = 1 - half, own + 1, half * (own + 1)
    known = pl.ds(pl.multiple_of(first * LANES, LANES), count * LANES)
    source = pl.ds(pl.multiple_of((first + shift) * LANES, LANES), count * LANES)
    loads = [
        pltpu.make_async_copy(hbm.at[source, :], ref.at[known, :], sems.at[i])
        for i, (hbm, ref) in enumerate(((volt_hbm, volt_ref), (diag_hbm, diag_ref)))
    ]
    for load in loads:
        load.start()
    clear_pads(plane_ref)
    plane_ref[span(outer, RADIUS), :] = jnp.zeros((LANES, 2 * LANES), BF16)
    begin = place()[1] * blocks + shift * LANES

    def bands(tile, size):
        for i in range(size):
            lanes = pl.ds(pl.multiple_of((tile + i + shift) * LANES, LANES), LANES)
            band_ref[tile + i] = build_band(
                begin + (tile + i) * LANES - RADIUS, pat_ref[:, lanes], wgt_ref[:, lanes]
            )

    in_chunks(first, count, bands)
    band_out = pltpu.make_async_copy(
        band_ref.at[pl.ds(first, count)], band_hbm.at[pl.ds(first, count)], sems.at[2]
    )
    band_out.start()
    for load in loads:
        load.wait()

    def spread(tile, size):
        cut = span(tile, 0, size * LANES)
        store(plane_ref, tile, volt_ref[cut, :])
        inv_ref[cut, :] = reciprocal(diag_ref[cut, :])

    in_chunks(first, count, spread)
    inv_out = pltpu.make_async_copy(inv_ref.at[known, :], inv_hbm.at[known, :], sems.at[3])
    inv_out.start()
    mix = mixer(coup_ref)

    def base(tile, size):
        def write(tile, values):
            base_ref[span(tile), :] = values

        couple(plane_ref, tile, [band_ref[tile + i] for i in range(size)], mix, write)
        cut = span(tile, 0, size * LANES)
        pltpu.make_async_copy(base_ref.at[cut, :], base_hbm.at[cut, :], sems.at[4]).start()

    in_chunks(first, count, base)
    edge = 1 + half * (own - 1)
    lanes = pl.ds(pl.multiple_of((edge + shift) * LANES, LANES), LANES)
    neighbours = pat_ref.shape[0]
    pack_ref[0:LANES, :] = volt_ref[span(edge), :]
    pack_ref[LANES : 2 * LANES, :] = diag_ref[span(edge), :]
    at = 2 * LANES
    pack_ref[at : at + neighbours, :] = pat_ref[:, lanes].astype(F32)
    pack_ref[at + neighbours : at + 2 * neighbours, :] = wgt_ref[:, lanes]
    near_ref[0:RADIUS, :] = volt_ref[2 * LANES : 2 * LANES + RADIUS, :]
    near_ref[RADIUS:, :] = volt_ref[own * LANES - RADIUS : own * LANES, :]
    band_out.wait()
    inv_out.wait()
    pltpu.make_async_copy(
        base_ref.at[known, :], base_hbm.at[known, :], sems.at[4]
    ).wait()


def slot_places(cap, ids_ref):
    per_row = LANES // cap
    lane = lax.broadcasted_iota(jnp.int32, (1, LANES), 1)
    places = []
    for at in range(0, ids_ref.shape[0], per_row):
        total = None
        for i in range(per_row):
            row = jnp.where(lane < cap, ids_ref[at + i : at + i + 1, :], 0)
            row = pltpu.roll(row, i * cap, 1) if i else row
            total = row if total is None else total + row
        places.append(total)
    return places


def gather_inflow(places, first, rows, current):
    at = lax.broadcasted_iota(jnp.int32, (rows, LANES), 0) + first
    hits = [jnp.where(at == place, 1.0, 0.0).astype(BF16) for place in places]
    both = jnp.dot(jnp.concatenate(hits, axis=1), current, preferred_element_type=F32)
    return both[:, :LANES] + both[:, LANES:]


def ends_body(cap, tiles, ids_ref, current_ref, out_ref):
    half, _, _ = half_of(tiles)
    places = slot_places(cap, ids_ref)
    current = jnp.concatenate(halves(current_ref[...]), axis=1)
    out_ref[...] = gather_inflow(places, half * (tiles - 1) * LANES, LANES, current)


def inflow_body(
    cap, tiles, ids_ref, current_ref, coup_ref, own_ref, halo_ref, near_ref, after_ref,
    out_ref, band_ref, inv_ref, base_ref, plane_ref,
):
    half, own, shift = half_of(tiles)
    first, count = 1 - half, own + 1
    places = slot_places(cap, ids_ref)
    current = jnp.concatenate(halves(current_ref[...]), axis=1)

    def inflow(tile, size):
        cut = span(tile, 0, size * LANES)
        out_ref[cut, :] = gather_inflow(
            places, (tile + shift) * LANES, size * LANES, current
        )

    in_chunks(first, count, inflow)
    out_ref[span(half * (own + 1)), :] = jnp.zeros((LANES, LANES), F32)

    neighbours = (own_ref.shape[0] - 2 * LANES) // 2
    begin = (place()[1] * tiles + 2 * half * own - 1) * LANES
    packs = [jnp.where(half == at, halo_ref[...], own_ref[...]) for at in range(2)]
    at = 2 * LANES
    bands = []
    for tile, pack in enumerate(packs):
        bands.append(
            build_band(
                begin + tile * LANES - RADIUS,
                pack[at : at + neighbours].astype(jnp.int32),
                pack[at + neighbours : at + 2 * neighbours],
            )
        )
        store(plane_ref, tile, pack[:LANES])
    none = jnp.zeros((RADIUS, 2 * LANES), BF16)
    low, high = (
        jnp.concatenate(halves(near_ref[cut, :]), axis=1)
        for cut in (slice(0, RADIUS), slice(RADIUS, 2 * RADIUS))
    )
    size = plane_ref.shape[0]
    plane_ref[0:RADIUS, :] = jnp.where(half == 0, none, high)
    plane_ref[size - RADIUS : size, :] = jnp.where(half == 0, low, none)
    results = []
    couple(plane_ref, 0, bands, mixer(coup_ref), lambda tile, values: results.append(values))
    band_ref[...] = jnp.where(half == 0, bands[0], bands[1])
    inv_ref[...] = reciprocal(halo_ref[LANES : 2 * LANES, :])
    base_ref[0:LANES, :] = jnp.where(half == 0, results[0], results[1])
    base_ref[LANES:, :] = jnp.where(half == 0, results[1], results[0])


def iterate_body(
    cap, die_count, asked_ref, coup_ref, halo_ref, inflow_ref, band_ref, base_ref, inv_ref,
    halo_band_ref, halo_inv_ref, edge_base_ref, out_hbm, full_hbm, picked_ref, out_ref, here_ref, there_ref, sems,
):
    own = out_hbm.shape[0] // LANES
    half, _, _ = half_of(2 * own)
    first, count, outer = 1 - half, own + 1, half * (own + 1)
    edge = 1 + half * (own - 1)
    for ref in (here_ref, there_ref):
        clear_pads(ref)

    def start(tile, size):
        cut = span(tile, 0, size * LANES)
        store(here_ref, tile, -(inflow_ref[cut, :] + base_ref[cut, :]) * inv_ref[cut, :])

    in_chunks(first, count, start)
    halo_inv = halo_inv_ref[...]
    store(here_ref, outer, -(halo_ref[...] + edge_base_ref[0:LANES, :]) * halo_inv)
    cut = span(edge)
    store(here_ref, edge, -(inflow_ref[cut, :] + edge_base_ref[LANES:, :]) * inv_ref[cut, :])
    mix = mixer(coup_ref)
    refs = (here_ref, there_ref)
    for iteration in range(1, ITERS):
        source, target = refs[(iteration - 1) % 2], refs[iteration % 2]
        last = iteration == ITERS - 1

        def write(tile, coupled, target=target, last=last):
            values = -(inflow_ref[span(tile), :] + coupled) * inv_ref[span(tile), :]
            if last:
                out_ref[span(tile - 1), :] = values
            else:
                store(target, tile, values)

        def step(tile, size, source=source, write=write):
            bands = [band_ref[tile + i] for i in range(size)]
            couple(source, tile, bands, mix, write)

        def final(tile, size, step=step):
            step(tile, size)
            cut = span(tile - 1, 0, size * LANES)
            whole = span(half * own + tile - 1, 0, size * LANES)
            pltpu.make_async_copy(out_ref.at[cut, :], out_hbm.at[cut, :], sems.at[0]).start()
            pltpu.make_async_copy(out_ref.at[cut, :], full_hbm.at[whole, :], sems.at[1]).start()

        def write_halo(tile, coupled, target=target):
            store(target, tile, -(halo_ref[...] + coupled) * halo_inv)

        if last:
            in_chunks(1, own, final)
        else:
            couple(source, outer, [halo_band_ref[...]], mix, write_halo)
            in_chunks(first, count, step)

    base_row = half * own * LANES
    group, _ = place()
    pair = group - lax.rem(group, 2)
    for member in range(2):
        offset = member * (picked_ref.shape[0] // 2)
        for at, row in asked_rows(cap, die_count, pair + member, asked_ref):
            row = row - base_row
            inside = (row >= 0) & (row < own * LANES)
            safe = jnp.clip(row, 0, own * LANES - 1)
            values = out_ref[pl.ds(safe, 1), :]
            picked_ref[pl.ds(offset + at, 1), :] = jnp.where(inside, values, 0.0)
    pltpu.make_async_copy(out_ref, out_hbm, sems.at[0]).wait()
    pltpu.make_async_copy(out_ref, full_hbm.at[0 : own * LANES, :], sems.at[1]).wait()


def join_body(other_ref, full_in_hbm, full_hbm, done_ref, sem):
    rows = other_ref.shape[0]
    half, _, _ = half_of(2 * rows // LANES)
    start = pl.multiple_of((1 - half) * rows, LANES)
    copy = pltpu.make_async_copy(other_ref, full_hbm.at[pl.ds(start, rows), :], sem)
    copy.start()
    done_ref[...] = jnp.zeros(done_ref.shape, F32)
    copy.wait()


def add_body(parts_ref, after_ref, out_ref):
    rows = out_ref.shape[0]
    out_ref[...] = parts_ref[0:rows, :] + parts_ref[rows:, :]


def scatter_body(cols, node_ref, cond_ref, start_ref, volt_ref, load_ref, shunt_ref,
                 right_ref, inv_ref, inner_ref, outer_ref):
    blocks = node_ref.shape[0]
    rows = volt_ref.shape[0]
    group = 8
    row_at = lax.broadcasted_iota(jnp.int32, (rows, LANES), 0)
    col_at = lax.broadcasted_iota(jnp.int32, (cols, LANES), 0)
    total = jnp.zeros((4 * rows, cols), F32)
    for first in range(0, blocks, group):
        node = node_ref[first : first + group, :]
        live = node >= 0
        cond = jnp.where(live, cond_ref[first : first + group, :], 0.0)
        flow = cond * start_ref[first : first + group, :]
        safe = jnp.where(live, node, 0)
        row, col = safe // cols, safe % cols
        parts = halves(cond) + halves(flow)
        left, right = [], []
        for i in range(group):
            spot = jnp.where(row_at == row[i : i + 1, :], 1.0, 0.0).astype(BF16)
            left.append(
                jnp.concatenate([spot * part[i : i + 1, :] for part in parts], axis=0)
            )
            right.append(jnp.where(col_at == col[i : i + 1, :], 1.0, 0.0).astype(BF16))
        total = total + lax.dot_general(
            jnp.concatenate(left, axis=1),
            jnp.concatenate(right, axis=1),
            (((1,), (1,)), ((), ())),
            preferred_element_type=F32,
        )
    gsum = total[:rows] + total[rows : 2 * rows]
    inject = total[2 * rows : 3 * rows] + total[3 * rows :]
    inv = 1.0 / (4.0 + shunt_ref[...] + gsum)
    right_side = (inject - load_ref[...]) * inv
    right_ref[...] = right_side
    inv_ref[...] = inv
    volt = volt_ref[...]
    top, bottom = (
        jnp.concatenate([volt[cut], right_side[cut], inv[cut]], axis=0)
        for cut in (slice(0, HALO_ROWS), slice(rows - HALO_ROWS, rows))
    )
    swap_parts(inner_ref, outer_ref, place()[0], top, bottom)


def swap_parts(inner_ref, outer_ref, mine, first, last):
    even = lax.rem(mine, 2) == 0
    inner_ref[...] = jnp.where(even, last, first)
    outer_ref[...] = jnp.where(even, first, last)


def swapped(inner, outer, mine):
    even = lax.rem(mine, 2) == 0
    return jnp.where(even, outer, inner), jnp.where(even, inner, outer)


def swap(inner, outer, axis):
    count = lax.axis_size(axis)

    def pairs(start):
        return [
            pair
            for i in range(start, count - 1, 2)
            for pair in ((i, i + 1), (i + 1, i))
        ]

    return lax.ppermute(inner, axis, pairs(0)), lax.ppermute(outer, axis, pairs(1))


def extended(own, top, bottom, index):
    cut = slice(index * HALO_ROWS, (index + 1) * HALO_ROWS)
    return jnp.concatenate([top[cut], own, bottom[cut]], axis=0)


def edge_body(volt_ref, right_ref, inv_ref, inner_ref, outer_ref, west_ref, east_ref):
    cols = volt_ref.shape[1]
    top, bottom = swapped(inner_ref[...], outer_ref[...], place()[0])
    out_rows, high = west_ref.shape
    west, east = None, None
    for index, ref in enumerate((volt_ref, right_ref, inv_ref)):
        whole = extended(ref[...], top, bottom, index)
        lane = lax.broadcasted_iota(jnp.int32, (whole.shape[0], LANES), 1)
        head, tail = whole[:, :LANES], whole[:, cols - LANES :]
        at = index * SWEEPS
        head = pltpu.roll(head, at, 1) if at else head
        tail = pltpu.roll(tail, at + SWEEPS, 1)
        west = head if west is None else jnp.where(lane >= at, head, west)
        east = tail if east is None else jnp.where(lane >= at, tail, east)
    fill = jnp.zeros((high - west.shape[0], LANES), F32)
    west, east = (
        jnp.concatenate([part, fill], axis=0).T[:out_rows] for part in (west, east)
    )
    swap_parts(west_ref, east_ref, place()[1], west, east)


def sweep_body(copies, node_ref, cond_ref, start_ref, volt_ref, right_ref, inv_ref,
               row_in_ref, row_out_ref, col_in_ref, col_out_ref, out_ref, current_ref):
    rows, cols = volt_ref.shape
    blocks = node_ref.shape[0]
    cap = current_ref.shape[1]
    whole = []
    top, bottom = swapped(row_in_ref[...], row_out_ref[...], place()[0])
    out_rows, high = col_in_ref.shape
    fill = jnp.zeros((LANES - out_rows, high), F32)
    wests, easts = (
        jnp.concatenate([part, fill], axis=0).T[: rows + 2 * HALO_ROWS]
        for part in swapped(col_in_ref[...], col_out_ref[...], place()[1])
    )
    for index, ref in enumerate((volt_ref, right_ref, inv_ref)):
        own = extended(ref[...], top, bottom, index)
        at = index * SWEEPS
        west = pltpu.roll(wests, LANES - SWEEPS - at, 1)
        east = pltpu.roll(easts, LANES - at, 1) if at else easts
        whole.append(jnp.concatenate([west, own, east], axis=1))
    volt, right_side, inv = whole
    high, wide = volt.shape
    for weight in sweep_weights(SWEEPS):
        beside = (
            pltpu.roll(volt, 1, 0)
            + pltpu.roll(volt, high - 1, 0)
            + pltpu.roll(volt, 1, 1)
            + pltpu.roll(volt, wide - 1, 1)
        )
        volt = (1.0 - weight) * volt + weight * (right_side + beside * inv)
    volt = volt[HALO_ROWS : HALO_ROWS + rows, LANES : LANES + cols]
    out_ref[...] = volt
    both = jnp.concatenate(halves(volt), axis=0)
    group = 8
    row_at = lax.broadcasted_iota(jnp.int32, (rows, LANES), 0)
    col_at = lax.broadcasted_iota(jnp.int32, (cols, LANES), 0)
    dies = blocks // cap
    for first in range(0, blocks, group):
        node = node_ref[first : first + group, :]
        live = node >= 0
        cond = jnp.where(live, cond_ref[first : first + group, :], 0.0)
        safe = jnp.where(live, node, 0)
        row, col = safe // cols, safe % cols
        spots = jnp.concatenate(
            [
                jnp.where(col_at == col[i : i + 1, :], 1.0, 0.0).astype(BF16)
                for i in range(group)
            ],
            axis=1,
        )
        found = jnp.dot(both, spots, preferred_element_type=F32)
        found = found[:rows] + found[rows:]
        for i in range(group):
            mine = found[:, i * LANES : (i + 1) * LANES]
            at_bump = jnp.sum(
                jnp.where(row_at == row[i : i + 1, :], mine, 0.0), axis=0, keepdims=True
            )
            block = first + i
            current = cond[i : i + 1, :] * (start_ref[block : block + 1, :] - at_bump)
            current_ref[block // cap, block % cap : block % cap + 1, :] = current
    for copy in range(1, copies):
        current_ref[copy * dies : (copy + 1) * dies] = current_ref[0:dies]


def local(
    die_volt,
    die_load,
    die_shunt,
    bump_node,
    bump_block,
    bump_cond,
    pkg_volt,
    pkg_diag,
    pkg_pattern,
    pkg_weight,
    block_coupling,
):
    die_count = lax.axis_size("die")
    group_count = lax.axis_size("grp")
    devices = die_count * group_count
    blocks = pkg_volt.shape[0]
    tiles = blocks // LANES
    neighbours = pkg_pattern.shape[0]
    slots = bump_block.shape[0]
    cap = slots // die_count
    rows, cols = die_volt.shape
    (spread,) = call(
        functools.partial(spread_body, cap, die_count, blocks),
        "spread_blocks",
        [shape(devices, 1, LANES, dtype=jnp.int32)],
        (bump_block.reshape(1, slots),),
        [VMEM],
    )
    ids = lax.all_to_all(
        spread, ("grp", "die"), split_axis=0, concat_axis=0, tiled=True
    ).reshape(devices, LANES)

    (picked,) = call(
        functools.partial(pick_body, cap, die_count),
        "pick_rows",
        [shape(slots, LANES)],
        (ids, pkg_volt),
        [SMEM, VMEM],
    )
    bump_start = lax.all_to_all(
        picked.reshape(die_count, cap, LANES), "die", split_axis=0, concat_axis=0, tiled=True
    ).reshape(slots, LANES)

    right_side, inv, *edges = call(
        functools.partial(scatter_body, cols),
        "scatter_bumps",
        [shape(rows, cols)] * 2 + [shape(3 * HALO_ROWS, cols)] * 2,
        (bump_node, bump_cond, bump_start, die_volt, die_load, die_shunt),
        [VMEM] * 6,
        work=3,
    )
    beside = swap(*edges, "grp")

    edge_rows = -(-3 * SWEEPS // 8) * 8
    edge_cols = -(-(rows + 2 * HALO_ROWS) // LANES) * LANES
    edges = call(
        edge_body,
        "edge_columns",
        [shape(edge_rows, edge_cols)] * 2,
        (die_volt, right_side, inv, *beside),
        [VMEM] * 5,
    )
    columns = swap(*edges, "die")

    die_out, current = call(
        functools.partial(sweep_body, group_count),
        "sweeps",
        [shape(rows, cols), shape(devices, cap, LANES)],
        (bump_node, bump_cond, bump_start, die_volt, right_side, inv, *beside, *columns),
        [VMEM] * 10,
        work=4,
    )
    own = tiles // 2
    dma = pltpu.SemaphoreType.DMA
    plane = pltpu.VMEM(((own + 2) * LANES + 2 * RADIUS, 2 * LANES), BF16)
    range_rows = pltpu.VMEM(((own + 2) * LANES, LANES), F32)
    range_bands = pltpu.VMEM((own + 2, 2 * LANES, 2 * LANES), BF16)
    pack_rows = 2 * LANES + 2 * neighbours
    band, base, pkg_inv, pack, near = call(
        prepare_body,
        "package_prepare",
        [
            shape(own + 2, 2 * LANES, 2 * LANES, dtype=BF16),
            shape((own + 2) * LANES, LANES),
            shape((own + 2) * LANES, LANES),
            shape(pack_rows, LANES),
            shape(2 * RADIUS, LANES),
        ],
        (pkg_pattern, pkg_weight, block_coupling, pkg_volt, pkg_diag, die_out),
        [VMEM] * 3 + [HBM] * 3,
        [range_rows, range_rows, range_bands, range_rows, range_rows, plane, dma((5,))],
        work=7,
        vmem=MOST_VMEM,
        out_specs=[HBM] * 3 + [VMEM] * 2,
    )

    current = lax.all_to_all(
        current, ("grp", "die"), split_axis=0, concat_axis=0, tiled=True
    ).reshape(devices * cap, LANES)

    beside_end = [
        (g * die_count + a, g * die_count + b)
        for g in range(group_count)
        for d in range((g + 1) % 2, die_count - 1, 2)
        for a, b in ((d, d + 1), (d + 1, d))
    ]
    halo = lax.ppermute(pack, ("grp", "die"), beside_end)
    (inflow,) = call(
        functools.partial(ends_body, cap, tiles),
        "package_end",
        [shape(LANES, LANES)],
        (ids, current),
        [VMEM, VMEM],
    )
    halo_inflow = lax.ppermute(inflow, ("grp", "die"), beside_end)
    all_inflow, halo_band, halo_inv, edge_base = call(
        functools.partial(inflow_body, cap, tiles),
        "package_inflow",
        [
            shape((own + 2) * LANES, LANES),
            shape(2 * LANES, 2 * LANES, dtype=BF16),
            shape(LANES, LANES),
            shape(2 * LANES, LANES),
        ],
        (ids, current, block_coupling, pack, halo, near, inflow),
        [VMEM] * 6 + [ANY],
        [pltpu.VMEM((2 * LANES + 2 * RADIUS, 2 * LANES), BF16)],
        work=3,
    )
    half_out, pkg_out, picked = call(
        functools.partial(iterate_body, cap, die_count),
        "package_iterations",
        [shape(own * LANES, LANES), shape(blocks, LANES), shape(2 * slots, LANES)],
        (
            ids, block_coupling, halo_inflow, all_inflow, band, base, pkg_inv,
            halo_band, halo_inv, edge_base,
        ),
        [SMEM] + [VMEM] * 9,
        [pltpu.VMEM((own * LANES, LANES), F32), plane, plane, dma((2,))],
        work=10,
        vmem=24,
        out_specs=[HBM, HBM, VMEM],
    )
    pair = 2 * die_count
    parts = lax.all_to_all(
        picked.reshape(pair, cap, LANES),
        ("grp", "die"),
        split_axis=0,
        concat_axis=0,
        axis_index_groups=[
            [first + i for i in range(pair)] for first in range(0, devices, pair)
        ],
        tiled=True,
    ).reshape(2 * slots, LANES)
    other = lax.ppermute(half_out, "grp", [(g, g ^ 1) for g in range(group_count)])
    pkg_out, done = call(
        join_body,
        "join_halves",
        [shape(blocks, LANES), shape(8, LANES)],
        (other, pkg_out),
        [VMEM, HBM],
        [dma(())],
        out_specs=[HBM, VMEM],
        aliases={1: 0},
    )
    (bump_out,) = call(
        add_body, "add_parts", [shape(slots, LANES)], (parts, done), [VMEM, ANY]
    )
    return (die_out, pkg_out, bump_out)


def solution(mesh):
    return jax.shard_map(
        local,
        mesh=mesh,
        in_specs=(
            P("grp", "die"),
            P("grp", "die"),
            P("grp", "die"),
            P(("grp", "die"), None),
            P(("grp", "die")),
            P(("grp", "die"), None),
            P("die", None),
            P("die", None),
            P(None, "die"),
            P(None, "die"),
            P(),
        ),
        out_specs=(P("grp", "die"), P("die", None), P(("grp", "die"), None)),
        check_vma=False,
    )
```

```python
import functools
import math

import jax
import jax.numpy as jnp
from jax import lax
from jax.experimental import pallas as pl
from jax.experimental.pallas import tpu as pltpu
from jax.sharding import PartitionSpec as P

RADIUS = 32
SWEEPS = 4
ITERS = 4
LANES = 128
HALO_ROWS = 8
REACH = RADIUS * ITERS
WINDOW = LANES + 2 * RADIUS
F32 = jnp.float32
BF16 = jnp.bfloat16
MOST_VMEM = 57
VMEM = pl.BlockSpec(memory_space=pltpu.VMEM)
SMEM = pl.BlockSpec(memory_space=pltpu.SMEM)
ANY = pl.BlockSpec(memory_space=pl.ANY)
HBM = pl.BlockSpec(memory_space=pltpu.HBM)


def sweep_weights(sweeps):
    return [
        1.0 / (1.0 + 0.8 * math.cos(math.pi * (2 * index + 1) / (2 * sweeps)))
        for index in range(sweeps)
    ]


def call(
    body, name, outs, args, specs, scratch=(), work=1, vmem=16, out_specs=None, aliases=None
):
    bytes_accessed = sum(4 * math.prod(arg.shape) for arg in args)
    return pl.pallas_call(
        body,
        name=name,
        out_shape=outs,
        in_specs=specs,
        out_specs=out_specs or [VMEM] * len(outs),
        input_output_aliases=aliases or {},
        scratch_shapes=list(scratch),
        compiler_params=pltpu.CompilerParams(vmem_limit_bytes=vmem * 1024 * 1024),
        cost_estimate=pl.CostEstimate(
            flops=work * 10**9, bytes_accessed=bytes_accessed, transcendentals=0
        ),
    )(*args)


def place():
    return lax.axis_index("grp"), lax.axis_index("die")


def shape(*dims, dtype=F32):
    return jax.ShapeDtypeStruct(dims, dtype)


def halves(values):
    high = values.astype(BF16)
    low = (values - high.astype(F32)).astype(BF16)
    return high, low


def spread_body(cap, die_count, blocks, block_ref, out_ref):
    slots = block_ref.shape[1]
    block = jnp.concatenate(
        [block_ref[...], jnp.zeros((1, LANES - slots), jnp.int32)], axis=1
    )
    for die in range(die_count):
        row = (pltpu.roll(block, LANES - die * cap, 1) if die else block) - die * blocks
        for at in range(die, out_ref.shape[0], die_count):
            out_ref[at] = row


def asked_rows(cap, die_count, group, ids_ref):
    for die in range(die_count):
        for slot in range(cap):
            yield die * cap + slot, ids_ref[group * die_count + die, slot]


def pick_body(cap, die_count, ids_ref, plane_ref, out_ref):
    group, _ = place()
    for at, row in asked_rows(cap, die_count, group, ids_ref):
        out_ref[pl.ds(at, 1), :] = plane_ref[pl.ds(row, 1), :]


def build_band(first, pattern, weights):
    place = lax.broadcasted_iota(jnp.int32, (WINDOW, LANES), 0)
    band = None
    for k in range(pattern.shape[0]):
        hit = place == (pattern[k : k + 1, :] - first)
        term = jnp.where(hit, weights[k : k + 1, :], 0.0)
        band = term if band is None else band + term
    fill = jnp.zeros((2 * LANES - WINDOW, LANES), F32)
    return jnp.concatenate(halves(jnp.concatenate([band, fill], axis=0).T), axis=0)


def reciprocal(diag):
    safe = jnp.where(diag > 0.0, diag, 1.0)
    return jnp.where(diag > 0.0, 1.0 / safe, 0.0)


def span(tile, offset=0, size=LANES):
    return pl.ds(pl.multiple_of(tile * LANES + offset, RADIUS), size)


def mixer(coup_ref):
    mix = jnp.concatenate(halves(coup_ref[...]), axis=1)
    return jnp.concatenate([mix, mix], axis=0)


def clear_pads(ref):
    pad = jnp.zeros((RADIUS, 2 * LANES), BF16)
    ref[0:RADIUS, :] = pad
    ref[ref.shape[0] - RADIUS :, :] = pad


def store(ref, tile, values):
    ref[span(tile, RADIUS, values.shape[0]), :] = jnp.concatenate(halves(values), axis=1)


def couple(source, tile, bands, mix, write):
    for at in range(0, len(bands), 4):
        couple_few(source, tile + at, bands[at : at + 4], mix, write)


def couple_few(source, tile, bands, mix, write):
    own = source[span(tile, RADIUS, len(bands) * LANES), :]
    within = jnp.dot(own, mix, preferred_element_type=F32)
    for i, band in enumerate(bands):
        window = source[span(tile + i, 0, WINDOW), :]
        beside = jnp.dot(band[:, :WINDOW], window, preferred_element_type=F32)
        both = beside[:LANES] + beside[LANES:] + within[i * LANES : (i + 1) * LANES]
        write(tile + i, both[:, :LANES] + both[:, LANES:])


def in_chunks(first, count, body, size=8):
    whole = count // size

    @pl.loop(0, whole)
    def _(chunk):
        body(first + chunk * size, size)

    if count % size:
        body(first + whole * size, count % size)


def half_of(tiles):
    half = lax.rem(sum(place()), 2)
    own = tiles // 2
    return half, own, half * own - 1


def prepare_body(
    pat_ref, wgt_ref, coup_ref, volt_hbm, diag_hbm, after_ref,
    band_hbm, base_hbm, inv_hbm, pack_ref, near_ref,
    volt_ref, diag_ref, band_ref, base_ref, inv_ref, plane_ref, sems,
):
    blocks = volt_hbm.shape[0]
    half, own, shift = half_of(blocks // LANES)
    first, count, outer = 1 - half, own + 1, half * (own + 1)
    known = pl.ds(pl.multiple_of(first * LANES, LANES), count * LANES)
    source = pl.ds(pl.multiple_of((first + shift) * LANES, LANES), count * LANES)
    loads = [
        pltpu.make_async_copy(hbm.at[source, :], ref.at[known, :], sems.at[i])
        for i, (hbm, ref) in enumerate(((volt_hbm, volt_ref), (diag_hbm, diag_ref)))
    ]
    for load in loads:
        load.start()
    clear_pads(plane_ref)
    plane_ref[span(outer, RADIUS), :] = jnp.zeros((LANES, 2 * LANES), BF16)
    begin = place()[1] * blocks + shift * LANES

    def bands(tile, size):
        for i in range(size):
            lanes = pl.ds(pl.multiple_of((tile + i + shift) * LANES, LANES), LANES)
            band_ref[tile + i] = build_band(
                begin + (tile + i) * LANES - RADIUS, pat_ref[:, lanes], wgt_ref[:, lanes]
            )

    in_chunks(first, count, bands)
    band_out = pltpu.make_async_copy(
        band_ref.at[pl.ds(first, count)], band_hbm.at[pl.ds(first, count)], sems.at[2]
    )
    band_out.start()
    for load in loads:
        load.wait()

    def spread(tile, size):
        cut = span(tile, 0, size * LANES)
        store(plane_ref, tile, volt_ref[cut, :])
        inv_ref[cut, :] = reciprocal(diag_ref[cut, :])

    in_chunks(first, count, spread)
    inv_out = pltpu.make_async_copy(inv_ref.at[known, :], inv_hbm.at[known, :], sems.at[3])
    inv_out.start()
    mix = mixer(coup_ref)

    def base(tile, size):
        def write(tile, values):
            base_ref[span(tile), :] = values

        couple(plane_ref, tile, [band_ref[tile + i] for i in range(size)], mix, write)
        cut = span(tile, 0, size * LANES)
        pltpu.make_async_copy(base_ref.at[cut, :], base_hbm.at[cut, :], sems.at[4]).start()

    in_chunks(first, count, base)
    edge = 1 + half * (own - 1)
    lanes = pl.ds(pl.multiple_of((edge + shift) * LANES, LANES), LANES)
    neighbours = pat_ref.shape[0]
    pack_ref[0:LANES, :] = volt_ref[span(edge), :]
    pack_ref[LANES : 2 * LANES, :] = diag_ref[span(edge), :]
    at = 2 * LANES
    pack_ref[at : at + neighbours, :] = pat_ref[:, lanes].astype(F32)
    pack_ref[at + neighbours : at + 2 * neighbours, :] = wgt_ref[:, lanes]
    near_ref[0:RADIUS, :] = volt_ref[2 * LANES : 2 * LANES + RADIUS, :]
    near_ref[RADIUS:, :] = volt_ref[own * LANES - RADIUS : own * LANES, :]
    band_out.wait()
    inv_out.wait()
    pltpu.make_async_copy(
        base_ref.at[known, :], base_hbm.at[known, :], sems.at[4]
    ).wait()


def slot_places(cap, ids_ref):
    per_row = LANES // cap
    lane = lax.broadcasted_iota(jnp.int32, (1, LANES), 1)
    places = []
    for at in range(0, ids_ref.shape[0], per_row):
        total = None
        for i in range(per_row):
            row = jnp.where(lane < cap, ids_ref[at + i : at + i + 1, :], 0)
            row = pltpu.roll(row, i * cap, 1) if i else row
            total = row if total is None else total + row
        places.append(total)
    return places


def gather_inflow(places, first, rows, current):
    at = lax.broadcasted_iota(jnp.int32, (rows, LANES), 0) + first
    hits = [jnp.where(at == place, 1.0, 0.0).astype(BF16) for place in places]
    both = jnp.dot(jnp.concatenate(hits, axis=1), current, preferred_element_type=F32)
    return both[:, :LANES] + both[:, LANES:]


def ends_body(cap, tiles, ids_ref, current_ref, out_ref):
    half, _, _ = half_of(tiles)
    places = slot_places(cap, ids_ref)
    current = jnp.concatenate(halves(current_ref[...]), axis=1)
    out_ref[...] = gather_inflow(places, half * (tiles - 1) * LANES, LANES, current)


def inflow_body(
    cap, tiles, ids_ref, current_ref, coup_ref, own_ref, halo_ref, near_ref, after_ref,
    out_ref, band_ref, inv_ref, base_ref, plane_ref,
):
    half, own, shift = half_of(tiles)
    first, count = 1 - half, own + 1
    places = slot_places(cap, ids_ref)
    current = jnp.concatenate(halves(current_ref[...]), axis=1)

    def inflow(tile, size):
        cut = span(tile, 0, size * LANES)
        out_ref[cut, :] = gather_inflow(
            places, (tile + shift) * LANES, size * LANES, current
        )

    in_chunks(first, count, inflow)
    out_ref[span(half * (own + 1)), :] = jnp.zeros((LANES, LANES), F32)

    neighbours = (own_ref.shape[0] - 2 * LANES) // 2
    begin = (place()[1] * tiles + 2 * half * own - 1) * LANES
    packs = [jnp.where(half == at, halo_ref[...], own_ref[...]) for at in range(2)]
    at = 2 * LANES
    bands = []
    for tile, pack in enumerate(packs):
        bands.append(
            build_band(
                begin + tile * LANES - RADIUS,
                pack[at : at + neighbours].astype(jnp.int32),
                pack[at + neighbours : at + 2 * neighbours],
            )
        )
        store(plane_ref, tile, pack[:LANES])
    none = jnp.zeros((RADIUS, 2 * LANES), BF16)
    low, high = (
        jnp.concatenate(halves(near_ref[cut, :]), axis=1)
        for cut in (slice(0, RADIUS), slice(RADIUS, 2 * RADIUS))
    )
    size = plane_ref.shape[0]
    plane_ref[0:RADIUS, :] = jnp.where(half == 0, none, high)
    plane_ref[size - RADIUS : size, :] = jnp.where(half == 0, low, none)
    results = []
    couple(plane_ref, 0, bands, mixer(coup_ref), lambda tile, values: results.append(values))
    band_ref[...] = jnp.where(half == 0, bands[0], bands[1])
    inv_ref[...] = reciprocal(halo_ref[LANES : 2 * LANES, :])
    base_ref[0:LANES, :] = jnp.where(half == 0, results[0], results[1])
    base_ref[LANES:, :] = jnp.where(half == 0, results[1], results[0])


def iterate_body(
    cap, die_count, asked_ref, coup_ref, halo_ref, inflow_ref, band_ref, base_ref, inv_ref,
    halo_band_ref, halo_inv_ref, edge_base_ref, out_hbm, full_hbm, picked_ref, out_ref, here_ref, there_ref, sems,
):
    own = out_hbm.shape[0] // LANES
    half, _, _ = half_of(2 * own)
    first, count, outer = 1 - half, own + 1, half * (own + 1)
    edge = 1 + half * (own - 1)
    for ref in (here_ref, there_ref):
        clear_pads(ref)

    def start(tile, size):
        cut = span(tile, 0, size * LANES)
        store(here_ref, tile, -(inflow_ref[cut, :] + base_ref[cut, :]) * inv_ref[cut, :])

    in_chunks(first, count, start)
    halo_inv = halo_inv_ref[...]
    store(here_ref, outer, -(halo_ref[...] + edge_base_ref[0:LANES, :]) * halo_inv)
    cut = span(edge)
    store(here_ref, edge, -(inflow_ref[cut, :] + edge_base_ref[LANES:, :]) * inv_ref[cut, :])
    mix = mixer(coup_ref)
    refs = (here_ref, there_ref)
    for iteration in range(1, ITERS):
        source, target = refs[(iteration - 1) % 2], refs[iteration % 2]
        last = iteration == ITERS - 1

        def write(tile, coupled, target=target, last=last):
            values = -(inflow_ref[span(tile), :] + coupled) * inv_ref[span(tile), :]
            if last:
                out_ref[span(tile - 1), :] = values
            else:
                store(target, tile, values)

        def step(tile, size, source=source, write=write):
            bands = [band_ref[tile + i] for i in range(size)]
            couple(source, tile, bands, mix, write)

        def final(tile, size, step=step):
            step(tile, size)
            cut = span(tile - 1, 0, size * LANES)
            whole = span(half * own + tile - 1, 0, size * LANES)
            pltpu.make_async_copy(out_ref.at[cut, :], out_hbm.at[cut, :], sems.at[0]).start()
            pltpu.make_async_copy(out_ref.at[cut, :], full_hbm.at[whole, :], sems.at[1]).start()

        def write_halo(tile, coupled, target=target):
            store(target, tile, -(halo_ref[...] + coupled) * halo_inv)

        if last:
            in_chunks(1, own, final)
        else:
            in_chunks(first, count, step)
            couple(source, outer, [halo_band_ref[...]], mix, write_halo)

    base_row = half * own * LANES
    group, _ = place()
    pair = group - lax.rem(group, 2)
    for member in range(2):
        offset = member * (picked_ref.shape[0] // 2)
        for at, row in asked_rows(cap, die_count, pair + member, asked_ref):
            row = row - base_row
            inside = (row >= 0) & (row < own * LANES)
            safe = jnp.clip(row, 0, own * LANES - 1)
            values = out_ref[pl.ds(safe, 1), :]
            picked_ref[pl.ds(offset + at, 1), :] = jnp.where(inside, values, 0.0)
    pltpu.make_async_copy(out_ref, out_hbm, sems.at[0]).wait()
    pltpu.make_async_copy(out_ref, full_hbm.at[0 : own * LANES, :], sems.at[1]).wait()


def join_body(other_ref, full_in_hbm, full_hbm, done_ref, sem):
    rows = other_ref.shape[0]
    half, _, _ = half_of(2 * rows // LANES)
    start = pl.multiple_of((1 - half) * rows, LANES)
    copy = pltpu.make_async_copy(other_ref, full_hbm.at[pl.ds(start, rows), :], sem)
    copy.start()
    done_ref[...] = jnp.zeros(done_ref.shape, F32)
    copy.wait()


def add_body(parts_ref, after_ref, out_ref):
    rows = out_ref.shape[0]
    out_ref[...] = parts_ref[0:rows, :] + parts_ref[rows:, :]


def scatter_body(cols, node_ref, cond_ref, start_ref, volt_ref, load_ref, shunt_ref,
                 right_ref, inv_ref, inner_ref, outer_ref):
    blocks = node_ref.shape[0]
    rows = volt_ref.shape[0]
    group = 8
    row_at = lax.broadcasted_iota(jnp.int32, (rows, LANES), 0)
    col_at = lax.broadcasted_iota(jnp.int32, (cols, LANES), 0)
    total = jnp.zeros((4 * rows, cols), F32)
    for first in range(0, blocks, group):
        node = node_ref[first : first + group, :]
        live = node >= 0
        cond = jnp.where(live, cond_ref[first : first + group, :], 0.0)
        flow = cond * start_ref[first : first + group, :]
        safe = jnp.where(live, node, 0)
        row, col = safe // cols, safe % cols
        parts = halves(cond) + halves(flow)
        left, right = [], []
        for i in range(group):
            spot = jnp.where(row_at == row[i : i + 1, :], 1.0, 0.0).astype(BF16)
            left.append(
                jnp.concatenate([spot * part[i : i + 1, :] for part in parts], axis=0)
            )
            right.append(jnp.where(col_at == col[i : i + 1, :], 1.0, 0.0).astype(BF16))
        total = total + lax.dot_general(
            jnp.concatenate(left, axis=1),
            jnp.concatenate(right, axis=1),
            (((1,), (1,)), ((), ())),
            preferred_element_type=F32,
        )
    gsum = total[:rows] + total[rows : 2 * rows]
    inject = total[2 * rows : 3 * rows] + total[3 * rows :]
    inv = 1.0 / (4.0 + shunt_ref[...] + gsum)
    right_side = (inject - load_ref[...]) * inv
    right_ref[...] = right_side
    inv_ref[...] = inv
    volt = volt_ref[...]
    top, bottom = (
        jnp.concatenate([volt[cut], right_side[cut], inv[cut]], axis=0)
        for cut in (slice(0, HALO_ROWS), slice(rows - HALO_ROWS, rows))
    )
    swap_parts(inner_ref, outer_ref, place()[0], top, bottom)


def swap_parts(inner_ref, outer_ref, mine, first, last):
    even = lax.rem(mine, 2) == 0
    inner_ref[...] = jnp.where(even, last, first)
    outer_ref[...] = jnp.where(even, first, last)


def swapped(inner, outer, mine):
    even = lax.rem(mine, 2) == 0
    return jnp.where(even, outer, inner), jnp.where(even, inner, outer)


def swap(inner, outer, axis):
    count = lax.axis_size(axis)

    def pairs(start):
        return [
            pair
            for i in range(start, count - 1, 2)
            for pair in ((i, i + 1), (i + 1, i))
        ]

    return lax.ppermute(inner, axis, pairs(0)), lax.ppermute(outer, axis, pairs(1))


def extended(own, top, bottom, index):
    cut = slice(index * HALO_ROWS, (index + 1) * HALO_ROWS)
    return jnp.concatenate([own, bottom[cut], top[cut]], axis=0)


def edge_body(volt_ref, right_ref, inv_ref, inner_ref, outer_ref, west_ref, east_ref):
    cols = volt_ref.shape[1]
    top, bottom = swapped(inner_ref[...], outer_ref[...], place()[0])
    out_rows, high = west_ref.shape
    west, east = None, None
    for index, ref in enumerate((volt_ref, right_ref, inv_ref)):
        whole = extended(ref[...], top, bottom, index)
        lane = lax.broadcasted_iota(jnp.int32, (whole.shape[0], LANES), 1)
        head, tail = whole[:, :LANES], whole[:, cols - LANES :]
        at = index * SWEEPS
        head = pltpu.roll(head, at, 1) if at else head
        tail = pltpu.roll(tail, at + SWEEPS, 1)
        west = head if west is None else jnp.where(lane >= at, head, west)
        east = tail if east is None else jnp.where(lane >= at, tail, east)
    fill = jnp.zeros((high - west.shape[0], LANES), F32)
    west, east = (
        jnp.concatenate([part, fill], axis=0).T[:out_rows] for part in (west, east)
    )
    swap_parts(west_ref, east_ref, place()[1], west, east)


def sweep_body(copies, node_ref, cond_ref, start_ref, volt_ref, right_ref, inv_ref,
               row_in_ref, row_out_ref, col_in_ref, col_out_ref, out_ref, current_ref):
    rows, cols = volt_ref.shape
    blocks = node_ref.shape[0]
    cap = current_ref.shape[1]
    whole = []
    top, bottom = swapped(row_in_ref[...], row_out_ref[...], place()[0])
    out_rows, high = col_in_ref.shape
    fill = jnp.zeros((LANES - out_rows, high), F32)
    wests, easts = (
        jnp.concatenate([part, fill], axis=0).T[: rows + 2 * HALO_ROWS]
        for part in swapped(col_in_ref[...], col_out_ref[...], place()[1])
    )
    eastern = lax.broadcasted_iota(jnp.int32, easts.shape, 1) < LANES // 2
    for index, ref in enumerate((volt_ref, right_ref, inv_ref)):
        own = extended(ref[...], top, bottom, index)
        at = index * SWEEPS
        west = pltpu.roll(wests, LANES - SWEEPS - at, 1)
        east = pltpu.roll(easts, LANES - at, 1) if at else easts
        whole.append(jnp.concatenate([own, jnp.where(eastern, east, west)], axis=1))
    volt, right_side, inv = whole
    high, wide = volt.shape
    for weight in sweep_weights(SWEEPS):
        beside = (
            pltpu.roll(volt, 1, 0)
            + pltpu.roll(volt, high - 1, 0)
            + pltpu.roll(volt, 1, 1)
            + pltpu.roll(volt, wide - 1, 1)
        )
        volt = (1.0 - weight) * volt + weight * (right_side + beside * inv)
    volt = volt[:rows, :cols]
    out_ref[...] = volt
    both = jnp.concatenate(halves(volt), axis=0)
    group = 8
    row_at = lax.broadcasted_iota(jnp.int32, (rows, LANES), 0)
    col_at = lax.broadcasted_iota(jnp.int32, (cols, LANES), 0)
    dies = blocks // cap
    for first in range(0, blocks, group):
        node = node_ref[first : first + group, :]
        live = node >= 0
        cond = jnp.where(live, cond_ref[first : first + group, :], 0.0)
        safe = jnp.where(live, node, 0)
        row, col = safe // cols, safe % cols
        spots = jnp.concatenate(
            [
                jnp.where(col_at == col[i : i + 1, :], 1.0, 0.0).astype(BF16)
                for i in range(group)
            ],
            axis=1,
        )
        found = jnp.dot(both, spots, preferred_element_type=F32)
        found = found[:rows] + found[rows:]
        for i in range(group):
            mine = found[:, i * LANES : (i + 1) * LANES]
            at_bump = jnp.sum(
                jnp.where(row_at == row[i : i + 1, :], mine, 0.0), axis=0, keepdims=True
            )
            block = first + i
            current = cond[i : i + 1, :] * (start_ref[block : block + 1, :] - at_bump)
            current_ref[block // cap, block % cap : block % cap + 1, :] = current
    for copy in range(1, copies):
        current_ref[copy * dies : (copy + 1) * dies] = current_ref[0:dies]


def local(
    die_volt,
    die_load,
    die_shunt,
    bump_node,
    bump_block,
    bump_cond,
    pkg_volt,
    pkg_diag,
    pkg_pattern,
    pkg_weight,
    block_coupling,
):
    die_count = lax.axis_size("die")
    group_count = lax.axis_size("grp")
    devices = die_count * group_count
    blocks = pkg_volt.shape[0]
    tiles = blocks // LANES
    neighbours = pkg_pattern.shape[0]
    slots = bump_block.shape[0]
    cap = slots // die_count
    rows, cols = die_volt.shape
    (spread,) = call(
        functools.partial(spread_body, cap, die_count, blocks),
        "spread_blocks",
        [shape(devices, 1, LANES, dtype=jnp.int32)],
        (bump_block.reshape(1, slots),),
        [VMEM],
    )
    ids = lax.all_to_all(
        spread, ("grp", "die"), split_axis=0, concat_axis=0, tiled=True
    ).reshape(devices, LANES)

    (picked,) = call(
        functools.partial(pick_body, cap, die_count),
        "pick_rows",
        [shape(slots, LANES)],
        (ids, pkg_volt),
        [SMEM, VMEM],
    )
    bump_start = lax.all_to_all(
        picked.reshape(die_count, cap, LANES), "die", split_axis=0, concat_axis=0, tiled=True
    ).reshape(slots, LANES)

    right_side, inv, *edges = call(
        functools.partial(scatter_body, cols),
        "scatter_bumps",
        [shape(rows, cols)] * 2 + [shape(3 * HALO_ROWS, cols)] * 2,
        (bump_node, bump_cond, bump_start, die_volt, die_load, die_shunt),
        [VMEM] * 6,
        work=3,
    )
    beside = swap(*edges, "grp")

    edge_rows = -(-3 * SWEEPS // 8) * 8
    edge_cols = -(-(rows + 2 * HALO_ROWS) // LANES) * LANES
    edges = call(
        edge_body,
        "edge_columns",
        [shape(edge_rows, edge_cols)] * 2,
        (die_volt, right_side, inv, *beside),
        [VMEM] * 5,
    )
    columns = swap(*edges, "die")

    die_out, current = call(
        functools.partial(sweep_body, group_count),
        "sweeps",
        [shape(rows, cols), shape(devices, cap, LANES)],
        (bump_node, bump_cond, bump_start, die_volt, right_side, inv, *beside, *columns),
        [VMEM] * 10,
        work=4,
    )
    own = tiles // 2
    dma = pltpu.SemaphoreType.DMA
    plane = pltpu.VMEM(((own + 2) * LANES + 2 * RADIUS, 2 * LANES), BF16)
    range_rows = pltpu.VMEM(((own + 2) * LANES, LANES), F32)
    range_bands = pltpu.VMEM((own + 2, 2 * LANES, 2 * LANES), BF16)
    pack_rows = 2 * LANES + 2 * neighbours
    band, base, pkg_inv, pack, near = call(
        prepare_body,
        "package_prepare",
        [
            shape(own + 2, 2 * LANES, 2 * LANES, dtype=BF16),
            shape((own + 2) * LANES, LANES),
            shape((own + 2) * LANES, LANES),
            shape(pack_rows, LANES),
            shape(2 * RADIUS, LANES),
        ],
        (pkg_pattern, pkg_weight, block_coupling, pkg_volt, pkg_diag, die_out),
        [VMEM] * 3 + [HBM] * 3,
        [range_rows, range_rows, range_bands, range_rows, range_rows, plane, dma((5,))],
        work=7,
        vmem=MOST_VMEM,
        out_specs=[HBM] * 3 + [VMEM] * 2,
    )

    current = lax.all_to_all(
        current, ("grp", "die"), split_axis=0, concat_axis=0, tiled=True
    ).reshape(devices * cap, LANES)

    beside_end = [
        (g * die_count + a, g * die_count + b)
        for g in range(group_count)
        for d in range((g + 1) % 2, die_count - 1, 2)
        for a, b in ((d, d + 1), (d + 1, d))
    ]
    halo = lax.ppermute(pack, ("grp", "die"), beside_end)
    (inflow,) = call(
        functools.partial(ends_body, cap, tiles),
        "package_end",
        [shape(LANES, LANES)],
        (ids, current),
        [VMEM, VMEM],
    )
    halo_inflow = lax.ppermute(inflow, ("grp", "die"), beside_end)
    all_inflow, halo_band, halo_inv, edge_base = call(
        functools.partial(inflow_body, cap, tiles),
        "package_inflow",
        [
            shape((own + 2) * LANES, LANES),
            shape(2 * LANES, 2 * LANES, dtype=BF16),
            shape(LANES, LANES),
            shape(2 * LANES, LANES),
        ],
        (ids, current, block_coupling, pack, halo, near, inflow),
        [VMEM] * 6 + [ANY],
        [pltpu.VMEM((2 * LANES + 2 * RADIUS, 2 * LANES), BF16)],
        work=3,
    )
    half_out, pkg_out, picked = call(
        functools.partial(iterate_body, cap, die_count),
        "package_iterations",
        [shape(own * LANES, LANES), shape(blocks, LANES), shape(2 * slots, LANES)],
        (
            ids, block_coupling, halo_inflow, all_inflow, band, base, pkg_inv,
            halo_band, halo_inv, edge_base,
        ),
        [SMEM] + [VMEM] * 9,
        [pltpu.VMEM((own * LANES, LANES), F32), plane, plane, dma((2,))],
        work=10,
        vmem=24,
        out_specs=[HBM, HBM, VMEM],
    )
    pair = 2 * die_count
    parts = lax.all_to_all(
        picked.reshape(pair, cap, LANES),
        ("grp", "die"),
        split_axis=0,
        concat_axis=0,
        axis_index_groups=[
            [first + i for i in range(pair)] for first in range(0, devices, pair)
        ],
        tiled=True,
    ).reshape(2 * slots, LANES)
    other = lax.ppermute(half_out, "grp", [(g, g ^ 1) for g in range(group_count)])
    pkg_out, done = call(
        join_body,
        "join_halves",
        [shape(blocks, LANES), shape(8, LANES)],
        (other, pkg_out),
        [VMEM, HBM],
        [dma(())],
        out_specs=[HBM, VMEM],
        aliases={1: 0},
    )
    (bump_out,) = call(
        add_body, "add_parts", [shape(slots, LANES)], (parts, done), [VMEM, ANY]
    )
    return (die_out, pkg_out, bump_out)


def solution(mesh):
    return jax.shard_map(
        local,
        mesh=mesh,
        in_specs=(
            P("grp", "die"),
            P("grp", "die"),
            P("grp", "die"),
            P(("grp", "die"), None),
            P(("grp", "die")),
            P(("grp", "die"), None),
            P("die", None),
            P("die", None),
            P(None, "die"),
            P(None, "die"),
            P(),
        ),
        out_specs=(P("grp", "die"), P("die", None), P(("grp", "die"), None)),
        check_vma=False,
    )
```

```python
import functools
import math

import jax
import jax.numpy as jnp
from jax import lax
from jax.experimental import pallas as pl
from jax.experimental.pallas import tpu as pltpu
from jax.sharding import PartitionSpec as P

RADIUS = 32
SWEEPS = 4
ITERS = 4
LANES = 128
HALO_ROWS = 8
REACH = RADIUS * ITERS
WINDOW = LANES + 2 * RADIUS
F32 = jnp.float32
BF16 = jnp.bfloat16
MOST_VMEM = 57
VMEM = pl.BlockSpec(memory_space=pltpu.VMEM)
SMEM = pl.BlockSpec(memory_space=pltpu.SMEM)
ANY = pl.BlockSpec(memory_space=pl.ANY)
HBM = pl.BlockSpec(memory_space=pltpu.HBM)


def sweep_weights(sweeps):
    return [
        1.0 / (1.0 + 0.8 * math.cos(math.pi * (2 * index + 1) / (2 * sweeps)))
        for index in range(sweeps)
    ]


def call(
    body, name, outs, args, specs, scratch=(), work=1, vmem=16, out_specs=None, aliases=None
):
    bytes_accessed = sum(4 * math.prod(arg.shape) for arg in args)
    return pl.pallas_call(
        body,
        name=name,
        out_shape=outs,
        in_specs=specs,
        out_specs=out_specs or [VMEM] * len(outs),
        input_output_aliases=aliases or {},
        scratch_shapes=list(scratch),
        compiler_params=pltpu.CompilerParams(vmem_limit_bytes=vmem * 1024 * 1024),
        cost_estimate=pl.CostEstimate(
            flops=work * 10**9, bytes_accessed=bytes_accessed, transcendentals=0
        ),
    )(*args)


def place():
    return lax.axis_index("grp"), lax.axis_index("die")


def shape(*dims, dtype=F32):
    return jax.ShapeDtypeStruct(dims, dtype)


def halves(values):
    high = values.astype(BF16)
    low = (values - high.astype(F32)).astype(BF16)
    return high, low


def spread_body(cap, die_count, blocks, block_ref, out_ref):
    slots = block_ref.shape[1]
    block = jnp.concatenate(
        [block_ref[...], jnp.zeros((1, LANES - slots), jnp.int32)], axis=1
    )
    for die in range(die_count):
        row = (pltpu.roll(block, LANES - die * cap, 1) if die else block) - die * blocks
        for at in range(die, out_ref.shape[0], die_count):
            out_ref[at] = row


def asked_rows(cap, die_count, group, ids_ref):
    for die in range(die_count):
        for slot in range(cap):
            yield die * cap + slot, ids_ref[group * die_count + die, slot]


def pick_body(cap, die_count, ids_ref, plane_ref, out_ref):
    group, _ = place()
    for at, row in asked_rows(cap, die_count, group, ids_ref):
        out_ref[pl.ds(at, 1), :] = plane_ref[pl.ds(row, 1), :]


def build_band(first, pattern, weights):
    place = lax.broadcasted_iota(jnp.int32, (WINDOW, LANES), 0)
    band = None
    for k in range(pattern.shape[0]):
        hit = place == (pattern[k : k + 1, :] - first)
        term = jnp.where(hit, weights[k : k + 1, :], 0.0)
        band = term if band is None else band + term
    fill = jnp.zeros((2 * LANES - WINDOW, LANES), F32)
    return jnp.concatenate(halves(jnp.concatenate([band, fill], axis=0).T), axis=0)


def reciprocal(diag):
    safe = jnp.where(diag > 0.0, diag, 1.0)
    return jnp.where(diag > 0.0, 1.0 / safe, 0.0)


def span(tile, offset=0, size=LANES):
    return pl.ds(pl.multiple_of(tile * LANES + offset, RADIUS), size)


def mixer(coup_ref):
    mix = jnp.concatenate(halves(coup_ref[...]), axis=1)
    return jnp.concatenate([mix, mix], axis=0)


def clear_pads(ref):
    pad = jnp.zeros((RADIUS, 2 * LANES), BF16)
    ref[0:RADIUS, :] = pad
    ref[ref.shape[0] - RADIUS :, :] = pad


def store(ref, tile, values):
    ref[span(tile, RADIUS, values.shape[0]), :] = jnp.concatenate(halves(values), axis=1)


def couple(source, tile, bands, mix, write):
    for at in range(0, len(bands), 4):
        couple_few(source, tile + at, bands[at : at + 4], mix, write)


def couple_few(source, tile, bands, mix, write):
    own = source[span(tile, RADIUS, len(bands) * LANES), :]
    within = jnp.dot(own, mix, preferred_element_type=F32)
    for i, band in enumerate(bands):
        window = source[span(tile + i, 0, WINDOW), :]
        beside = jnp.dot(band[:, :WINDOW], window, preferred_element_type=F32)
        both = beside[:LANES] + beside[LANES:] + within[i * LANES : (i + 1) * LANES]
        write(tile + i, both[:, :LANES] + both[:, LANES:])


def in_chunks(first, count, body, size=16):
    whole = count // size

    @pl.loop(0, whole)
    def _(chunk):
        body(first + chunk * size, size)

    if count % size:
        body(first + whole * size, count % size)


def half_of(tiles):
    half = lax.rem(sum(place()), 2)
    own = tiles // 2
    return half, own, half * own - 1


def prepare_body(
    pat_ref, wgt_ref, coup_ref, volt_hbm, diag_hbm, after_ref,
    band_hbm, base_hbm, inv_hbm, pack_ref, near_ref,
    volt_ref, diag_ref, band_ref, base_ref, inv_ref, plane_ref, sems,
):
    blocks = volt_hbm.shape[0]
    half, own, shift = half_of(blocks // LANES)
    first, count, outer = 1 - half, own + 1, half * (own + 1)
    known = pl.ds(pl.multiple_of(first * LANES, LANES), count * LANES)
    source = pl.ds(pl.multiple_of((first + shift) * LANES, LANES), count * LANES)
    loads = [
        pltpu.make_async_copy(hbm.at[source, :], ref.at[known, :], sems.at[i])
        for i, (hbm, ref) in enumerate(((volt_hbm, volt_ref), (diag_hbm, diag_ref)))
    ]
    for load in loads:
        load.start()
    clear_pads(plane_ref)
    plane_ref[span(outer, RADIUS), :] = jnp.zeros((LANES, 2 * LANES), BF16)
    begin = place()[1] * blocks + shift * LANES

    def bands(tile, size):
        for i in range(size):
            lanes = pl.ds(pl.multiple_of((tile + i + shift) * LANES, LANES), LANES)
            band_ref[tile + i] = build_band(
                begin + (tile + i) * LANES - RADIUS, pat_ref[:, lanes], wgt_ref[:, lanes]
            )

    in_chunks(first, count, bands)
    band_out = pltpu.make_async_copy(
        band_ref.at[pl.ds(first, count)], band_hbm.at[pl.ds(first, count)], sems.at[2]
    )
    band_out.start()
    for load in loads:
        load.wait()

    def spread(tile, size):
        cut = span(tile, 0, size * LANES)
        store(plane_ref, tile, volt_ref[cut, :])
        inv_ref[cut, :] = reciprocal(diag_ref[cut, :])

    in_chunks(first, count, spread)
    inv_out = pltpu.make_async_copy(inv_ref.at[known, :], inv_hbm.at[known, :], sems.at[3])
    inv_out.start()
    mix = mixer(coup_ref)

    def base(tile, size):
        def write(tile, values):
            base_ref[span(tile), :] = values

        couple(plane_ref, tile, [band_ref[tile + i] for i in range(size)], mix, write)
        cut = span(tile, 0, size * LANES)
        pltpu.make_async_copy(base_ref.at[cut, :], base_hbm.at[cut, :], sems.at[4]).start()

    in_chunks(first, count, base)
    edge = 1 + half * (own - 1)
    lanes = pl.ds(pl.multiple_of((edge + shift) * LANES, LANES), LANES)
    neighbours = pat_ref.shape[0]
    pack_ref[0:LANES, :] = volt_ref[span(edge), :]
    pack_ref[LANES : 2 * LANES, :] = diag_ref[span(edge), :]
    at = 2 * LANES
    pack_ref[at : at + neighbours, :] = pat_ref[:, lanes].astype(F32)
    pack_ref[at + neighbours : at + 2 * neighbours, :] = wgt_ref[:, lanes]
    near_ref[0:RADIUS, :] = volt_ref[2 * LANES : 2 * LANES + RADIUS, :]
    near_ref[RADIUS:, :] = volt_ref[own * LANES - RADIUS : own * LANES, :]
    band_out.wait()
    inv_out.wait()
    pltpu.make_async_copy(
        base_ref.at[known, :], base_hbm.at[known, :], sems.at[4]
    ).wait()


def slot_places(cap, ids_ref):
    per_row = LANES // cap
    lane = lax.broadcasted_iota(jnp.int32, (1, LANES), 1)
    places = []
    for at in range(0, ids_ref.shape[0], per_row):
        total = None
        for i in range(per_row):
            row = jnp.where(lane < cap, ids_ref[at + i : at + i + 1, :], 0)
            row = pltpu.roll(row, i * cap, 1) if i else row
            total = row if total is None else total + row
        places.append(total)
    return places


def gather_inflow(places, first, rows, current):
    at = lax.broadcasted_iota(jnp.int32, (rows, LANES), 0) + first
    hits = [jnp.where(at == place, 1.0, 0.0).astype(BF16) for place in places]
    both = jnp.dot(jnp.concatenate(hits, axis=1), current, preferred_element_type=F32)
    return both[:, :LANES] + both[:, LANES:]


def ends_body(cap, tiles, ids_ref, current_ref, out_ref):
    half, _, _ = half_of(tiles)
    places = slot_places(cap, ids_ref)
    current = jnp.concatenate(halves(current_ref[...]), axis=1)
    out_ref[...] = gather_inflow(places, half * (tiles - 1) * LANES, LANES, current)


def inflow_body(
    cap, tiles, ids_ref, current_ref, coup_ref, own_ref, halo_ref, near_ref, after_ref,
    out_ref, band_ref, inv_ref, base_ref, plane_ref,
):
    half, own, shift = half_of(tiles)
    first, count = 1 - half, own + 1
    places = slot_places(cap, ids_ref)
    current = jnp.concatenate(halves(current_ref[...]), axis=1)

    def inflow(tile, size):
        cut = span(tile, 0, size * LANES)
        out_ref[cut, :] = gather_inflow(
            places, (tile + shift) * LANES, size * LANES, current
        )

    in_chunks(first, count, inflow)
    out_ref[span(half * (own + 1)), :] = jnp.zeros((LANES, LANES), F32)

    neighbours = (own_ref.shape[0] - 2 * LANES) // 2
    begin = (place()[1] * tiles + 2 * half * own - 1) * LANES
    packs = [jnp.where(half == at, halo_ref[...], own_ref[...]) for at in range(2)]
    at = 2 * LANES
    bands = []
    for tile, pack in enumerate(packs):
        bands.append(
            build_band(
                begin + tile * LANES - RADIUS,
                pack[at : at + neighbours].astype(jnp.int32),
                pack[at + neighbours : at + 2 * neighbours],
            )
        )
        store(plane_ref, tile, pack[:LANES])
    none = jnp.zeros((RADIUS, 2 * LANES), BF16)
    low, high = (
        jnp.concatenate(halves(near_ref[cut, :]), axis=1)
        for cut in (slice(0, RADIUS), slice(RADIUS, 2 * RADIUS))
    )
    size = plane_ref.shape[0]
    plane_ref[0:RADIUS, :] = jnp.where(half == 0, none, high)
    plane_ref[size - RADIUS : size, :] = jnp.where(half == 0, low, none)
    results = []
    couple(plane_ref, 0, bands, mixer(coup_ref), lambda tile, values: results.append(values))
    band_ref[...] = jnp.where(half == 0, bands[0], bands[1])
    inv_ref[...] = reciprocal(halo_ref[LANES : 2 * LANES, :])
    base_ref[0:LANES, :] = jnp.where(half == 0, results[0], results[1])
    base_ref[LANES:, :] = jnp.where(half == 0, results[1], results[0])


def iterate_body(
    cap, die_count, asked_ref, coup_ref, halo_ref, inflow_ref, band_ref, base_ref, inv_ref,
    halo_band_ref, halo_inv_ref, edge_base_ref, out_hbm, full_hbm, picked_ref, out_ref, here_ref, there_ref, sems,
):
    own = out_hbm.shape[0] // LANES
    half, _, _ = half_of(2 * own)
    first, count, outer = 1 - half, own + 1, half * (own + 1)
    edge = 1 + half * (own - 1)
    for ref in (here_ref, there_ref):
        clear_pads(ref)

    def start(tile, size):
        cut = span(tile, 0, size * LANES)
        store(here_ref, tile, -(inflow_ref[cut, :] + base_ref[cut, :]) * inv_ref[cut, :])

    in_chunks(first, count, start)
    halo_inv = halo_inv_ref[...]
    store(here_ref, outer, -(halo_ref[...] + edge_base_ref[0:LANES, :]) * halo_inv)
    cut = span(edge)
    store(here_ref, edge, -(inflow_ref[cut, :] + edge_base_ref[LANES:, :]) * inv_ref[cut, :])
    mix = mixer(coup_ref)
    refs = (here_ref, there_ref)
    for iteration in range(1, ITERS):
        source, target = refs[(iteration - 1) % 2], refs[iteration % 2]
        last = iteration == ITERS - 1

        def write(tile, coupled, target=target, last=last):
            values = -(inflow_ref[span(tile), :] + coupled) * inv_ref[span(tile), :]
            if last:
                out_ref[span(tile - 1), :] = values
            else:
                store(target, tile, values)

        def step(tile, size, source=source, write=write):
            bands = [band_ref[tile + i] for i in range(size)]
            couple(source, tile, bands, mix, write)

        def final(tile, size, step=step):
            step(tile, size)
            cut = span(tile - 1, 0, size * LANES)
            whole = span(half * own + tile - 1, 0, size * LANES)
            pltpu.make_async_copy(out_ref.at[cut, :], out_hbm.at[cut, :], sems.at[0]).start()
            pltpu.make_async_copy(out_ref.at[cut, :], full_hbm.at[whole, :], sems.at[1]).start()

        def write_halo(tile, coupled, target=target):
            store(target, tile, -(halo_ref[...] + coupled) * halo_inv)

        if last:
            in_chunks(1, own, final)
        else:
            in_chunks(first, count, step)
            couple(source, outer, [halo_band_ref[...]], mix, write_halo)

    base_row = half * own * LANES
    group, _ = place()
    pair = group - lax.rem(group, 2)
    for member in range(2):
        offset = member * (picked_ref.shape[0] // 2)
        for at, row in asked_rows(cap, die_count, pair + member, asked_ref):
            row = row - base_row
            inside = (row >= 0) & (row < own * LANES)
            safe = jnp.clip(row, 0, own * LANES - 1)
            values = out_ref[pl.ds(safe, 1), :]
            picked_ref[pl.ds(offset + at, 1), :] = jnp.where(inside, values, 0.0)
    pltpu.make_async_copy(out_ref, out_hbm, sems.at[0]).wait()
    pltpu.make_async_copy(out_ref, full_hbm.at[0 : own * LANES, :], sems.at[1]).wait()


def join_body(other_ref, full_in_hbm, full_hbm, done_ref, sem):
    rows = other_ref.shape[0]
    half, _, _ = half_of(2 * rows // LANES)
    start = pl.multiple_of((1 - half) * rows, LANES)
    copy = pltpu.make_async_copy(other_ref, full_hbm.at[pl.ds(start, rows), :], sem)
    copy.start()
    done_ref[...] = jnp.zeros(done_ref.shape, F32)
    copy.wait()


def add_body(parts_ref, after_ref, out_ref):
    rows = out_ref.shape[0]
    out_ref[...] = parts_ref[0:rows, :] + parts_ref[rows:, :]


def add_at_nodes(rows, cols, node_ref, part):
    group = 8
    row_at = lax.broadcasted_iota(jnp.int32, (rows, LANES), 0)
    col_at = lax.broadcasted_iota(jnp.int32, (cols, LANES), 0)
    total = jnp.zeros((2 * rows, cols), F32)
    for first in range(0, node_ref.shape[0], group):
        cut = slice(first, first + group)
        node = node_ref[cut, :]
        live = node >= 0
        safe = jnp.where(live, node, 0)
        row, col = safe // cols, safe % cols
        parts = halves(jnp.where(live, part(cut), 0.0))
        left, right = [], []
        for i in range(group):
            spot = jnp.where(row_at == row[i : i + 1, :], 1.0, 0.0).astype(BF16)
            left.append(
                jnp.concatenate([spot * half[i : i + 1, :] for half in parts], axis=0)
            )
            right.append(jnp.where(col_at == col[i : i + 1, :], 1.0, 0.0).astype(BF16))
        total = total + lax.dot_general(
            jnp.concatenate(left, axis=1),
            jnp.concatenate(right, axis=1),
            (((1,), (1,)), ((), ())),
            preferred_element_type=F32,
        )
    return total[:rows] + total[rows:]


def diagonal_body(node_ref, cond_ref, shunt_ref, after_ref, inv_ref):
    rows, cols = shunt_ref.shape
    gsum = add_at_nodes(rows, cols, node_ref, lambda cut: cond_ref[cut, :])
    inv_ref[...] = 1.0 / (4.0 + shunt_ref[...] + gsum)


def scatter_body(node_ref, cond_ref, start_ref, volt_ref, load_ref, inv_ref,
                 right_ref, inner_ref, outer_ref):
    rows, cols = volt_ref.shape
    inject = add_at_nodes(
        rows, cols, node_ref, lambda cut: cond_ref[cut, :] * start_ref[cut, :]
    )
    inv = inv_ref[...]
    right_side = (inject - load_ref[...]) * inv
    right_ref[...] = right_side
    volt = volt_ref[...]
    top, bottom = (
        jnp.concatenate([volt[cut], right_side[cut], inv[cut]], axis=0)
        for cut in (slice(0, HALO_ROWS), slice(rows - HALO_ROWS, rows))
    )
    swap_parts(inner_ref, outer_ref, place()[0], top, bottom)


def swap_parts(inner_ref, outer_ref, mine, first, last):
    even = lax.rem(mine, 2) == 0
    inner_ref[...] = jnp.where(even, last, first)
    outer_ref[...] = jnp.where(even, first, last)


def swapped(inner, outer, mine):
    even = lax.rem(mine, 2) == 0
    return jnp.where(even, outer, inner), jnp.where(even, inner, outer)


def swap(inner, outer, axis):
    count = lax.axis_size(axis)

    def pairs(start):
        return [
            pair
            for i in range(start, count - 1, 2)
            for pair in ((i, i + 1), (i + 1, i))
        ]

    return lax.ppermute(outer, axis, pairs(1)), lax.ppermute(inner, axis, pairs(0))


def extended(own, top, bottom, index):
    cut = slice(index * HALO_ROWS, (index + 1) * HALO_ROWS)
    return jnp.concatenate([own, bottom[cut], top[cut]], axis=0)


def edge_body(volt_ref, right_ref, inv_ref, outer_ref, inner_ref, west_ref, east_ref):
    cols = volt_ref.shape[1]
    top, bottom = swapped(inner_ref[...], outer_ref[...], place()[0])
    out_rows, high = west_ref.shape
    west, east = None, None
    for index, ref in enumerate((volt_ref, right_ref, inv_ref)):
        whole = extended(ref[...], top, bottom, index)
        lane = lax.broadcasted_iota(jnp.int32, (whole.shape[0], LANES), 1)
        head, tail = whole[:, :LANES], whole[:, cols - LANES :]
        at = index * SWEEPS
        head = pltpu.roll(head, at, 1) if at else head
        tail = pltpu.roll(tail, at + SWEEPS, 1)
        west = head if west is None else jnp.where(lane >= at, head, west)
        east = tail if east is None else jnp.where(lane >= at, tail, east)
    fill = jnp.zeros((high - west.shape[0], LANES), F32)
    west, east = (
        jnp.concatenate([part, fill], axis=0).T[:out_rows] for part in (west, east)
    )
    swap_parts(west_ref, east_ref, place()[1], west, east)


def sweep_body(copies, node_ref, cond_ref, start_ref, volt_ref, right_ref, inv_ref,
               row_out_ref, row_in_ref, col_out_ref, col_in_ref, out_ref, current_ref):
    rows, cols = volt_ref.shape
    blocks = node_ref.shape[0]
    cap = current_ref.shape[1]
    whole = []
    top, bottom = swapped(row_in_ref[...], row_out_ref[...], place()[0])
    out_rows, high = col_in_ref.shape
    fill = jnp.zeros((LANES - out_rows, high), F32)
    wests, easts = (
        jnp.concatenate([part, fill], axis=0).T[: rows + 2 * HALO_ROWS]
        for part in swapped(col_in_ref[...], col_out_ref[...], place()[1])
    )
    eastern = lax.broadcasted_iota(jnp.int32, easts.shape, 1) < LANES // 2
    for index, ref in enumerate((volt_ref, right_ref, inv_ref)):
        own = extended(ref[...], top, bottom, index)
        at = index * SWEEPS
        west = pltpu.roll(wests, LANES - SWEEPS - at, 1)
        east = pltpu.roll(easts, LANES - at, 1) if at else easts
        whole.append(jnp.concatenate([own, jnp.where(eastern, east, west)], axis=1))
    volt, right_side, inv = whole
    high, wide = volt.shape
    for weight in sweep_weights(SWEEPS):
        beside = (
            pltpu.roll(volt, 1, 0)
            + pltpu.roll(volt, high - 1, 0)
            + pltpu.roll(volt, 1, 1)
            + pltpu.roll(volt, wide - 1, 1)
        )
        volt = (1.0 - weight) * volt + weight * (right_side + beside * inv)
    volt = volt[:rows, :cols]
    out_ref[...] = volt
    both = jnp.concatenate(halves(volt), axis=0)
    group = 8
    row_at = lax.broadcasted_iota(jnp.int32, (rows, LANES), 0)
    col_at = lax.broadcasted_iota(jnp.int32, (cols, LANES), 0)
    dies = blocks // cap
    for first in range(0, blocks, group):
        node = node_ref[first : first + group, :]
        live = node >= 0
        cond = jnp.where(live, cond_ref[first : first + group, :], 0.0)
        safe = jnp.where(live, node, 0)
        row, col = safe // cols, safe % cols
        spots = jnp.concatenate(
            [
                jnp.where(col_at == col[i : i + 1, :], 1.0, 0.0).astype(BF16)
                for i in range(group)
            ],
            axis=1,
        )
        found = jnp.dot(both, spots, preferred_element_type=F32)
        found = found[:rows] + found[rows:]
        for i in range(group):
            mine = found[:, i * LANES : (i + 1) * LANES]
            at_bump = jnp.sum(
                jnp.where(row_at == row[i : i + 1, :], mine, 0.0), axis=0, keepdims=True
            )
            block = first + i
            current = cond[i : i + 1, :] * (start_ref[block : block + 1, :] - at_bump)
            current_ref[block // cap, block % cap : block % cap + 1, :] = current
    for copy in range(1, copies):
        current_ref[copy * dies : (copy + 1) * dies] = current_ref[0:dies]


def local(
    die_volt,
    die_load,
    die_shunt,
    bump_node,
    bump_block,
    bump_cond,
    pkg_volt,
    pkg_diag,
    pkg_pattern,
    pkg_weight,
    block_coupling,
):
    die_count = lax.axis_size("die")
    group_count = lax.axis_size("grp")
    devices = die_count * group_count
    blocks = pkg_volt.shape[0]
    tiles = blocks // LANES
    neighbours = pkg_pattern.shape[0]
    slots = bump_block.shape[0]
    cap = slots // die_count
    rows, cols = die_volt.shape
    (spread,) = call(
        functools.partial(spread_body, cap, die_count, blocks),
        "spread_blocks",
        [shape(devices, 1, LANES, dtype=jnp.int32)],
        (bump_block.reshape(1, slots),),
        [VMEM],
    )
    ids = lax.all_to_all(
        spread, ("grp", "die"), split_axis=0, concat_axis=0, tiled=True
    ).reshape(devices, LANES)

    (picked,) = call(
        functools.partial(pick_body, cap, die_count),
        "pick_rows",
        [shape(slots, LANES)],
        (ids, pkg_volt),
        [SMEM, VMEM],
    )
    bump_start = lax.all_to_all(
        picked.reshape(die_count, cap, LANES), "die", split_axis=0, concat_axis=0, tiled=True
    ).reshape(slots, LANES)

    (inv,) = call(
        diagonal_body,
        "die_diagonal",
        [shape(rows, cols)],
        (bump_node, bump_cond, die_shunt, picked),
        [VMEM] * 3 + [ANY],
        work=3,
    )
    right_side, *edges = call(
        scatter_body,
        "scatter_bumps",
        [shape(rows, cols)] + [shape(3 * HALO_ROWS, cols)] * 2,
        (bump_node, bump_cond, bump_start, die_volt, die_load, inv),
        [VMEM] * 6,
        work=3,
    )
    beside = swap(*edges, "grp")

    edge_rows = -(-3 * SWEEPS // 8) * 8
    edge_cols = -(-(rows + 2 * HALO_ROWS) // LANES) * LANES
    edges = call(
        edge_body,
        "edge_columns",
        [shape(edge_rows, edge_cols)] * 2,
        (die_volt, right_side, inv, *beside),
        [VMEM] * 5,
    )
    columns = swap(*edges, "die")

    die_out, current = call(
        functools.partial(sweep_body, group_count),
        "sweeps",
        [shape(rows, cols), shape(devices, cap, LANES)],
        (bump_node, bump_cond, bump_start, die_volt, right_side, inv, *beside, *columns),
        [VMEM] * 10,
        work=4,
    )
    own = tiles // 2
    dma = pltpu.SemaphoreType.DMA
    plane = pltpu.VMEM(((own + 2) * LANES + 2 * RADIUS, 2 * LANES), BF16)
    range_rows = pltpu.VMEM(((own + 2) * LANES, LANES), F32)
    range_bands = pltpu.VMEM((own + 2, 2 * LANES, 2 * LANES), BF16)
    pack_rows = 2 * LANES + 2 * neighbours
    band, base, pkg_inv, pack, near = call(
        prepare_body,
        "package_prepare",
        [
            shape(own + 2, 2 * LANES, 2 * LANES, dtype=BF16),
            shape((own + 2) * LANES, LANES),
            shape((own + 2) * LANES, LANES),
            shape(pack_rows, LANES),
            shape(2 * RADIUS, LANES),
        ],
        (pkg_pattern, pkg_weight, block_coupling, pkg_volt, pkg_diag, die_out),
        [VMEM] * 3 + [HBM] * 3,
        [range_rows, range_rows, range_bands, range_rows, range_rows, plane, dma((5,))],
        work=7,
        vmem=MOST_VMEM,
        out_specs=[HBM] * 3 + [VMEM] * 2,
    )

    current = lax.all_to_all(
        current, ("grp", "die"), split_axis=0, concat_axis=0, tiled=True
    ).reshape(devices * cap, LANES)

    beside_end = [
        (g * die_count + a, g * die_count + b)
        for g in range(group_count)
        for d in range((g + 1) % 2, die_count - 1, 2)
        for a, b in ((d, d + 1), (d + 1, d))
    ]
    halo = lax.ppermute(pack, ("grp", "die"), beside_end)
    (inflow,) = call(
        functools.partial(ends_body, cap, tiles),
        "package_end",
        [shape(LANES, LANES)],
        (ids, current),
        [VMEM, VMEM],
    )
    halo_inflow = lax.ppermute(inflow, ("grp", "die"), beside_end)
    all_inflow, halo_band, halo_inv, edge_base = call(
        functools.partial(inflow_body, cap, tiles),
        "package_inflow",
        [
            shape((own + 2) * LANES, LANES),
            shape(2 * LANES, 2 * LANES, dtype=BF16),
            shape(LANES, LANES),
            shape(2 * LANES, LANES),
        ],
        (ids, current, block_coupling, pack, halo, near, inflow),
        [VMEM] * 6 + [ANY],
        [pltpu.VMEM((2 * LANES + 2 * RADIUS, 2 * LANES), BF16)],
        work=3,
    )
    half_out, pkg_out, picked = call(
        functools.partial(iterate_body, cap, die_count),
        "package_iterations",
        [shape(own * LANES, LANES), shape(blocks, LANES), shape(2 * slots, LANES)],
        (
            ids, block_coupling, halo_inflow, all_inflow, band, base, pkg_inv,
            halo_band, halo_inv, edge_base,
        ),
        [SMEM] + [VMEM] * 9,
        [pltpu.VMEM((own * LANES, LANES), F32), plane, plane, dma((2,))],
        work=10,
        vmem=24,
        out_specs=[HBM, HBM, VMEM],
    )
    pair = 2 * die_count
    parts = lax.all_to_all(
        picked.reshape(pair, cap, LANES),
        ("grp", "die"),
        split_axis=0,
        concat_axis=0,
        axis_index_groups=[
            [first + i for i in range(pair)] for first in range(0, devices, pair)
        ],
        tiled=True,
    ).reshape(2 * slots, LANES)
    other = lax.ppermute(half_out, "grp", [(g, g ^ 1) for g in range(group_count)])
    pkg_out, done = call(
        join_body,
        "join_halves",
        [shape(blocks, LANES), shape(8, LANES)],
        (other, pkg_out),
        [VMEM, HBM],
        [dma(())],
        out_specs=[HBM, VMEM],
        aliases={1: 0},
    )
    (bump_out,) = call(
        add_body, "add_parts", [shape(slots, LANES)], (parts, done), [VMEM, ANY]
    )
    return (die_out, pkg_out, bump_out)


def solution(mesh):
    return jax.shard_map(
        local,
        mesh=mesh,
        in_specs=(
            P("grp", "die"),
            P("grp", "die"),
            P("grp", "die"),
            P(("grp", "die"), None),
            P(("grp", "die")),
            P(("grp", "die"), None),
            P("die", None),
            P("die", None),
            P(None, "die"),
            P(None, "die"),
            P(),
        ),
        out_specs=(P("grp", "die"), P("die", None), P(("grp", "die"), None)),
        check_vma=False,
    )
```

```python
import functools
import math

import jax
import jax.numpy as jnp
from jax import lax
from jax.experimental import pallas as pl
from jax.experimental.pallas import tpu as pltpu
from jax.sharding import PartitionSpec as P

RADIUS = 32
SWEEPS = 4
ITERS = 4
LANES = 128
HALO_ROWS = 8
REACH = RADIUS * ITERS
WINDOW = LANES + 2 * RADIUS
F32 = jnp.float32
BF16 = jnp.bfloat16
MOST_VMEM = 57
VMEM = pl.BlockSpec(memory_space=pltpu.VMEM)
SMEM = pl.BlockSpec(memory_space=pltpu.SMEM)
ANY = pl.BlockSpec(memory_space=pl.ANY)
HBM = pl.BlockSpec(memory_space=pltpu.HBM)


def sweep_weights(sweeps):
    return [
        1.0 / (1.0 + 0.8 * math.cos(math.pi * (2 * index + 1) / (2 * sweeps)))
        for index in range(sweeps)
    ]


def call(
    body, name, outs, args, specs, scratch=(), work=1, vmem=16, out_specs=None, aliases=None
):
    bytes_accessed = sum(4 * math.prod(arg.shape) for arg in args)
    return pl.pallas_call(
        body,
        name=name,
        out_shape=outs,
        in_specs=specs,
        out_specs=out_specs or [VMEM] * len(outs),
        input_output_aliases=aliases or {},
        scratch_shapes=list(scratch),
        compiler_params=pltpu.CompilerParams(vmem_limit_bytes=vmem * 1024 * 1024),
        cost_estimate=pl.CostEstimate(
            flops=work * 10**9, bytes_accessed=bytes_accessed, transcendentals=0
        ),
    )(*args)


def place():
    return lax.axis_index("grp"), lax.axis_index("die")


def shape(*dims, dtype=F32):
    return jax.ShapeDtypeStruct(dims, dtype)


def halves(values):
    high = values.astype(BF16)
    low = (values - high.astype(F32)).astype(BF16)
    return high, low


def spread_body(cap, die_count, blocks, block_ref, out_ref):
    slots = block_ref.shape[1]
    block = jnp.concatenate(
        [block_ref[...], jnp.zeros((1, LANES - slots), jnp.int32)], axis=1
    )
    for die in range(die_count):
        row = (pltpu.roll(block, LANES - die * cap, 1) if die else block) - die * blocks
        for at in range(die, out_ref.shape[0], die_count):
            out_ref[at] = row


def asked_rows(cap, die_count, group, ids_ref):
    for die in range(die_count):
        for slot in range(cap):
            yield die * cap + slot, ids_ref[group * die_count + die, slot]


def pick_body(cap, die_count, ids_ref, plane_ref, out_ref):
    group, _ = place()
    for at, row in asked_rows(cap, die_count, group, ids_ref):
        out_ref[pl.ds(at, 1), :] = plane_ref[pl.ds(row, 1), :]


def build_band(first, pattern, weights):
    place = lax.broadcasted_iota(jnp.int32, (WINDOW, LANES), 0)
    band = None
    for k in range(pattern.shape[0]):
        hit = place == (pattern[k : k + 1, :] - first)
        term = jnp.where(hit, weights[k : k + 1, :], 0.0)
        band = term if band is None else band + term
    fill = jnp.zeros((2 * LANES - WINDOW, LANES), F32)
    return jnp.concatenate(halves(jnp.concatenate([band, fill], axis=0).T), axis=0)


def reciprocal(diag):
    safe = jnp.where(diag > 0.0, diag, 1.0)
    return jnp.where(diag > 0.0, 1.0 / safe, 0.0)


def span(tile, offset=0, size=LANES):
    return pl.ds(pl.multiple_of(tile * LANES + offset, RADIUS), size)


def mixer(coup_ref):
    mix = jnp.concatenate(halves(coup_ref[...]), axis=1)
    return jnp.concatenate([mix, mix], axis=0)


def clear_pads(ref):
    pad = jnp.zeros((RADIUS, 2 * LANES), BF16)
    ref[0:RADIUS, :] = pad
    ref[ref.shape[0] - RADIUS :, :] = pad


def store(ref, tile, values):
    ref[span(tile, RADIUS, values.shape[0]), :] = jnp.concatenate(halves(values), axis=1)


def couple(source, tile, bands, mix, write):
    for at in range(0, len(bands), 4):
        couple_few(source, tile + at, bands[at : at + 4], mix, write)


def couple_few(source, tile, bands, mix, write):
    own = source[span(tile, RADIUS, len(bands) * LANES), :]
    within = jnp.dot(own, mix, preferred_element_type=F32)
    for i, band in enumerate(bands):
        window = source[span(tile + i, 0, WINDOW), :]
        beside = jnp.dot(band[:, :WINDOW], window, preferred_element_type=F32)
        both = beside[:LANES] + beside[LANES:] + within[i * LANES : (i + 1) * LANES]
        write(tile + i, both[:, :LANES] + both[:, LANES:])


def in_chunks(first, count, body, size=16):
    whole = count // size

    @pl.loop(0, whole)
    def _(chunk):
        body(first + chunk * size, size)

    if count % size:
        body(first + whole * size, count % size)


def half_of(tiles):
    half = lax.rem(sum(place()), 2)
    own = tiles // 2
    return half, own, half * own - 1


def prepare_body(
    pat_ref, wgt_ref, coup_ref, volt_hbm, diag_hbm, after_ref,
    band_hbm, base_hbm, inv_hbm, pack_ref, near_ref,
    volt_ref, diag_ref, band_ref, base_ref, inv_ref, plane_ref, sems,
):
    blocks = volt_hbm.shape[0]
    half, own, shift = half_of(blocks // LANES)
    first, count, outer = 1 - half, own + 1, half * (own + 1)
    known = pl.ds(pl.multiple_of(first * LANES, LANES), count * LANES)
    source = pl.ds(pl.multiple_of((first + shift) * LANES, LANES), count * LANES)
    loads = [
        pltpu.make_async_copy(hbm.at[source, :], ref.at[known, :], sems.at[i])
        for i, (hbm, ref) in enumerate(((volt_hbm, volt_ref), (diag_hbm, diag_ref)))
    ]
    for load in loads:
        load.start()
    clear_pads(plane_ref)
    plane_ref[span(outer, RADIUS), :] = jnp.zeros((LANES, 2 * LANES), BF16)
    begin = place()[1] * blocks + shift * LANES

    def bands(tile, size):
        for i in range(size):
            lanes = pl.ds(pl.multiple_of((tile + i + shift) * LANES, LANES), LANES)
            band_ref[tile + i] = build_band(
                begin + (tile + i) * LANES - RADIUS, pat_ref[:, lanes], wgt_ref[:, lanes]
            )

    in_chunks(first, count, bands, 8)
    band_out = pltpu.make_async_copy(
        band_ref.at[pl.ds(first, count)], band_hbm.at[pl.ds(first, count)], sems.at[2]
    )
    band_out.start()
    for load in loads:
        load.wait()

    def spread(tile, size):
        cut = span(tile, 0, size * LANES)
        store(plane_ref, tile, volt_ref[cut, :])
        inv_ref[cut, :] = reciprocal(diag_ref[cut, :])

    in_chunks(first, count, spread)
    inv_out = pltpu.make_async_copy(inv_ref.at[known, :], inv_hbm.at[known, :], sems.at[3])
    inv_out.start()
    mix = mixer(coup_ref)

    def base(tile, size):
        def write(tile, values):
            base_ref[span(tile), :] = values

        couple(plane_ref, tile, [band_ref[tile + i] for i in range(size)], mix, write)
        cut = span(tile, 0, size * LANES)
        pltpu.make_async_copy(base_ref.at[cut, :], base_hbm.at[cut, :], sems.at[4]).start()

    in_chunks(first, count, base)
    edge = 1 + half * (own - 1)
    lanes = pl.ds(pl.multiple_of((edge + shift) * LANES, LANES), LANES)
    neighbours = pat_ref.shape[0]
    pack_ref[0:LANES, :] = volt_ref[span(edge), :]
    pack_ref[LANES : 2 * LANES, :] = diag_ref[span(edge), :]
    at = 2 * LANES
    pack_ref[at : at + neighbours, :] = pat_ref[:, lanes].astype(F32)
    pack_ref[at + neighbours : at + 2 * neighbours, :] = wgt_ref[:, lanes]
    near_ref[0:RADIUS, :] = volt_ref[2 * LANES : 2 * LANES + RADIUS, :]
    near_ref[RADIUS:, :] = volt_ref[own * LANES - RADIUS : own * LANES, :]
    band_out.wait()
    inv_out.wait()
    pltpu.make_async_copy(
        base_ref.at[known, :], base_hbm.at[known, :], sems.at[4]
    ).wait()


def slot_places(cap, ids_ref):
    per_row = LANES // cap
    lane = lax.broadcasted_iota(jnp.int32, (1, LANES), 1)
    places = []
    for at in range(0, ids_ref.shape[0], per_row):
        total = None
        for i in range(per_row):
            row = jnp.where(lane < cap, ids_ref[at + i : at + i + 1, :], 0)
            row = pltpu.roll(row, i * cap, 1) if i else row
            total = row if total is None else total + row
        places.append(total)
    return places


def gather_inflow(places, first, rows, current):
    at = lax.broadcasted_iota(jnp.int32, (rows, LANES), 0) + first
    hits = [jnp.where(at == place, 1.0, 0.0).astype(BF16) for place in places]
    both = jnp.dot(jnp.concatenate(hits, axis=1), current, preferred_element_type=F32)
    return both[:, :LANES] + both[:, LANES:]


def ends_body(cap, tiles, ids_ref, current_ref, out_ref):
    half, _, _ = half_of(tiles)
    places = slot_places(cap, ids_ref)
    current = jnp.concatenate(halves(current_ref[...]), axis=1)
    out_ref[...] = gather_inflow(places, half * (tiles - 1) * LANES, LANES, current)


def inflow_body(
    cap, tiles, ids_ref, current_ref, coup_ref, own_ref, halo_ref, near_ref, after_ref,
    out_ref, band_ref, inv_ref, base_ref, plane_ref,
):
    half, own, shift = half_of(tiles)
    first, count = 1 - half, own + 1
    places = slot_places(cap, ids_ref)
    current = jnp.concatenate(halves(current_ref[...]), axis=1)

    def inflow(tile, size):
        cut = span(tile, 0, size * LANES)
        out_ref[cut, :] = gather_inflow(
            places, (tile + shift) * LANES, size * LANES, current
        )

    in_chunks(first, count, inflow)
    out_ref[span(half * (own + 1)), :] = jnp.zeros((LANES, LANES), F32)

    neighbours = (own_ref.shape[0] - 2 * LANES) // 2
    begin = (place()[1] * tiles + 2 * half * own - 1) * LANES
    packs = [jnp.where(half == at, halo_ref[...], own_ref[...]) for at in range(2)]
    at = 2 * LANES
    bands = []
    for tile, pack in enumerate(packs):
        bands.append(
            build_band(
                begin + tile * LANES - RADIUS,
                pack[at : at + neighbours].astype(jnp.int32),
                pack[at + neighbours : at + 2 * neighbours],
            )
        )
        store(plane_ref, tile, pack[:LANES])
    none = jnp.zeros((RADIUS, 2 * LANES), BF16)
    low, high = (
        jnp.concatenate(halves(near_ref[cut, :]), axis=1)
        for cut in (slice(0, RADIUS), slice(RADIUS, 2 * RADIUS))
    )
    size = plane_ref.shape[0]
    plane_ref[0:RADIUS, :] = jnp.where(half == 0, none, high)
    plane_ref[size - RADIUS : size, :] = jnp.where(half == 0, low, none)
    results = []
    couple(plane_ref, 0, bands, mixer(coup_ref), lambda tile, values: results.append(values))
    band_ref[...] = jnp.where(half == 0, bands[0], bands[1])
    inv_ref[...] = reciprocal(halo_ref[LANES : 2 * LANES, :])
    base_ref[0:LANES, :] = jnp.where(half == 0, results[0], results[1])
    base_ref[LANES:, :] = jnp.where(half == 0, results[1], results[0])


def iterate_body(
    cap, die_count, asked_ref, coup_ref, halo_ref, inflow_ref, band_ref, base_ref, inv_ref,
    halo_band_ref, halo_inv_ref, edge_base_ref, out_hbm, full_hbm, picked_ref, out_ref, here_ref, there_ref, sems,
):
    own = out_hbm.shape[0] // LANES
    half, _, _ = half_of(2 * own)
    first, count, outer = 1 - half, own + 1, half * (own + 1)
    edge = 1 + half * (own - 1)
    for ref in (here_ref, there_ref):
        clear_pads(ref)

    def start(tile, size):
        cut = span(tile, 0, size * LANES)
        store(here_ref, tile, -(inflow_ref[cut, :] + base_ref[cut, :]) * inv_ref[cut, :])

    in_chunks(first, count, start)
    halo_inv = halo_inv_ref[...]
    store(here_ref, outer, -(halo_ref[...] + edge_base_ref[0:LANES, :]) * halo_inv)
    cut = span(edge)
    store(here_ref, edge, -(inflow_ref[cut, :] + edge_base_ref[LANES:, :]) * inv_ref[cut, :])
    mix = mixer(coup_ref)
    refs = (here_ref, there_ref)
    for iteration in range(1, ITERS):
        source, target = refs[(iteration - 1) % 2], refs[iteration % 2]
        last = iteration == ITERS - 1

        def write(tile, coupled, target=target, last=last):
            values = -(inflow_ref[span(tile), :] + coupled) * inv_ref[span(tile), :]
            if last:
                out_ref[span(tile - 1), :] = values
            else:
                store(target, tile, values)

        def step(tile, size, source=source, write=write):
            bands = [band_ref[tile + i] for i in range(size)]
            couple(source, tile, bands, mix, write)

        def final(tile, size, step=step):
            step(tile, size)
            cut = span(tile - 1, 0, size * LANES)
            whole = span(half * own + tile - 1, 0, size * LANES)
            pltpu.make_async_copy(out_ref.at[cut, :], out_hbm.at[cut, :], sems.at[0]).start()
            pltpu.make_async_copy(out_ref.at[cut, :], full_hbm.at[whole, :], sems.at[1]).start()

        def write_halo(tile, coupled, target=target):
            store(target, tile, -(halo_ref[...] + coupled) * halo_inv)

        if last:
            in_chunks(1, own, final)
        else:
            in_chunks(first, count, step)
            couple(source, outer, [halo_band_ref[...]], mix, write_halo)

    base_row = half * own * LANES
    group, _ = place()
    pair = group - lax.rem(group, 2)
    for member in range(2):
        offset = member * (picked_ref.shape[0] // 2)
        for at, row in asked_rows(cap, die_count, pair + member, asked_ref):
            row = row - base_row
            inside = (row >= 0) & (row < own * LANES)
            safe = jnp.clip(row, 0, own * LANES - 1)
            values = out_ref[pl.ds(safe, 1), :]
            picked_ref[pl.ds(offset + at, 1), :] = jnp.where(inside, values, 0.0)
    pltpu.make_async_copy(out_ref, out_hbm, sems.at[0]).wait()
    pltpu.make_async_copy(out_ref, full_hbm.at[0 : own * LANES, :], sems.at[1]).wait()


def join_body(other_ref, full_in_hbm, full_hbm, done_ref, sem):
    rows = other_ref.shape[0]
    half, _, _ = half_of(2 * rows // LANES)
    start = pl.multiple_of((1 - half) * rows, LANES)
    copy = pltpu.make_async_copy(other_ref, full_hbm.at[pl.ds(start, rows), :], sem)
    copy.start()
    done_ref[...] = jnp.zeros(done_ref.shape, F32)
    copy.wait()


def add_body(parts_ref, after_ref, out_ref):
    rows = out_ref.shape[0]
    out_ref[...] = parts_ref[0:rows, :] + parts_ref[rows:, :]


def scatter_body(cols, node_ref, cond_ref, start_ref, volt_ref, load_ref, shunt_ref,
                 right_ref, inv_ref, inner_ref, outer_ref):
    blocks = node_ref.shape[0]
    rows = volt_ref.shape[0]
    group = 8
    row_at = lax.broadcasted_iota(jnp.int32, (rows, LANES), 0)
    col_at = lax.broadcasted_iota(jnp.int32, (cols, LANES), 0)
    total = jnp.zeros((4 * rows, cols), F32)
    for first in range(0, blocks, group):
        node = node_ref[first : first + group, :]
        live = node >= 0
        cond = jnp.where(live, cond_ref[first : first + group, :], 0.0)
        flow = cond * start_ref[first : first + group, :]
        safe = jnp.where(live, node, 0)
        row, col = safe // cols, safe % cols
        parts = halves(cond) + halves(flow)
        left, right = [], []
        for i in range(group):
            spot = jnp.where(row_at == row[i : i + 1, :], 1.0, 0.0).astype(BF16)
            left.append(
                jnp.concatenate([spot * part[i : i + 1, :] for part in parts], axis=0)
            )
            right.append(jnp.where(col_at == col[i : i + 1, :], 1.0, 0.0).astype(BF16))
        total = total + lax.dot_general(
            jnp.concatenate(left, axis=1),
            jnp.concatenate(right, axis=1),
            (((1,), (1,)), ((), ())),
            preferred_element_type=F32,
        )
    gsum = total[:rows] + total[rows : 2 * rows]
    inject = total[2 * rows : 3 * rows] + total[3 * rows :]
    inv = 1.0 / (4.0 + shunt_ref[...] + gsum)
    right_side = (inject - load_ref[...]) * inv
    right_ref[...] = right_side
    inv_ref[...] = inv
    volt = volt_ref[...]
    top, bottom = (
        jnp.concatenate([volt[cut], right_side[cut], inv[cut]], axis=0)
        for cut in (slice(0, HALO_ROWS), slice(rows - HALO_ROWS, rows))
    )
    swap_parts(inner_ref, outer_ref, place()[0], top, bottom)


def swap_parts(inner_ref, outer_ref, mine, first, last):
    even = lax.rem(mine, 2) == 0
    inner_ref[...] = jnp.where(even, last, first)
    outer_ref[...] = jnp.where(even, first, last)


def swapped(inner, outer, mine):
    even = lax.rem(mine, 2) == 0
    return jnp.where(even, outer, inner), jnp.where(even, inner, outer)


def swap(inner, outer, axis):
    count = lax.axis_size(axis)

    def pairs(start):
        return [
            pair
            for i in range(start, count - 1, 2)
            for pair in ((i, i + 1), (i + 1, i))
        ]

    return lax.ppermute(outer, axis, pairs(1)), lax.ppermute(inner, axis, pairs(0))


def extended(own, top, bottom, index):
    cut = slice(index * HALO_ROWS, (index + 1) * HALO_ROWS)
    return jnp.concatenate([own, bottom[cut], top[cut]], axis=0)


def edge_body(volt_ref, right_ref, inv_ref, outer_ref, inner_ref, west_ref, east_ref):
    cols = volt_ref.shape[1]
    top, bottom = swapped(inner_ref[...], outer_ref[...], place()[0])
    out_rows, high = west_ref.shape
    west, east = None, None
    for index, ref in enumerate((volt_ref, right_ref, inv_ref)):
        whole = extended(ref[...], top, bottom, index)
        lane = lax.broadcasted_iota(jnp.int32, (whole.shape[0], LANES), 1)
        head, tail = whole[:, :LANES], whole[:, cols - LANES :]
        at = index * SWEEPS
        head = pltpu.roll(head, at, 1) if at else head
        tail = pltpu.roll(tail, at + SWEEPS, 1)
        west = head if west is None else jnp.where(lane >= at, head, west)
        east = tail if east is None else jnp.where(lane >= at, tail, east)
    fill = jnp.zeros((high - west.shape[0], LANES), F32)
    west, east = (
        jnp.concatenate([part, fill], axis=0).T[:out_rows] for part in (west, east)
    )
    swap_parts(west_ref, east_ref, place()[1], west, east)


def sweep_body(copies, node_ref, cond_ref, start_ref, volt_ref, right_ref, inv_ref,
               row_out_ref, row_in_ref, col_out_ref, col_in_ref, out_ref, current_ref):
    rows, cols = volt_ref.shape
    blocks = node_ref.shape[0]
    cap = current_ref.shape[1]
    whole = []
    top, bottom = swapped(row_in_ref[...], row_out_ref[...], place()[0])
    out_rows, high = col_in_ref.shape
    fill = jnp.zeros((LANES - out_rows, high), F32)
    wests, easts = (
        jnp.concatenate([part, fill], axis=0).T[: rows + 2 * HALO_ROWS]
        for part in swapped(col_in_ref[...], col_out_ref[...], place()[1])
    )
    eastern = lax.broadcasted_iota(jnp.int32, easts.shape, 1) < LANES // 2
    for index, ref in enumerate((volt_ref, right_ref, inv_ref)):
        own = extended(ref[...], top, bottom, index)
        at = index * SWEEPS
        west = pltpu.roll(wests, LANES - SWEEPS - at, 1)
        east = pltpu.roll(easts, LANES - at, 1) if at else easts
        whole.append(jnp.concatenate([own, jnp.where(eastern, east, west)], axis=1))
    volt, right_side, inv = whole
    high, wide = volt.shape
    for weight in sweep_weights(SWEEPS):
        beside = (
            pltpu.roll(volt, 1, 0)
            + pltpu.roll(volt, high - 1, 0)
            + pltpu.roll(volt, 1, 1)
            + pltpu.roll(volt, wide - 1, 1)
        )
        volt = (1.0 - weight) * volt + weight * (right_side + beside * inv)
    volt = volt[:rows, :cols]
    out_ref[...] = volt
    both = jnp.concatenate(halves(volt), axis=0)
    group = 8
    row_at = lax.broadcasted_iota(jnp.int32, (rows, LANES), 0)
    col_at = lax.broadcasted_iota(jnp.int32, (cols, LANES), 0)
    dies = blocks // cap
    for first in range(0, blocks, group):
        node = node_ref[first : first + group, :]
        live = node >= 0
        cond = jnp.where(live, cond_ref[first : first + group, :], 0.0)
        safe = jnp.where(live, node, 0)
        row, col = safe // cols, safe % cols
        spots = jnp.concatenate(
            [
                jnp.where(col_at == col[i : i + 1, :], 1.0, 0.0).astype(BF16)
                for i in range(group)
            ],
            axis=1,
        )
        found = jnp.dot(both, spots, preferred_element_type=F32)
        found = found[:rows] + found[rows:]
        for i in range(group):
            mine = found[:, i * LANES : (i + 1) * LANES]
            at_bump = jnp.sum(
                jnp.where(row_at == row[i : i + 1, :], mine, 0.0), axis=0, keepdims=True
            )
            block = first + i
            current = cond[i : i + 1, :] * (start_ref[block : block + 1, :] - at_bump)
            current_ref[block // cap, block % cap : block % cap + 1, :] = current
    for copy in range(1, copies):
        current_ref[copy * dies : (copy + 1) * dies] = current_ref[0:dies]


def local(
    die_volt,
    die_load,
    die_shunt,
    bump_node,
    bump_block,
    bump_cond,
    pkg_volt,
    pkg_diag,
    pkg_pattern,
    pkg_weight,
    block_coupling,
):
    die_count = lax.axis_size("die")
    group_count = lax.axis_size("grp")
    devices = die_count * group_count
    blocks = pkg_volt.shape[0]
    tiles = blocks // LANES
    neighbours = pkg_pattern.shape[0]
    slots = bump_block.shape[0]
    cap = slots // die_count
    rows, cols = die_volt.shape
    (spread,) = call(
        functools.partial(spread_body, cap, die_count, blocks),
        "spread_blocks",
        [shape(devices, 1, LANES, dtype=jnp.int32)],
        (bump_block.reshape(1, slots),),
        [VMEM],
    )
    ids = lax.all_to_all(
        spread, ("grp", "die"), split_axis=0, concat_axis=0, tiled=True
    ).reshape(devices, LANES)

    (picked,) = call(
        functools.partial(pick_body, cap, die_count),
        "pick_rows",
        [shape(slots, LANES)],
        (ids, pkg_volt),
        [SMEM, VMEM],
    )
    bump_start = lax.all_to_all(
        picked.reshape(die_count, cap, LANES), "die", split_axis=0, concat_axis=0, tiled=True
    ).reshape(slots, LANES)

    right_side, inv, *edges = call(
        functools.partial(scatter_body, cols),
        "scatter_bumps",
        [shape(rows, cols)] * 2 + [shape(3 * HALO_ROWS, cols)] * 2,
        (bump_node, bump_cond, bump_start, die_volt, die_load, die_shunt),
        [VMEM] * 6,
        work=3,
    )
    beside = swap(*edges, "grp")

    edge_rows = -(-3 * SWEEPS // 8) * 8
    edge_cols = -(-(rows + 2 * HALO_ROWS) // LANES) * LANES
    edges = call(
        edge_body,
        "edge_columns",
        [shape(edge_rows, edge_cols)] * 2,
        (die_volt, right_side, inv, *beside),
        [VMEM] * 5,
    )
    columns = swap(*edges, "die")

    die_out, current = call(
        functools.partial(sweep_body, group_count),
        "sweeps",
        [shape(rows, cols), shape(devices, cap, LANES)],
        (bump_node, bump_cond, bump_start, die_volt, right_side, inv, *beside, *columns),
        [VMEM] * 10,
        work=4,
    )
    own = tiles // 2
    dma = pltpu.SemaphoreType.DMA
    plane = pltpu.VMEM(((own + 2) * LANES + 2 * RADIUS, 2 * LANES), BF16)
    range_rows = pltpu.VMEM(((own + 2) * LANES, LANES), F32)
    range_bands = pltpu.VMEM((own + 2, 2 * LANES, 2 * LANES), BF16)
    pack_rows = 2 * LANES + 2 * neighbours
    band, base, pkg_inv, pack, near = call(
        prepare_body,
        "package_prepare",
        [
            shape(own + 2, 2 * LANES, 2 * LANES, dtype=BF16),
            shape((own + 2) * LANES, LANES),
            shape((own + 2) * LANES, LANES),
            shape(pack_rows, LANES),
            shape(2 * RADIUS, LANES),
        ],
        (pkg_pattern, pkg_weight, block_coupling, pkg_volt, pkg_diag, die_out),
        [VMEM] * 3 + [HBM] * 3,
        [range_rows, range_rows, range_bands, range_rows, range_rows, plane, dma((5,))],
        work=7,
        vmem=MOST_VMEM,
        out_specs=[HBM] * 3 + [VMEM] * 2,
    )

    current = lax.all_to_all(
        current, ("grp", "die"), split_axis=0, concat_axis=0, tiled=True
    ).reshape(devices * cap, LANES)

    beside_end = [
        (g * die_count + a, g * die_count + b)
        for g in range(group_count)
        for d in range((g + 1) % 2, die_count - 1, 2)
        for a, b in ((d, d + 1), (d + 1, d))
    ]
    halo = lax.ppermute(pack, ("grp", "die"), beside_end)
    (inflow,) = call(
        functools.partial(ends_body, cap, tiles),
        "package_end",
        [shape(LANES, LANES)],
        (ids, current),
        [VMEM, VMEM],
    )
    halo_inflow = lax.ppermute(inflow, ("grp", "die"), beside_end)
    all_inflow, halo_band, halo_inv, edge_base = call(
        functools.partial(inflow_body, cap, tiles),
        "package_inflow",
        [
            shape((own + 2) * LANES, LANES),
            shape(2 * LANES, 2 * LANES, dtype=BF16),
            shape(LANES, LANES),
            shape(2 * LANES, LANES),
        ],
        (ids, current, block_coupling, pack, halo, near, inflow),
        [VMEM] * 6 + [ANY],
        [pltpu.VMEM((2 * LANES + 2 * RADIUS, 2 * LANES), BF16)],
        work=3,
    )
    half_out, pkg_out, picked = call(
        functools.partial(iterate_body, cap, die_count),
        "package_iterations",
        [shape(own * LANES, LANES), shape(blocks, LANES), shape(2 * slots, LANES)],
        (
            ids, block_coupling, halo_inflow, all_inflow, band, base, pkg_inv,
            halo_band, halo_inv, edge_base,
        ),
        [SMEM] + [VMEM] * 9,
        [pltpu.VMEM((own * LANES, LANES), F32), plane, plane, dma((2,))],
        work=10,
        vmem=24,
        out_specs=[HBM, HBM, VMEM],
    )
    pair = 2 * die_count
    parts = lax.all_to_all(
        picked.reshape(pair, cap, LANES),
        ("grp", "die"),
        split_axis=0,
        concat_axis=0,
        axis_index_groups=[
            [first + i for i in range(pair)] for first in range(0, devices, pair)
        ],
        tiled=True,
    ).reshape(2 * slots, LANES)
    other = lax.ppermute(half_out, "grp", [(g, g ^ 1) for g in range(group_count)])
    pkg_out, done = call(
        join_body,
        "join_halves",
        [shape(blocks, LANES), shape(8, LANES)],
        (other, pkg_out),
        [VMEM, HBM],
        [dma(())],
        out_specs=[HBM, VMEM],
        aliases={1: 0},
    )
    (bump_out,) = call(
        add_body, "add_parts", [shape(slots, LANES)], (parts, done), [VMEM, ANY]
    )
    return (die_out, pkg_out, bump_out)


def solution(mesh):
    return jax.shard_map(
        local,
        mesh=mesh,
        in_specs=(
            P("grp", "die"),
            P("grp", "die"),
            P("grp", "die"),
            P(("grp", "die"), None),
            P(("grp", "die")),
            P(("grp", "die"), None),
            P("die", None),
            P("die", None),
            P(None, "die"),
            P(None, "die"),
            P(),
        ),
        out_specs=(P("grp", "die"), P("die", None), P(("grp", "die"), None)),
        check_vma=False,
    )
```

```python
import functools
import math

import jax
import jax.numpy as jnp
from jax import lax
from jax.experimental import pallas as pl
from jax.experimental.pallas import tpu as pltpu
from jax.sharding import PartitionSpec as P

RADIUS = 32
SWEEPS = 4
ITERS = 4
LANES = 128
HALO_ROWS = 8
REACH = RADIUS * ITERS
WINDOW = LANES + 2 * RADIUS
F32 = jnp.float32
BF16 = jnp.bfloat16
MOST_VMEM = 57
VMEM = pl.BlockSpec(memory_space=pltpu.VMEM)
SMEM = pl.BlockSpec(memory_space=pltpu.SMEM)
ANY = pl.BlockSpec(memory_space=pl.ANY)
HBM = pl.BlockSpec(memory_space=pltpu.HBM)


def sweep_weights(sweeps):
    return [
        1.0 / (1.0 + 0.8 * math.cos(math.pi * (2 * index + 1) / (2 * sweeps)))
        for index in range(sweeps)
    ]


def call(
    body, name, outs, args, specs, scratch=(), work=1, vmem=16, out_specs=None, aliases=None
):
    bytes_accessed = sum(4 * math.prod(arg.shape) for arg in args)
    return pl.pallas_call(
        body,
        name=name,
        out_shape=outs,
        in_specs=specs,
        out_specs=out_specs or [VMEM] * len(outs),
        input_output_aliases=aliases or {},
        scratch_shapes=list(scratch),
        compiler_params=pltpu.CompilerParams(vmem_limit_bytes=vmem * 1024 * 1024),
        cost_estimate=pl.CostEstimate(
            flops=work * 10**9, bytes_accessed=bytes_accessed, transcendentals=0
        ),
    )(*args)


def place():
    return lax.axis_index("grp"), lax.axis_index("die")


def shape(*dims, dtype=F32):
    return jax.ShapeDtypeStruct(dims, dtype)


def halves(values):
    high = values.astype(BF16)
    low = (values - high.astype(F32)).astype(BF16)
    return high, low


def spread_body(cap, die_count, blocks, block_ref, out_ref):
    slots = block_ref.shape[1]
    block = jnp.concatenate(
        [block_ref[...], jnp.zeros((1, LANES - slots), jnp.int32)], axis=1
    )
    for die in range(die_count):
        row = (pltpu.roll(block, LANES - die * cap, 1) if die else block) - die * blocks
        for at in range(die, out_ref.shape[0], die_count):
            out_ref[at] = row


def asked_rows(cap, die_count, group, ids_ref):
    for die in range(die_count):
        for slot in range(cap):
            yield die * cap + slot, ids_ref[group * die_count + die, slot]


def pick_body(cap, die_count, ids_ref, plane_ref, out_ref):
    group, _ = place()
    for at, row in asked_rows(cap, die_count, group, ids_ref):
        out_ref[pl.ds(at, 1), :] = plane_ref[pl.ds(row, 1), :]


def build_band(first, pattern, weights):
    place = lax.broadcasted_iota(jnp.int32, (WINDOW, LANES), 0)
    band = None
    for k in range(pattern.shape[0]):
        hit = place == (pattern[k : k + 1, :] - first)
        term = jnp.where(hit, weights[k : k + 1, :], 0.0)
        band = term if band is None else band + term
    fill = jnp.zeros((2 * LANES - WINDOW, LANES), F32)
    return jnp.concatenate(halves(jnp.concatenate([band, fill], axis=0).T), axis=0)


def reciprocal(diag):
    safe = jnp.where(diag > 0.0, diag, 1.0)
    return jnp.where(diag > 0.0, 1.0 / safe, 0.0)


def span(tile, offset=0, size=LANES):
    return pl.ds(pl.multiple_of(tile * LANES + offset, RADIUS), size)


def mixer(coup_ref):
    mix = jnp.concatenate(halves(coup_ref[...]), axis=1)
    return jnp.concatenate([mix, mix], axis=0)


def clear_pads(ref):
    pad = jnp.zeros((RADIUS, 2 * LANES), BF16)
    ref[0:RADIUS, :] = pad
    ref[ref.shape[0] - RADIUS :, :] = pad


def store(ref, tile, values):
    ref[span(tile, RADIUS, values.shape[0]), :] = jnp.concatenate(halves(values), axis=1)


def couple(source, tile, bands, mix, write):
    for at in range(0, len(bands), 4):
        couple_few(source, tile + at, bands[at : at + 4], mix, write)


def couple_few(source, tile, bands, mix, write):
    own = source[span(tile, RADIUS, len(bands) * LANES), :]
    within = jnp.dot(own, mix, preferred_element_type=F32)
    for i, band in enumerate(bands):
        window = source[span(tile + i, 0, WINDOW), :]
        beside = jnp.dot(band[:, :WINDOW], window, preferred_element_type=F32)
        both = beside[:LANES] + beside[LANES:] + within[i * LANES : (i + 1) * LANES]
        write(tile + i, both[:, :LANES] + both[:, LANES:])


def in_chunks(first, count, body, size=16):
    whole = count // size

    @pl.loop(0, whole)
    def _(chunk):
        body(first + chunk * size, size)

    if count % size:
        body(first + whole * size, count % size)


def half_of(tiles):
    half = lax.rem(sum(place()), 2)
    own = tiles // 2
    return half, own, half * own - 1


def bands_body(pat_ref, wgt_ref, after_ref, band_ref, done_ref):
    blocks = pat_ref.shape[1]
    half, own, shift = half_of(blocks // LANES)
    begin = place()[1] * blocks + shift * LANES

    def bands(tile, size):
        for i in range(size):
            lanes = pl.ds(pl.multiple_of((tile + i + shift) * LANES, LANES), LANES)
            band_ref[tile + i] = build_band(
                begin + (tile + i) * LANES - RADIUS, pat_ref[:, lanes], wgt_ref[:, lanes]
            )

    in_chunks(1 - half, own + 1, bands, 8)
    band_ref[half * (own + 1)] = jnp.zeros(band_ref.shape[1:], BF16)
    done_ref[...] = jnp.zeros(done_ref.shape, F32)


def prepare_body(
    pat_ref, wgt_ref, coup_ref, band_hbm, volt_hbm, diag_hbm, after_ref,
    base_hbm, inv_hbm, pack_ref, near_ref,
    volt_ref, diag_ref, band_ref, base_ref, inv_ref, plane_ref, sems,
):
    blocks = volt_hbm.shape[0]
    half, own, shift = half_of(blocks // LANES)
    first, count, outer = 1 - half, own + 1, half * (own + 1)
    known = pl.ds(pl.multiple_of(first * LANES, LANES), count * LANES)
    source = pl.ds(pl.multiple_of((first + shift) * LANES, LANES), count * LANES)
    loads = [
        pltpu.make_async_copy(hbm.at[source, :], ref.at[known, :], sems.at[i])
        for i, (hbm, ref) in enumerate(((volt_hbm, volt_ref), (diag_hbm, diag_ref)))
    ]
    loads.append(pltpu.make_async_copy(band_hbm, band_ref, sems.at[2]))
    for load in loads:
        load.start()
    clear_pads(plane_ref)
    plane_ref[span(outer, RADIUS), :] = jnp.zeros((LANES, 2 * LANES), BF16)
    for load in loads[:2]:
        load.wait()

    def spread(tile, size):
        cut = span(tile, 0, size * LANES)
        store(plane_ref, tile, volt_ref[cut, :])
        inv_ref[cut, :] = reciprocal(diag_ref[cut, :])

    in_chunks(first, count, spread, 8)
    inv_out = pltpu.make_async_copy(inv_ref.at[known, :], inv_hbm.at[known, :], sems.at[3])
    inv_out.start()
    mix = mixer(coup_ref)
    loads[2].wait()

    def base(tile, size):
        def write(tile, values):
            base_ref[span(tile), :] = values

        couple(plane_ref, tile, [band_ref[tile + i] for i in range(size)], mix, write)
        cut = span(tile, 0, size * LANES)
        pltpu.make_async_copy(base_ref.at[cut, :], base_hbm.at[cut, :], sems.at[4]).start()

    in_chunks(first, count, base, 8)
    edge = 1 + half * (own - 1)
    lanes = pl.ds(pl.multiple_of((edge + shift) * LANES, LANES), LANES)
    neighbours = pat_ref.shape[0]
    pack_ref[0:LANES, :] = volt_ref[span(edge), :]
    pack_ref[LANES : 2 * LANES, :] = diag_ref[span(edge), :]
    at = 2 * LANES
    pack_ref[at : at + neighbours, :] = pat_ref[:, lanes].astype(F32)
    pack_ref[at + neighbours : at + 2 * neighbours, :] = wgt_ref[:, lanes]
    near_ref[0:RADIUS, :] = volt_ref[2 * LANES : 2 * LANES + RADIUS, :]
    near_ref[RADIUS:, :] = volt_ref[own * LANES - RADIUS : own * LANES, :]
    inv_out.wait()
    pltpu.make_async_copy(
        base_ref.at[known, :], base_hbm.at[known, :], sems.at[4]
    ).wait()


def slot_places(cap, ids_ref):
    per_row = LANES // cap
    lane = lax.broadcasted_iota(jnp.int32, (1, LANES), 1)
    places = []
    for at in range(0, ids_ref.shape[0], per_row):
        total = None
        for i in range(per_row):
            row = jnp.where(lane < cap, ids_ref[at + i : at + i + 1, :], 0)
            row = pltpu.roll(row, i * cap, 1) if i else row
            total = row if total is None else total + row
        places.append(total)
    return places


def gather_inflow(places, first, rows, current):
    at = lax.broadcasted_iota(jnp.int32, (rows, LANES), 0) + first
    hits = [jnp.where(at == place, 1.0, 0.0).astype(BF16) for place in places]
    both = jnp.dot(jnp.concatenate(hits, axis=1), current, preferred_element_type=F32)
    return both[:, :LANES] + both[:, LANES:]


def ends_body(cap, tiles, ids_ref, current_ref, out_ref):
    half, _, _ = half_of(tiles)
    places = slot_places(cap, ids_ref)
    current = jnp.concatenate(halves(current_ref[...]), axis=1)
    out_ref[...] = gather_inflow(places, half * (tiles - 1) * LANES, LANES, current)


def inflow_body(
    cap, tiles, ids_ref, current_ref, coup_ref, own_ref, halo_ref, near_ref, after_ref,
    out_ref, band_ref, inv_ref, base_ref, plane_ref,
):
    half, own, shift = half_of(tiles)
    first, count = 1 - half, own + 1
    places = slot_places(cap, ids_ref)
    current = jnp.concatenate(halves(current_ref[...]), axis=1)

    def inflow(tile, size):
        cut = span(tile, 0, size * LANES)
        out_ref[cut, :] = gather_inflow(
            places, (tile + shift) * LANES, size * LANES, current
        )

    in_chunks(first, count, inflow)
    out_ref[span(half * (own + 1)), :] = jnp.zeros((LANES, LANES), F32)

    neighbours = (own_ref.shape[0] - 2 * LANES) // 2
    begin = (place()[1] * tiles + 2 * half * own - 1) * LANES
    packs = [jnp.where(half == at, halo_ref[...], own_ref[...]) for at in range(2)]
    at = 2 * LANES
    bands = []
    for tile, pack in enumerate(packs):
        bands.append(
            build_band(
                begin + tile * LANES - RADIUS,
                pack[at : at + neighbours].astype(jnp.int32),
                pack[at + neighbours : at + 2 * neighbours],
            )
        )
        store(plane_ref, tile, pack[:LANES])
    none = jnp.zeros((RADIUS, 2 * LANES), BF16)
    low, high = (
        jnp.concatenate(halves(near_ref[cut, :]), axis=1)
        for cut in (slice(0, RADIUS), slice(RADIUS, 2 * RADIUS))
    )
    size = plane_ref.shape[0]
    plane_ref[0:RADIUS, :] = jnp.where(half == 0, none, high)
    plane_ref[size - RADIUS : size, :] = jnp.where(half == 0, low, none)
    results = []
    couple(plane_ref, 0, bands, mixer(coup_ref), lambda tile, values: results.append(values))
    band_ref[...] = jnp.where(half == 0, bands[0], bands[1])
    inv_ref[...] = reciprocal(halo_ref[LANES : 2 * LANES, :])
    base_ref[0:LANES, :] = jnp.where(half == 0, results[0], results[1])
    base_ref[LANES:, :] = jnp.where(half == 0, results[1], results[0])


def iterate_body(
    cap, die_count, asked_ref, coup_ref, halo_ref, inflow_ref, band_ref, base_ref, inv_ref,
    halo_band_ref, halo_inv_ref, edge_base_ref, out_hbm, full_hbm, picked_ref, out_ref, here_ref, there_ref, sems,
):
    own = out_hbm.shape[0] // LANES
    half, _, _ = half_of(2 * own)
    first, count, outer = 1 - half, own + 1, half * (own + 1)
    edge = 1 + half * (own - 1)
    for ref in (here_ref, there_ref):
        clear_pads(ref)

    def start(tile, size):
        cut = span(tile, 0, size * LANES)
        store(here_ref, tile, -(inflow_ref[cut, :] + base_ref[cut, :]) * inv_ref[cut, :])

    in_chunks(first, count, start)
    halo_inv = halo_inv_ref[...]
    store(here_ref, outer, -(halo_ref[...] + edge_base_ref[0:LANES, :]) * halo_inv)
    cut = span(edge)
    store(here_ref, edge, -(inflow_ref[cut, :] + edge_base_ref[LANES:, :]) * inv_ref[cut, :])
    mix = mixer(coup_ref)
    refs = (here_ref, there_ref)
    for iteration in range(1, ITERS):
        source, target = refs[(iteration - 1) % 2], refs[iteration % 2]
        last = iteration == ITERS - 1

        def write(tile, coupled, target=target, last=last):
            values = -(inflow_ref[span(tile), :] + coupled) * inv_ref[span(tile), :]
            if last:
                out_ref[span(tile - 1), :] = values
            else:
                store(target, tile, values)

        def step(tile, size, source=source, write=write):
            bands = [band_ref[tile + i] for i in range(size)]
            couple(source, tile, bands, mix, write)

        def final(tile, size, step=step):
            step(tile, size)
            cut = span(tile - 1, 0, size * LANES)
            whole = span(half * own + tile - 1, 0, size * LANES)
            pltpu.make_async_copy(out_ref.at[cut, :], out_hbm.at[cut, :], sems.at[0]).start()
            pltpu.make_async_copy(out_ref.at[cut, :], full_hbm.at[whole, :], sems.at[1]).start()

        def write_halo(tile, coupled, target=target):
            store(target, tile, -(halo_ref[...] + coupled) * halo_inv)

        if last:
            in_chunks(1, own, final)
        else:
            in_chunks(first, count, step)
            couple(source, outer, [halo_band_ref[...]], mix, write_halo)

    base_row = half * own * LANES
    group, _ = place()
    pair = group - lax.rem(group, 2)
    for member in range(2):
        offset = member * (picked_ref.shape[0] // 2)
        for at, row in asked_rows(cap, die_count, pair + member, asked_ref):
            row = row - base_row
            inside = (row >= 0) & (row < own * LANES)
            safe = jnp.clip(row, 0, own * LANES - 1)
            values = out_ref[pl.ds(safe, 1), :]
            picked_ref[pl.ds(offset + at, 1), :] = jnp.where(inside, values, 0.0)
    pltpu.make_async_copy(out_ref, out_hbm, sems.at[0]).wait()
    pltpu.make_async_copy(out_ref, full_hbm.at[0 : own * LANES, :], sems.at[1]).wait()


def join_body(other_ref, full_in_hbm, full_hbm, done_ref, sem):
    rows = other_ref.shape[0]
    half, _, _ = half_of(2 * rows // LANES)
    start = pl.multiple_of((1 - half) * rows, LANES)
    copy = pltpu.make_async_copy(other_ref, full_hbm.at[pl.ds(start, rows), :], sem)
    copy.start()
    done_ref[...] = jnp.zeros(done_ref.shape, F32)
    copy.wait()


def add_body(parts_ref, after_ref, out_ref):
    rows = out_ref.shape[0]
    out_ref[...] = parts_ref[0:rows, :] + parts_ref[rows:, :]


def scatter_body(cols, node_ref, cond_ref, start_ref, volt_ref, load_ref, shunt_ref,
                 right_ref, inv_ref, inner_ref, outer_ref):
    blocks = node_ref.shape[0]
    rows = volt_ref.shape[0]
    group = 8
    row_at = lax.broadcasted_iota(jnp.int32, (rows, LANES), 0)
    col_at = lax.broadcasted_iota(jnp.int32, (cols, LANES), 0)
    total = jnp.zeros((4 * rows, cols), F32)
    for first in range(0, blocks, group):
        node = node_ref[first : first + group, :]
        live = node >= 0
        cond = jnp.where(live, cond_ref[first : first + group, :], 0.0)
        flow = cond * start_ref[first : first + group, :]
        safe = jnp.where(live, node, 0)
        row, col = safe // cols, safe % cols
        parts = halves(cond) + halves(flow)
        left, right = [], []
        for i in range(group):
            spot = jnp.where(row_at == row[i : i + 1, :], 1.0, 0.0).astype(BF16)
            left.append(
                jnp.concatenate([spot * part[i : i + 1, :] for part in parts], axis=0)
            )
            right.append(jnp.where(col_at == col[i : i + 1, :], 1.0, 0.0).astype(BF16))
        total = total + lax.dot_general(
            jnp.concatenate(left, axis=1),
            jnp.concatenate(right, axis=1),
            (((1,), (1,)), ((), ())),
            preferred_element_type=F32,
        )
    gsum = total[:rows] + total[rows : 2 * rows]
    inject = total[2 * rows : 3 * rows] + total[3 * rows :]
    inv = 1.0 / (4.0 + shunt_ref[...] + gsum)
    right_side = (inject - load_ref[...]) * inv
    right_ref[...] = right_side
    inv_ref[...] = inv
    volt = volt_ref[...]
    top, bottom = (
        jnp.concatenate([volt[cut], right_side[cut], inv[cut]], axis=0)
        for cut in (slice(0, HALO_ROWS), slice(rows - HALO_ROWS, rows))
    )
    swap_parts(inner_ref, outer_ref, place()[0], top, bottom)


def swap_parts(inner_ref, outer_ref, mine, first, last):
    even = lax.rem(mine, 2) == 0
    inner_ref[...] = jnp.where(even, last, first)
    outer_ref[...] = jnp.where(even, first, last)


def swapped(inner, outer, mine):
    even = lax.rem(mine, 2) == 0
    return jnp.where(even, outer, inner), jnp.where(even, inner, outer)


def swap(inner, outer, axis):
    count = lax.axis_size(axis)

    def pairs(start):
        return [
            pair
            for i in range(start, count - 1, 2)
            for pair in ((i, i + 1), (i + 1, i))
        ]

    return lax.ppermute(outer, axis, pairs(1)), lax.ppermute(inner, axis, pairs(0))


def extended(own, top, bottom, index):
    cut = slice(index * HALO_ROWS, (index + 1) * HALO_ROWS)
    return jnp.concatenate([own, bottom[cut], top[cut]], axis=0)


def edge_body(
    volt_ref, right_ref, inv_ref, outer_ref, inner_ref, after_ref, west_ref, east_ref
):
    cols = volt_ref.shape[1]
    top, bottom = swapped(inner_ref[...], outer_ref[...], place()[0])
    out_rows, high = west_ref.shape
    west, east = None, None
    for index, ref in enumerate((volt_ref, right_ref, inv_ref)):
        whole = extended(ref[...], top, bottom, index)
        lane = lax.broadcasted_iota(jnp.int32, (whole.shape[0], LANES), 1)
        head, tail = whole[:, :LANES], whole[:, cols - LANES :]
        at = index * SWEEPS
        head = pltpu.roll(head, at, 1) if at else head
        tail = pltpu.roll(tail, at + SWEEPS, 1)
        west = head if west is None else jnp.where(lane >= at, head, west)
        east = tail if east is None else jnp.where(lane >= at, tail, east)
    fill = jnp.zeros((high - west.shape[0], LANES), F32)
    west, east = (
        jnp.concatenate([part, fill], axis=0).T[:out_rows] for part in (west, east)
    )
    swap_parts(west_ref, east_ref, place()[1], west, east)


def sweep_body(copies, node_ref, cond_ref, start_ref, volt_ref, right_ref, inv_ref,
               row_out_ref, row_in_ref, col_out_ref, col_in_ref, out_ref, current_ref):
    rows, cols = volt_ref.shape
    blocks = node_ref.shape[0]
    cap = current_ref.shape[1]
    whole = []
    top, bottom = swapped(row_in_ref[...], row_out_ref[...], place()[0])
    out_rows, high = col_in_ref.shape
    fill = jnp.zeros((LANES - out_rows, high), F32)
    wests, easts = (
        jnp.concatenate([part, fill], axis=0).T[: rows + 2 * HALO_ROWS]
        for part in swapped(col_in_ref[...], col_out_ref[...], place()[1])
    )
    eastern = lax.broadcasted_iota(jnp.int32, easts.shape, 1) < LANES // 2
    for index, ref in enumerate((volt_ref, right_ref, inv_ref)):
        own = extended(ref[...], top, bottom, index)
        at = index * SWEEPS
        west = pltpu.roll(wests, LANES - SWEEPS - at, 1)
        east = pltpu.roll(easts, LANES - at, 1) if at else easts
        whole.append(jnp.concatenate([own, jnp.where(eastern, east, west)], axis=1))
    volt, right_side, inv = whole
    high, wide = volt.shape
    for weight in sweep_weights(SWEEPS):
        beside = (
            pltpu.roll(volt, 1, 0)
            + pltpu.roll(volt, high - 1, 0)
            + pltpu.roll(volt, 1, 1)
            + pltpu.roll(volt, wide - 1, 1)
        )
        volt = (1.0 - weight) * volt + weight * (right_side + beside * inv)
    volt = volt[:rows, :cols]
    out_ref[...] = volt
    both = jnp.concatenate(halves(volt), axis=0)
    group = 8
    row_at = lax.broadcasted_iota(jnp.int32, (rows, LANES), 0)
    col_at = lax.broadcasted_iota(jnp.int32, (cols, LANES), 0)
    dies = blocks // cap
    for first in range(0, blocks, group):
        node = node_ref[first : first + group, :]
        live = node >= 0
        cond = jnp.where(live, cond_ref[first : first + group, :], 0.0)
        safe = jnp.where(live, node, 0)
        row, col = safe // cols, safe % cols
        spots = jnp.concatenate(
            [
                jnp.where(col_at == col[i : i + 1, :], 1.0, 0.0).astype(BF16)
                for i in range(group)
            ],
            axis=1,
        )
        found = jnp.dot(both, spots, preferred_element_type=F32)
        found = found[:rows] + found[rows:]
        for i in range(group):
            mine = found[:, i * LANES : (i + 1) * LANES]
            at_bump = jnp.sum(
                jnp.where(row_at == row[i : i + 1, :], mine, 0.0), axis=0, keepdims=True
            )
            block = first + i
            current = cond[i : i + 1, :] * (start_ref[block : block + 1, :] - at_bump)
            current_ref[block // cap, block % cap : block % cap + 1, :] = current
    for copy in range(1, copies):
        current_ref[copy * dies : (copy + 1) * dies] = current_ref[0:dies]


def local(
    die_volt,
    die_load,
    die_shunt,
    bump_node,
    bump_block,
    bump_cond,
    pkg_volt,
    pkg_diag,
    pkg_pattern,
    pkg_weight,
    block_coupling,
):
    die_count = lax.axis_size("die")
    group_count = lax.axis_size("grp")
    devices = die_count * group_count
    blocks = pkg_volt.shape[0]
    tiles = blocks // LANES
    neighbours = pkg_pattern.shape[0]
    slots = bump_block.shape[0]
    cap = slots // die_count
    rows, cols = die_volt.shape
    (spread,) = call(
        functools.partial(spread_body, cap, die_count, blocks),
        "spread_blocks",
        [shape(devices, 1, LANES, dtype=jnp.int32)],
        (bump_block.reshape(1, slots),),
        [VMEM],
    )
    ids = lax.all_to_all(
        spread, ("grp", "die"), split_axis=0, concat_axis=0, tiled=True
    ).reshape(devices, LANES)

    (picked,) = call(
        functools.partial(pick_body, cap, die_count),
        "pick_rows",
        [shape(slots, LANES)],
        (ids, pkg_volt),
        [SMEM, VMEM],
    )
    bump_start = lax.all_to_all(
        picked.reshape(die_count, cap, LANES), "die", split_axis=0, concat_axis=0, tiled=True
    ).reshape(slots, LANES)

    right_side, inv, *edges = call(
        functools.partial(scatter_body, cols),
        "scatter_bumps",
        [shape(rows, cols)] * 2 + [shape(3 * HALO_ROWS, cols)] * 2,
        (bump_node, bump_cond, bump_start, die_volt, die_load, die_shunt),
        [VMEM] * 6,
        work=3,
    )
    own = tiles // 2
    dma = pltpu.SemaphoreType.DMA
    plane = pltpu.VMEM(((own + 2) * LANES + 2 * RADIUS, 2 * LANES), BF16)
    range_rows = pltpu.VMEM(((own + 2) * LANES, LANES), F32)
    range_bands = pltpu.VMEM((own + 2, 2 * LANES, 2 * LANES), BF16)
    beside = swap(*edges, "grp")
    band, banded = call(
        bands_body,
        "package_bands",
        [shape(own + 2, 2 * LANES, 2 * LANES, dtype=BF16), shape(8, LANES)],
        (pkg_pattern, pkg_weight, right_side),
        [VMEM, VMEM, ANY],
        work=2,
    )

    edge_rows = -(-3 * SWEEPS // 8) * 8
    edge_cols = -(-(rows + 2 * HALO_ROWS) // LANES) * LANES
    edges = call(
        edge_body,
        "edge_columns",
        [shape(edge_rows, edge_cols)] * 2,
        (die_volt, right_side, inv, *beside, banded),
        [VMEM] * 5 + [ANY],
    )
    columns = swap(*edges, "die")

    die_out, current = call(
        functools.partial(sweep_body, group_count),
        "sweeps",
        [shape(rows, cols), shape(devices, cap, LANES)],
        (bump_node, bump_cond, bump_start, die_volt, right_side, inv, *beside, *columns),
        [VMEM] * 10,
        work=4,
    )
    pack_rows = 2 * LANES + 2 * neighbours
    base, pkg_inv, pack, near = call(
        prepare_body,
        "package_prepare",
        [
            shape((own + 2) * LANES, LANES),
            shape((own + 2) * LANES, LANES),
            shape(pack_rows, LANES),
            shape(2 * RADIUS, LANES),
        ],
        (pkg_pattern, pkg_weight, block_coupling, band, pkg_volt, pkg_diag, die_out),
        [VMEM] * 3 + [HBM] * 4,
        [range_rows, range_rows, range_bands, range_rows, range_rows, plane, dma((5,))],
        work=7,
        vmem=MOST_VMEM,
        out_specs=[HBM] * 2 + [VMEM] * 2,
    )

    current = lax.all_to_all(
        current, ("grp", "die"), split_axis=0, concat_axis=0, tiled=True
    ).reshape(devices * cap, LANES)

    beside_end = [
        (g * die_count + a, g * die_count + b)
        for g in range(group_count)
        for d in range((g + 1) % 2, die_count - 1, 2)
        for a, b in ((d, d + 1), (d + 1, d))
    ]
    halo = lax.ppermute(pack, ("grp", "die"), beside_end)
    (inflow,) = call(
        functools.partial(ends_body, cap, tiles),
        "package_end",
        [shape(LANES, LANES)],
        (ids, current),
        [VMEM, VMEM],
    )
    halo_inflow = lax.ppermute(inflow, ("grp", "die"), beside_end)
    all_inflow, halo_band, halo_inv, edge_base = call(
        functools.partial(inflow_body, cap, tiles),
        "package_inflow",
        [
            shape((own + 2) * LANES, LANES),
            shape(2 * LANES, 2 * LANES, dtype=BF16),
            shape(LANES, LANES),
            shape(2 * LANES, LANES),
        ],
        (ids, current, block_coupling, pack, halo, near, inflow),
        [VMEM] * 6 + [ANY],
        [pltpu.VMEM((2 * LANES + 2 * RADIUS, 2 * LANES), BF16)],
        work=3,
    )
    half_out, pkg_out, picked = call(
        functools.partial(iterate_body, cap, die_count),
        "package_iterations",
        [shape(own * LANES, LANES), shape(blocks, LANES), shape(2 * slots, LANES)],
        (
            ids, block_coupling, halo_inflow, all_inflow, band, base, pkg_inv,
            halo_band, halo_inv, edge_base,
        ),
        [SMEM] + [VMEM] * 9,
        [pltpu.VMEM((own * LANES, LANES), F32), plane, plane, dma((2,))],
        work=10,
        vmem=24,
        out_specs=[HBM, HBM, VMEM],
    )
    pair = 2 * die_count
    parts = lax.all_to_all(
        picked.reshape(pair, cap, LANES),
        ("grp", "die"),
        split_axis=0,
        concat_axis=0,
        axis_index_groups=[
            [first + i for i in range(pair)] for first in range(0, devices, pair)
        ],
        tiled=True,
    ).reshape(2 * slots, LANES)
    other = lax.ppermute(half_out, "grp", [(g, g ^ 1) for g in range(group_count)])
    pkg_out, done = call(
        join_body,
        "join_halves",
        [shape(blocks, LANES), shape(8, LANES)],
        (other, pkg_out),
        [VMEM, HBM],
        [dma(())],
        out_specs=[HBM, VMEM],
        aliases={1: 0},
    )
    (bump_out,) = call(
        add_body, "add_parts", [shape(slots, LANES)], (parts, done), [VMEM, ANY]
    )
    return (die_out, pkg_out, bump_out)


def solution(mesh):
    return jax.shard_map(
        local,
        mesh=mesh,
        in_specs=(
            P("grp", "die"),
            P("grp", "die"),
            P("grp", "die"),
            P(("grp", "die"), None),
            P(("grp", "die")),
            P(("grp", "die"), None),
            P("die", None),
            P("die", None),
            P(None, "die"),
            P(None, "die"),
            P(),
        ),
        out_specs=(P("grp", "die"), P("die", None), P(("grp", "die"), None)),
        check_vma=False,
    )
```

```python
import functools
import math

import jax
import jax.numpy as jnp
from jax import lax
from jax.experimental import pallas as pl
from jax.experimental.pallas import tpu as pltpu
from jax.sharding import PartitionSpec as P

RADIUS = 32
SWEEPS = 4
ITERS = 4
LANES = 128
HALO_ROWS = 8
REACH = RADIUS * ITERS
WINDOW = LANES + 2 * RADIUS
F32 = jnp.float32
BF16 = jnp.bfloat16
MOST_VMEM = 57
VMEM = pl.BlockSpec(memory_space=pltpu.VMEM)
SMEM = pl.BlockSpec(memory_space=pltpu.SMEM)
ANY = pl.BlockSpec(memory_space=pl.ANY)
HBM = pl.BlockSpec(memory_space=pltpu.HBM)


def sweep_weights(sweeps):
    return [
        1.0 / (1.0 + 0.8 * math.cos(math.pi * (2 * index + 1) / (2 * sweeps)))
        for index in range(sweeps)
    ]


def call(
    body, name, outs, args, specs, scratch=(), work=1, vmem=16, out_specs=None, aliases=None
):
    bytes_accessed = sum(4 * math.prod(arg.shape) for arg in args)
    return pl.pallas_call(
        body,
        name=name,
        out_shape=outs,
        in_specs=specs,
        out_specs=out_specs or [VMEM] * len(outs),
        input_output_aliases=aliases or {},
        scratch_shapes=list(scratch),
        compiler_params=pltpu.CompilerParams(vmem_limit_bytes=vmem * 1024 * 1024),
        cost_estimate=pl.CostEstimate(
            flops=work * 10**9, bytes_accessed=bytes_accessed, transcendentals=0
        ),
    )(*args)


def place():
    return lax.axis_index("grp"), lax.axis_index("die")


def shape(*dims, dtype=F32):
    return jax.ShapeDtypeStruct(dims, dtype)


def halves(values):
    high = values.astype(BF16)
    low = (values - high.astype(F32)).astype(BF16)
    return high, low


def spread_body(cap, die_count, blocks, block_ref, out_ref):
    slots = block_ref.shape[1]
    block = jnp.concatenate(
        [block_ref[...], jnp.zeros((1, LANES - slots), jnp.int32)], axis=1
    )
    for die in range(die_count):
        row = (pltpu.roll(block, LANES - die * cap, 1) if die else block) - die * blocks
        for at in range(die, out_ref.shape[0], die_count):
            out_ref[at] = row


def asked_rows(cap, die_count, group, ids_ref):
    for die in range(die_count):
        for slot in range(cap):
            yield die * cap + slot, ids_ref[group * die_count + die, slot]


def pick_body(cap, die_count, ids_ref, plane_ref, out_ref):
    group, _ = place()
    for at, row in asked_rows(cap, die_count, group, ids_ref):
        out_ref[pl.ds(at, 1), :] = plane_ref[pl.ds(row, 1), :]


def build_band(first, pattern, weights):
    place = lax.broadcasted_iota(jnp.int32, (WINDOW, LANES), 0)
    band = None
    for k in range(pattern.shape[0]):
        hit = place == (pattern[k : k + 1, :] - first)
        term = jnp.where(hit, weights[k : k + 1, :], 0.0)
        band = term if band is None else band + term
    fill = jnp.zeros((2 * LANES - WINDOW, LANES), F32)
    return jnp.concatenate(halves(jnp.concatenate([band, fill], axis=0).T), axis=0)


def reciprocal(diag):
    safe = jnp.where(diag > 0.0, diag, 1.0)
    return jnp.where(diag > 0.0, 1.0 / safe, 0.0)


def span(tile, offset=0, size=LANES):
    return pl.ds(pl.multiple_of(tile * LANES + offset, RADIUS), size)


def mixer(coup_ref):
    mix = jnp.concatenate(halves(coup_ref[...]), axis=1)
    return jnp.concatenate([mix, mix], axis=0)


def clear_pads(ref):
    pad = jnp.zeros((RADIUS, 2 * LANES), BF16)
    ref[0:RADIUS, :] = pad
    ref[ref.shape[0] - RADIUS :, :] = pad


def store(ref, tile, values):
    ref[span(tile, RADIUS, values.shape[0]), :] = jnp.concatenate(halves(values), axis=1)


def couple(source, tile, bands, mix, write):
    for at in range(0, len(bands), 4):
        couple_few(source, tile + at, bands[at : at + 4], mix, write)


def couple_few(source, tile, bands, mix, write):
    own = source[span(tile, RADIUS, len(bands) * LANES), :]
    within = jnp.dot(own, mix, preferred_element_type=F32)
    for i, band in enumerate(bands):
        window = source[span(tile + i, 0, WINDOW), :]
        beside = jnp.dot(band[:, :WINDOW], window, preferred_element_type=F32)
        both = beside[:LANES] + beside[LANES:] + within[i * LANES : (i + 1) * LANES]
        write(tile + i, both[:, :LANES] + both[:, LANES:])


def in_chunks(first, count, body, size=16):
    whole = count // size

    @pl.loop(0, whole)
    def _(chunk):
        body(first + chunk * size, size)

    if count % size:
        body(first + whole * size, count % size)


def half_of(tiles):
    half = lax.rem(sum(place()), 2)
    own = tiles // 2
    return half, own, half * own - 1


def bands_body(pat_ref, wgt_ref, after_ref, band_ref, done_ref):
    blocks = pat_ref.shape[1]
    half, own, shift = half_of(blocks // LANES)
    begin = place()[1] * blocks + shift * LANES

    def bands(tile, size):
        for i in range(size):
            lanes = pl.ds(pl.multiple_of((tile + i + shift) * LANES, LANES), LANES)
            band_ref[tile + i] = build_band(
                begin + (tile + i) * LANES - RADIUS, pat_ref[:, lanes], wgt_ref[:, lanes]
            )

    in_chunks(1 - half, own + 1, bands, 8)
    band_ref[half * (own + 1)] = jnp.zeros(band_ref.shape[1:], BF16)
    done_ref[...] = jnp.zeros(done_ref.shape, F32)


def prepare_body(
    pat_hbm, wgt_hbm, coup_hbm, band_hbm, volt_hbm, diag_hbm, after_ref,
    base_hbm, inv_hbm, pack_hbm, near_hbm,
    volt_ref, diag_ref, band_ref, base_ref, inv_ref, plane_ref, coup_ref, pat_ref, wgt_ref,
    sems, out_sems,
):
    blocks = volt_hbm.shape[0]
    half, own, shift = half_of(blocks // LANES)
    first, count, outer = 1 - half, own + 1, half * (own + 1)
    edge = 1 + half * (own - 1)
    known = pl.ds(pl.multiple_of(first * LANES, LANES), count * LANES)
    source = pl.ds(pl.multiple_of((first + shift) * LANES, LANES), count * LANES)
    lanes = pl.ds(pl.multiple_of((edge + shift) * LANES, LANES), LANES)
    neighbours = pat_hbm.shape[0]
    loads = [
        pltpu.make_async_copy(hbm, ref, sems.at[i])
        for i, (hbm, ref) in enumerate(
            (
                (volt_hbm.at[source, :], volt_ref.at[known, :]),
                (diag_hbm.at[source, :], diag_ref.at[known, :]),
                (coup_hbm, coup_ref),
                (pat_hbm.at[:, lanes], pat_ref),
                (wgt_hbm.at[:, lanes], wgt_ref.at[neighbours : 2 * neighbours, :]),
                (band_hbm, band_ref),
            )
        )
    ]
    for load in loads:
        load.start()
    writes = []

    def write_out(ref, hbm):
        writes.append(pltpu.make_async_copy(ref, hbm, out_sems.at[len(writes)]))
        writes[-1].start()

    clear_pads(plane_ref)
    plane_ref[span(outer, RADIUS), :] = jnp.zeros((LANES, 2 * LANES), BF16)
    for load in loads[:5]:
        load.wait()
    at = 2 * LANES
    write_out(volt_ref.at[span(edge), :], pack_hbm.at[0:LANES, :])
    write_out(diag_ref.at[span(edge), :], pack_hbm.at[LANES:at, :])
    wgt_ref[0:neighbours, :] = pat_ref[...].astype(F32)
    write_out(wgt_ref, pack_hbm.at[at : at + 2 * neighbours, :])
    write_out(
        volt_ref.at[2 * LANES : 2 * LANES + RADIUS, :], near_hbm.at[0:RADIUS, :]
    )
    write_out(
        volt_ref.at[own * LANES - RADIUS : own * LANES, :],
        near_hbm.at[RADIUS : 2 * RADIUS, :],
    )

    def spread(tile, size):
        cut = span(tile, 0, size * LANES)
        store(plane_ref, tile, volt_ref[cut, :])
        inv_ref[cut, :] = reciprocal(diag_ref[cut, :])

    in_chunks(first, count, spread, 8)
    write_out(inv_ref.at[known, :], inv_hbm.at[known, :])
    mix = mixer(coup_ref)
    loads[5].wait()

    def base(tile, size):
        def write(tile, values):
            base_ref[span(tile), :] = values

        couple(plane_ref, tile, [band_ref[tile + i] for i in range(size)], mix, write)
        cut = span(tile, 0, size * LANES)
        pltpu.make_async_copy(
            base_ref.at[cut, :], base_hbm.at[cut, :], out_sems.at[6]
        ).start()

    in_chunks(first, count, base, 8)
    for write in writes:
        write.wait()
    pltpu.make_async_copy(
        base_ref.at[known, :], base_hbm.at[known, :], out_sems.at[6]
    ).wait()


def slot_places(cap, ids_ref):
    per_row = LANES // cap
    lane = lax.broadcasted_iota(jnp.int32, (1, LANES), 1)
    places = []
    for at in range(0, ids_ref.shape[0], per_row):
        total = None
        for i in range(per_row):
            row = jnp.where(lane < cap, ids_ref[at + i : at + i + 1, :], 0)
            row = pltpu.roll(row, i * cap, 1) if i else row
            total = row if total is None else total + row
        places.append(total)
    return places


def gather_inflow(places, first, rows, current):
    at = lax.broadcasted_iota(jnp.int32, (rows, LANES), 0) + first
    hits = [jnp.where(at == place, 1.0, 0.0).astype(BF16) for place in places]
    both = jnp.dot(jnp.concatenate(hits, axis=1), current, preferred_element_type=F32)
    return both[:, :LANES] + both[:, LANES:]


def ends_body(cap, tiles, ids_ref, current_ref, out_ref):
    half, _, _ = half_of(tiles)
    places = slot_places(cap, ids_ref)
    current = jnp.concatenate(halves(current_ref[...]), axis=1)
    out_ref[...] = gather_inflow(places, half * (tiles - 1) * LANES, LANES, current)


def inflow_body(
    cap, tiles, ids_ref, current_ref, coup_ref, own_ref, halo_ref, near_ref, after_ref,
    out_ref, band_ref, inv_ref, base_ref, plane_ref,
):
    half, own, shift = half_of(tiles)
    first, count = 1 - half, own + 1
    places = slot_places(cap, ids_ref)
    current = jnp.concatenate(halves(current_ref[...]), axis=1)

    def inflow(tile, size):
        cut = span(tile, 0, size * LANES)
        out_ref[cut, :] = gather_inflow(
            places, (tile + shift) * LANES, size * LANES, current
        )

    in_chunks(first, count, inflow)
    out_ref[span(half * (own + 1)), :] = jnp.zeros((LANES, LANES), F32)

    neighbours = (own_ref.shape[0] - 2 * LANES) // 2
    begin = (place()[1] * tiles + 2 * half * own - 1) * LANES
    packs = [jnp.where(half == at, halo_ref[...], own_ref[...]) for at in range(2)]
    at = 2 * LANES
    bands = []
    for tile, pack in enumerate(packs):
        bands.append(
            build_band(
                begin + tile * LANES - RADIUS,
                pack[at : at + neighbours].astype(jnp.int32),
                pack[at + neighbours : at + 2 * neighbours],
            )
        )
        store(plane_ref, tile, pack[:LANES])
    none = jnp.zeros((RADIUS, 2 * LANES), BF16)
    low, high = (
        jnp.concatenate(halves(near_ref[cut, :]), axis=1)
        for cut in (slice(0, RADIUS), slice(RADIUS, 2 * RADIUS))
    )
    size = plane_ref.shape[0]
    plane_ref[0:RADIUS, :] = jnp.where(half == 0, none, high)
    plane_ref[size - RADIUS : size, :] = jnp.where(half == 0, low, none)
    results = []
    couple(plane_ref, 0, bands, mixer(coup_ref), lambda tile, values: results.append(values))
    band_ref[...] = jnp.where(half == 0, bands[0], bands[1])
    inv_ref[...] = reciprocal(halo_ref[LANES : 2 * LANES, :])
    base_ref[0:LANES, :] = jnp.where(half == 0, results[0], results[1])
    base_ref[LANES:, :] = jnp.where(half == 0, results[1], results[0])


def iterate_body(
    cap, die_count, asked_ref, coup_ref, halo_ref, inflow_ref, band_ref, base_ref, inv_ref,
    halo_band_ref, halo_inv_ref, edge_base_ref, out_hbm, full_hbm, picked_ref, out_ref, here_ref, there_ref, sems,
):
    own = out_hbm.shape[0] // LANES
    half, _, _ = half_of(2 * own)
    first, count, outer = 1 - half, own + 1, half * (own + 1)
    edge = 1 + half * (own - 1)
    for ref in (here_ref, there_ref):
        clear_pads(ref)

    def start(tile, size):
        cut = span(tile, 0, size * LANES)
        store(here_ref, tile, -(inflow_ref[cut, :] + base_ref[cut, :]) * inv_ref[cut, :])

    in_chunks(first, count, start)
    halo_inv = halo_inv_ref[...]
    store(here_ref, outer, -(halo_ref[...] + edge_base_ref[0:LANES, :]) * halo_inv)
    cut = span(edge)
    store(here_ref, edge, -(inflow_ref[cut, :] + edge_base_ref[LANES:, :]) * inv_ref[cut, :])
    mix = mixer(coup_ref)
    refs = (here_ref, there_ref)
    for iteration in range(1, ITERS):
        source, target = refs[(iteration - 1) % 2], refs[iteration % 2]
        last = iteration == ITERS - 1

        def write(tile, coupled, target=target, last=last):
            values = -(inflow_ref[span(tile), :] + coupled) * inv_ref[span(tile), :]
            if last:
                out_ref[span(tile - 1), :] = values
            else:
                store(target, tile, values)

        def step(tile, size, source=source, write=write):
            bands = [band_ref[tile + i] for i in range(size)]
            couple(source, tile, bands, mix, write)

        def final(tile, size, step=step):
            step(tile, size)
            cut = span(tile - 1, 0, size * LANES)
            whole = span(half * own + tile - 1, 0, size * LANES)
            pltpu.make_async_copy(out_ref.at[cut, :], out_hbm.at[cut, :], sems.at[0]).start()
            pltpu.make_async_copy(out_ref.at[cut, :], full_hbm.at[whole, :], sems.at[1]).start()

        def write_halo(tile, coupled, target=target):
            store(target, tile, -(halo_ref[...] + coupled) * halo_inv)

        if last:
            in_chunks(1, own, final)
        else:
            in_chunks(first, count, step)
            couple(source, outer, [halo_band_ref[...]], mix, write_halo)

    base_row = half * own * LANES
    group, _ = place()
    pair = group - lax.rem(group, 2)
    for member in range(2):
        offset = member * (picked_ref.shape[0] // 2)
        for at, row in asked_rows(cap, die_count, pair + member, asked_ref):
            row = row - base_row
            inside = (row >= 0) & (row < own * LANES)
            safe = jnp.clip(row, 0, own * LANES - 1)
            values = out_ref[pl.ds(safe, 1), :]
            picked_ref[pl.ds(offset + at, 1), :] = jnp.where(inside, values, 0.0)
    pltpu.make_async_copy(out_ref, out_hbm, sems.at[0]).wait()
    pltpu.make_async_copy(out_ref, full_hbm.at[0 : own * LANES, :], sems.at[1]).wait()


def join_body(other_ref, full_in_hbm, full_hbm, done_ref, sem):
    rows = other_ref.shape[0]
    half, _, _ = half_of(2 * rows // LANES)
    start = pl.multiple_of((1 - half) * rows, LANES)
    copy = pltpu.make_async_copy(other_ref, full_hbm.at[pl.ds(start, rows), :], sem)
    copy.start()
    done_ref[...] = jnp.zeros(done_ref.shape, F32)
    copy.wait()


def add_body(parts_ref, after_ref, out_ref):
    rows = out_ref.shape[0]
    out_ref[...] = parts_ref[0:rows, :] + parts_ref[rows:, :]


def scatter_body(cols, node_ref, cond_ref, start_ref, volt_ref, load_ref, shunt_ref,
                 right_ref, inv_ref, inner_ref, outer_ref):
    blocks = node_ref.shape[0]
    rows = volt_ref.shape[0]
    group = 8
    row_at = lax.broadcasted_iota(jnp.int32, (rows, LANES), 0)
    col_at = lax.broadcasted_iota(jnp.int32, (cols, LANES), 0)
    total = jnp.zeros((4 * rows, cols), F32)
    for first in range(0, blocks, group):
        node = node_ref[first : first + group, :]
        live = node >= 0
        cond = jnp.where(live, cond_ref[first : first + group, :], 0.0)
        flow = cond * start_ref[first : first + group, :]
        safe = jnp.where(live, node, 0)
        row, col = safe // cols, safe % cols
        parts = halves(cond) + halves(flow)
        left, right = [], []
        for i in range(group):
            spot = jnp.where(row_at == row[i : i + 1, :], 1.0, 0.0).astype(BF16)
            left.append(
                jnp.concatenate([spot * part[i : i + 1, :] for part in parts], axis=0)
            )
            right.append(jnp.where(col_at == col[i : i + 1, :], 1.0, 0.0).astype(BF16))
        total = total + lax.dot_general(
            jnp.concatenate(left, axis=1),
            jnp.concatenate(right, axis=1),
            (((1,), (1,)), ((), ())),
            preferred_element_type=F32,
        )
    gsum = total[:rows] + total[rows : 2 * rows]
    inject = total[2 * rows : 3 * rows] + total[3 * rows :]
    inv = 1.0 / (4.0 + shunt_ref[...] + gsum)
    right_side = (inject - load_ref[...]) * inv
    right_ref[...] = right_side
    inv_ref[...] = inv
    volt = volt_ref[...]
    top, bottom = (
        jnp.concatenate([volt[cut], right_side[cut], inv[cut]], axis=0)
        for cut in (slice(0, HALO_ROWS), slice(rows - HALO_ROWS, rows))
    )
    swap_parts(inner_ref, outer_ref, place()[0], top, bottom)


def swap_parts(inner_ref, outer_ref, mine, first, last):
    even = lax.rem(mine, 2) == 0
    inner_ref[...] = jnp.where(even, last, first)
    outer_ref[...] = jnp.where(even, first, last)


def swapped(inner, outer, mine):
    even = lax.rem(mine, 2) == 0
    return jnp.where(even, outer, inner), jnp.where(even, inner, outer)


def swap(inner, outer, axis):
    count = lax.axis_size(axis)

    def pairs(start):
        return [
            pair
            for i in range(start, count - 1, 2)
            for pair in ((i, i + 1), (i + 1, i))
        ]

    return lax.ppermute(outer, axis, pairs(1)), lax.ppermute(inner, axis, pairs(0))


def extended(own, top, bottom, index):
    cut = slice(index * HALO_ROWS, (index + 1) * HALO_ROWS)
    return jnp.concatenate([own, bottom[cut], top[cut]], axis=0)


def edge_body(
    volt_ref, right_ref, inv_ref, outer_ref, inner_ref, after_ref, west_ref, east_ref
):
    cols = volt_ref.shape[1]
    top, bottom = swapped(inner_ref[...], outer_ref[...], place()[0])
    out_rows, high = west_ref.shape
    west, east = None, None
    for index, ref in enumerate((volt_ref, right_ref, inv_ref)):
        whole = extended(ref[...], top, bottom, index)
        lane = lax.broadcasted_iota(jnp.int32, (whole.shape[0], LANES), 1)
        head, tail = whole[:, :LANES], whole[:, cols - LANES :]
        at = index * SWEEPS
        head = pltpu.roll(head, at, 1) if at else head
        tail = pltpu.roll(tail, at + SWEEPS, 1)
        west = head if west is None else jnp.where(lane >= at, head, west)
        east = tail if east is None else jnp.where(lane >= at, tail, east)
    fill = jnp.zeros((high - west.shape[0], LANES), F32)
    west, east = (
        jnp.concatenate([part, fill], axis=0).T[:out_rows] for part in (west, east)
    )
    swap_parts(west_ref, east_ref, place()[1], west, east)


def sweep_body(copies, node_ref, cond_ref, start_ref, volt_ref, right_ref, inv_ref,
               row_out_ref, row_in_ref, col_out_ref, col_in_ref, out_ref, current_ref):
    rows, cols = volt_ref.shape
    blocks = node_ref.shape[0]
    cap = current_ref.shape[1]
    whole = []
    top, bottom = swapped(row_in_ref[...], row_out_ref[...], place()[0])
    out_rows, high = col_in_ref.shape
    fill = jnp.zeros((LANES - out_rows, high), F32)
    wests, easts = (
        jnp.concatenate([part, fill], axis=0).T[: rows + 2 * HALO_ROWS]
        for part in swapped(col_in_ref[...], col_out_ref[...], place()[1])
    )
    eastern = lax.broadcasted_iota(jnp.int32, easts.shape, 1) < LANES // 2
    for index, ref in enumerate((volt_ref, right_ref, inv_ref)):
        own = extended(ref[...], top, bottom, index)
        at = index * SWEEPS
        west = pltpu.roll(wests, LANES - SWEEPS - at, 1)
        east = pltpu.roll(easts, LANES - at, 1) if at else easts
        whole.append(jnp.concatenate([own, jnp.where(eastern, east, west)], axis=1))
    volt, right_side, inv = whole
    high, wide = volt.shape
    for weight in sweep_weights(SWEEPS):
        beside = (
            pltpu.roll(volt, 1, 0)
            + pltpu.roll(volt, high - 1, 0)
            + pltpu.roll(volt, 1, 1)
            + pltpu.roll(volt, wide - 1, 1)
        )
        volt = (1.0 - weight) * volt + weight * (right_side + beside * inv)
    volt = volt[:rows, :cols]
    out_ref[...] = volt
    both = jnp.concatenate(halves(volt), axis=0)
    group = 8
    row_at = lax.broadcasted_iota(jnp.int32, (rows, LANES), 0)
    col_at = lax.broadcasted_iota(jnp.int32, (cols, LANES), 0)
    dies = blocks // cap
    for first in range(0, blocks, group):
        node = node_ref[first : first + group, :]
        live = node >= 0
        cond = jnp.where(live, cond_ref[first : first + group, :], 0.0)
        safe = jnp.where(live, node, 0)
        row, col = safe // cols, safe % cols
        spots = jnp.concatenate(
            [
                jnp.where(col_at == col[i : i + 1, :], 1.0, 0.0).astype(BF16)
                for i in range(group)
            ],
            axis=1,
        )
        found = jnp.dot(both, spots, preferred_element_type=F32)
        found = found[:rows] + found[rows:]
        for i in range(group):
            mine = found[:, i * LANES : (i + 1) * LANES]
            at_bump = jnp.sum(
                jnp.where(row_at == row[i : i + 1, :], mine, 0.0), axis=0, keepdims=True
            )
            block = first + i
            current = cond[i : i + 1, :] * (start_ref[block : block + 1, :] - at_bump)
            current_ref[block // cap, block % cap : block % cap + 1, :] = current
    for copy in range(1, copies):
        current_ref[copy * dies : (copy + 1) * dies] = current_ref[0:dies]


def local(
    die_volt,
    die_load,
    die_shunt,
    bump_node,
    bump_block,
    bump_cond,
    pkg_volt,
    pkg_diag,
    pkg_pattern,
    pkg_weight,
    block_coupling,
):
    die_count = lax.axis_size("die")
    group_count = lax.axis_size("grp")
    devices = die_count * group_count
    blocks = pkg_volt.shape[0]
    tiles = blocks // LANES
    neighbours = pkg_pattern.shape[0]
    slots = bump_block.shape[0]
    cap = slots // die_count
    rows, cols = die_volt.shape
    (spread,) = call(
        functools.partial(spread_body, cap, die_count, blocks),
        "spread_blocks",
        [shape(devices, 1, LANES, dtype=jnp.int32)],
        (bump_block.reshape(1, slots),),
        [VMEM],
    )
    ids = lax.all_to_all(
        spread, ("grp", "die"), split_axis=0, concat_axis=0, tiled=True
    ).reshape(devices, LANES)

    (picked,) = call(
        functools.partial(pick_body, cap, die_count),
        "pick_rows",
        [shape(slots, LANES)],
        (ids, pkg_volt),
        [SMEM, VMEM],
    )
    bump_start = lax.all_to_all(
        picked.reshape(die_count, cap, LANES), "die", split_axis=0, concat_axis=0, tiled=True
    ).reshape(slots, LANES)

    right_side, inv, *edges = call(
        functools.partial(scatter_body, cols),
        "scatter_bumps",
        [shape(rows, cols)] * 2 + [shape(3 * HALO_ROWS, cols)] * 2,
        (bump_node, bump_cond, bump_start, die_volt, die_load, die_shunt),
        [VMEM] * 6,
        work=3,
    )
    own = tiles // 2
    dma = pltpu.SemaphoreType.DMA
    plane = pltpu.VMEM(((own + 2) * LANES + 2 * RADIUS, 2 * LANES), BF16)
    range_rows = pltpu.VMEM(((own + 2) * LANES, LANES), F32)
    range_bands = pltpu.VMEM((own + 2, 2 * LANES, 2 * LANES), BF16)
    beside = swap(*edges, "grp")
    band, banded = call(
        bands_body,
        "package_bands",
        [shape(own + 2, 2 * LANES, 2 * LANES, dtype=BF16), shape(8, LANES)],
        (pkg_pattern, pkg_weight, right_side),
        [VMEM, VMEM, ANY],
        work=2,
    )

    edge_rows = -(-3 * SWEEPS // 8) * 8
    edge_cols = -(-(rows + 2 * HALO_ROWS) // LANES) * LANES
    edges = call(
        edge_body,
        "edge_columns",
        [shape(edge_rows, edge_cols)] * 2,
        (die_volt, right_side, inv, *beside, banded),
        [VMEM] * 5 + [ANY],
    )
    columns = swap(*edges, "die")

    die_out, current = call(
        functools.partial(sweep_body, group_count),
        "sweeps",
        [shape(rows, cols), shape(devices, cap, LANES)],
        (bump_node, bump_cond, bump_start, die_volt, right_side, inv, *beside, *columns),
        [VMEM] * 10,
        work=4,
    )
    pack_rows = 2 * LANES + 2 * neighbours
    base, pkg_inv, pack, near = call(
        prepare_body,
        "package_prepare",
        [
            shape((own + 2) * LANES, LANES),
            shape((own + 2) * LANES, LANES),
            shape(pack_rows, LANES),
            shape(2 * RADIUS, LANES),
        ],
        (pkg_pattern, pkg_weight, block_coupling, band, pkg_volt, pkg_diag, die_out),
        [HBM] * 7,
        [
            range_rows, range_rows, range_bands, range_rows, range_rows, plane,
            pltpu.VMEM((LANES, LANES), F32), pltpu.VMEM((neighbours, LANES), jnp.int32),
            pltpu.VMEM((2 * neighbours, LANES), F32), dma((6,)), dma((7,)),
        ],
        work=5,
        vmem=MOST_VMEM,
        out_specs=[HBM] * 4,
    )

    current = lax.all_to_all(
        current, ("grp", "die"), split_axis=0, concat_axis=0, tiled=True
    ).reshape(devices * cap, LANES)

    beside_end = [
        (g * die_count + a, g * die_count + b)
        for g in range(group_count)
        for d in range((g + 1) % 2, die_count - 1, 2)
        for a, b in ((d, d + 1), (d + 1, d))
    ]
    halo = lax.ppermute(pack, ("grp", "die"), beside_end)
    (inflow,) = call(
        functools.partial(ends_body, cap, tiles),
        "package_end",
        [shape(LANES, LANES)],
        (ids, current),
        [VMEM, VMEM],
    )
    halo_inflow = lax.ppermute(inflow, ("grp", "die"), beside_end)
    all_inflow, halo_band, halo_inv, edge_base = call(
        functools.partial(inflow_body, cap, tiles),
        "package_inflow",
        [
            shape((own + 2) * LANES, LANES),
            shape(2 * LANES, 2 * LANES, dtype=BF16),
            shape(LANES, LANES),
            shape(2 * LANES, LANES),
        ],
        (ids, current, block_coupling, pack, halo, near, inflow),
        [VMEM] * 6 + [ANY],
        [pltpu.VMEM((2 * LANES + 2 * RADIUS, 2 * LANES), BF16)],
        work=3,
    )
    half_out, pkg_out, picked = call(
        functools.partial(iterate_body, cap, die_count),
        "package_iterations",
        [shape(own * LANES, LANES), shape(blocks, LANES), shape(2 * slots, LANES)],
        (
            ids, block_coupling, halo_inflow, all_inflow, band, base, pkg_inv,
            halo_band, halo_inv, edge_base,
        ),
        [SMEM] + [VMEM] * 9,
        [pltpu.VMEM((own * LANES, LANES), F32), plane, plane, dma((2,))],
        work=10,
        vmem=24,
        out_specs=[HBM, HBM, VMEM],
    )
    pair = 2 * die_count
    parts = lax.all_to_all(
        picked.reshape(pair, cap, LANES),
        ("grp", "die"),
        split_axis=0,
        concat_axis=0,
        axis_index_groups=[
            [first + i for i in range(pair)] for first in range(0, devices, pair)
        ],
        tiled=True,
    ).reshape(2 * slots, LANES)
    other = lax.ppermute(half_out, "grp", [(g, g ^ 1) for g in range(group_count)])
    pkg_out, done = call(
        join_body,
        "join_halves",
        [shape(blocks, LANES), shape(8, LANES)],
        (other, pkg_out),
        [VMEM, HBM],
        [dma(())],
        out_specs=[HBM, VMEM],
        aliases={1: 0},
    )
    (bump_out,) = call(
        add_body, "add_parts", [shape(slots, LANES)], (parts, done), [VMEM, ANY]
    )
    return (die_out, pkg_out, bump_out)


def solution(mesh):
    return jax.shard_map(
        local,
        mesh=mesh,
        in_specs=(
            P("grp", "die"),
            P("grp", "die"),
            P("grp", "die"),
            P(("grp", "die"), None),
            P(("grp", "die")),
            P(("grp", "die"), None),
            P("die", None),
            P("die", None),
            P(None, "die"),
            P(None, "die"),
            P(),
        ),
        out_specs=(P("grp", "die"), P("die", None), P(("grp", "die"), None)),
        check_vma=False,
    )
```

```python
import functools
import math

import jax
import jax.numpy as jnp
from jax import lax
from jax.experimental import pallas as pl
from jax.experimental.pallas import tpu as pltpu
from jax.sharding import PartitionSpec as P

RADIUS = 32
SWEEPS = 4
ITERS = 4
LANES = 128
HALO_ROWS = 8
REACH = RADIUS * ITERS
WINDOW = LANES + 2 * RADIUS
F32 = jnp.float32
BF16 = jnp.bfloat16
MOST_VMEM = 57
VMEM = pl.BlockSpec(memory_space=pltpu.VMEM)
SMEM = pl.BlockSpec(memory_space=pltpu.SMEM)
ANY = pl.BlockSpec(memory_space=pl.ANY)
HBM = pl.BlockSpec(memory_space=pltpu.HBM)


def sweep_weights(sweeps):
    return [
        1.0 / (1.0 + 0.8 * math.cos(math.pi * (2 * index + 1) / (2 * sweeps)))
        for index in range(sweeps)
    ]


def call(
    body, name, outs, args, specs, scratch=(), work=1, vmem=16, out_specs=None, aliases=None
):
    bytes_accessed = sum(4 * math.prod(arg.shape) for arg in args)
    return pl.pallas_call(
        body,
        name=name,
        out_shape=outs,
        in_specs=specs,
        out_specs=out_specs or [VMEM] * len(outs),
        input_output_aliases=aliases or {},
        scratch_shapes=list(scratch),
        compiler_params=pltpu.CompilerParams(vmem_limit_bytes=vmem * 1024 * 1024),
        cost_estimate=pl.CostEstimate(
            flops=work * 10**9, bytes_accessed=bytes_accessed, transcendentals=0
        ),
    )(*args)


def place():
    return lax.axis_index("grp"), lax.axis_index("die")


def shape(*dims, dtype=F32):
    return jax.ShapeDtypeStruct(dims, dtype)


def halves(values):
    high = values.astype(BF16)
    low = (values - high.astype(F32)).astype(BF16)
    return high, low


def spread_body(cap, die_count, blocks, block_ref, out_ref):
    slots = block_ref.shape[1]
    block = jnp.concatenate(
        [block_ref[...], jnp.zeros((1, LANES - slots), jnp.int32)], axis=1
    )
    for die in range(die_count):
        row = (pltpu.roll(block, LANES - die * cap, 1) if die else block) - die * blocks
        for at in range(die, out_ref.shape[0], die_count):
            out_ref[at] = row


def asked_rows(cap, die_count, group, ids_ref):
    for die in range(die_count):
        for slot in range(cap):
            yield die * cap + slot, ids_ref[group * die_count + die, slot]


def pick_body(cap, die_count, ids_ref, plane_ref, out_ref):
    group, _ = place()
    for at, row in asked_rows(cap, die_count, group, ids_ref):
        out_ref[pl.ds(at, 1), :] = plane_ref[pl.ds(row, 1), :]


def build_band(first, pattern, weights):
    place = lax.broadcasted_iota(jnp.int32, (WINDOW, LANES), 0)
    band = None
    for k in range(pattern.shape[0]):
        hit = place == (pattern[k : k + 1, :] - first)
        term = jnp.where(hit, weights[k : k + 1, :], 0.0)
        band = term if band is None else band + term
    fill = jnp.zeros((2 * LANES - WINDOW, LANES), F32)
    return jnp.concatenate(halves(jnp.concatenate([band, fill], axis=0).T), axis=0)


def reciprocal(diag):
    safe = jnp.where(diag > 0.0, diag, 1.0)
    return jnp.where(diag > 0.0, 1.0 / safe, 0.0)


def span(tile, offset=0, size=LANES):
    return pl.ds(pl.multiple_of(tile * LANES + offset, RADIUS), size)


def mixer(coup_ref):
    mix = jnp.concatenate(halves(coup_ref[...]), axis=1)
    return jnp.concatenate([mix, mix], axis=0)


def clear_pads(ref):
    pad = jnp.zeros((RADIUS, 2 * LANES), BF16)
    ref[0:RADIUS, :] = pad
    ref[ref.shape[0] - RADIUS :, :] = pad


def store(ref, tile, values):
    ref[span(tile, RADIUS, values.shape[0]), :] = jnp.concatenate(halves(values), axis=1)


def couple(source, tile, bands, mix, write):
    for at in range(0, len(bands), 4):
        couple_few(source, tile + at, bands[at : at + 4], mix, write)


def couple_few(source, tile, bands, mix, write):
    own = source[span(tile, RADIUS, len(bands) * LANES), :]
    within = jnp.dot(own, mix, preferred_element_type=F32)
    for i, band in enumerate(bands):
        window = source[span(tile + i, 0, WINDOW), :]
        beside = jnp.dot(band[:, :WINDOW], window, preferred_element_type=F32)
        both = beside[:LANES] + beside[LANES:] + within[i * LANES : (i + 1) * LANES]
        write(tile + i, both[:, :LANES] + both[:, LANES:])


def in_chunks(first, count, body, size=16):
    whole = count // size

    @pl.loop(0, whole)
    def _(chunk):
        body(first + chunk * size, size)

    if count % size:
        body(first + whole * size, count % size)


def half_of(tiles):
    half = lax.rem(sum(place()), 2)
    own = tiles // 2
    return half, own, half * own - 1


def bands_body(pat_ref, wgt_ref, after_ref, band_ref, done_ref):
    blocks = pat_ref.shape[1]
    half, own, shift = half_of(blocks // LANES)
    begin = place()[1] * blocks + shift * LANES

    def bands(tile, size):
        for i in range(size):
            lanes = pl.ds(pl.multiple_of((tile + i + shift) * LANES, LANES), LANES)
            band_ref[tile + i] = build_band(
                begin + (tile + i) * LANES - RADIUS, pat_ref[:, lanes], wgt_ref[:, lanes]
            )

    in_chunks(1 - half, own + 1, bands, 8)
    band_ref[half * (own + 1)] = jnp.zeros(band_ref.shape[1:], BF16)
    done_ref[...] = jnp.zeros(done_ref.shape, F32)


def prepare_body(
    pat_hbm, wgt_hbm, coup_hbm, band_hbm, volt_hbm, diag_hbm, after_ref,
    base_hbm, inv_hbm, pack_hbm, near_hbm,
    volt_ref, diag_ref, band_ref, base_ref, inv_ref, plane_ref, coup_ref, pat_ref, wgt_ref,
    sems, out_sems,
):
    blocks = volt_hbm.shape[0]
    half, own, shift = half_of(blocks // LANES)
    first, count, outer = 1 - half, own + 1, half * (own + 1)
    edge = 1 + half * (own - 1)
    known = pl.ds(pl.multiple_of(first * LANES, LANES), count * LANES)
    source = pl.ds(pl.multiple_of((first + shift) * LANES, LANES), count * LANES)
    lanes = pl.ds(pl.multiple_of((edge + shift) * LANES, LANES), LANES)
    neighbours = pat_hbm.shape[0]
    loads = [
        pltpu.make_async_copy(hbm, ref, sems.at[i])
        for i, (hbm, ref) in enumerate(
            (
                (volt_hbm.at[source, :], volt_ref.at[known, :]),
                (diag_hbm.at[source, :], diag_ref.at[known, :]),
                (coup_hbm, coup_ref),
                (pat_hbm.at[:, lanes], pat_ref),
                (wgt_hbm.at[:, lanes], wgt_ref.at[neighbours : 2 * neighbours, :]),
                (band_hbm, band_ref),
            )
        )
    ]
    for load in loads:
        load.start()
    writes = []

    def write_out(ref, hbm):
        writes.append(pltpu.make_async_copy(ref, hbm, out_sems.at[len(writes)]))
        writes[-1].start()

    clear_pads(plane_ref)
    plane_ref[span(outer, RADIUS), :] = jnp.zeros((LANES, 2 * LANES), BF16)
    for load in loads[:5]:
        load.wait()
    at = 2 * LANES
    write_out(volt_ref.at[span(edge), :], pack_hbm.at[0:LANES, :])
    write_out(diag_ref.at[span(edge), :], pack_hbm.at[LANES:at, :])
    wgt_ref[0:neighbours, :] = pat_ref[...].astype(F32)
    write_out(wgt_ref, pack_hbm.at[at : at + 2 * neighbours, :])
    write_out(
        volt_ref.at[2 * LANES : 2 * LANES + RADIUS, :], near_hbm.at[0:RADIUS, :]
    )
    write_out(
        volt_ref.at[own * LANES - RADIUS : own * LANES, :],
        near_hbm.at[RADIUS : 2 * RADIUS, :],
    )

    def spread(tile, size):
        cut = span(tile, 0, size * LANES)
        store(plane_ref, tile, volt_ref[cut, :])
        inv_ref[cut, :] = reciprocal(diag_ref[cut, :])

    in_chunks(first, count, spread, 8)
    write_out(inv_ref.at[known, :], inv_hbm.at[known, :])
    mix = mixer(coup_ref)
    loads[5].wait()

    def base(tile, size):
        def write(tile, values):
            base_ref[span(tile), :] = values

        couple(plane_ref, tile, [band_ref[tile + i] for i in range(size)], mix, write)
        cut = span(tile, 0, size * LANES)
        pltpu.make_async_copy(
            base_ref.at[cut, :], base_hbm.at[cut, :], out_sems.at[6]
        ).start()

    in_chunks(first, count, base, 8)
    for write in writes:
        write.wait()
    pltpu.make_async_copy(
        base_ref.at[known, :], base_hbm.at[known, :], out_sems.at[6]
    ).wait()


def slot_places(cap, ids_ref):
    per_row = LANES // cap
    lane = lax.broadcasted_iota(jnp.int32, (1, LANES), 1)
    places = []
    for at in range(0, ids_ref.shape[0], per_row):
        total = None
        for i in range(per_row):
            row = jnp.where(lane < cap, ids_ref[at + i : at + i + 1, :], 0)
            row = pltpu.roll(row, i * cap, 1) if i else row
            total = row if total is None else total + row
        places.append(total)
    return places


def gather_inflow(places, first, rows, current):
    at = lax.broadcasted_iota(jnp.int32, (rows, LANES), 0) + first
    hits = [jnp.where(at == place, 1.0, 0.0).astype(BF16) for place in places]
    both = jnp.dot(jnp.concatenate(hits, axis=1), current, preferred_element_type=F32)
    return both[:, :LANES] + both[:, LANES:]


def ends_body(cap, tiles, ids_ref, current_ref, out_ref):
    half, _, _ = half_of(tiles)
    places = slot_places(cap, ids_ref)
    current = jnp.concatenate(halves(current_ref[...]), axis=1)
    out_ref[...] = gather_inflow(places, half * (tiles - 1) * LANES, LANES, current)


def inflow_body(
    cap, tiles, ids_ref, current_ref, coup_ref, own_ref, halo_ref, near_ref, after_ref,
    out_ref, band_ref, inv_ref, base_ref, plane_ref,
):
    half, own, shift = half_of(tiles)
    first, count = 1 - half, own + 1
    places = slot_places(cap, ids_ref)
    current = jnp.concatenate(halves(current_ref[...]), axis=1)

    def inflow(tile, size):
        cut = span(tile, 0, size * LANES)
        out_ref[cut, :] = gather_inflow(
            places, (tile + shift) * LANES, size * LANES, current
        )

    in_chunks(first, count, inflow)
    out_ref[span(half * (own + 1)), :] = jnp.zeros((LANES, LANES), F32)

    neighbours = (own_ref.shape[0] - 2 * LANES) // 2
    begin = (place()[1] * tiles + 2 * half * own - 1) * LANES
    packs = [jnp.where(half == at, halo_ref[...], own_ref[...]) for at in range(2)]
    at = 2 * LANES
    bands = []
    for tile, pack in enumerate(packs):
        bands.append(
            build_band(
                begin + tile * LANES - RADIUS,
                pack[at : at + neighbours].astype(jnp.int32),
                pack[at + neighbours : at + 2 * neighbours],
            )
        )
        store(plane_ref, tile, pack[:LANES])
    none = jnp.zeros((RADIUS, 2 * LANES), BF16)
    low, high = (
        jnp.concatenate(halves(near_ref[cut, :]), axis=1)
        for cut in (slice(0, RADIUS), slice(RADIUS, 2 * RADIUS))
    )
    size = plane_ref.shape[0]
    plane_ref[0:RADIUS, :] = jnp.where(half == 0, none, high)
    plane_ref[size - RADIUS : size, :] = jnp.where(half == 0, low, none)
    results = []
    couple(plane_ref, 0, bands, mixer(coup_ref), lambda tile, values: results.append(values))
    band_ref[...] = jnp.where(half == 0, bands[0], bands[1])
    inv_ref[...] = reciprocal(halo_ref[LANES : 2 * LANES, :])
    base_ref[0:LANES, :] = jnp.where(half == 0, results[0], results[1])
    base_ref[LANES:, :] = jnp.where(half == 0, results[1], results[0])


def iterate_body(
    cap, die_count, asked_ref, coup_ref, halo_ref, inflow_ref, band_ref, base_ref, inv_ref,
    halo_band_ref, halo_inv_ref, edge_base_ref, out_hbm, full_hbm, picked_ref, out_ref, here_ref, there_ref, sems,
):
    own = out_hbm.shape[0] // LANES
    half, _, _ = half_of(2 * own)
    first, count, outer = 1 - half, own + 1, half * (own + 1)
    edge = 1 + half * (own - 1)
    for ref in (here_ref, there_ref):
        clear_pads(ref)

    def start(tile, size):
        cut = span(tile, 0, size * LANES)
        store(here_ref, tile, -(inflow_ref[cut, :] + base_ref[cut, :]) * inv_ref[cut, :])

    in_chunks(first, count, start)
    halo_inv = halo_inv_ref[...]
    store(here_ref, outer, -(halo_ref[...] + edge_base_ref[0:LANES, :]) * halo_inv)
    cut = span(edge)
    store(here_ref, edge, -(inflow_ref[cut, :] + edge_base_ref[LANES:, :]) * inv_ref[cut, :])
    mix = mixer(coup_ref)
    refs = (here_ref, there_ref)
    for iteration in range(1, ITERS):
        source, target = refs[(iteration - 1) % 2], refs[iteration % 2]
        last = iteration == ITERS - 1

        def write(tile, coupled, target=target, last=last):
            values = -(inflow_ref[span(tile), :] + coupled) * inv_ref[span(tile), :]
            if last:
                out_ref[span(tile - 1), :] = values
            else:
                store(target, tile, values)

        def step(tile, size, source=source, write=write):
            bands = [band_ref[tile + i] for i in range(size)]
            couple(source, tile, bands, mix, write)

        def final(tile, size, step=step):
            step(tile, size)
            cut = span(tile - 1, 0, size * LANES)
            whole = span(half * own + tile - 1, 0, size * LANES)
            pltpu.make_async_copy(out_ref.at[cut, :], out_hbm.at[cut, :], sems.at[0]).start()
            pltpu.make_async_copy(out_ref.at[cut, :], full_hbm.at[whole, :], sems.at[1]).start()

        def write_halo(tile, coupled, target=target):
            store(target, tile, -(halo_ref[...] + coupled) * halo_inv)

        if last:
            in_chunks(1, own, final)
        else:
            in_chunks(first, count, step)
            couple(source, outer, [halo_band_ref[...]], mix, write_halo)

    base_row = half * own * LANES
    group, _ = place()
    pair = group - lax.rem(group, 2)
    for member in range(2):
        offset = member * (picked_ref.shape[0] // 2)
        for at, row in asked_rows(cap, die_count, pair + member, asked_ref):
            row = row - base_row
            inside = (row >= 0) & (row < own * LANES)
            safe = jnp.clip(row, 0, own * LANES - 1)
            values = out_ref[pl.ds(safe, 1), :]
            picked_ref[pl.ds(offset + at, 1), :] = jnp.where(inside, values, 0.0)
    pltpu.make_async_copy(out_ref, out_hbm, sems.at[0]).wait()
    pltpu.make_async_copy(out_ref, full_hbm.at[0 : own * LANES, :], sems.at[1]).wait()


def join_body(other_ref, full_in_hbm, full_hbm, done_ref, sem):
    rows = other_ref.shape[0]
    half, _, _ = half_of(2 * rows // LANES)
    start = pl.multiple_of((1 - half) * rows, LANES)
    copy = pltpu.make_async_copy(other_ref, full_hbm.at[pl.ds(start, rows), :], sem)
    copy.start()
    done_ref[...] = jnp.zeros(done_ref.shape, F32)
    copy.wait()


def add_body(parts_ref, after_ref, out_ref):
    rows = out_ref.shape[0]
    out_ref[...] = parts_ref[0:rows, :] + parts_ref[rows:, :]


def scatter_body(cols, node_ref, cond_ref, start_ref, volt_ref, load_ref, shunt_ref,
                 right_ref, inv_ref, inner_ref, outer_ref):
    blocks = node_ref.shape[0]
    rows = volt_ref.shape[0]
    group = 8
    row_at = lax.broadcasted_iota(jnp.int32, (rows, LANES), 0)
    col_at = lax.broadcasted_iota(jnp.int32, (cols, LANES), 0)
    total = jnp.zeros((4 * rows, cols), F32)
    for first in range(0, blocks, group):
        node = node_ref[first : first + group, :]
        live = node >= 0
        cond = jnp.where(live, cond_ref[first : first + group, :], 0.0)
        flow = cond * start_ref[first : first + group, :]
        safe = jnp.where(live, node, 0)
        row, col = safe // cols, safe % cols
        parts = halves(cond) + halves(flow)
        left, right = [], []
        for i in range(group):
            spot = jnp.where(row_at == row[i : i + 1, :], 1.0, 0.0).astype(BF16)
            left.append(
                jnp.concatenate([spot * part[i : i + 1, :] for part in parts], axis=0)
            )
            right.append(jnp.where(col_at == col[i : i + 1, :], 1.0, 0.0).astype(BF16))
        total = total + lax.dot_general(
            jnp.concatenate(left, axis=1),
            jnp.concatenate(right, axis=1),
            (((1,), (1,)), ((), ())),
            preferred_element_type=F32,
        )
    gsum = total[:rows] + total[rows : 2 * rows]
    inject = total[2 * rows : 3 * rows] + total[3 * rows :]
    inv = 1.0 / (4.0 + shunt_ref[...] + gsum)
    right_side = (inject - load_ref[...]) * inv
    right_ref[...] = right_side
    inv_ref[...] = inv
    volt = volt_ref[...]
    top, bottom = (
        jnp.concatenate([volt[cut], right_side[cut], inv[cut]], axis=0)
        for cut in (slice(0, HALO_ROWS), slice(rows - HALO_ROWS, rows))
    )
    swap_parts(inner_ref, outer_ref, place()[0], top, bottom)


def swap_parts(inner_ref, outer_ref, mine, first, last):
    even = lax.rem(mine, 2) == 0
    inner_ref[...] = jnp.where(even, last, first)
    outer_ref[...] = jnp.where(even, first, last)


def swapped(inner, outer, mine):
    even = lax.rem(mine, 2) == 0
    return jnp.where(even, outer, inner), jnp.where(even, inner, outer)


def swap(inner, outer, axis):
    count = lax.axis_size(axis)

    def pairs(start):
        return [
            pair
            for i in range(start, count - 1, 2)
            for pair in ((i, i + 1), (i + 1, i))
        ]

    return lax.ppermute(outer, axis, pairs(1)), lax.ppermute(inner, axis, pairs(0))


def extended(own, top, bottom, index):
    cut = slice(index * HALO_ROWS, (index + 1) * HALO_ROWS)
    return jnp.concatenate([own, bottom[cut], top[cut]], axis=0)


def edge_body(
    volt_ref, right_ref, inv_ref, outer_ref, inner_ref, after_ref, west_ref, east_ref
):
    cols = volt_ref.shape[1]
    top, bottom = swapped(inner_ref[...], outer_ref[...], place()[0])
    out_rows, high = west_ref.shape
    west, east = None, None
    for index, ref in enumerate((volt_ref, right_ref, inv_ref)):
        whole = extended(ref[...], top, bottom, index)
        lane = lax.broadcasted_iota(jnp.int32, (whole.shape[0], LANES), 1)
        head, tail = whole[:, :LANES], whole[:, cols - LANES :]
        at = index * SWEEPS
        head = pltpu.roll(head, at, 1) if at else head
        tail = pltpu.roll(tail, at + SWEEPS, 1)
        west = head if west is None else jnp.where(lane >= at, head, west)
        east = tail if east is None else jnp.where(lane >= at, tail, east)
    fill = jnp.zeros((high - west.shape[0], LANES), F32)
    west, east = (
        jnp.concatenate([part, fill], axis=0).T[:out_rows] for part in (west, east)
    )
    swap_parts(west_ref, east_ref, place()[1], west, east)


def swept(volt, right_side, inv):
    high, wide = volt.shape
    for weight in sweep_weights(SWEEPS):
        beside = (
            pltpu.roll(volt, 1, 0)
            + pltpu.roll(volt, high - 1, 0)
            + pltpu.roll(volt, 1, 1)
            + pltpu.roll(volt, wide - 1, 1)
        )
        volt = (1.0 - weight) * volt + weight * (right_side + beside * inv)
    return volt


GROUP = 8


def one_hot(rows, places):
    at = lax.broadcasted_iota(jnp.int32, (rows, LANES), 0)
    return jnp.concatenate(
        [
            jnp.where(at == places[i : i + 1, :], 1.0, 0.0).astype(BF16)
            for i in range(places.shape[0])
        ],
        axis=1,
    )


def pick_rows(found, places):
    at = lax.broadcasted_iota(jnp.int32, (found.shape[0], LANES), 0)
    return [
        jnp.sum(
            jnp.where(at == places[i : i + 1, :], found[:, i * LANES : (i + 1) * LANES], 0.0),
            axis=0,
            keepdims=True,
        )
        for i in range(places.shape[0])
    ]


def inner_body(node_ref, volt_ref, right_ref, inv_ref, row_out_ref, row_in_ref, out_ref, found_ref):
    rows, cols = volt_ref.shape
    top, bottom = swapped(row_in_ref[...], row_out_ref[...], place()[0])
    volt = swept(
        *(
            extended(ref[...], top, bottom, index)
            for index, ref in enumerate((volt_ref, right_ref, inv_ref))
        )
    )[:rows]
    out_ref[...] = volt
    col = lax.broadcasted_iota(jnp.int32, volt.shape, 1)
    volt = jnp.where((col >= SWEEPS) & (col < cols - SWEEPS), volt, 0.0)
    both = jnp.concatenate(halves(volt), axis=0)
    for first in range(0, node_ref.shape[0], GROUP):
        safe = jnp.maximum(node_ref[first : first + GROUP, :], 0)
        found = jnp.dot(both, one_hot(cols, safe % cols), preferred_element_type=F32)
        found = pick_rows(found[:rows] + found[rows:], safe // cols)
        for i, values in enumerate(found):
            found_ref[first + i : first + i + 1, :] = values


def sweep_body(copies, node_ref, cond_ref, start_ref, volt_ref, right_ref, inv_ref,
               row_out_ref, row_in_ref, col_out_ref, col_in_ref, inner_ref, found_ref,
               out_ref, current_ref):
    rows, cols = volt_ref.shape
    blocks = node_ref.shape[0]
    cap = current_ref.shape[1]
    quarter = LANES // 4
    strip = []
    top, bottom = swapped(row_in_ref[...], row_out_ref[...], place()[0])
    out_rows, high = col_in_ref.shape
    fill = jnp.zeros((LANES - out_rows, high), F32)
    wests, easts = (
        jnp.concatenate([part, fill], axis=0).T[: rows + 2 * HALO_ROWS]
        for part in swapped(col_in_ref[...], col_out_ref[...], place()[1])
    )
    lane = lax.broadcasted_iota(jnp.int32, easts.shape, 1)
    for index, ref in enumerate((volt_ref, right_ref, inv_ref)):
        own = extended(ref[...], top, bottom, index)
        at = index * SWEEPS
        west = pltpu.roll(wests, LANES - SWEEPS - at, 1)
        east = pltpu.roll(easts, 3 * quarter - at, 1)
        tail = pltpu.roll(own[:, cols - LANES :], LANES - quarter, 1)
        strip.append(
            jnp.where(
                lane < 3 * quarter,
                jnp.where(lane < quarter + quarter // 2, own[:, :LANES], tail),
                jnp.where(lane < 3 * quarter + quarter // 2, east, west),
            )
        )
    strip = swept(*strip)[:rows]
    lane = lane[:rows]
    inner = inner_ref[...]
    out_ref[...] = inner
    out_ref[:, :LANES] = jnp.where(lane < SWEEPS, strip, inner[:, :LANES])
    out_ref[:, cols - LANES :] = jnp.where(
        lane >= LANES - SWEEPS, pltpu.roll(strip, quarter, 1), inner[:, cols - LANES :]
    )
    turned = strip.T
    edge = jnp.concatenate([turned[:8], turned[3 * quarter - 8 : 3 * quarter]], axis=0)
    count = edge.shape[0]
    edge = jnp.concatenate(halves(edge), axis=0)
    dies = blocks // cap
    for first in range(0, blocks, GROUP):
        cut = slice(first, first + GROUP)
        node = node_ref[cut, :]
        safe = jnp.maximum(node, 0)
        row, col = safe // cols, safe % cols
        from_end = col - (cols - SWEEPS)
        at_edge = jnp.where(
            col < SWEEPS, col, jnp.where(from_end >= 0, from_end + count - SWEEPS, -1)
        )
        found = jnp.dot(edge, one_hot(rows, row), preferred_element_type=F32)
        found = jnp.concatenate(pick_rows(found[:count] + found[count:], at_edge), axis=0)
        cond = jnp.where(node >= 0, cond_ref[cut, :], 0.0)
        current = cond * (start_ref[cut, :] - (found_ref[cut, :] + found))
        for i in range(GROUP):
            block = first + i
            current_ref[block // cap, block % cap : block % cap + 1, :] = current[i : i + 1, :]
    for copy in range(1, copies):
        current_ref[copy * dies : (copy + 1) * dies] = current_ref[0:dies]


def local(
    die_volt,
    die_load,
    die_shunt,
    bump_node,
    bump_block,
    bump_cond,
    pkg_volt,
    pkg_diag,
    pkg_pattern,
    pkg_weight,
    block_coupling,
):
    die_count = lax.axis_size("die")
    group_count = lax.axis_size("grp")
    devices = die_count * group_count
    blocks = pkg_volt.shape[0]
    tiles = blocks // LANES
    neighbours = pkg_pattern.shape[0]
    slots = bump_block.shape[0]
    cap = slots // die_count
    rows, cols = die_volt.shape
    (spread,) = call(
        functools.partial(spread_body, cap, die_count, blocks),
        "spread_blocks",
        [shape(devices, 1, LANES, dtype=jnp.int32)],
        (bump_block.reshape(1, slots),),
        [VMEM],
    )
    ids = lax.all_to_all(
        spread, ("grp", "die"), split_axis=0, concat_axis=0, tiled=True
    ).reshape(devices, LANES)

    (picked,) = call(
        functools.partial(pick_body, cap, die_count),
        "pick_rows",
        [shape(slots, LANES)],
        (ids, pkg_volt),
        [SMEM, VMEM],
    )
    bump_start = lax.all_to_all(
        picked.reshape(die_count, cap, LANES), "die", split_axis=0, concat_axis=0, tiled=True
    ).reshape(slots, LANES)

    right_side, inv, *edges = call(
        functools.partial(scatter_body, cols),
        "scatter_bumps",
        [shape(rows, cols)] * 2 + [shape(3 * HALO_ROWS, cols)] * 2,
        (bump_node, bump_cond, bump_start, die_volt, die_load, die_shunt),
        [VMEM] * 6,
        work=3,
    )
    own = tiles // 2
    dma = pltpu.SemaphoreType.DMA
    plane = pltpu.VMEM(((own + 2) * LANES + 2 * RADIUS, 2 * LANES), BF16)
    range_rows = pltpu.VMEM(((own + 2) * LANES, LANES), F32)
    range_bands = pltpu.VMEM((own + 2, 2 * LANES, 2 * LANES), BF16)
    beside = swap(*edges, "grp")
    band, banded = call(
        bands_body,
        "package_bands",
        [shape(own + 2, 2 * LANES, 2 * LANES, dtype=BF16), shape(8, LANES)],
        (pkg_pattern, pkg_weight, right_side),
        [VMEM, VMEM, ANY],
        work=2,
    )

    edge_rows = -(-3 * SWEEPS // 8) * 8
    edge_cols = -(-(rows + 2 * HALO_ROWS) // LANES) * LANES
    edges = call(
        edge_body,
        "edge_columns",
        [shape(edge_rows, edge_cols)] * 2,
        (die_volt, right_side, inv, *beside, banded),
        [VMEM] * 5 + [ANY],
    )
    columns = swap(*edges, "die")

    inner, found = call(
        inner_body,
        "inner_sweeps",
        [shape(rows, cols), shape(slots, LANES)],
        (bump_node, die_volt, right_side, inv, *beside),
        [VMEM] * 6,
        work=3,
    )
    die_out, current = call(
        functools.partial(sweep_body, group_count),
        "sweeps",
        [shape(rows, cols), shape(devices, cap, LANES)],
        (
            bump_node, bump_cond, bump_start, die_volt, right_side, inv, *beside, *columns,
            inner, found,
        ),
        [VMEM] * 12,
        work=4,
    )
    pack_rows = 2 * LANES + 2 * neighbours
    base, pkg_inv, pack, near = call(
        prepare_body,
        "package_prepare",
        [
            shape((own + 2) * LANES, LANES),
            shape((own + 2) * LANES, LANES),
            shape(pack_rows, LANES),
            shape(2 * RADIUS, LANES),
        ],
        (pkg_pattern, pkg_weight, block_coupling, band, pkg_volt, pkg_diag, die_out),
        [HBM] * 7,
        [
            range_rows, range_rows, range_bands, range_rows, range_rows, plane,
            pltpu.VMEM((LANES, LANES), F32), pltpu.VMEM((neighbours, LANES), jnp.int32),
            pltpu.VMEM((2 * neighbours, LANES), F32), dma((6,)), dma((7,)),
        ],
        work=5,
        vmem=MOST_VMEM,
        out_specs=[HBM] * 4,
    )

    current = lax.all_to_all(
        current, ("grp", "die"), split_axis=0, concat_axis=0, tiled=True
    ).reshape(devices * cap, LANES)

    beside_end = [
        (g * die_count + a, g * die_count + b)
        for g in range(group_count)
        for d in range((g + 1) % 2, die_count - 1, 2)
        for a, b in ((d, d + 1), (d + 1, d))
    ]
    halo = lax.ppermute(pack, ("grp", "die"), beside_end)
    (inflow,) = call(
        functools.partial(ends_body, cap, tiles),
        "package_end",
        [shape(LANES, LANES)],
        (ids, current),
        [VMEM, VMEM],
    )
    halo_inflow = lax.ppermute(inflow, ("grp", "die"), beside_end)
    all_inflow, halo_band, halo_inv, edge_base = call(
        functools.partial(inflow_body, cap, tiles),
        "package_inflow",
        [
            shape((own + 2) * LANES, LANES),
            shape(2 * LANES, 2 * LANES, dtype=BF16),
            shape(LANES, LANES),
            shape(2 * LANES, LANES),
        ],
        (ids, current, block_coupling, pack, halo, near, inflow),
        [VMEM] * 6 + [ANY],
        [pltpu.VMEM((2 * LANES + 2 * RADIUS, 2 * LANES), BF16)],
        work=3,
    )
    half_out, pkg_out, picked = call(
        functools.partial(iterate_body, cap, die_count),
        "package_iterations",
        [shape(own * LANES, LANES), shape(blocks, LANES), shape(2 * slots, LANES)],
        (
            ids, block_coupling, halo_inflow, all_inflow, band, base, pkg_inv,
            halo_band, halo_inv, edge_base,
        ),
        [SMEM] + [VMEM] * 9,
        [pltpu.VMEM((own * LANES, LANES), F32), plane, plane, dma((2,))],
        work=10,
        vmem=24,
        out_specs=[HBM, HBM, VMEM],
    )
    pair = 2 * die_count
    parts = lax.all_to_all(
        picked.reshape(pair, cap, LANES),
        ("grp", "die"),
        split_axis=0,
        concat_axis=0,
        axis_index_groups=[
            [first + i for i in range(pair)] for first in range(0, devices, pair)
        ],
        tiled=True,
    ).reshape(2 * slots, LANES)
    other = lax.ppermute(half_out, "grp", [(g, g ^ 1) for g in range(group_count)])
    pkg_out, done = call(
        join_body,
        "join_halves",
        [shape(blocks, LANES), shape(8, LANES)],
        (other, pkg_out),
        [VMEM, HBM],
        [dma(())],
        out_specs=[HBM, VMEM],
        aliases={1: 0},
    )
    (bump_out,) = call(
        add_body, "add_parts", [shape(slots, LANES)], (parts, done), [VMEM, ANY]
    )
    return (die_out, pkg_out, bump_out)


def solution(mesh):
    return jax.shard_map(
        local,
        mesh=mesh,
        in_specs=(
            P("grp", "die"),
            P("grp", "die"),
            P("grp", "die"),
            P(("grp", "die"), None),
            P(("grp", "die")),
            P(("grp", "die"), None),
            P("die", None),
            P("die", None),
            P(None, "die"),
            P(None, "die"),
            P(),
        ),
        out_specs=(P("grp", "die"), P("die", None), P(("grp", "die"), None)),
        check_vma=False,
    )
```

```python
import functools
import math

import jax
import jax.numpy as jnp
from jax import lax
from jax.experimental import pallas as pl
from jax.experimental.pallas import tpu as pltpu
from jax.sharding import PartitionSpec as P

RADIUS = 32
SWEEPS = 4
ITERS = 4
LANES = 128
HALO_ROWS = 8
REACH = RADIUS * ITERS
WINDOW = LANES + 2 * RADIUS
F32 = jnp.float32
BF16 = jnp.bfloat16
MOST_VMEM = 57
VMEM = pl.BlockSpec(memory_space=pltpu.VMEM)
SMEM = pl.BlockSpec(memory_space=pltpu.SMEM)
ANY = pl.BlockSpec(memory_space=pl.ANY)
HBM = pl.BlockSpec(memory_space=pltpu.HBM)


def sweep_weights(sweeps):
    return [
        1.0 / (1.0 + 0.8 * math.cos(math.pi * (2 * index + 1) / (2 * sweeps)))
        for index in range(sweeps)
    ]


def call(
    body, name, outs, args, specs, scratch=(), work=1, vmem=16, out_specs=None, aliases=None
):
    bytes_accessed = sum(4 * math.prod(arg.shape) for arg in args)
    return pl.pallas_call(
        body,
        name=name,
        out_shape=outs,
        in_specs=specs,
        out_specs=out_specs or [VMEM] * len(outs),
        input_output_aliases=aliases or {},
        scratch_shapes=list(scratch),
        compiler_params=pltpu.CompilerParams(vmem_limit_bytes=vmem * 1024 * 1024),
        cost_estimate=pl.CostEstimate(
            flops=work * 10**9, bytes_accessed=bytes_accessed, transcendentals=0
        ),
    )(*args)


def place():
    return lax.axis_index("grp"), lax.axis_index("die")


def shape(*dims, dtype=F32):
    return jax.ShapeDtypeStruct(dims, dtype)


def halves(values):
    high = values.astype(BF16)
    low = (values - high.astype(F32)).astype(BF16)
    return high, low


def spread_body(cap, die_count, blocks, block_ref, out_ref):
    slots = block_ref.shape[1]
    block = jnp.concatenate(
        [block_ref[...], jnp.zeros((1, LANES - slots), jnp.int32)], axis=1
    )
    for die in range(die_count):
        row = (pltpu.roll(block, LANES - die * cap, 1) if die else block) - die * blocks
        for at in range(die, out_ref.shape[0], die_count):
            out_ref[at] = row


def asked_rows(cap, die_count, group, ids_ref):
    for die in range(die_count):
        for slot in range(cap):
            yield die * cap + slot, ids_ref[group * die_count + die, slot]


def pick_body(cap, die_count, ids_ref, plane_ref, out_ref):
    group, _ = place()
    for at, row in asked_rows(cap, die_count, group, ids_ref):
        out_ref[pl.ds(at, 1), :] = plane_ref[pl.ds(row, 1), :]


def build_band(first, pattern, weights):
    place = lax.broadcasted_iota(jnp.int32, (WINDOW, LANES), 0)
    band = None
    for k in range(pattern.shape[0]):
        hit = place == (pattern[k : k + 1, :] - first)
        term = jnp.where(hit, weights[k : k + 1, :], 0.0)
        band = term if band is None else band + term
    fill = jnp.zeros((2 * LANES - WINDOW, LANES), F32)
    return jnp.concatenate(halves(jnp.concatenate([band, fill], axis=0).T), axis=0)


def reciprocal(diag):
    safe = jnp.where(diag > 0.0, diag, 1.0)
    return jnp.where(diag > 0.0, 1.0 / safe, 0.0)


def span(tile, offset=0, size=LANES):
    return pl.ds(pl.multiple_of(tile * LANES + offset, RADIUS), size)


def mixer(coup_ref):
    mix = jnp.concatenate(halves(coup_ref[...]), axis=1)
    return jnp.concatenate([mix, mix], axis=0)


def clear_pads(ref):
    pad = jnp.zeros((RADIUS, 2 * LANES), BF16)
    ref[0:RADIUS, :] = pad
    ref[ref.shape[0] - RADIUS :, :] = pad


def store(ref, tile, values):
    ref[span(tile, RADIUS, values.shape[0]), :] = jnp.concatenate(halves(values), axis=1)


def couple(source, tile, bands, mix, write):
    for at in range(0, len(bands), 4):
        couple_few(source, tile + at, bands[at : at + 4], mix, write)


def couple_few(source, tile, bands, mix, write):
    own = source[span(tile, RADIUS, len(bands) * LANES), :]
    within = jnp.dot(own, mix, preferred_element_type=F32)
    for i, band in enumerate(bands):
        window = source[span(tile + i, 0, WINDOW), :]
        beside = jnp.dot(band[:, :WINDOW], window, preferred_element_type=F32)
        both = beside[:LANES] + beside[LANES:] + within[i * LANES : (i + 1) * LANES]
        write(tile + i, both[:, :LANES] + both[:, LANES:])


def in_chunks(first, count, body, size=16):
    whole = count // size

    @pl.loop(0, whole)
    def _(chunk):
        body(first + chunk * size, size)

    if count % size:
        body(first + whole * size, count % size)


def half_of(tiles):
    half = lax.rem(sum(place()), 2)
    own = tiles // 2
    return half, own, half * own - 1


def bands_body(pat_ref, wgt_ref, after_ref, band_ref, done_ref):
    blocks = pat_ref.shape[1]
    half, own, shift = half_of(blocks // LANES)
    begin = place()[1] * blocks + shift * LANES

    def bands(tile, size):
        for i in range(size):
            lanes = pl.ds(pl.multiple_of((tile + i + shift) * LANES, LANES), LANES)
            band_ref[tile + i] = build_band(
                begin + (tile + i) * LANES - RADIUS, pat_ref[:, lanes], wgt_ref[:, lanes]
            )

    in_chunks(1 - half, own + 1, bands, 8)
    band_ref[half * (own + 1)] = jnp.zeros(band_ref.shape[1:], BF16)
    done_ref[...] = jnp.zeros(done_ref.shape, F32)


def prepare_body(
    pat_hbm, wgt_hbm, coup_hbm, band_hbm, volt_hbm, diag_hbm, after_ref,
    base_hbm, inv_hbm, pack_hbm, near_hbm,
    volt_ref, diag_ref, band_ref, base_ref, inv_ref, plane_ref, coup_ref, pat_ref, wgt_ref,
    sems, out_sems,
):
    blocks = volt_hbm.shape[0]
    half, own, shift = half_of(blocks // LANES)
    first, count, outer = 1 - half, own + 1, half * (own + 1)
    edge = 1 + half * (own - 1)
    known = pl.ds(pl.multiple_of(first * LANES, LANES), count * LANES)
    source = pl.ds(pl.multiple_of((first + shift) * LANES, LANES), count * LANES)
    lanes = pl.ds(pl.multiple_of((edge + shift) * LANES, LANES), LANES)
    neighbours = pat_hbm.shape[0]
    steps = [(at, min(8, count - at)) for at in range(0, count, 8)]

    def some(ref, at, size):
        return ref.at[pl.ds(first + at, size)]

    pairs = [
        (volt_hbm.at[source, :], volt_ref.at[known, :]),
        (coup_hbm, coup_ref),
        (some(band_hbm, *steps[0]), some(band_ref, *steps[0])),
        (diag_hbm.at[source, :], diag_ref.at[known, :]),
        (pat_hbm.at[:, lanes], pat_ref),
        (wgt_hbm.at[:, lanes], wgt_ref.at[neighbours : 2 * neighbours, :]),
    ] + [(some(band_hbm, *step), some(band_ref, *step)) for step in steps[1:]]
    loads = [
        pltpu.make_async_copy(hbm, ref, sems.at[i]) for i, (hbm, ref) in enumerate(pairs)
    ]
    for load in loads:
        load.start()
    writes = []

    def write_out(ref, hbm):
        writes.append(pltpu.make_async_copy(ref, hbm, out_sems.at[len(writes)]))
        writes[-1].start()

    def spread(tile, size):
        store(plane_ref, tile, volt_ref[span(tile, 0, size * LANES), :])

    def invert(tile, size):
        cut = span(tile, 0, size * LANES)
        inv_ref[cut, :] = reciprocal(diag_ref[cut, :])

    def base(tile, size):
        def write(tile, values):
            base_ref[span(tile), :] = values

        couple(plane_ref, tile, [band_ref[tile + i] for i in range(size)], mix, write)
        cut = span(tile, 0, size * LANES)
        write_out(base_ref.at[cut, :], base_hbm.at[cut, :])

    clear_pads(plane_ref)
    plane_ref[span(outer, RADIUS), :] = jnp.zeros((LANES, 2 * LANES), BF16)
    loads[0].wait()
    in_chunks(first, count, spread, 8)
    at = 2 * LANES
    write_out(volt_ref.at[span(edge), :], pack_hbm.at[0:LANES, :])
    write_out(
        volt_ref.at[2 * LANES : 2 * LANES + RADIUS, :], near_hbm.at[0:RADIUS, :]
    )
    write_out(
        volt_ref.at[own * LANES - RADIUS : own * LANES, :],
        near_hbm.at[RADIUS : 2 * RADIUS, :],
    )
    loads[1].wait()
    loads[2].wait()
    mix = mixer(coup_ref)
    base(first, steps[0][1])
    for load in loads[3:6]:
        load.wait()
    wgt_ref[0:neighbours, :] = pat_ref[...].astype(F32)
    write_out(wgt_ref, pack_hbm.at[at : at + 2 * neighbours, :])
    write_out(diag_ref.at[span(edge), :], pack_hbm.at[LANES:at, :])
    in_chunks(first, count, invert, 8)
    write_out(inv_ref.at[known, :], inv_hbm.at[known, :])
    for load, (start, size) in zip(loads[6:], steps[1:]):
        load.wait()
        base(first + start, size)
    for write in writes:
        write.wait()


def slot_places(cap, ids_ref):
    per_row = LANES // cap
    lane = lax.broadcasted_iota(jnp.int32, (1, LANES), 1)
    places = []
    for at in range(0, ids_ref.shape[0], per_row):
        total = None
        for i in range(per_row):
            row = jnp.where(lane < cap, ids_ref[at + i : at + i + 1, :], 0)
            row = pltpu.roll(row, i * cap, 1) if i else row
            total = row if total is None else total + row
        places.append(total)
    return places


def gather_inflow(places, first, rows, current):
    at = lax.broadcasted_iota(jnp.int32, (rows, LANES), 0) + first
    hits = [jnp.where(at == place, 1.0, 0.0).astype(BF16) for place in places]
    both = jnp.dot(jnp.concatenate(hits, axis=1), current, preferred_element_type=F32)
    return both[:, :LANES] + both[:, LANES:]


def ends_body(cap, tiles, ids_ref, current_ref, out_ref):
    half, _, _ = half_of(tiles)
    places = slot_places(cap, ids_ref)
    current = jnp.concatenate(halves(current_ref[...]), axis=1)
    out_ref[...] = gather_inflow(places, half * (tiles - 1) * LANES, LANES, current)


def inflow_body(
    cap, tiles, ids_ref, current_ref, coup_ref, own_ref, halo_ref, near_ref, after_ref,
    out_ref, band_ref, inv_ref, base_ref, plane_ref,
):
    half, own, shift = half_of(tiles)
    first, count = 1 - half, own + 1
    places = slot_places(cap, ids_ref)
    current = jnp.concatenate(halves(current_ref[...]), axis=1)

    def inflow(tile, size):
        cut = span(tile, 0, size * LANES)
        out_ref[cut, :] = gather_inflow(
            places, (tile + shift) * LANES, size * LANES, current
        )

    in_chunks(first, count, inflow)
    out_ref[span(half * (own + 1)), :] = jnp.zeros((LANES, LANES), F32)

    neighbours = (own_ref.shape[0] - 2 * LANES) // 2
    begin = (place()[1] * tiles + 2 * half * own - 1) * LANES
    packs = [jnp.where(half == at, halo_ref[...], own_ref[...]) for at in range(2)]
    at = 2 * LANES
    bands = []
    for tile, pack in enumerate(packs):
        bands.append(
            build_band(
                begin + tile * LANES - RADIUS,
                pack[at : at + neighbours].astype(jnp.int32),
                pack[at + neighbours : at + 2 * neighbours],
            )
        )
        store(plane_ref, tile, pack[:LANES])
    none = jnp.zeros((RADIUS, 2 * LANES), BF16)
    low, high = (
        jnp.concatenate(halves(near_ref[cut, :]), axis=1)
        for cut in (slice(0, RADIUS), slice(RADIUS, 2 * RADIUS))
    )
    size = plane_ref.shape[0]
    plane_ref[0:RADIUS, :] = jnp.where(half == 0, none, high)
    plane_ref[size - RADIUS : size, :] = jnp.where(half == 0, low, none)
    results = []
    couple(plane_ref, 0, bands, mixer(coup_ref), lambda tile, values: results.append(values))
    band_ref[...] = jnp.where(half == 0, bands[0], bands[1])
    inv_ref[...] = reciprocal(halo_ref[LANES : 2 * LANES, :])
    base_ref[0:LANES, :] = jnp.where(half == 0, results[0], results[1])
    base_ref[LANES:, :] = jnp.where(half == 0, results[1], results[0])


def iterate_body(
    cap, die_count, asked_ref, coup_ref, halo_ref, inflow_ref, band_ref, base_ref, inv_ref,
    halo_band_ref, halo_inv_ref, edge_base_ref, out_hbm, full_hbm, picked_ref, out_ref, here_ref, there_ref, sems,
):
    own = out_hbm.shape[0] // LANES
    half, _, _ = half_of(2 * own)
    first, count, outer = 1 - half, own + 1, half * (own + 1)
    edge = 1 + half * (own - 1)
    for ref in (here_ref, there_ref):
        clear_pads(ref)

    def start(tile, size):
        cut = span(tile, 0, size * LANES)
        store(here_ref, tile, -(inflow_ref[cut, :] + base_ref[cut, :]) * inv_ref[cut, :])

    in_chunks(first, count, start)
    halo_inv = halo_inv_ref[...]
    store(here_ref, outer, -(halo_ref[...] + edge_base_ref[0:LANES, :]) * halo_inv)
    cut = span(edge)
    store(here_ref, edge, -(inflow_ref[cut, :] + edge_base_ref[LANES:, :]) * inv_ref[cut, :])
    mix = mixer(coup_ref)
    refs = (here_ref, there_ref)
    for iteration in range(1, ITERS):
        source, target = refs[(iteration - 1) % 2], refs[iteration % 2]
        last = iteration == ITERS - 1

        def write(tile, coupled, target=target, last=last):
            values = -(inflow_ref[span(tile), :] + coupled) * inv_ref[span(tile), :]
            if last:
                out_ref[span(tile - 1), :] = values
            else:
                store(target, tile, values)

        def step(tile, size, source=source, write=write):
            bands = [band_ref[tile + i] for i in range(size)]
            couple(source, tile, bands, mix, write)

        def final(tile, size, step=step):
            step(tile, size)
            cut = span(tile - 1, 0, size * LANES)
            whole = span(half * own + tile - 1, 0, size * LANES)
            pltpu.make_async_copy(out_ref.at[cut, :], out_hbm.at[cut, :], sems.at[0]).start()
            pltpu.make_async_copy(out_ref.at[cut, :], full_hbm.at[whole, :], sems.at[1]).start()

        def write_halo(tile, coupled, target=target):
            store(target, tile, -(halo_ref[...] + coupled) * halo_inv)

        if last:
            in_chunks(1, own, final)
        else:
            in_chunks(first, count, step)
            couple(source, outer, [halo_band_ref[...]], mix, write_halo)

    base_row = half * own * LANES
    group, _ = place()
    pair = group - lax.rem(group, 2)
    for member in range(2):
        offset = member * (picked_ref.shape[0] // 2)
        for at, row in asked_rows(cap, die_count, pair + member, asked_ref):
            row = row - base_row
            inside = (row >= 0) & (row < own * LANES)
            safe = jnp.clip(row, 0, own * LANES - 1)
            values = out_ref[pl.ds(safe, 1), :]
            picked_ref[pl.ds(offset + at, 1), :] = jnp.where(inside, values, 0.0)
    pltpu.make_async_copy(out_ref, out_hbm, sems.at[0]).wait()
    pltpu.make_async_copy(out_ref, full_hbm.at[0 : own * LANES, :], sems.at[1]).wait()


def join_body(other_ref, full_in_hbm, full_hbm, done_ref, sem):
    rows = other_ref.shape[0]
    half, _, _ = half_of(2 * rows // LANES)
    start = pl.multiple_of((1 - half) * rows, LANES)
    copy = pltpu.make_async_copy(other_ref, full_hbm.at[pl.ds(start, rows), :], sem)
    copy.start()
    done_ref[...] = jnp.zeros(done_ref.shape, F32)
    copy.wait()


def add_body(parts_ref, after_ref, out_ref):
    rows = out_ref.shape[0]
    out_ref[...] = parts_ref[0:rows, :] + parts_ref[rows:, :]


def scatter_body(cols, node_ref, cond_ref, start_ref, volt_ref, load_ref, shunt_ref,
                 right_ref, inv_ref, inner_ref, outer_ref):
    blocks = node_ref.shape[0]
    rows = volt_ref.shape[0]
    group = 8
    row_at = lax.broadcasted_iota(jnp.int32, (rows, LANES), 0)
    col_at = lax.broadcasted_iota(jnp.int32, (cols, LANES), 0)
    total = jnp.zeros((4 * rows, cols), F32)
    for first in range(0, blocks, group):
        node = node_ref[first : first + group, :]
        live = node >= 0
        cond = jnp.where(live, cond_ref[first : first + group, :], 0.0)
        flow = cond * start_ref[first : first + group, :]
        safe = jnp.where(live, node, 0)
        row, col = safe // cols, safe % cols
        parts = halves(cond) + halves(flow)
        left, right = [], []
        for i in range(group):
            spot = jnp.where(row_at == row[i : i + 1, :], 1.0, 0.0).astype(BF16)
            left.append(
                jnp.concatenate([spot * part[i : i + 1, :] for part in parts], axis=0)
            )
            right.append(jnp.where(col_at == col[i : i + 1, :], 1.0, 0.0).astype(BF16))
        total = total + lax.dot_general(
            jnp.concatenate(left, axis=1),
            jnp.concatenate(right, axis=1),
            (((1,), (1,)), ((), ())),
            preferred_element_type=F32,
        )
    gsum = total[:rows] + total[rows : 2 * rows]
    inject = total[2 * rows : 3 * rows] + total[3 * rows :]
    inv = 1.0 / (4.0 + shunt_ref[...] + gsum)
    right_side = (inject - load_ref[...]) * inv
    right_ref[...] = right_side
    inv_ref[...] = inv
    volt = volt_ref[...]
    top, bottom = (
        jnp.concatenate([volt[cut], right_side[cut], inv[cut]], axis=0)
        for cut in (slice(0, HALO_ROWS), slice(rows - HALO_ROWS, rows))
    )
    swap_parts(inner_ref, outer_ref, place()[0], top, bottom)


def swap_parts(inner_ref, outer_ref, mine, first, last):
    even = lax.rem(mine, 2) == 0
    inner_ref[...] = jnp.where(even, last, first)
    outer_ref[...] = jnp.where(even, first, last)


def swapped(inner, outer, mine):
    even = lax.rem(mine, 2) == 0
    return jnp.where(even, outer, inner), jnp.where(even, inner, outer)


def swap(inner, outer, axis):
    count = lax.axis_size(axis)

    def pairs(start):
        return [
            pair
            for i in range(start, count - 1, 2)
            for pair in ((i, i + 1), (i + 1, i))
        ]

    return lax.ppermute(outer, axis, pairs(1)), lax.ppermute(inner, axis, pairs(0))


def extended(own, top, bottom, index):
    cut = slice(index * HALO_ROWS, (index + 1) * HALO_ROWS)
    return jnp.concatenate([own, bottom[cut], top[cut]], axis=0)


def edge_body(
    volt_ref, right_ref, inv_ref, outer_ref, inner_ref, after_ref, west_ref, east_ref
):
    cols = volt_ref.shape[1]
    top, bottom = swapped(inner_ref[...], outer_ref[...], place()[0])
    out_rows, high = west_ref.shape
    west, east = None, None
    for index, ref in enumerate((volt_ref, right_ref, inv_ref)):
        whole = extended(ref[...], top, bottom, index)
        lane = lax.broadcasted_iota(jnp.int32, (whole.shape[0], LANES), 1)
        head, tail = whole[:, :LANES], whole[:, cols - LANES :]
        at = index * SWEEPS
        head = pltpu.roll(head, at, 1) if at else head
        tail = pltpu.roll(tail, at + SWEEPS, 1)
        west = head if west is None else jnp.where(lane >= at, head, west)
        east = tail if east is None else jnp.where(lane >= at, tail, east)
    fill = jnp.zeros((high - west.shape[0], LANES), F32)
    west, east = (
        jnp.concatenate([part, fill], axis=0).T[:out_rows] for part in (west, east)
    )
    swap_parts(west_ref, east_ref, place()[1], west, east)


def swept(volt, right_side, inv):
    high, wide = volt.shape
    for weight in sweep_weights(SWEEPS):
        beside = (
            pltpu.roll(volt, 1, 0)
            + pltpu.roll(volt, high - 1, 0)
            + pltpu.roll(volt, 1, 1)
            + pltpu.roll(volt, wide - 1, 1)
        )
        volt = (1.0 - weight) * volt + weight * (right_side + beside * inv)
    return volt


GROUP = 8


def one_hot(rows, places):
    at = lax.broadcasted_iota(jnp.int32, (rows, LANES), 0)
    return jnp.concatenate(
        [
            jnp.where(at == places[i : i + 1, :], 1.0, 0.0).astype(BF16)
            for i in range(places.shape[0])
        ],
        axis=1,
    )


def pick_rows(found, places):
    at = lax.broadcasted_iota(jnp.int32, (found.shape[0], LANES), 0)
    return [
        jnp.sum(
            jnp.where(at == places[i : i + 1, :], found[:, i * LANES : (i + 1) * LANES], 0.0),
            axis=0,
            keepdims=True,
        )
        for i in range(places.shape[0])
    ]


def inner_body(node_ref, volt_ref, right_ref, inv_ref, row_out_ref, row_in_ref, out_ref, found_ref):
    rows, cols = volt_ref.shape
    top, bottom = swapped(row_in_ref[...], row_out_ref[...], place()[0])
    volt = swept(
        *(
            extended(ref[...], top, bottom, index)
            for index, ref in enumerate((volt_ref, right_ref, inv_ref))
        )
    )[:rows]
    out_ref[...] = volt
    col = lax.broadcasted_iota(jnp.int32, volt.shape, 1)
    volt = jnp.where((col >= SWEEPS) & (col < cols - SWEEPS), volt, 0.0)
    both = jnp.concatenate(halves(volt), axis=0)
    for first in range(0, node_ref.shape[0], GROUP):
        safe = jnp.maximum(node_ref[first : first + GROUP, :], 0)
        found = jnp.dot(both, one_hot(cols, safe % cols), preferred_element_type=F32)
        found = pick_rows(found[:rows] + found[rows:], safe // cols)
        for i, values in enumerate(found):
            found_ref[first + i : first + i + 1, :] = values


def sweep_body(copies, node_ref, cond_ref, start_ref, volt_ref, right_ref, inv_ref,
               row_out_ref, row_in_ref, col_out_ref, col_in_ref, inner_ref, found_ref,
               out_ref, current_ref):
    rows, cols = volt_ref.shape
    blocks = node_ref.shape[0]
    cap = current_ref.shape[1]
    quarter = LANES // 4
    strip = []
    top, bottom = swapped(row_in_ref[...], row_out_ref[...], place()[0])
    out_rows, high = col_in_ref.shape
    fill = jnp.zeros((LANES - out_rows, high), F32)
    wests, easts = (
        jnp.concatenate([part, fill], axis=0).T[: rows + 2 * HALO_ROWS]
        for part in swapped(col_in_ref[...], col_out_ref[...], place()[1])
    )
    lane = lax.broadcasted_iota(jnp.int32, easts.shape, 1)
    for index, ref in enumerate((volt_ref, right_ref, inv_ref)):
        own = extended(ref[...], top, bottom, index)
        at = index * SWEEPS
        west = pltpu.roll(wests, LANES - SWEEPS - at, 1)
        east = pltpu.roll(easts, 3 * quarter - at, 1)
        tail = pltpu.roll(own[:, cols - LANES :], LANES - quarter, 1)
        strip.append(
            jnp.where(
                lane < 3 * quarter,
                jnp.where(lane < quarter + quarter // 2, own[:, :LANES], tail),
                jnp.where(lane < 3 * quarter + quarter // 2, east, west),
            )
        )
    strip = swept(*strip)[:rows]
    lane = lane[:rows]
    inner = inner_ref[...]
    out_ref[...] = inner
    out_ref[:, :LANES] = jnp.where(lane < SWEEPS, strip, inner[:, :LANES])
    out_ref[:, cols - LANES :] = jnp.where(
        lane >= LANES - SWEEPS, pltpu.roll(strip, quarter, 1), inner[:, cols - LANES :]
    )
    turned = strip.T
    edge = jnp.concatenate([turned[:8], turned[3 * quarter - 8 : 3 * quarter]], axis=0)
    count = edge.shape[0]
    edge = jnp.concatenate(halves(edge), axis=0)
    dies = blocks // cap
    for first in range(0, blocks, GROUP):
        cut = slice(first, first + GROUP)
        node = node_ref[cut, :]
        safe = jnp.maximum(node, 0)
        row, col = safe // cols, safe % cols
        from_end = col - (cols - SWEEPS)
        at_edge = jnp.where(
            col < SWEEPS, col, jnp.where(from_end >= 0, from_end + count - SWEEPS, -1)
        )
        found = jnp.dot(edge, one_hot(rows, row), preferred_element_type=F32)
        found = jnp.concatenate(pick_rows(found[:count] + found[count:], at_edge), axis=0)
        cond = jnp.where(node >= 0, cond_ref[cut, :], 0.0)
        current = cond * (start_ref[cut, :] - (found_ref[cut, :] + found))
        for i in range(GROUP):
            block = first + i
            current_ref[block // cap, block % cap : block % cap + 1, :] = current[i : i + 1, :]
    for copy in range(1, copies):
        current_ref[copy * dies : (copy + 1) * dies] = current_ref[0:dies]


def local(
    die_volt,
    die_load,
    die_shunt,
    bump_node,
    bump_block,
    bump_cond,
    pkg_volt,
    pkg_diag,
    pkg_pattern,
    pkg_weight,
    block_coupling,
):
    die_count = lax.axis_size("die")
    group_count = lax.axis_size("grp")
    devices = die_count * group_count
    blocks = pkg_volt.shape[0]
    tiles = blocks // LANES
    neighbours = pkg_pattern.shape[0]
    slots = bump_block.shape[0]
    cap = slots // die_count
    rows, cols = die_volt.shape
    (spread,) = call(
        functools.partial(spread_body, cap, die_count, blocks),
        "spread_blocks",
        [shape(devices, 1, LANES, dtype=jnp.int32)],
        (bump_block.reshape(1, slots),),
        [VMEM],
    )
    ids = lax.all_to_all(
        spread, ("grp", "die"), split_axis=0, concat_axis=0, tiled=True
    ).reshape(devices, LANES)

    (picked,) = call(
        functools.partial(pick_body, cap, die_count),
        "pick_rows",
        [shape(slots, LANES)],
        (ids, pkg_volt),
        [SMEM, VMEM],
    )
    bump_start = lax.all_to_all(
        picked.reshape(die_count, cap, LANES), "die", split_axis=0, concat_axis=0, tiled=True
    ).reshape(slots, LANES)

    right_side, inv, *edges = call(
        functools.partial(scatter_body, cols),
        "scatter_bumps",
        [shape(rows, cols)] * 2 + [shape(3 * HALO_ROWS, cols)] * 2,
        (bump_node, bump_cond, bump_start, die_volt, die_load, die_shunt),
        [VMEM] * 6,
        work=3,
    )
    own = tiles // 2
    dma = pltpu.SemaphoreType.DMA
    plane = pltpu.VMEM(((own + 2) * LANES + 2 * RADIUS, 2 * LANES), BF16)
    range_rows = pltpu.VMEM(((own + 2) * LANES, LANES), F32)
    range_bands = pltpu.VMEM((own + 2, 2 * LANES, 2 * LANES), BF16)
    beside = swap(*edges, "grp")
    band, banded = call(
        bands_body,
        "package_bands",
        [shape(own + 2, 2 * LANES, 2 * LANES, dtype=BF16), shape(8, LANES)],
        (pkg_pattern, pkg_weight, right_side),
        [VMEM, VMEM, ANY],
        work=2,
    )

    edge_rows = -(-3 * SWEEPS // 8) * 8
    edge_cols = -(-(rows + 2 * HALO_ROWS) // LANES) * LANES
    edges = call(
        edge_body,
        "edge_columns",
        [shape(edge_rows, edge_cols)] * 2,
        (die_volt, right_side, inv, *beside, banded),
        [VMEM] * 5 + [ANY],
    )
    columns = swap(*edges, "die")

    inner, found = call(
        inner_body,
        "inner_sweeps",
        [shape(rows, cols), shape(slots, LANES)],
        (bump_node, die_volt, right_side, inv, *beside),
        [VMEM] * 6,
        work=3,
    )
    die_out, current = call(
        functools.partial(sweep_body, group_count),
        "sweeps",
        [shape(rows, cols), shape(devices, cap, LANES)],
        (
            bump_node, bump_cond, bump_start, die_volt, right_side, inv, *beside, *columns,
            inner, found,
        ),
        [VMEM] * 12,
        work=4,
    )
    pack_rows = 2 * LANES + 2 * neighbours
    base, pkg_inv, pack, near = call(
        prepare_body,
        "package_prepare",
        [
            shape((own + 2) * LANES, LANES),
            shape((own + 2) * LANES, LANES),
            shape(pack_rows, LANES),
            shape(2 * RADIUS, LANES),
        ],
        (pkg_pattern, pkg_weight, block_coupling, band, pkg_volt, pkg_diag, die_out),
        [HBM] * 7,
        [
            range_rows, range_rows, range_bands, range_rows, range_rows, plane,
            pltpu.VMEM((LANES, LANES), F32), pltpu.VMEM((neighbours, LANES), jnp.int32),
            pltpu.VMEM((2 * neighbours, LANES), F32), dma((6 + own // 8,)), dma((7 + own // 8,)),
        ],
        work=5,
        vmem=MOST_VMEM,
        out_specs=[HBM] * 4,
    )

    current = lax.all_to_all(
        current, ("grp", "die"), split_axis=0, concat_axis=0, tiled=True
    ).reshape(devices * cap, LANES)

    beside_end = [
        (g * die_count + a, g * die_count + b)
        for g in range(group_count)
        for d in range((g + 1) % 2, die_count - 1, 2)
        for a, b in ((d, d + 1), (d + 1, d))
    ]
    halo = lax.ppermute(pack, ("grp", "die"), beside_end)
    (inflow,) = call(
        functools.partial(ends_body, cap, tiles),
        "package_end",
        [shape(LANES, LANES)],
        (ids, current),
        [VMEM, VMEM],
    )
    halo_inflow = lax.ppermute(inflow, ("grp", "die"), beside_end)
    all_inflow, halo_band, halo_inv, edge_base = call(
        functools.partial(inflow_body, cap, tiles),
        "package_inflow",
        [
            shape((own + 2) * LANES, LANES),
            shape(2 * LANES, 2 * LANES, dtype=BF16),
            shape(LANES, LANES),
            shape(2 * LANES, LANES),
        ],
        (ids, current, block_coupling, pack, halo, near, inflow),
        [VMEM] * 6 + [ANY],
        [pltpu.VMEM((2 * LANES + 2 * RADIUS, 2 * LANES), BF16)],
        work=3,
    )
    half_out, pkg_out, picked = call(
        functools.partial(iterate_body, cap, die_count),
        "package_iterations",
        [shape(own * LANES, LANES), shape(blocks, LANES), shape(2 * slots, LANES)],
        (
            ids, block_coupling, halo_inflow, all_inflow, band, base, pkg_inv,
            halo_band, halo_inv, edge_base,
        ),
        [SMEM] + [VMEM] * 9,
        [pltpu.VMEM((own * LANES, LANES), F32), plane, plane, dma((2,))],
        work=10,
        vmem=24,
        out_specs=[HBM, HBM, VMEM],
    )
    pair = 2 * die_count
    parts = lax.all_to_all(
        picked.reshape(pair, cap, LANES),
        ("grp", "die"),
        split_axis=0,
        concat_axis=0,
        axis_index_groups=[
            [first + i for i in range(pair)] for first in range(0, devices, pair)
        ],
        tiled=True,
    ).reshape(2 * slots, LANES)
    other = lax.ppermute(half_out, "grp", [(g, g ^ 1) for g in range(group_count)])
    pkg_out, done = call(
        join_body,
        "join_halves",
        [shape(blocks, LANES), shape(8, LANES)],
        (other, pkg_out),
        [VMEM, HBM],
        [dma(())],
        out_specs=[HBM, VMEM],
        aliases={1: 0},
    )
    (bump_out,) = call(
        add_body, "add_parts", [shape(slots, LANES)], (parts, done), [VMEM, ANY]
    )
    return (die_out, pkg_out, bump_out)


def solution(mesh):
    return jax.shard_map(
        local,
        mesh=mesh,
        in_specs=(
            P("grp", "die"),
            P("grp", "die"),
            P("grp", "die"),
            P(("grp", "die"), None),
            P(("grp", "die")),
            P(("grp", "die"), None),
            P("die", None),
            P("die", None),
            P(None, "die"),
            P(None, "die"),
            P(),
        ),
        out_specs=(P("grp", "die"), P("die", None), P(("grp", "die"), None)),
        check_vma=False,
    )
```

```python
import functools
import math

import jax
import jax.numpy as jnp
from jax import lax
from jax.experimental import pallas as pl
from jax.experimental.pallas import tpu as pltpu
from jax.sharding import PartitionSpec as P

RADIUS = 32
SWEEPS = 4
ITERS = 4
LANES = 128
HALO_ROWS = 8
REACH = RADIUS * ITERS
WINDOW = LANES + 2 * RADIUS
F32 = jnp.float32
BF16 = jnp.bfloat16
MOST_VMEM = 57
VMEM = pl.BlockSpec(memory_space=pltpu.VMEM)
SMEM = pl.BlockSpec(memory_space=pltpu.SMEM)
ANY = pl.BlockSpec(memory_space=pl.ANY)
HBM = pl.BlockSpec(memory_space=pltpu.HBM)


def sweep_weights(sweeps):
    return [
        1.0 / (1.0 + 0.8 * math.cos(math.pi * (2 * index + 1) / (2 * sweeps)))
        for index in range(sweeps)
    ]


def call(
    body, name, outs, args, specs, scratch=(), work=1, vmem=16, out_specs=None, aliases=None
):
    bytes_accessed = sum(4 * math.prod(arg.shape) for arg in args)
    return pl.pallas_call(
        body,
        name=name,
        out_shape=outs,
        in_specs=specs,
        out_specs=out_specs or [VMEM] * len(outs),
        input_output_aliases=aliases or {},
        scratch_shapes=list(scratch),
        compiler_params=pltpu.CompilerParams(vmem_limit_bytes=vmem * 1024 * 1024),
        cost_estimate=pl.CostEstimate(
            flops=work * 10**9, bytes_accessed=bytes_accessed, transcendentals=0
        ),
    )(*args)


def place():
    return lax.axis_index("grp"), lax.axis_index("die")


def shape(*dims, dtype=F32):
    return jax.ShapeDtypeStruct(dims, dtype)


def halves(values):
    high = values.astype(BF16)
    low = (values - high.astype(F32)).astype(BF16)
    return high, low


def spread_body(cap, die_count, blocks, block_ref, out_ref):
    slots = block_ref.shape[1]
    block = jnp.concatenate(
        [block_ref[...], jnp.zeros((1, LANES - slots), jnp.int32)], axis=1
    )
    for die in range(die_count):
        row = (pltpu.roll(block, LANES - die * cap, 1) if die else block) - die * blocks
        for at in range(die, out_ref.shape[0], die_count):
            out_ref[at] = row


def asked_rows(cap, die_count, group, ids_ref):
    for die in range(die_count):
        for slot in range(cap):
            yield die * cap + slot, ids_ref[group * die_count + die, slot]


def pick_body(cap, die_count, ids_ref, plane_ref, out_ref):
    group, _ = place()
    for at, row in asked_rows(cap, die_count, group, ids_ref):
        out_ref[pl.ds(at, 1), :] = plane_ref[pl.ds(row, 1), :]


def build_band(first, pattern, weights):
    place = lax.broadcasted_iota(jnp.int32, (WINDOW, LANES), 0)
    band = None
    for k in range(pattern.shape[0]):
        hit = place == (pattern[k : k + 1, :] - first)
        term = jnp.where(hit, weights[k : k + 1, :], 0.0)
        band = term if band is None else band + term
    fill = jnp.zeros((2 * LANES - WINDOW, LANES), F32)
    return jnp.concatenate(halves(jnp.concatenate([band, fill], axis=0).T), axis=0)


def reciprocal(diag):
    safe = jnp.where(diag > 0.0, diag, 1.0)
    return jnp.where(diag > 0.0, 1.0 / safe, 0.0)


def span(tile, offset=0, size=LANES):
    return pl.ds(pl.multiple_of(tile * LANES + offset, RADIUS), size)


def mixer(coup_ref):
    mix = jnp.concatenate(halves(coup_ref[...]), axis=1)
    return jnp.concatenate([mix, mix], axis=0)


def clear_pads(ref):
    pad = jnp.zeros((RADIUS, 2 * LANES), BF16)
    ref[0:RADIUS, :] = pad
    ref[ref.shape[0] - RADIUS :, :] = pad


def store(ref, tile, values):
    ref[span(tile, RADIUS, values.shape[0]), :] = jnp.concatenate(halves(values), axis=1)


def couple(source, tile, bands, mix, write):
    for at in range(0, len(bands), 4):
        couple_few(source, tile + at, bands[at : at + 4], mix, write)


def couple_few(source, tile, bands, mix, write):
    own = source[span(tile, RADIUS, len(bands) * LANES), :]
    within = jnp.dot(own, mix, preferred_element_type=F32)
    for i, band in enumerate(bands):
        window = source[span(tile + i, 0, WINDOW), :]
        beside = jnp.dot(band[:, :WINDOW], window, preferred_element_type=F32)
        both = beside[:LANES] + beside[LANES:] + within[i * LANES : (i + 1) * LANES]
        write(tile + i, both[:, :LANES] + both[:, LANES:])


def in_chunks(first, count, body, size=16):
    whole = count // size

    @pl.loop(0, whole)
    def _(chunk):
        body(first + chunk * size, size)

    if count % size:
        body(first + whole * size, count % size)


def half_of(tiles):
    half = lax.rem(sum(place()), 2)
    own = tiles // 2
    return half, own, half * own - 1


def bands_body(pat_ref, wgt_ref, after_ref, band_ref, done_ref):
    blocks = pat_ref.shape[1]
    half, own, shift = half_of(blocks // LANES)
    begin = place()[1] * blocks + shift * LANES

    def bands(tile, size):
        for i in range(size):
            lanes = pl.ds(pl.multiple_of((tile + i + shift) * LANES, LANES), LANES)
            band_ref[tile + i] = build_band(
                begin + (tile + i) * LANES - RADIUS, pat_ref[:, lanes], wgt_ref[:, lanes]
            )

    in_chunks(1 - half, own + 1, bands, 8)
    band_ref[half * (own + 1)] = jnp.zeros(band_ref.shape[1:], BF16)
    done_ref[...] = jnp.zeros(done_ref.shape, F32)


def prepare_body(
    pat_hbm, wgt_hbm, coup_hbm, band_hbm, volt_hbm, diag_hbm, after_ref,
    base_hbm, inv_hbm, pack_hbm, near_hbm,
    volt_ref, diag_ref, band_ref, base_ref, inv_ref, plane_ref, coup_ref, pat_ref, wgt_ref,
    sems, out_sems,
):
    blocks = volt_hbm.shape[0]
    half, own, shift = half_of(blocks // LANES)
    first, count, outer = 1 - half, own + 1, half * (own + 1)
    edge = 1 + half * (own - 1)
    known = pl.ds(pl.multiple_of(first * LANES, LANES), count * LANES)
    source = pl.ds(pl.multiple_of((first + shift) * LANES, LANES), count * LANES)
    lanes = pl.ds(pl.multiple_of((edge + shift) * LANES, LANES), LANES)
    neighbours = pat_hbm.shape[0]
    steps = [(at, min(8, count - at)) for at in range(0, count, 8)]

    def some(ref, at, size):
        return ref.at[pl.ds(first + at, size)]

    pairs = [
        (volt_hbm.at[source, :], volt_ref.at[known, :]),
        (coup_hbm, coup_ref),
        (some(band_hbm, *steps[0]), some(band_ref, *steps[0])),
        (diag_hbm.at[source, :], diag_ref.at[known, :]),
        (pat_hbm.at[:, lanes], pat_ref),
        (wgt_hbm.at[:, lanes], wgt_ref.at[neighbours : 2 * neighbours, :]),
    ] + [(some(band_hbm, *step), some(band_ref, *step)) for step in steps[1:]]
    loads = [
        pltpu.make_async_copy(hbm, ref, sems.at[i]) for i, (hbm, ref) in enumerate(pairs)
    ]
    for load in loads:
        load.start()
    writes = []

    def write_out(ref, hbm):
        writes.append(pltpu.make_async_copy(ref, hbm, out_sems.at[len(writes)]))
        writes[-1].start()

    def spread(tile, size):
        store(plane_ref, tile, volt_ref[span(tile, 0, size * LANES), :])

    def invert(tile, size):
        cut = span(tile, 0, size * LANES)
        inv_ref[cut, :] = reciprocal(diag_ref[cut, :])

    def base(tile, size):
        def write(tile, values):
            base_ref[span(tile), :] = values

        couple(plane_ref, tile, [band_ref[tile + i] for i in range(size)], mix, write)
        cut = span(tile, 0, size * LANES)
        write_out(base_ref.at[cut, :], base_hbm.at[cut, :])

    clear_pads(plane_ref)
    plane_ref[span(outer, RADIUS), :] = jnp.zeros((LANES, 2 * LANES), BF16)
    loads[0].wait()
    in_chunks(first, count, spread, 8)
    at = 2 * LANES
    write_out(volt_ref.at[span(edge), :], pack_hbm.at[0:LANES, :])
    write_out(
        volt_ref.at[2 * LANES : 2 * LANES + RADIUS, :], near_hbm.at[0:RADIUS, :]
    )
    write_out(
        volt_ref.at[own * LANES - RADIUS : own * LANES, :],
        near_hbm.at[RADIUS : 2 * RADIUS, :],
    )
    loads[1].wait()
    loads[2].wait()
    mix = mixer(coup_ref)
    base(first, steps[0][1])
    for load in loads[3:6]:
        load.wait()
    wgt_ref[0:neighbours, :] = pat_ref[...].astype(F32)
    write_out(wgt_ref, pack_hbm.at[at : at + 2 * neighbours, :])
    write_out(diag_ref.at[span(edge), :], pack_hbm.at[LANES:at, :])
    in_chunks(first, count, invert, 8)
    write_out(inv_ref.at[known, :], inv_hbm.at[known, :])
    for load, (start, size) in zip(loads[6:], steps[1:]):
        load.wait()
        base(first + start, size)
    for write in writes:
        write.wait()


def slot_places(cap, ids_ref):
    per_row = LANES // cap
    lane = lax.broadcasted_iota(jnp.int32, (1, LANES), 1)
    places = []
    for at in range(0, ids_ref.shape[0], per_row):
        total = None
        for i in range(per_row):
            row = jnp.where(lane < cap, ids_ref[at + i : at + i + 1, :], 0)
            row = pltpu.roll(row, i * cap, 1) if i else row
            total = row if total is None else total + row
        places.append(total)
    return places


def gather_inflow(places, first, rows, current):
    at = lax.broadcasted_iota(jnp.int32, (rows, LANES), 0) + first
    hits = [jnp.where(at == place, 1.0, 0.0).astype(BF16) for place in places]
    both = jnp.dot(jnp.concatenate(hits, axis=1), current, preferred_element_type=F32)
    return both[:, :LANES] + both[:, LANES:]


def ends_body(cap, tiles, ids_ref, current_ref, out_ref):
    half, _, _ = half_of(tiles)
    places = slot_places(cap, ids_ref)
    current = jnp.concatenate(halves(current_ref[...]), axis=1)
    out_ref[...] = gather_inflow(places, half * (tiles - 1) * LANES, LANES, current)


def inflow_body(
    cap, tiles, ids_ref, current_ref, coup_ref, own_ref, halo_ref, near_ref, after_ref,
    out_ref, band_ref, inv_ref, base_ref, plane_ref,
):
    half, own, shift = half_of(tiles)
    first, count = 1 - half, own + 1
    places = slot_places(cap, ids_ref)
    current = jnp.concatenate(halves(current_ref[...]), axis=1)

    def inflow(tile, size):
        cut = span(tile, 0, size * LANES)
        out_ref[cut, :] = gather_inflow(
            places, (tile + shift) * LANES, size * LANES, current
        )

    in_chunks(first, count, inflow)
    out_ref[span(half * (own + 1)), :] = jnp.zeros((LANES, LANES), F32)

    neighbours = (own_ref.shape[0] - 2 * LANES) // 2
    begin = (place()[1] * tiles + 2 * half * own - 1) * LANES
    packs = [jnp.where(half == at, halo_ref[...], own_ref[...]) for at in range(2)]
    at = 2 * LANES
    bands = []
    for tile, pack in enumerate(packs):
        bands.append(
            build_band(
                begin + tile * LANES - RADIUS,
                pack[at : at + neighbours].astype(jnp.int32),
                pack[at + neighbours : at + 2 * neighbours],
            )
        )
        store(plane_ref, tile, pack[:LANES])
    none = jnp.zeros((RADIUS, 2 * LANES), BF16)
    low, high = (
        jnp.concatenate(halves(near_ref[cut, :]), axis=1)
        for cut in (slice(0, RADIUS), slice(RADIUS, 2 * RADIUS))
    )
    size = plane_ref.shape[0]
    plane_ref[0:RADIUS, :] = jnp.where(half == 0, none, high)
    plane_ref[size - RADIUS : size, :] = jnp.where(half == 0, low, none)
    results = []
    couple(plane_ref, 0, bands, mixer(coup_ref), lambda tile, values: results.append(values))
    band_ref[...] = jnp.where(half == 0, bands[0], bands[1])
    inv_ref[...] = reciprocal(halo_ref[LANES : 2 * LANES, :])
    base_ref[0:LANES, :] = jnp.where(half == 0, results[0], results[1])
    base_ref[LANES:, :] = jnp.where(half == 0, results[1], results[0])


def iterate_body(
    cap, die_count, asked_ref, coup_ref, halo_ref, inflow_ref, band_ref, base_ref, inv_ref,
    halo_band_ref, halo_inv_ref, edge_base_ref, out_hbm, full_hbm, picked_ref, out_ref, here_ref, there_ref, sems,
):
    own = out_hbm.shape[0] // LANES
    half, _, _ = half_of(2 * own)
    first, count, outer = 1 - half, own + 1, half * (own + 1)
    edge = 1 + half * (own - 1)
    for ref in (here_ref, there_ref):
        clear_pads(ref)

    def start(tile, size):
        cut = span(tile, 0, size * LANES)
        store(here_ref, tile, -(inflow_ref[cut, :] + base_ref[cut, :]) * inv_ref[cut, :])

    in_chunks(first, count, start)
    halo_inv = halo_inv_ref[...]
    store(here_ref, outer, -(halo_ref[...] + edge_base_ref[0:LANES, :]) * halo_inv)
    cut = span(edge)
    store(here_ref, edge, -(inflow_ref[cut, :] + edge_base_ref[LANES:, :]) * inv_ref[cut, :])
    mix = mixer(coup_ref)
    refs = (here_ref, there_ref)
    for iteration in range(1, ITERS):
        source, target = refs[(iteration - 1) % 2], refs[iteration % 2]
        last = iteration == ITERS - 1

        def write(tile, coupled, target=target, last=last):
            values = -(inflow_ref[span(tile), :] + coupled) * inv_ref[span(tile), :]
            if last:
                out_ref[span(tile - 1), :] = values
            else:
                store(target, tile, values)

        def step(tile, size, source=source, write=write):
            bands = [band_ref[tile + i] for i in range(size)]
            couple(source, tile, bands, mix, write)

        def final(tile, size, step=step):
            step(tile, size)
            cut = span(tile - 1, 0, size * LANES)
            whole = span(half * own + tile - 1, 0, size * LANES)
            pltpu.make_async_copy(out_ref.at[cut, :], out_hbm.at[cut, :], sems.at[0]).start()
            pltpu.make_async_copy(out_ref.at[cut, :], full_hbm.at[whole, :], sems.at[1]).start()

        def write_halo(tile, coupled, target=target):
            store(target, tile, -(halo_ref[...] + coupled) * halo_inv)

        if last:
            in_chunks(1, own, final)
        else:
            in_chunks(first, count, step)
            couple(source, outer, [halo_band_ref[...]], mix, write_halo)

    base_row = half * own * LANES
    group, _ = place()
    pair = group - lax.rem(group, 2)
    for member in range(2):
        offset = member * (picked_ref.shape[0] // 2)
        for at, row in asked_rows(cap, die_count, pair + member, asked_ref):
            row = row - base_row
            inside = (row >= 0) & (row < own * LANES)
            safe = jnp.clip(row, 0, own * LANES - 1)
            values = out_ref[pl.ds(safe, 1), :]
            picked_ref[pl.ds(offset + at, 1), :] = jnp.where(inside, values, 0.0)
    pltpu.make_async_copy(out_ref, out_hbm, sems.at[0]).wait()
    pltpu.make_async_copy(out_ref, full_hbm.at[0 : own * LANES, :], sems.at[1]).wait()


def join_body(other_ref, full_in_hbm, full_hbm, done_ref, sem):
    rows = other_ref.shape[0]
    half, _, _ = half_of(2 * rows // LANES)
    start = pl.multiple_of((1 - half) * rows, LANES)
    copy = pltpu.make_async_copy(other_ref, full_hbm.at[pl.ds(start, rows), :], sem)
    copy.start()
    done_ref[...] = jnp.zeros(done_ref.shape, F32)
    copy.wait()


def add_body(parts_ref, after_ref, out_ref):
    rows = out_ref.shape[0]
    out_ref[...] = parts_ref[0:rows, :] + parts_ref[rows:, :]


def scatter_body(cols, node_ref, cond_ref, start_ref, volt_ref, load_ref, shunt_ref,
                 right_ref, inv_ref, inner_ref, outer_ref):
    blocks = node_ref.shape[0]
    rows = volt_ref.shape[0]
    group = math.gcd(blocks, 16)
    row_at = lax.broadcasted_iota(jnp.int32, (rows, LANES), 0)
    col_at = lax.broadcasted_iota(jnp.int32, (cols, LANES), 0)
    total = jnp.zeros((4 * rows, cols), F32)
    for first in range(0, blocks, group):
        node = node_ref[first : first + group, :]
        live = node >= 0
        cond = jnp.where(live, cond_ref[first : first + group, :], 0.0)
        flow = cond * start_ref[first : first + group, :]
        safe = jnp.where(live, node, 0)
        row, col = safe // cols, safe % cols
        parts = halves(cond) + halves(flow)
        left, right = [], []
        for i in range(group):
            spot = jnp.where(row_at == row[i : i + 1, :], 1.0, 0.0).astype(BF16)
            left.append(
                jnp.concatenate([spot * part[i : i + 1, :] for part in parts], axis=0)
            )
            right.append(jnp.where(col_at == col[i : i + 1, :], 1.0, 0.0).astype(BF16))
        total = total + lax.dot_general(
            jnp.concatenate(left, axis=1),
            jnp.concatenate(right, axis=1),
            (((1,), (1,)), ((), ())),
            preferred_element_type=F32,
        )
    gsum = total[:rows] + total[rows : 2 * rows]
    inject = total[2 * rows : 3 * rows] + total[3 * rows :]
    inv = 1.0 / (4.0 + shunt_ref[...] + gsum)
    right_side = (inject - load_ref[...]) * inv
    right_ref[...] = right_side
    inv_ref[...] = inv
    volt = volt_ref[...]
    top, bottom = (
        jnp.concatenate([volt[cut], right_side[cut], inv[cut]], axis=0)
        for cut in (slice(0, HALO_ROWS), slice(rows - HALO_ROWS, rows))
    )
    swap_parts(inner_ref, outer_ref, place()[0], top, bottom)


def swap_parts(inner_ref, outer_ref, mine, first, last):
    even = lax.rem(mine, 2) == 0
    inner_ref[...] = jnp.where(even, last, first)
    outer_ref[...] = jnp.where(even, first, last)


def swapped(inner, outer, mine):
    even = lax.rem(mine, 2) == 0
    return jnp.where(even, outer, inner), jnp.where(even, inner, outer)


def swap(inner, outer, axis):
    count = lax.axis_size(axis)

    def pairs(start):
        return [
            pair
            for i in range(start, count - 1, 2)
            for pair in ((i, i + 1), (i + 1, i))
        ]

    return lax.ppermute(outer, axis, pairs(1)), lax.ppermute(inner, axis, pairs(0))


def extended(own, top, bottom, index):
    cut = slice(index * HALO_ROWS, (index + 1) * HALO_ROWS)
    return jnp.concatenate([own, bottom[cut], top[cut]], axis=0)


def edge_body(
    volt_ref, right_ref, inv_ref, outer_ref, inner_ref, after_ref, west_ref, east_ref
):
    cols = volt_ref.shape[1]
    top, bottom = swapped(inner_ref[...], outer_ref[...], place()[0])
    out_rows, high = west_ref.shape
    west, east = None, None
    for index, ref in enumerate((volt_ref, right_ref, inv_ref)):
        whole = extended(ref[...], top, bottom, index)
        lane = lax.broadcasted_iota(jnp.int32, (whole.shape[0], LANES), 1)
        head, tail = whole[:, :LANES], whole[:, cols - LANES :]
        at = index * SWEEPS
        head = pltpu.roll(head, at, 1) if at else head
        tail = pltpu.roll(tail, at + SWEEPS, 1)
        west = head if west is None else jnp.where(lane >= at, head, west)
        east = tail if east is None else jnp.where(lane >= at, tail, east)
    fill = jnp.zeros((high - west.shape[0], LANES), F32)
    west, east = (
        jnp.concatenate([part, fill], axis=0).T[:out_rows] for part in (west, east)
    )
    swap_parts(west_ref, east_ref, place()[1], west, east)


def swept(volt, right_side, inv):
    high, wide = volt.shape
    for weight in sweep_weights(SWEEPS):
        beside = (
            pltpu.roll(volt, 1, 0)
            + pltpu.roll(volt, high - 1, 0)
            + pltpu.roll(volt, 1, 1)
            + pltpu.roll(volt, wide - 1, 1)
        )
        volt = (1.0 - weight) * volt + weight * (right_side + beside * inv)
    return volt


GROUP = 8


def one_hot(rows, places):
    at = lax.broadcasted_iota(jnp.int32, (rows, LANES), 0)
    return jnp.concatenate(
        [
            jnp.where(at == places[i : i + 1, :], 1.0, 0.0).astype(BF16)
            for i in range(places.shape[0])
        ],
        axis=1,
    )


def pick_rows(found, places):
    at = lax.broadcasted_iota(jnp.int32, (found.shape[0], LANES), 0)
    return [
        jnp.sum(
            jnp.where(at == places[i : i + 1, :], found[:, i * LANES : (i + 1) * LANES], 0.0),
            axis=0,
            keepdims=True,
        )
        for i in range(places.shape[0])
    ]


def inner_body(node_ref, volt_ref, right_ref, inv_ref, row_out_ref, row_in_ref, out_ref, found_ref):
    rows, cols = volt_ref.shape
    top, bottom = swapped(row_in_ref[...], row_out_ref[...], place()[0])
    volt = swept(
        *(
            extended(ref[...], top, bottom, index)
            for index, ref in enumerate((volt_ref, right_ref, inv_ref))
        )
    )[:rows]
    out_ref[...] = volt
    col = lax.broadcasted_iota(jnp.int32, volt.shape, 1)
    volt = jnp.where((col >= SWEEPS) & (col < cols - SWEEPS), volt, 0.0)
    both = jnp.concatenate(halves(volt), axis=0)
    for first in range(0, node_ref.shape[0], GROUP):
        safe = jnp.maximum(node_ref[first : first + GROUP, :], 0)
        found = jnp.dot(both, one_hot(cols, safe % cols), preferred_element_type=F32)
        found = pick_rows(found[:rows] + found[rows:], safe // cols)
        for i, values in enumerate(found):
            found_ref[first + i : first + i + 1, :] = values


def sweep_body(copies, node_ref, cond_ref, start_ref, volt_ref, right_ref, inv_ref,
               row_out_ref, row_in_ref, col_out_ref, col_in_ref, inner_ref, found_ref,
               out_ref, current_ref):
    rows, cols = volt_ref.shape
    blocks = node_ref.shape[0]
    cap = current_ref.shape[1]
    quarter = LANES // 4
    strip = []
    top, bottom = swapped(row_in_ref[...], row_out_ref[...], place()[0])
    out_rows, high = col_in_ref.shape
    fill = jnp.zeros((LANES - out_rows, high), F32)
    wests, easts = (
        jnp.concatenate([part, fill], axis=0).T[: rows + 2 * HALO_ROWS]
        for part in swapped(col_in_ref[...], col_out_ref[...], place()[1])
    )
    lane = lax.broadcasted_iota(jnp.int32, easts.shape, 1)
    for index, ref in enumerate((volt_ref, right_ref, inv_ref)):
        own = extended(ref[...], top, bottom, index)
        at = index * SWEEPS
        west = pltpu.roll(wests, LANES - SWEEPS - at, 1)
        east = pltpu.roll(easts, 3 * quarter - at, 1)
        tail = pltpu.roll(own[:, cols - LANES :], LANES - quarter, 1)
        strip.append(
            jnp.where(
                lane < 3 * quarter,
                jnp.where(lane < quarter + quarter // 2, own[:, :LANES], tail),
                jnp.where(lane < 3 * quarter + quarter // 2, east, west),
            )
        )
    strip = swept(*strip)[:rows]
    lane = lane[:rows]
    inner = inner_ref[...]
    out_ref[...] = inner
    out_ref[:, :LANES] = jnp.where(lane < SWEEPS, strip, inner[:, :LANES])
    out_ref[:, cols - LANES :] = jnp.where(
        lane >= LANES - SWEEPS, pltpu.roll(strip, quarter, 1), inner[:, cols - LANES :]
    )
    turned = strip.T
    edge = jnp.concatenate([turned[:8], turned[3 * quarter - 8 : 3 * quarter]], axis=0)
    count = edge.shape[0]
    edge = jnp.concatenate(halves(edge), axis=0)
    dies = blocks // cap
    for first in range(0, blocks, GROUP):
        cut = slice(first, first + GROUP)
        node = node_ref[cut, :]
        safe = jnp.maximum(node, 0)
        row, col = safe // cols, safe % cols
        from_end = col - (cols - SWEEPS)
        at_edge = jnp.where(
            col < SWEEPS, col, jnp.where(from_end >= 0, from_end + count - SWEEPS, -1)
        )
        found = jnp.dot(edge, one_hot(rows, row), preferred_element_type=F32)
        found = jnp.concatenate(pick_rows(found[:count] + found[count:], at_edge), axis=0)
        cond = jnp.where(node >= 0, cond_ref[cut, :], 0.0)
        current = cond * (start_ref[cut, :] - (found_ref[cut, :] + found))
        for i in range(GROUP):
            block = first + i
            current_ref[block // cap, block % cap : block % cap + 1, :] = current[i : i + 1, :]
    for copy in range(1, copies):
        current_ref[copy * dies : (copy + 1) * dies] = current_ref[0:dies]


def local(
    die_volt,
    die_load,
    die_shunt,
    bump_node,
    bump_block,
    bump_cond,
    pkg_volt,
    pkg_diag,
    pkg_pattern,
    pkg_weight,
    block_coupling,
):
    die_count = lax.axis_size("die")
    group_count = lax.axis_size("grp")
    devices = die_count * group_count
    blocks = pkg_volt.shape[0]
    tiles = blocks // LANES
    neighbours = pkg_pattern.shape[0]
    slots = bump_block.shape[0]
    cap = slots // die_count
    rows, cols = die_volt.shape
    (spread,) = call(
        functools.partial(spread_body, cap, die_count, blocks),
        "spread_blocks",
        [shape(devices, 1, LANES, dtype=jnp.int32)],
        (bump_block.reshape(1, slots),),
        [VMEM],
    )
    ids = lax.all_to_all(
        spread, ("grp", "die"), split_axis=0, concat_axis=0, tiled=True
    ).reshape(devices, LANES)

    (picked,) = call(
        functools.partial(pick_body, cap, die_count),
        "pick_rows",
        [shape(slots, LANES)],
        (ids, pkg_volt),
        [SMEM, VMEM],
    )
    bump_start = lax.all_to_all(
        picked.reshape(die_count, cap, LANES), "die", split_axis=0, concat_axis=0, tiled=True
    ).reshape(slots, LANES)

    right_side, inv, *edges = call(
        functools.partial(scatter_body, cols),
        "scatter_bumps",
        [shape(rows, cols)] * 2 + [shape(3 * HALO_ROWS, cols)] * 2,
        (bump_node, bump_cond, bump_start, die_volt, die_load, die_shunt),
        [VMEM] * 6,
        work=3,
    )
    own = tiles // 2
    dma = pltpu.SemaphoreType.DMA
    plane = pltpu.VMEM(((own + 2) * LANES + 2 * RADIUS, 2 * LANES), BF16)
    range_rows = pltpu.VMEM(((own + 2) * LANES, LANES), F32)
    range_bands = pltpu.VMEM((own + 2, 2 * LANES, 2 * LANES), BF16)
    beside = swap(*edges, "grp")
    band, banded = call(
        bands_body,
        "package_bands",
        [shape(own + 2, 2 * LANES, 2 * LANES, dtype=BF16), shape(8, LANES)],
        (pkg_pattern, pkg_weight, right_side),
        [VMEM, VMEM, ANY],
        work=2,
    )

    edge_rows = -(-3 * SWEEPS // 8) * 8
    edge_cols = -(-(rows + 2 * HALO_ROWS) // LANES) * LANES
    edges = call(
        edge_body,
        "edge_columns",
        [shape(edge_rows, edge_cols)] * 2,
        (die_volt, right_side, inv, *beside, banded),
        [VMEM] * 5 + [ANY],
    )
    columns = swap(*edges, "die")

    inner, found = call(
        inner_body,
        "inner_sweeps",
        [shape(rows, cols), shape(slots, LANES)],
        (bump_node, die_volt, right_side, inv, *beside),
        [VMEM] * 6,
        work=3,
    )
    die_out, current = call(
        functools.partial(sweep_body, group_count),
        "sweeps",
        [shape(rows, cols), shape(devices, cap, LANES)],
        (
            bump_node, bump_cond, bump_start, die_volt, right_side, inv, *beside, *columns,
            inner, found,
        ),
        [VMEM] * 12,
        work=4,
    )
    pack_rows = 2 * LANES + 2 * neighbours
    base, pkg_inv, pack, near = call(
        prepare_body,
        "package_prepare",
        [
            shape((own + 2) * LANES, LANES),
            shape((own + 2) * LANES, LANES),
            shape(pack_rows, LANES),
            shape(2 * RADIUS, LANES),
        ],
        (pkg_pattern, pkg_weight, block_coupling, band, pkg_volt, pkg_diag, die_out),
        [HBM] * 7,
        [
            range_rows, range_rows, range_bands, range_rows, range_rows, plane,
            pltpu.VMEM((LANES, LANES), F32), pltpu.VMEM((neighbours, LANES), jnp.int32),
            pltpu.VMEM((2 * neighbours, LANES), F32), dma((6 + own // 8,)), dma((7 + own // 8,)),
        ],
        work=5,
        vmem=MOST_VMEM,
        out_specs=[HBM] * 4,
    )

    current = lax.all_to_all(
        current, ("grp", "die"), split_axis=0, concat_axis=0, tiled=True
    ).reshape(devices * cap, LANES)

    beside_end = [
        (g * die_count + a, g * die_count + b)
        for g in range(group_count)
        for d in range((g + 1) % 2, die_count - 1, 2)
        for a, b in ((d, d + 1), (d + 1, d))
    ]
    halo = lax.ppermute(pack, ("grp", "die"), beside_end)
    (inflow,) = call(
        functools.partial(ends_body, cap, tiles),
        "package_end",
        [shape(LANES, LANES)],
        (ids, current),
        [VMEM, VMEM],
    )
    halo_inflow = lax.ppermute(inflow, ("grp", "die"), beside_end)
    all_inflow, halo_band, halo_inv, edge_base = call(
        functools.partial(inflow_body, cap, tiles),
        "package_inflow",
        [
            shape((own + 2) * LANES, LANES),
            shape(2 * LANES, 2 * LANES, dtype=BF16),
            shape(LANES, LANES),
            shape(2 * LANES, LANES),
        ],
        (ids, current, block_coupling, pack, halo, near, inflow),
        [VMEM] * 6 + [ANY],
        [pltpu.VMEM((2 * LANES + 2 * RADIUS, 2 * LANES), BF16)],
        work=3,
    )
    half_out, pkg_out, picked = call(
        functools.partial(iterate_body, cap, die_count),
        "package_iterations",
        [shape(own * LANES, LANES), shape(blocks, LANES), shape(2 * slots, LANES)],
        (
            ids, block_coupling, halo_inflow, all_inflow, band, base, pkg_inv,
            halo_band, halo_inv, edge_base,
        ),
        [SMEM] + [VMEM] * 9,
        [pltpu.VMEM((own * LANES, LANES), F32), plane, plane, dma((2,))],
        work=10,
        vmem=24,
        out_specs=[HBM, HBM, VMEM],
    )
    pair = 2 * die_count
    parts = lax.all_to_all(
        picked.reshape(pair, cap, LANES),
        ("grp", "die"),
        split_axis=0,
        concat_axis=0,
        axis_index_groups=[
            [first + i for i in range(pair)] for first in range(0, devices, pair)
        ],
        tiled=True,
    ).reshape(2 * slots, LANES)
    other = lax.ppermute(half_out, "grp", [(g, g ^ 1) for g in range(group_count)])
    pkg_out, done = call(
        join_body,
        "join_halves",
        [shape(blocks, LANES), shape(8, LANES)],
        (other, pkg_out),
        [VMEM, HBM],
        [dma(())],
        out_specs=[HBM, VMEM],
        aliases={1: 0},
    )
    (bump_out,) = call(
        add_body, "add_parts", [shape(slots, LANES)], (parts, done), [VMEM, ANY]
    )
    return (die_out, pkg_out, bump_out)


def solution(mesh):
    return jax.shard_map(
        local,
        mesh=mesh,
        in_specs=(
            P("grp", "die"),
            P("grp", "die"),
            P("grp", "die"),
            P(("grp", "die"), None),
            P(("grp", "die")),
            P(("grp", "die"), None),
            P("die", None),
            P("die", None),
            P(None, "die"),
            P(None, "die"),
            P(),
        ),
        out_specs=(P("grp", "die"), P("die", None), P(("grp", "die"), None)),
        check_vma=False,
    )
```

```python
import functools
import math

import jax
import jax.numpy as jnp
from jax import lax
from jax.experimental import pallas as pl
from jax.experimental.pallas import tpu as pltpu
from jax.sharding import PartitionSpec as P

RADIUS = 32
SWEEPS = 4
ITERS = 4
LANES = 128
HALO_ROWS = 8
REACH = RADIUS * ITERS
WINDOW = LANES + 2 * RADIUS
F32 = jnp.float32
BF16 = jnp.bfloat16
MOST_VMEM = 57
VMEM = pl.BlockSpec(memory_space=pltpu.VMEM)
SMEM = pl.BlockSpec(memory_space=pltpu.SMEM)
ANY = pl.BlockSpec(memory_space=pl.ANY)
HBM = pl.BlockSpec(memory_space=pltpu.HBM)


def sweep_weights(sweeps):
    return [
        1.0 / (1.0 + 0.8 * math.cos(math.pi * (2 * index + 1) / (2 * sweeps)))
        for index in range(sweeps)
    ]


def call(
    body, name, outs, args, specs, scratch=(), work=1, vmem=16, out_specs=None, aliases=None
):
    bytes_accessed = sum(4 * math.prod(arg.shape) for arg in args)
    return pl.pallas_call(
        body,
        name=name,
        out_shape=outs,
        in_specs=specs,
        out_specs=out_specs or [VMEM] * len(outs),
        input_output_aliases=aliases or {},
        scratch_shapes=list(scratch),
        compiler_params=pltpu.CompilerParams(vmem_limit_bytes=vmem * 1024 * 1024),
        cost_estimate=pl.CostEstimate(
            flops=work * 10**9, bytes_accessed=bytes_accessed, transcendentals=0
        ),
    )(*args)


def place():
    return lax.axis_index("grp"), lax.axis_index("die")


def shape(*dims, dtype=F32):
    return jax.ShapeDtypeStruct(dims, dtype)


def halves(values):
    high = values.astype(BF16)
    low = (values - high.astype(F32)).astype(BF16)
    return high, low


def spread_body(cap, die_count, blocks, block_ref, out_ref):
    slots = block_ref.shape[1]
    block = jnp.concatenate(
        [block_ref[...], jnp.zeros((1, LANES - slots), jnp.int32)], axis=1
    )
    for die in range(die_count):
        row = (pltpu.roll(block, LANES - die * cap, 1) if die else block) - die * blocks
        for at in range(die, out_ref.shape[0], die_count):
            out_ref[at] = row


def asked_rows(cap, die_count, group, ids_ref):
    for die in range(die_count):
        for slot in range(cap):
            yield die * cap + slot, ids_ref[group * die_count + die, slot]


def pick_body(cap, die_count, ids_ref, plane_ref, out_ref):
    group, _ = place()
    for at, row in asked_rows(cap, die_count, group, ids_ref):
        out_ref[pl.ds(at, 1), :] = plane_ref[pl.ds(row, 1), :]


def build_band(first, pattern, weights):
    place = lax.broadcasted_iota(jnp.int32, (WINDOW, LANES), 0)
    band = None
    for k in range(pattern.shape[0]):
        hit = place == (pattern[k : k + 1, :] - first)
        term = jnp.where(hit, weights[k : k + 1, :], 0.0)
        band = term if band is None else band + term
    fill = jnp.zeros((2 * LANES - WINDOW, LANES), F32)
    return jnp.concatenate(halves(jnp.concatenate([band, fill], axis=0).T), axis=0)


def reciprocal(diag):
    safe = jnp.where(diag > 0.0, diag, 1.0)
    return jnp.where(diag > 0.0, 1.0 / safe, 0.0)


def span(tile, offset=0, size=LANES):
    return pl.ds(pl.multiple_of(tile * LANES + offset, RADIUS), size)


def mixer(coup_ref):
    mix = jnp.concatenate(halves(coup_ref[...]), axis=1)
    return jnp.concatenate([mix, mix], axis=0)


def clear_pads(ref):
    size = ref.shape[0]
    ref[0:RADIUS, :] = jnp.zeros((RADIUS, 2 * LANES), BF16)
    ref[size - LANES + RADIUS : size, :] = jnp.zeros((LANES - RADIUS, 2 * LANES), BF16)


def store(ref, tile, values):
    ref[span(tile, RADIUS, values.shape[0]), :] = jnp.concatenate(halves(values), axis=1)


def couple(source, tile, bands, mix, write):
    for at in range(0, len(bands), 4):
        couple_few(source, tile + at, bands[at : at + 4], mix, write)


def couple_few(source, tile, bands, mix, write):
    own = source[span(tile, RADIUS, len(bands) * LANES), :]
    within = jnp.dot(own, mix, preferred_element_type=F32)
    for i, band in enumerate(bands):
        window = source[span(tile + i, 0, 2 * LANES), :]
        beside = jnp.dot(band, window, preferred_element_type=F32)
        both = beside[:LANES] + beside[LANES:] + within[i * LANES : (i + 1) * LANES]
        write(tile + i, both[:, :LANES] + both[:, LANES:])


def in_chunks(first, count, body, size=16):
    whole = count // size

    @pl.loop(0, whole)
    def _(chunk):
        body(first + chunk * size, size)

    if count % size:
        body(first + whole * size, count % size)


def half_of(tiles):
    half = lax.rem(sum(place()), 2)
    own = tiles // 2
    return half, own, half * own - 1


def bands_body(pat_ref, wgt_ref, after_ref, band_ref, done_ref):
    blocks = pat_ref.shape[1]
    half, own, shift = half_of(blocks // LANES)
    begin = place()[1] * blocks + shift * LANES

    def bands(tile, size):
        for i in range(size):
            lanes = pl.ds(pl.multiple_of((tile + i + shift) * LANES, LANES), LANES)
            band_ref[tile + i] = build_band(
                begin + (tile + i) * LANES - RADIUS, pat_ref[:, lanes], wgt_ref[:, lanes]
            )

    in_chunks(1 - half, own + 1, bands, 8)
    band_ref[half * (own + 1)] = jnp.zeros(band_ref.shape[1:], BF16)
    done_ref[...] = jnp.zeros(done_ref.shape, F32)


def prepare_body(
    pat_hbm, wgt_hbm, coup_hbm, band_hbm, volt_hbm, diag_hbm, after_ref,
    base_hbm, inv_hbm, pack_hbm, near_hbm,
    volt_ref, diag_ref, band_ref, base_ref, inv_ref, plane_ref, coup_ref, pat_ref, wgt_ref,
    sems, out_sems,
):
    blocks = volt_hbm.shape[0]
    half, own, shift = half_of(blocks // LANES)
    first, count, outer = 1 - half, own + 1, half * (own + 1)
    edge = 1 + half * (own - 1)
    known = pl.ds(pl.multiple_of(first * LANES, LANES), count * LANES)
    source = pl.ds(pl.multiple_of((first + shift) * LANES, LANES), count * LANES)
    lanes = pl.ds(pl.multiple_of((edge + shift) * LANES, LANES), LANES)
    neighbours = pat_hbm.shape[0]
    steps = [(at, min(8, count - at)) for at in range(0, count, 8)]

    def some(ref, at, size):
        return ref.at[pl.ds(first + at, size)]

    pairs = [
        (volt_hbm.at[source, :], volt_ref.at[known, :]),
        (coup_hbm, coup_ref),
        (some(band_hbm, *steps[0]), some(band_ref, *steps[0])),
        (diag_hbm.at[source, :], diag_ref.at[known, :]),
        (pat_hbm.at[:, lanes], pat_ref),
        (wgt_hbm.at[:, lanes], wgt_ref.at[neighbours : 2 * neighbours, :]),
    ] + [(some(band_hbm, *step), some(band_ref, *step)) for step in steps[1:]]
    loads = [
        pltpu.make_async_copy(hbm, ref, sems.at[i]) for i, (hbm, ref) in enumerate(pairs)
    ]
    for load in loads:
        load.start()
    writes = []

    def write_out(ref, hbm):
        writes.append(pltpu.make_async_copy(ref, hbm, out_sems.at[len(writes)]))
        writes[-1].start()

    def spread(tile, size):
        store(plane_ref, tile, volt_ref[span(tile, 0, size * LANES), :])

    def invert(tile, size):
        cut = span(tile, 0, size * LANES)
        inv_ref[cut, :] = reciprocal(diag_ref[cut, :])

    def base(tile, size):
        def write(tile, values):
            base_ref[span(tile), :] = values

        couple(plane_ref, tile, [band_ref[tile + i] for i in range(size)], mix, write)
        cut = span(tile, 0, size * LANES)
        write_out(base_ref.at[cut, :], base_hbm.at[cut, :])

    clear_pads(plane_ref)
    plane_ref[span(outer, RADIUS), :] = jnp.zeros((LANES, 2 * LANES), BF16)
    loads[0].wait()
    in_chunks(first, count, spread, 8)
    at = 2 * LANES
    write_out(volt_ref.at[span(edge), :], pack_hbm.at[0:LANES, :])
    write_out(
        volt_ref.at[2 * LANES : 2 * LANES + RADIUS, :], near_hbm.at[0:RADIUS, :]
    )
    write_out(
        volt_ref.at[own * LANES - RADIUS : own * LANES, :],
        near_hbm.at[RADIUS : 2 * RADIUS, :],
    )
    loads[1].wait()
    loads[2].wait()
    mix = mixer(coup_ref)
    base(first, steps[0][1])
    for load in loads[3:6]:
        load.wait()
    wgt_ref[0:neighbours, :] = pat_ref[...].astype(F32)
    write_out(wgt_ref, pack_hbm.at[at : at + 2 * neighbours, :])
    write_out(diag_ref.at[span(edge), :], pack_hbm.at[LANES:at, :])
    in_chunks(first, count, invert, 8)
    write_out(inv_ref.at[known, :], inv_hbm.at[known, :])
    for load, (start, size) in zip(loads[6:], steps[1:]):
        load.wait()
        base(first + start, size)
    for write in writes:
        write.wait()


def slot_places(cap, ids_ref):
    per_row = LANES // cap
    lane = lax.broadcasted_iota(jnp.int32, (1, LANES), 1)
    places = []
    for at in range(0, ids_ref.shape[0], per_row):
        total = None
        for i in range(per_row):
            row = jnp.where(lane < cap, ids_ref[at + i : at + i + 1, :], 0)
            row = pltpu.roll(row, i * cap, 1) if i else row
            total = row if total is None else total + row
        places.append(total)
    return places


def gather_inflow(places, first, rows, current):
    at = lax.broadcasted_iota(jnp.int32, (rows, LANES), 0) + first
    hits = [jnp.where(at == place, 1.0, 0.0).astype(BF16) for place in places]
    both = jnp.dot(jnp.concatenate(hits, axis=1), current, preferred_element_type=F32)
    return both[:, :LANES] + both[:, LANES:]


def ends_body(cap, tiles, ids_ref, current_ref, out_ref):
    half, _, _ = half_of(tiles)
    places = slot_places(cap, ids_ref)
    current = jnp.concatenate(halves(current_ref[...]), axis=1)
    out_ref[...] = gather_inflow(places, half * (tiles - 1) * LANES, LANES, current)


def inflow_body(
    cap, tiles, ids_ref, current_ref, coup_ref, own_ref, halo_ref, near_ref, after_ref,
    out_ref, band_ref, inv_ref, base_ref, plane_ref,
):
    half, own, shift = half_of(tiles)
    first, count = 1 - half, own + 1
    places = slot_places(cap, ids_ref)
    current = jnp.concatenate(halves(current_ref[...]), axis=1)

    def inflow(tile, size):
        cut = span(tile, 0, size * LANES)
        out_ref[cut, :] = gather_inflow(
            places, (tile + shift) * LANES, size * LANES, current
        )

    in_chunks(first, count, inflow)
    out_ref[span(half * (own + 1)), :] = jnp.zeros((LANES, LANES), F32)

    neighbours = (own_ref.shape[0] - 2 * LANES) // 2
    begin = (place()[1] * tiles + 2 * half * own - 1) * LANES
    packs = [jnp.where(half == at, halo_ref[...], own_ref[...]) for at in range(2)]
    at = 2 * LANES
    bands = []
    for tile, pack in enumerate(packs):
        bands.append(
            build_band(
                begin + tile * LANES - RADIUS,
                pack[at : at + neighbours].astype(jnp.int32),
                pack[at + neighbours : at + 2 * neighbours],
            )
        )
        store(plane_ref, tile, pack[:LANES])
    none = jnp.zeros((RADIUS, 2 * LANES), BF16)
    low, high = (
        jnp.concatenate(halves(near_ref[cut, :]), axis=1)
        for cut in (slice(0, RADIUS), slice(RADIUS, 2 * RADIUS))
    )
    clear_pads(plane_ref)
    end = 2 * LANES + RADIUS
    plane_ref[0:RADIUS, :] = jnp.where(half == 0, none, high)
    plane_ref[end : end + RADIUS, :] = jnp.where(half == 0, low, none)
    results = []
    couple(plane_ref, 0, bands, mixer(coup_ref), lambda tile, values: results.append(values))
    band_ref[...] = jnp.where(half == 0, bands[0], bands[1])
    inv_ref[...] = reciprocal(halo_ref[LANES : 2 * LANES, :])
    base_ref[0:LANES, :] = jnp.where(half == 0, results[0], results[1])
    base_ref[LANES:, :] = jnp.where(half == 0, results[1], results[0])


def iterate_body(
    cap, die_count, asked_ref, coup_ref, halo_ref, inflow_ref, band_ref, base_ref, inv_ref,
    halo_band_ref, halo_inv_ref, edge_base_ref, out_hbm, full_hbm, picked_ref, out_ref, here_ref, there_ref, sems,
):
    own = out_hbm.shape[0] // LANES
    half, _, _ = half_of(2 * own)
    first, count, outer = 1 - half, own + 1, half * (own + 1)
    edge = 1 + half * (own - 1)
    for ref in (here_ref, there_ref):
        clear_pads(ref)

    def start(tile, size):
        cut = span(tile, 0, size * LANES)
        store(here_ref, tile, -(inflow_ref[cut, :] + base_ref[cut, :]) * inv_ref[cut, :])

    in_chunks(first, count, start)
    halo_inv = halo_inv_ref[...]
    store(here_ref, outer, -(halo_ref[...] + edge_base_ref[0:LANES, :]) * halo_inv)
    cut = span(edge)
    store(here_ref, edge, -(inflow_ref[cut, :] + edge_base_ref[LANES:, :]) * inv_ref[cut, :])
    mix = mixer(coup_ref)
    refs = (here_ref, there_ref)
    for iteration in range(1, ITERS):
        source, target = refs[(iteration - 1) % 2], refs[iteration % 2]
        last = iteration == ITERS - 1

        def write(tile, coupled, target=target, last=last):
            values = -(inflow_ref[span(tile), :] + coupled) * inv_ref[span(tile), :]
            if last:
                out_ref[span(tile - 1), :] = values
            else:
                store(target, tile, values)

        def step(tile, size, source=source, write=write):
            bands = [band_ref[tile + i] for i in range(size)]
            couple(source, tile, bands, mix, write)

        def final(tile, size, step=step):
            step(tile, size)
            cut = span(tile - 1, 0, size * LANES)
            whole = span(half * own + tile - 1, 0, size * LANES)
            pltpu.make_async_copy(out_ref.at[cut, :], out_hbm.at[cut, :], sems.at[0]).start()
            pltpu.make_async_copy(out_ref.at[cut, :], full_hbm.at[whole, :], sems.at[1]).start()

        def write_halo(tile, coupled, target=target):
            store(target, tile, -(halo_ref[...] + coupled) * halo_inv)

        if last:
            in_chunks(1, own, final)
        else:
            in_chunks(first, count, step)
            couple(source, outer, [halo_band_ref[...]], mix, write_halo)

    base_row = half * own * LANES
    group, _ = place()
    pair = group - lax.rem(group, 2)
    for member in range(2):
        offset = member * (picked_ref.shape[0] // 2)
        for at, row in asked_rows(cap, die_count, pair + member, asked_ref):
            row = row - base_row
            inside = (row >= 0) & (row < own * LANES)
            safe = jnp.clip(row, 0, own * LANES - 1)
            values = out_ref[pl.ds(safe, 1), :]
            picked_ref[pl.ds(offset + at, 1), :] = jnp.where(inside, values, 0.0)
    pltpu.make_async_copy(out_ref, out_hbm, sems.at[0]).wait()
    pltpu.make_async_copy(out_ref, full_hbm.at[0 : own * LANES, :], sems.at[1]).wait()


def join_body(other_ref, full_in_hbm, full_hbm, done_ref, sem):
    rows = other_ref.shape[0]
    half, _, _ = half_of(2 * rows // LANES)
    start = pl.multiple_of((1 - half) * rows, LANES)
    copy = pltpu.make_async_copy(other_ref, full_hbm.at[pl.ds(start, rows), :], sem)
    copy.start()
    done_ref[...] = jnp.zeros(done_ref.shape, F32)
    copy.wait()


def add_body(parts_ref, after_ref, out_ref):
    rows = out_ref.shape[0]
    out_ref[...] = parts_ref[0:rows, :] + parts_ref[rows:, :]


def scatter_body(cols, node_ref, cond_ref, start_ref, volt_ref, load_ref, shunt_ref,
                 right_ref, inv_ref, inner_ref, outer_ref):
    blocks = node_ref.shape[0]
    rows = volt_ref.shape[0]
    group = 8
    row_at = lax.broadcasted_iota(jnp.int32, (rows, LANES), 0)
    col_at = lax.broadcasted_iota(jnp.int32, (cols, LANES), 0)
    total = jnp.zeros((4 * rows, cols), F32)
    for first in range(0, blocks, group):
        node = node_ref[first : first + group, :]
        live = node >= 0
        cond = jnp.where(live, cond_ref[first : first + group, :], 0.0)
        flow = cond * start_ref[first : first + group, :]
        safe = jnp.where(live, node, 0)
        row, col = safe // cols, safe % cols
        parts = halves(cond) + halves(flow)
        left, right = [], []
        for i in range(group):
            spot = jnp.where(row_at == row[i : i + 1, :], 1.0, 0.0).astype(BF16)
            left.append(
                jnp.concatenate([spot * part[i : i + 1, :] for part in parts], axis=0)
            )
            right.append(jnp.where(col_at == col[i : i + 1, :], 1.0, 0.0).astype(BF16))
        total = total + lax.dot_general(
            jnp.concatenate(left, axis=1),
            jnp.concatenate(right, axis=1),
            (((1,), (1,)), ((), ())),
            preferred_element_type=F32,
        )
    gsum = total[:rows] + total[rows : 2 * rows]
    inject = total[2 * rows : 3 * rows] + total[3 * rows :]
    inv = 1.0 / (4.0 + shunt_ref[...] + gsum)
    right_side = (inject - load_ref[...]) * inv
    right_ref[...] = right_side
    inv_ref[...] = inv
    volt = volt_ref[...]
    top, bottom = (
        jnp.concatenate([volt[cut], right_side[cut], inv[cut]], axis=0)
        for cut in (slice(0, HALO_ROWS), slice(rows - HALO_ROWS, rows))
    )
    swap_parts(inner_ref, outer_ref, place()[0], top, bottom)


def swap_parts(inner_ref, outer_ref, mine, first, last):
    even = lax.rem(mine, 2) == 0
    inner_ref[...] = jnp.where(even, last, first)
    outer_ref[...] = jnp.where(even, first, last)


def swapped(inner, outer, mine):
    even = lax.rem(mine, 2) == 0
    return jnp.where(even, outer, inner), jnp.where(even, inner, outer)


def swap(inner, outer, axis):
    count = lax.axis_size(axis)

    def pairs(start):
        return [
            pair
            for i in range(start, count - 1, 2)
            for pair in ((i, i + 1), (i + 1, i))
        ]

    return lax.ppermute(outer, axis, pairs(1)), lax.ppermute(inner, axis, pairs(0))


def extended(own, top, bottom, index):
    cut = slice(index * HALO_ROWS, (index + 1) * HALO_ROWS)
    return jnp.concatenate([own, bottom[cut], top[cut]], axis=0)


def edge_body(
    volt_ref, right_ref, inv_ref, outer_ref, inner_ref, after_ref, west_ref, east_ref
):
    cols = volt_ref.shape[1]
    top, bottom = swapped(inner_ref[...], outer_ref[...], place()[0])
    out_rows, high = west_ref.shape
    west, east = None, None
    for index, ref in enumerate((volt_ref, right_ref, inv_ref)):
        whole = extended(ref[...], top, bottom, index)
        lane = lax.broadcasted_iota(jnp.int32, (whole.shape[0], LANES), 1)
        head, tail = whole[:, :LANES], whole[:, cols - LANES :]
        at = index * SWEEPS
        head = pltpu.roll(head, at, 1) if at else head
        tail = pltpu.roll(tail, at + SWEEPS, 1)
        west = head if west is None else jnp.where(lane >= at, head, west)
        east = tail if east is None else jnp.where(lane >= at, tail, east)
    fill = jnp.zeros((high - west.shape[0], LANES), F32)
    west, east = (
        jnp.concatenate([part, fill], axis=0).T[:out_rows] for part in (west, east)
    )
    swap_parts(west_ref, east_ref, place()[1], west, east)


def swept(volt, right_side, inv):
    high, wide = volt.shape
    for weight in sweep_weights(SWEEPS):
        beside = (
            pltpu.roll(volt, 1, 0)
            + pltpu.roll(volt, high - 1, 0)
            + pltpu.roll(volt, 1, 1)
            + pltpu.roll(volt, wide - 1, 1)
        )
        volt = (1.0 - weight) * volt + weight * (right_side + beside * inv)
    return volt


GROUP = 8


def one_hot(rows, places):
    at = lax.broadcasted_iota(jnp.int32, (rows, LANES), 0)
    return jnp.concatenate(
        [
            jnp.where(at == places[i : i + 1, :], 1.0, 0.0).astype(BF16)
            for i in range(places.shape[0])
        ],
        axis=1,
    )


def pick_rows(found, places):
    at = lax.broadcasted_iota(jnp.int32, (found.shape[0], LANES), 0)
    return [
        jnp.sum(
            jnp.where(at == places[i : i + 1, :], found[:, i * LANES : (i + 1) * LANES], 0.0),
            axis=0,
            keepdims=True,
        )
        for i in range(places.shape[0])
    ]


def inner_body(node_ref, volt_ref, right_ref, inv_ref, row_out_ref, row_in_ref, out_ref, found_ref):
    rows, cols = volt_ref.shape
    top, bottom = swapped(row_in_ref[...], row_out_ref[...], place()[0])
    volt = swept(
        *(
            extended(ref[...], top, bottom, index)
            for index, ref in enumerate((volt_ref, right_ref, inv_ref))
        )
    )[:rows]
    out_ref[...] = volt
    col = lax.broadcasted_iota(jnp.int32, volt.shape, 1)
    volt = jnp.where((col >= SWEEPS) & (col < cols - SWEEPS), volt, 0.0)
    both = jnp.concatenate(halves(volt), axis=0)
    for first in range(0, node_ref.shape[0], GROUP):
        safe = jnp.maximum(node_ref[first : first + GROUP, :], 0)
        found = jnp.dot(both, one_hot(cols, safe % cols), preferred_element_type=F32)
        found = pick_rows(found[:rows] + found[rows:], safe // cols)
        for i, values in enumerate(found):
            found_ref[first + i : first + i + 1, :] = values


def sweep_body(copies, node_ref, cond_ref, start_ref, volt_ref, right_ref, inv_ref,
               row_out_ref, row_in_ref, col_out_ref, col_in_ref, inner_ref, found_ref,
               out_ref, current_ref):
    rows, cols = volt_ref.shape
    blocks = node_ref.shape[0]
    cap = current_ref.shape[1]
    quarter = LANES // 4
    strip = []
    top, bottom = swapped(row_in_ref[...], row_out_ref[...], place()[0])
    out_rows, high = col_in_ref.shape
    fill = jnp.zeros((LANES - out_rows, high), F32)
    wests, easts = (
        jnp.concatenate([part, fill], axis=0).T[: rows + 2 * HALO_ROWS]
        for part in swapped(col_in_ref[...], col_out_ref[...], place()[1])
    )
    lane = lax.broadcasted_iota(jnp.int32, easts.shape, 1)
    for index, ref in enumerate((volt_ref, right_ref, inv_ref)):
        own = extended(ref[...], top, bottom, index)
        at = index * SWEEPS
        west = pltpu.roll(wests, LANES - SWEEPS - at, 1)
        east = pltpu.roll(easts, 3 * quarter - at, 1)
        tail = pltpu.roll(own[:, cols - LANES :], LANES - quarter, 1)
        strip.append(
            jnp.where(
                lane < 3 * quarter,
                jnp.where(lane < quarter + quarter // 2, own[:, :LANES], tail),
                jnp.where(lane < 3 * quarter + quarter // 2, east, west),
            )
        )
    strip = swept(*strip)[:rows]
    lane = lane[:rows]
    inner = inner_ref[...]
    out_ref[...] = inner
    out_ref[:, :LANES] = jnp.where(lane < SWEEPS, strip, inner[:, :LANES])
    out_ref[:, cols - LANES :] = jnp.where(
        lane >= LANES - SWEEPS, pltpu.roll(strip, quarter, 1), inner[:, cols - LANES :]
    )
    turned = strip.T
    edge = jnp.concatenate([turned[:8], turned[3 * quarter - 8 : 3 * quarter]], axis=0)
    count = edge.shape[0]
    edge = jnp.concatenate(halves(edge), axis=0)
    dies = blocks // cap
    for first in range(0, blocks, GROUP):
        cut = slice(first, first + GROUP)
        node = node_ref[cut, :]
        safe = jnp.maximum(node, 0)
        row, col = safe // cols, safe % cols
        from_end = col - (cols - SWEEPS)
        at_edge = jnp.where(
            col < SWEEPS, col, jnp.where(from_end >= 0, from_end + count - SWEEPS, -1)
        )
        found = jnp.dot(edge, one_hot(rows, row), preferred_element_type=F32)
        found = jnp.concatenate(pick_rows(found[:count] + found[count:], at_edge), axis=0)
        cond = jnp.where(node >= 0, cond_ref[cut, :], 0.0)
        current = cond * (start_ref[cut, :] - (found_ref[cut, :] + found))
        for i in range(GROUP):
            block = first + i
            current_ref[block // cap, block % cap : block % cap + 1, :] = current[i : i + 1, :]
    for copy in range(1, copies):
        current_ref[copy * dies : (copy + 1) * dies] = current_ref[0:dies]


def local(
    die_volt,
    die_load,
    die_shunt,
    bump_node,
    bump_block,
    bump_cond,
    pkg_volt,
    pkg_diag,
    pkg_pattern,
    pkg_weight,
    block_coupling,
):
    die_count = lax.axis_size("die")
    group_count = lax.axis_size("grp")
    devices = die_count * group_count
    blocks = pkg_volt.shape[0]
    tiles = blocks // LANES
    neighbours = pkg_pattern.shape[0]
    slots = bump_block.shape[0]
    cap = slots // die_count
    rows, cols = die_volt.shape
    (spread,) = call(
        functools.partial(spread_body, cap, die_count, blocks),
        "spread_blocks",
        [shape(devices, 1, LANES, dtype=jnp.int32)],
        (bump_block.reshape(1, slots),),
        [VMEM],
    )
    ids = lax.all_to_all(
        spread, ("grp", "die"), split_axis=0, concat_axis=0, tiled=True
    ).reshape(devices, LANES)

    (picked,) = call(
        functools.partial(pick_body, cap, die_count),
        "pick_rows",
        [shape(slots, LANES)],
        (ids, pkg_volt),
        [SMEM, VMEM],
    )
    bump_start = lax.all_to_all(
        picked.reshape(die_count, cap, LANES), "die", split_axis=0, concat_axis=0, tiled=True
    ).reshape(slots, LANES)

    right_side, inv, *edges = call(
        functools.partial(scatter_body, cols),
        "scatter_bumps",
        [shape(rows, cols)] * 2 + [shape(3 * HALO_ROWS, cols)] * 2,
        (bump_node, bump_cond, bump_start, die_volt, die_load, die_shunt),
        [VMEM] * 6,
        work=3,
    )
    own = tiles // 2
    dma = pltpu.SemaphoreType.DMA
    plane = pltpu.VMEM(((own + 3) * LANES, 2 * LANES), BF16)
    range_rows = pltpu.VMEM(((own + 2) * LANES, LANES), F32)
    range_bands = pltpu.VMEM((own + 2, 2 * LANES, 2 * LANES), BF16)
    beside = swap(*edges, "grp")
    band, banded = call(
        bands_body,
        "package_bands",
        [shape(own + 2, 2 * LANES, 2 * LANES, dtype=BF16), shape(8, LANES)],
        (pkg_pattern, pkg_weight, right_side),
        [VMEM, VMEM, ANY],
        work=2,
    )

    edge_rows = -(-3 * SWEEPS // 8) * 8
    edge_cols = -(-(rows + 2 * HALO_ROWS) // LANES) * LANES
    edges = call(
        edge_body,
        "edge_columns",
        [shape(edge_rows, edge_cols)] * 2,
        (die_volt, right_side, inv, *beside, banded),
        [VMEM] * 5 + [ANY],
    )
    columns = swap(*edges, "die")

    inner, found = call(
        inner_body,
        "inner_sweeps",
        [shape(rows, cols), shape(slots, LANES)],
        (bump_node, die_volt, right_side, inv, *beside),
        [VMEM] * 6,
        work=3,
    )
    die_out, current = call(
        functools.partial(sweep_body, group_count),
        "sweeps",
        [shape(rows, cols), shape(devices, cap, LANES)],
        (
            bump_node, bump_cond, bump_start, die_volt, right_side, inv, *beside, *columns,
            inner, found,
        ),
        [VMEM] * 12,
        work=4,
    )
    pack_rows = 2 * LANES + 2 * neighbours
    base, pkg_inv, pack, near = call(
        prepare_body,
        "package_prepare",
        [
            shape((own + 2) * LANES, LANES),
            shape((own + 2) * LANES, LANES),
            shape(pack_rows, LANES),
            shape(2 * RADIUS, LANES),
        ],
        (pkg_pattern, pkg_weight, block_coupling, band, pkg_volt, pkg_diag, die_out),
        [HBM] * 7,
        [
            range_rows, range_rows, range_bands, range_rows, range_rows, plane,
            pltpu.VMEM((LANES, LANES), F32), pltpu.VMEM((neighbours, LANES), jnp.int32),
            pltpu.VMEM((2 * neighbours, LANES), F32), dma((6 + own // 8,)), dma((7 + own // 8,)),
        ],
        work=5,
        vmem=MOST_VMEM,
        out_specs=[HBM] * 4,
    )

    current = lax.all_to_all(
        current, ("grp", "die"), split_axis=0, concat_axis=0, tiled=True
    ).reshape(devices * cap, LANES)

    beside_end = [
        (g * die_count + a, g * die_count + b)
        for g in range(group_count)
        for d in range((g + 1) % 2, die_count - 1, 2)
        for a, b in ((d, d + 1), (d + 1, d))
    ]
    halo = lax.ppermute(pack, ("grp", "die"), beside_end)
    (inflow,) = call(
        functools.partial(ends_body, cap, tiles),
        "package_end",
        [shape(LANES, LANES)],
        (ids, current),
        [VMEM, VMEM],
    )
    halo_inflow = lax.ppermute(inflow, ("grp", "die"), beside_end)
    all_inflow, halo_band, halo_inv, edge_base = call(
        functools.partial(inflow_body, cap, tiles),
        "package_inflow",
        [
            shape((own + 2) * LANES, LANES),
            shape(2 * LANES, 2 * LANES, dtype=BF16),
            shape(LANES, LANES),
            shape(2 * LANES, LANES),
        ],
        (ids, current, block_coupling, pack, halo, near, inflow),
        [VMEM] * 6 + [ANY],
        [pltpu.VMEM((3 * LANES, 2 * LANES), BF16)],
        work=3,
    )
    half_out, pkg_out, picked = call(
        functools.partial(iterate_body, cap, die_count),
        "package_iterations",
        [shape(own * LANES, LANES), shape(blocks, LANES), shape(2 * slots, LANES)],
        (
            ids, block_coupling, halo_inflow, all_inflow, band, base, pkg_inv,
            halo_band, halo_inv, edge_base,
        ),
        [SMEM] + [VMEM] * 9,
        [pltpu.VMEM((own * LANES, LANES), F32), plane, plane, dma((2,))],
        work=10,
        vmem=24,
        out_specs=[HBM, HBM, VMEM],
    )
    pair = 2 * die_count
    parts = lax.all_to_all(
        picked.reshape(pair, cap, LANES),
        ("grp", "die"),
        split_axis=0,
        concat_axis=0,
        axis_index_groups=[
            [first + i for i in range(pair)] for first in range(0, devices, pair)
        ],
        tiled=True,
    ).reshape(2 * slots, LANES)
    other = lax.ppermute(half_out, "grp", [(g, g ^ 1) for g in range(group_count)])
    pkg_out, done = call(
        join_body,
        "join_halves",
        [shape(blocks, LANES), shape(8, LANES)],
        (other, pkg_out),
        [VMEM, HBM],
        [dma(())],
        out_specs=[HBM, VMEM],
        aliases={1: 0},
    )
    (bump_out,) = call(
        add_body, "add_parts", [shape(slots, LANES)], (parts, done), [VMEM, ANY]
    )
    return (die_out, pkg_out, bump_out)


def solution(mesh):
    return jax.shard_map(
        local,
        mesh=mesh,
        in_specs=(
            P("grp", "die"),
            P("grp", "die"),
            P("grp", "die"),
            P(("grp", "die"), None),
            P(("grp", "die")),
            P(("grp", "die"), None),
            P("die", None),
            P("die", None),
            P(None, "die"),
            P(None, "die"),
            P(),
        ),
        out_specs=(P("grp", "die"), P("die", None), P(("grp", "die"), None)),
        check_vma=False,
    )
```

```python
import functools
import math

import jax
import jax.numpy as jnp
from jax import lax
from jax.experimental import pallas as pl
from jax.experimental.pallas import tpu as pltpu
from jax.sharding import PartitionSpec as P

RADIUS = 32
SWEEPS = 4
ITERS = 4
LANES = 128
HALO_ROWS = 8
REACH = RADIUS * ITERS
WINDOW = LANES + 2 * RADIUS
F32 = jnp.float32
BF16 = jnp.bfloat16
MOST_VMEM = 57
VMEM = pl.BlockSpec(memory_space=pltpu.VMEM)
SMEM = pl.BlockSpec(memory_space=pltpu.SMEM)
ANY = pl.BlockSpec(memory_space=pl.ANY)
HBM = pl.BlockSpec(memory_space=pltpu.HBM)


def sweep_weights(sweeps):
    return [
        1.0 / (1.0 + 0.8 * math.cos(math.pi * (2 * index + 1) / (2 * sweeps)))
        for index in range(sweeps)
    ]


def call(
    body, name, outs, args, specs, scratch=(), work=1, vmem=16, out_specs=None, aliases=None
):
    bytes_accessed = sum(4 * math.prod(arg.shape) for arg in args)
    return pl.pallas_call(
        body,
        name=name,
        out_shape=outs,
        in_specs=specs,
        out_specs=out_specs or [VMEM] * len(outs),
        input_output_aliases=aliases or {},
        scratch_shapes=list(scratch),
        compiler_params=pltpu.CompilerParams(vmem_limit_bytes=vmem * 1024 * 1024),
        cost_estimate=pl.CostEstimate(
            flops=work * 10**9, bytes_accessed=bytes_accessed, transcendentals=0
        ),
    )(*args)


def place():
    return lax.axis_index("grp"), lax.axis_index("die")


def shape(*dims, dtype=F32):
    return jax.ShapeDtypeStruct(dims, dtype)


def halves(values):
    high = values.astype(BF16)
    low = (values - high.astype(F32)).astype(BF16)
    return high, low


def spread_body(cap, die_count, blocks, block_ref, out_ref):
    slots = block_ref.shape[1]
    block = jnp.concatenate(
        [block_ref[...], jnp.zeros((1, LANES - slots), jnp.int32)], axis=1
    )
    for die in range(die_count):
        row = (pltpu.roll(block, LANES - die * cap, 1) if die else block) - die * blocks
        for at in range(die, out_ref.shape[0], die_count):
            out_ref[at] = row


def asked_rows(cap, die_count, group, ids_ref):
    for die in range(die_count):
        for slot in range(cap):
            yield die * cap + slot, ids_ref[group * die_count + die, slot]


def pick_body(cap, die_count, ids_ref, plane_ref, out_ref):
    group, _ = place()
    for at, row in asked_rows(cap, die_count, group, ids_ref):
        out_ref[pl.ds(at, 1), :] = plane_ref[pl.ds(row, 1), :]


def build_band(first, pattern, weights):
    place = lax.broadcasted_iota(jnp.int32, (WINDOW, LANES), 0)
    band = None
    for k in range(pattern.shape[0]):
        hit = place == (pattern[k : k + 1, :] - first)
        term = jnp.where(hit, weights[k : k + 1, :], 0.0)
        band = term if band is None else band + term
    fill = jnp.zeros((2 * LANES - WINDOW, LANES), F32)
    return jnp.concatenate(halves(jnp.concatenate([band, fill], axis=0).T), axis=0)


def reciprocal(diag):
    safe = jnp.where(diag > 0.0, diag, 1.0)
    return jnp.where(diag > 0.0, 1.0 / safe, 0.0)


def span(tile, offset=0, size=LANES):
    return pl.ds(pl.multiple_of(tile * LANES + offset, RADIUS), size)


def mixer(coup_ref):
    mix = jnp.concatenate(halves(coup_ref[...]), axis=1)
    return jnp.concatenate([mix, mix], axis=0)


def clear_pads(ref):
    size = ref.shape[0]
    ref[0:RADIUS, :] = jnp.zeros((RADIUS, 2 * LANES), BF16)
    ref[size - LANES + RADIUS : size, :] = jnp.zeros((LANES - RADIUS, 2 * LANES), BF16)


def store(ref, tile, values):
    ref[span(tile, RADIUS, values.shape[0]), :] = jnp.concatenate(halves(values), axis=1)


def couple(source, tile, bands, mix, write):
    for at in range(0, len(bands), 4):
        couple_few(source, tile + at, bands[at : at + 4], mix, write)


def couple_few(source, tile, bands, mix, write):
    own = source[span(tile, RADIUS, len(bands) * LANES), :]
    within = jnp.dot(own, mix, preferred_element_type=F32)
    for i, band in enumerate(bands):
        window = source[span(tile + i, 0, 2 * LANES), :]
        beside = jnp.dot(band, window, preferred_element_type=F32)
        both = beside[:LANES] + beside[LANES:] + within[i * LANES : (i + 1) * LANES]
        write(tile + i, both[:, :LANES] + both[:, LANES:])


def in_chunks(first, count, body, size=16):
    whole = count // size

    if whole == 1:
        body(first, size)
    else:

        @pl.loop(0, whole)
        def _(chunk):
            body(first + chunk * size, size)

    if count % size:
        body(first + whole * size, count % size)


def half_of(tiles):
    half = lax.rem(sum(place()), 2)
    own = tiles // 2
    return half, own, half * own - 1


def bands_body(pat_ref, wgt_ref, after_ref, band_ref, done_ref):
    blocks = pat_ref.shape[1]
    half, own, shift = half_of(blocks // LANES)
    begin = place()[1] * blocks + shift * LANES

    def bands(tile, size):
        for i in range(size):
            lanes = pl.ds(pl.multiple_of((tile + i + shift) * LANES, LANES), LANES)
            band_ref[tile + i] = build_band(
                begin + (tile + i) * LANES - RADIUS, pat_ref[:, lanes], wgt_ref[:, lanes]
            )

    in_chunks(1 - half, own + 1, bands, 8)
    band_ref[half * (own + 1)] = jnp.zeros(band_ref.shape[1:], BF16)
    done_ref[...] = jnp.zeros(done_ref.shape, F32)


def prepare_body(
    pat_hbm, wgt_hbm, coup_hbm, band_hbm, volt_hbm, diag_hbm, after_ref,
    base_hbm, inv_hbm, pack_hbm, near_hbm,
    volt_ref, diag_ref, band_ref, base_ref, inv_ref, plane_ref, coup_ref, pat_ref, wgt_ref,
    sems, out_sems,
):
    blocks = volt_hbm.shape[0]
    half, own, shift = half_of(blocks // LANES)
    first, count, outer = 1 - half, own + 1, half * (own + 1)
    edge = 1 + half * (own - 1)
    known = pl.ds(pl.multiple_of(first * LANES, LANES), count * LANES)
    source = pl.ds(pl.multiple_of((first + shift) * LANES, LANES), count * LANES)
    lanes = pl.ds(pl.multiple_of((edge + shift) * LANES, LANES), LANES)
    neighbours = pat_hbm.shape[0]
    steps = [(at, min(8, count - at)) for at in range(0, count, 8)]

    def some(ref, at, size):
        return ref.at[pl.ds(first + at, size)]

    pairs = [
        (volt_hbm.at[source, :], volt_ref.at[known, :]),
        (coup_hbm, coup_ref),
        (some(band_hbm, *steps[0]), some(band_ref, *steps[0])),
        (diag_hbm.at[source, :], diag_ref.at[known, :]),
        (pat_hbm.at[:, lanes], pat_ref),
        (wgt_hbm.at[:, lanes], wgt_ref.at[neighbours : 2 * neighbours, :]),
    ] + [(some(band_hbm, *step), some(band_ref, *step)) for step in steps[1:]]
    loads = [
        pltpu.make_async_copy(hbm, ref, sems.at[i]) for i, (hbm, ref) in enumerate(pairs)
    ]
    for load in loads:
        load.start()
    writes = []

    def write_out(ref, hbm):
        writes.append(pltpu.make_async_copy(ref, hbm, out_sems.at[len(writes)]))
        writes[-1].start()

    def spread(tile, size):
        store(plane_ref, tile, volt_ref[span(tile, 0, size * LANES), :])

    def invert(tile, size):
        cut = span(tile, 0, size * LANES)
        inv_ref[cut, :] = reciprocal(diag_ref[cut, :])

    def base(tile, size):
        def write(tile, values):
            base_ref[span(tile), :] = values

        couple(plane_ref, tile, [band_ref[tile + i] for i in range(size)], mix, write)
        cut = span(tile, 0, size * LANES)
        write_out(base_ref.at[cut, :], base_hbm.at[cut, :])

    clear_pads(plane_ref)
    plane_ref[span(outer, RADIUS), :] = jnp.zeros((LANES, 2 * LANES), BF16)
    loads[0].wait()
    in_chunks(first, count, spread, 8)
    at = 2 * LANES
    write_out(volt_ref.at[span(edge), :], pack_hbm.at[0:LANES, :])
    write_out(
        volt_ref.at[2 * LANES : 2 * LANES + RADIUS, :], near_hbm.at[0:RADIUS, :]
    )
    write_out(
        volt_ref.at[own * LANES - RADIUS : own * LANES, :],
        near_hbm.at[RADIUS : 2 * RADIUS, :],
    )
    loads[1].wait()
    loads[2].wait()
    mix = mixer(coup_ref)
    base(first, steps[0][1])
    for load in loads[3:6]:
        load.wait()
    wgt_ref[0:neighbours, :] = pat_ref[...].astype(F32)
    write_out(wgt_ref, pack_hbm.at[at : at + 2 * neighbours, :])
    write_out(diag_ref.at[span(edge), :], pack_hbm.at[LANES:at, :])
    in_chunks(first, count, invert, 8)
    write_out(inv_ref.at[known, :], inv_hbm.at[known, :])
    for load, (start, size) in zip(loads[6:], steps[1:]):
        load.wait()
        base(first + start, size)
    for write in writes:
        write.wait()


def slot_places(cap, ids_ref):
    per_row = LANES // cap
    lane = lax.broadcasted_iota(jnp.int32, (1, LANES), 1)
    places = []
    for at in range(0, ids_ref.shape[0], per_row):
        total = None
        for i in range(per_row):
            row = jnp.where(lane < cap, ids_ref[at + i : at + i + 1, :], 0)
            row = pltpu.roll(row, i * cap, 1) if i else row
            total = row if total is None else total + row
        places.append(total)
    return places


def gather_inflow(places, first, rows, current):
    at = lax.broadcasted_iota(jnp.int32, (rows, LANES), 0) + first
    hits = [jnp.where(at == place, 1.0, 0.0).astype(BF16) for place in places]
    both = jnp.dot(jnp.concatenate(hits, axis=1), current, preferred_element_type=F32)
    return both[:, :LANES] + both[:, LANES:]


def ends_body(cap, tiles, ids_ref, current_ref, out_ref):
    half, _, _ = half_of(tiles)
    places = slot_places(cap, ids_ref)
    current = jnp.concatenate(halves(current_ref[...]), axis=1)
    out_ref[...] = gather_inflow(places, half * (tiles - 1) * LANES, LANES, current)


def inflow_body(
    cap, tiles, ids_ref, current_ref, coup_ref, own_ref, halo_ref, near_ref, after_ref,
    out_ref, band_ref, inv_ref, base_ref, plane_ref,
):
    half, own, shift = half_of(tiles)
    first, count = 1 - half, own + 1
    places = slot_places(cap, ids_ref)
    current = jnp.concatenate(halves(current_ref[...]), axis=1)

    def inflow(tile, size):
        cut = span(tile, 0, size * LANES)
        out_ref[cut, :] = gather_inflow(
            places, (tile + shift) * LANES, size * LANES, current
        )

    in_chunks(first, count, inflow)
    out_ref[span(half * (own + 1)), :] = jnp.zeros((LANES, LANES), F32)

    neighbours = (own_ref.shape[0] - 2 * LANES) // 2
    begin = (place()[1] * tiles + 2 * half * own - 1) * LANES
    packs = [jnp.where(half == at, halo_ref[...], own_ref[...]) for at in range(2)]
    at = 2 * LANES
    bands = []
    for tile, pack in enumerate(packs):
        bands.append(
            build_band(
                begin + tile * LANES - RADIUS,
                pack[at : at + neighbours].astype(jnp.int32),
                pack[at + neighbours : at + 2 * neighbours],
            )
        )
        store(plane_ref, tile, pack[:LANES])
    none = jnp.zeros((RADIUS, 2 * LANES), BF16)
    low, high = (
        jnp.concatenate(halves(near_ref[cut, :]), axis=1)
        for cut in (slice(0, RADIUS), slice(RADIUS, 2 * RADIUS))
    )
    clear_pads(plane_ref)
    end = 2 * LANES + RADIUS
    plane_ref[0:RADIUS, :] = jnp.where(half == 0, none, high)
    plane_ref[end : end + RADIUS, :] = jnp.where(half == 0, low, none)
    results = []
    couple(plane_ref, 0, bands, mixer(coup_ref), lambda tile, values: results.append(values))
    band_ref[...] = jnp.where(half == 0, bands[0], bands[1])
    inv_ref[...] = reciprocal(halo_ref[LANES : 2 * LANES, :])
    base_ref[0:LANES, :] = jnp.where(half == 0, results[0], results[1])
    base_ref[LANES:, :] = jnp.where(half == 0, results[1], results[0])


def iterate_body(
    cap, die_count, asked_ref, coup_ref, halo_ref, inflow_ref, band_ref, base_ref, inv_ref,
    halo_band_ref, halo_inv_ref, edge_base_ref, out_hbm, full_hbm, picked_ref, out_ref, here_ref, there_ref, sems,
):
    own = out_hbm.shape[0] // LANES
    half, _, _ = half_of(2 * own)
    first, count, outer = 1 - half, own + 1, half * (own + 1)
    edge = 1 + half * (own - 1)
    for ref in (here_ref, there_ref):
        clear_pads(ref)

    def start(tile, size):
        cut = span(tile, 0, size * LANES)
        store(here_ref, tile, -(inflow_ref[cut, :] + base_ref[cut, :]) * inv_ref[cut, :])

    in_chunks(first, count, start)
    halo_inv = halo_inv_ref[...]
    store(here_ref, outer, -(halo_ref[...] + edge_base_ref[0:LANES, :]) * halo_inv)
    cut = span(edge)
    store(here_ref, edge, -(inflow_ref[cut, :] + edge_base_ref[LANES:, :]) * inv_ref[cut, :])
    mix = mixer(coup_ref)
    refs = (here_ref, there_ref)
    for iteration in range(1, ITERS):
        source, target = refs[(iteration - 1) % 2], refs[iteration % 2]
        last = iteration == ITERS - 1

        def write(tile, coupled, target=target, last=last):
            values = -(inflow_ref[span(tile), :] + coupled) * inv_ref[span(tile), :]
            if last:
                out_ref[span(tile - 1), :] = values
            else:
                store(target, tile, values)

        def step(tile, size, source=source, write=write):
            bands = [band_ref[tile + i] for i in range(size)]
            couple(source, tile, bands, mix, write)

        def final(tile, size, step=step):
            step(tile, size)
            cut = span(tile - 1, 0, size * LANES)
            whole = span(half * own + tile - 1, 0, size * LANES)
            pltpu.make_async_copy(out_ref.at[cut, :], out_hbm.at[cut, :], sems.at[0]).start()
            pltpu.make_async_copy(out_ref.at[cut, :], full_hbm.at[whole, :], sems.at[1]).start()

        def write_halo(tile, coupled, target=target):
            store(target, tile, -(halo_ref[...] + coupled) * halo_inv)

        if last:
            in_chunks(1, own, final)
        else:
            in_chunks(first, count, step)
            couple(source, outer, [halo_band_ref[...]], mix, write_halo)

    base_row = half * own * LANES
    group, _ = place()
    pair = group - lax.rem(group, 2)
    for member in range(2):
        offset = member * (picked_ref.shape[0] // 2)
        for at, row in asked_rows(cap, die_count, pair + member, asked_ref):
            row = row - base_row
            inside = (row >= 0) & (row < own * LANES)
            safe = jnp.clip(row, 0, own * LANES - 1)
            values = out_ref[pl.ds(safe, 1), :]
            picked_ref[pl.ds(offset + at, 1), :] = jnp.where(inside, values, 0.0)
    pltpu.make_async_copy(out_ref, out_hbm, sems.at[0]).wait()
    pltpu.make_async_copy(out_ref, full_hbm.at[0 : own * LANES, :], sems.at[1]).wait()


def join_body(other_ref, full_in_hbm, full_hbm, done_ref, sem):
    rows = other_ref.shape[0]
    half, _, _ = half_of(2 * rows // LANES)
    start = pl.multiple_of((1 - half) * rows, LANES)
    copy = pltpu.make_async_copy(other_ref, full_hbm.at[pl.ds(start, rows), :], sem)
    copy.start()
    done_ref[...] = jnp.zeros(done_ref.shape, F32)
    copy.wait()


def add_body(parts_ref, after_ref, out_ref):
    rows = out_ref.shape[0]
    out_ref[...] = parts_ref[0:rows, :] + parts_ref[rows:, :]


def scatter_body(cols, node_ref, cond_ref, start_ref, volt_ref, load_ref, shunt_ref,
                 right_ref, inv_ref, inner_ref, outer_ref):
    blocks = node_ref.shape[0]
    rows = volt_ref.shape[0]
    group = 8
    row_at = lax.broadcasted_iota(jnp.int32, (rows, LANES), 0)
    col_at = lax.broadcasted_iota(jnp.int32, (cols, LANES), 0)
    total = jnp.zeros((4 * rows, cols), F32)
    for first in range(0, blocks, group):
        node = node_ref[first : first + group, :]
        live = node >= 0
        cond = jnp.where(live, cond_ref[first : first + group, :], 0.0)
        flow = cond * start_ref[first : first + group, :]
        safe = jnp.where(live, node, 0)
        row, col = safe // cols, safe % cols
        parts = halves(cond) + halves(flow)
        left, right = [], []
        for i in range(group):
            spot = jnp.where(row_at == row[i : i + 1, :], 1.0, 0.0).astype(BF16)
            left.append(
                jnp.concatenate([spot * part[i : i + 1, :] for part in parts], axis=0)
            )
            right.append(jnp.where(col_at == col[i : i + 1, :], 1.0, 0.0).astype(BF16))
        total = total + lax.dot_general(
            jnp.concatenate(left, axis=1),
            jnp.concatenate(right, axis=1),
            (((1,), (1,)), ((), ())),
            preferred_element_type=F32,
        )
    gsum = total[:rows] + total[rows : 2 * rows]
    inject = total[2 * rows : 3 * rows] + total[3 * rows :]
    inv = 1.0 / (4.0 + shunt_ref[...] + gsum)
    right_side = (inject - load_ref[...]) * inv
    right_ref[...] = right_side
    inv_ref[...] = inv
    volt = volt_ref[...]
    top, bottom = (
        jnp.concatenate([volt[cut], right_side[cut], inv[cut]], axis=0)
        for cut in (slice(0, HALO_ROWS), slice(rows - HALO_ROWS, rows))
    )
    swap_parts(inner_ref, outer_ref, place()[0], top, bottom)


def swap_parts(inner_ref, outer_ref, mine, first, last):
    even = lax.rem(mine, 2) == 0
    inner_ref[...] = jnp.where(even, last, first)
    outer_ref[...] = jnp.where(even, first, last)


def swapped(inner, outer, mine):
    even = lax.rem(mine, 2) == 0
    return jnp.where(even, outer, inner), jnp.where(even, inner, outer)


def swap(inner, outer, axis):
    count = lax.axis_size(axis)

    def pairs(start):
        return [
            pair
            for i in range(start, count - 1, 2)
            for pair in ((i, i + 1), (i + 1, i))
        ]

    return lax.ppermute(outer, axis, pairs(1)), lax.ppermute(inner, axis, pairs(0))


def extended(own, top, bottom, index):
    cut = slice(index * HALO_ROWS, (index + 1) * HALO_ROWS)
    return jnp.concatenate([own, bottom[cut], top[cut]], axis=0)


def edge_body(
    volt_ref, right_ref, inv_ref, outer_ref, inner_ref, after_ref, west_ref, east_ref
):
    cols = volt_ref.shape[1]
    top, bottom = swapped(inner_ref[...], outer_ref[...], place()[0])
    out_rows, high = west_ref.shape
    west, east = None, None
    for index, ref in enumerate((volt_ref, right_ref, inv_ref)):
        whole = extended(ref[...], top, bottom, index)
        lane = lax.broadcasted_iota(jnp.int32, (whole.shape[0], LANES), 1)
        head, tail = whole[:, :LANES], whole[:, cols - LANES :]
        at = index * SWEEPS
        head = pltpu.roll(head, at, 1) if at else head
        tail = pltpu.roll(tail, at + SWEEPS, 1)
        west = head if west is None else jnp.where(lane >= at, head, west)
        east = tail if east is None else jnp.where(lane >= at, tail, east)
    fill = jnp.zeros((high - west.shape[0], LANES), F32)
    west, east = (
        jnp.concatenate([part, fill], axis=0).T[:out_rows] for part in (west, east)
    )
    swap_parts(west_ref, east_ref, place()[1], west, east)


def swept(volt, right_side, inv):
    high, wide = volt.shape
    for weight in sweep_weights(SWEEPS):
        beside = (
            pltpu.roll(volt, 1, 0)
            + pltpu.roll(volt, high - 1, 0)
            + pltpu.roll(volt, 1, 1)
            + pltpu.roll(volt, wide - 1, 1)
        )
        volt = (1.0 - weight) * volt + weight * (right_side + beside * inv)
    return volt


GROUP = 8


def one_hot(rows, places):
    at = lax.broadcasted_iota(jnp.int32, (rows, LANES), 0)
    return jnp.concatenate(
        [
            jnp.where(at == places[i : i + 1, :], 1.0, 0.0).astype(BF16)
            for i in range(places.shape[0])
        ],
        axis=1,
    )


def pick_rows(found, places):
    at = lax.broadcasted_iota(jnp.int32, (found.shape[0], LANES), 0)
    return [
        jnp.sum(
            jnp.where(at == places[i : i + 1, :], found[:, i * LANES : (i + 1) * LANES], 0.0),
            axis=0,
            keepdims=True,
        )
        for i in range(places.shape[0])
    ]


def inner_body(node_ref, volt_ref, right_ref, inv_ref, row_out_ref, row_in_ref, out_ref, found_ref):
    rows, cols = volt_ref.shape
    top, bottom = swapped(row_in_ref[...], row_out_ref[...], place()[0])
    volt = swept(
        *(
            extended(ref[...], top, bottom, index)
            for index, ref in enumerate((volt_ref, right_ref, inv_ref))
        )
    )[:rows]
    out_ref[...] = volt
    col = lax.broadcasted_iota(jnp.int32, volt.shape, 1)
    volt = jnp.where((col >= SWEEPS) & (col < cols - SWEEPS), volt, 0.0)
    both = jnp.concatenate(halves(volt), axis=0)
    for first in range(0, node_ref.shape[0], GROUP):
        safe = jnp.maximum(node_ref[first : first + GROUP, :], 0)
        found = jnp.dot(both, one_hot(cols, safe % cols), preferred_element_type=F32)
        found = pick_rows(found[:rows] + found[rows:], safe // cols)
        for i, values in enumerate(found):
            found_ref[first + i : first + i + 1, :] = values


def sweep_body(copies, node_ref, cond_ref, start_ref, volt_ref, right_ref, inv_ref,
               row_out_ref, row_in_ref, col_out_ref, col_in_ref, inner_ref, found_ref,
               out_ref, current_ref):
    rows, cols = volt_ref.shape
    blocks = node_ref.shape[0]
    cap = current_ref.shape[1]
    quarter = LANES // 4
    strip = []
    top, bottom = swapped(row_in_ref[...], row_out_ref[...], place()[0])
    out_rows, high = col_in_ref.shape
    fill = jnp.zeros((LANES - out_rows, high), F32)
    wests, easts = (
        jnp.concatenate([part, fill], axis=0).T[: rows + 2 * HALO_ROWS]
        for part in swapped(col_in_ref[...], col_out_ref[...], place()[1])
    )
    lane = lax.broadcasted_iota(jnp.int32, easts.shape, 1)
    for index, ref in enumerate((volt_ref, right_ref, inv_ref)):
        own = extended(ref[...], top, bottom, index)
        at = index * SWEEPS
        west = pltpu.roll(wests, LANES - SWEEPS - at, 1)
        east = pltpu.roll(easts, 3 * quarter - at, 1)
        tail = pltpu.roll(own[:, cols - LANES :], LANES - quarter, 1)
        strip.append(
            jnp.where(
                lane < 3 * quarter,
                jnp.where(lane < quarter + quarter // 2, own[:, :LANES], tail),
                jnp.where(lane < 3 * quarter + quarter // 2, east, west),
            )
        )
    strip = swept(*strip)[:rows]
    lane = lane[:rows]
    inner = inner_ref[...]
    out_ref[...] = inner
    out_ref[:, :LANES] = jnp.where(lane < SWEEPS, strip, inner[:, :LANES])
    out_ref[:, cols - LANES :] = jnp.where(
        lane >= LANES - SWEEPS, pltpu.roll(strip, quarter, 1), inner[:, cols - LANES :]
    )
    turned = strip.T
    edge = jnp.concatenate([turned[:8], turned[3 * quarter - 8 : 3 * quarter]], axis=0)
    count = edge.shape[0]
    edge = jnp.concatenate(halves(edge), axis=0)
    dies = blocks // cap
    for first in range(0, blocks, GROUP):
        cut = slice(first, first + GROUP)
        node = node_ref[cut, :]
        safe = jnp.maximum(node, 0)
        row, col = safe // cols, safe % cols
        from_end = col - (cols - SWEEPS)
        at_edge = jnp.where(
            col < SWEEPS, col, jnp.where(from_end >= 0, from_end + count - SWEEPS, -1)
        )
        found = jnp.dot(edge, one_hot(rows, row), preferred_element_type=F32)
        found = jnp.concatenate(pick_rows(found[:count] + found[count:], at_edge), axis=0)
        cond = jnp.where(node >= 0, cond_ref[cut, :], 0.0)
        current = cond * (start_ref[cut, :] - (found_ref[cut, :] + found))
        for i in range(GROUP):
            block = first + i
            current_ref[block // cap, block % cap : block % cap + 1, :] = current[i : i + 1, :]
    for copy in range(1, copies):
        current_ref[copy * dies : (copy + 1) * dies] = current_ref[0:dies]


def local(
    die_volt,
    die_load,
    die_shunt,
    bump_node,
    bump_block,
    bump_cond,
    pkg_volt,
    pkg_diag,
    pkg_pattern,
    pkg_weight,
    block_coupling,
):
    die_count = lax.axis_size("die")
    group_count = lax.axis_size("grp")
    devices = die_count * group_count
    blocks = pkg_volt.shape[0]
    tiles = blocks // LANES
    neighbours = pkg_pattern.shape[0]
    slots = bump_block.shape[0]
    cap = slots // die_count
    rows, cols = die_volt.shape
    (spread,) = call(
        functools.partial(spread_body, cap, die_count, blocks),
        "spread_blocks",
        [shape(devices, 1, LANES, dtype=jnp.int32)],
        (bump_block.reshape(1, slots),),
        [VMEM],
    )
    ids = lax.all_to_all(
        spread, ("grp", "die"), split_axis=0, concat_axis=0, tiled=True
    ).reshape(devices, LANES)

    (picked,) = call(
        functools.partial(pick_body, cap, die_count),
        "pick_rows",
        [shape(slots, LANES)],
        (ids, pkg_volt),
        [SMEM, VMEM],
    )
    bump_start = lax.all_to_all(
        picked.reshape(die_count, cap, LANES), "die", split_axis=0, concat_axis=0, tiled=True
    ).reshape(slots, LANES)

    right_side, inv, *edges = call(
        functools.partial(scatter_body, cols),
        "scatter_bumps",
        [shape(rows, cols)] * 2 + [shape(3 * HALO_ROWS, cols)] * 2,
        (bump_node, bump_cond, bump_start, die_volt, die_load, die_shunt),
        [VMEM] * 6,
        work=3,
    )
    own = tiles // 2
    dma = pltpu.SemaphoreType.DMA
    plane = pltpu.VMEM(((own + 3) * LANES, 2 * LANES), BF16)
    range_rows = pltpu.VMEM(((own + 2) * LANES, LANES), F32)
    range_bands = pltpu.VMEM((own + 2, 2 * LANES, 2 * LANES), BF16)
    beside = swap(*edges, "grp")
    band, banded = call(
        bands_body,
        "package_bands",
        [shape(own + 2, 2 * LANES, 2 * LANES, dtype=BF16), shape(8, LANES)],
        (pkg_pattern, pkg_weight, right_side),
        [VMEM, VMEM, ANY],
        work=2,
    )

    edge_rows = -(-3 * SWEEPS // 8) * 8
    edge_cols = -(-(rows + 2 * HALO_ROWS) // LANES) * LANES
    edges = call(
        edge_body,
        "edge_columns",
        [shape(edge_rows, edge_cols)] * 2,
        (die_volt, right_side, inv, *beside, banded),
        [VMEM] * 5 + [ANY],
    )
    columns = swap(*edges, "die")

    inner, found = call(
        inner_body,
        "inner_sweeps",
        [shape(rows, cols), shape(slots, LANES)],
        (bump_node, die_volt, right_side, inv, *beside),
        [VMEM] * 6,
        work=3,
    )
    die_out, current = call(
        functools.partial(sweep_body, group_count),
        "sweeps",
        [shape(rows, cols), shape(devices, cap, LANES)],
        (
            bump_node, bump_cond, bump_start, die_volt, right_side, inv, *beside, *columns,
            inner, found,
        ),
        [VMEM] * 12,
        work=4,
    )
    pack_rows = 2 * LANES + 2 * neighbours
    base, pkg_inv, pack, near = call(
        prepare_body,
        "package_prepare",
        [
            shape((own + 2) * LANES, LANES),
            shape((own + 2) * LANES, LANES),
            shape(pack_rows, LANES),
            shape(2 * RADIUS, LANES),
        ],
        (pkg_pattern, pkg_weight, block_coupling, band, pkg_volt, pkg_diag, die_out),
        [HBM] * 7,
        [
            range_rows, range_rows, range_bands, range_rows, range_rows, plane,
            pltpu.VMEM((LANES, LANES), F32), pltpu.VMEM((neighbours, LANES), jnp.int32),
            pltpu.VMEM((2 * neighbours, LANES), F32), dma((6 + own // 8,)), dma((7 + own // 8,)),
        ],
        work=5,
        vmem=MOST_VMEM,
        out_specs=[HBM] * 4,
    )

    current = lax.all_to_all(
        current, ("grp", "die"), split_axis=0, concat_axis=0, tiled=True
    ).reshape(devices * cap, LANES)

    beside_end = [
        (g * die_count + a, g * die_count + b)
        for g in range(group_count)
        for d in range((g + 1) % 2, die_count - 1, 2)
        for a, b in ((d, d + 1), (d + 1, d))
    ]
    halo = lax.ppermute(pack, ("grp", "die"), beside_end)
    (inflow,) = call(
        functools.partial(ends_body, cap, tiles),
        "package_end",
        [shape(LANES, LANES)],
        (ids, current),
        [VMEM, VMEM],
    )
    halo_inflow = lax.ppermute(inflow, ("grp", "die"), beside_end)
    all_inflow, halo_band, halo_inv, edge_base = call(
        functools.partial(inflow_body, cap, tiles),
        "package_inflow",
        [
            shape((own + 2) * LANES, LANES),
            shape(2 * LANES, 2 * LANES, dtype=BF16),
            shape(LANES, LANES),
            shape(2 * LANES, LANES),
        ],
        (ids, current, block_coupling, pack, halo, near, inflow),
        [VMEM] * 6 + [ANY],
        [pltpu.VMEM((3 * LANES, 2 * LANES), BF16)],
        work=3,
    )
    half_out, pkg_out, picked = call(
        functools.partial(iterate_body, cap, die_count),
        "package_iterations",
        [shape(own * LANES, LANES), shape(blocks, LANES), shape(2 * slots, LANES)],
        (
            ids, block_coupling, halo_inflow, all_inflow, band, base, pkg_inv,
            halo_band, halo_inv, edge_base,
        ),
        [SMEM] + [VMEM] * 9,
        [pltpu.VMEM((own * LANES, LANES), F32), plane, plane, dma((2,))],
        work=10,
        vmem=24,
        out_specs=[HBM, HBM, VMEM],
    )
    pair = 2 * die_count
    parts = lax.all_to_all(
        picked.reshape(pair, cap, LANES),
        ("grp", "die"),
        split_axis=0,
        concat_axis=0,
        axis_index_groups=[
            [first + i for i in range(pair)] for first in range(0, devices, pair)
        ],
        tiled=True,
    ).reshape(2 * slots, LANES)
    other = lax.ppermute(half_out, "grp", [(g, g ^ 1) for g in range(group_count)])
    pkg_out, done = call(
        join_body,
        "join_halves",
        [shape(blocks, LANES), shape(8, LANES)],
        (other, pkg_out),
        [VMEM, HBM],
        [dma(())],
        out_specs=[HBM, VMEM],
        aliases={1: 0},
    )
    (bump_out,) = call(
        add_body, "add_parts", [shape(slots, LANES)], (parts, done), [VMEM, ANY]
    )
    return (die_out, pkg_out, bump_out)


def solution(mesh):
    return jax.shard_map(
        local,
        mesh=mesh,
        in_specs=(
            P("grp", "die"),
            P("grp", "die"),
            P("grp", "die"),
            P(("grp", "die"), None),
            P(("grp", "die")),
            P(("grp", "die"), None),
            P("die", None),
            P("die", None),
            P(None, "die"),
            P(None, "die"),
            P(),
        ),
        out_specs=(P("grp", "die"), P("die", None), P(("grp", "die"), None)),
        check_vma=False,
    )
```
